32 devices in a mesh: groups: 2 (over x), pos: 8 (over z, y), head: 2 (over core).
Axes of the slice: x: 2, y: 2, z: 4, core: 2. Of those that a mesh axis runs over, the one named last changes fastest.
Arguments:
- enc_keys: bfloat16 [8192, 2048], P(('groups', 'pos'), 'head'), parts along dimension 0, may hold values from -64 to 64
- enc_values: bfloat16 [8192, 2048], P(('groups', 'pos'), 'head'), parts along dimension 0, may hold values from -6 to 6
- input_ids: int32 [8192], P(('groups', 'pos')), parts along dimension 0, may hold values from 0 to 2
- latent_queries: bfloat16 [4096, 2048], P('groups', 'head'), parts along dimension 0, may hold values from -40 to 40
- latent_array: bfloat16 [4096, 2048], P(('groups', 'pos')), parts along dimension 0, may hold values from -0.29882812 to 0.29882812
- w_out: bfloat16 [2048, 2048], P('head', 'pos'), may hold values from -0.125 to 0.125
- norm_gain: float32 [2048], replicated, may hold values from 0.1 to 1.9
- w_key: bfloat16 [2048, 2048], P('pos', 'head'), may hold values from -0.125 to 0.125
- w_value: bfloat16 [2048, 2048], P('pos', 'head'), may hold values from -0.125 to 0.125
- query_features: bfloat16 [8192, 2048], P(('groups', 'pos'), 'head'), parts along dimension 0, may hold values from -120 to 120
- query_ids: int32 [8192], P(('groups', 'pos')), parts along dimension 0, may hold values from 0 to 2
- query_table: bfloat16 [3, 2048], P(None, 'head'), may hold values from -6 to 6
- enc_bias: float32 [3, 16], P(None, 'head'), may hold values from -2 to 2
- query_counts: int32 [6], P('groups'), parts along dimension 0, may hold values from 512 to 1364
Outputs:
- latents_out: float32 [4096, 2048], P(('groups', 'pos'), 'head'), parts along dimension 0
- decoded: float32 [8192, 2048], P(('groups', 'pos'), 'head'), parts along dimension 0
The draws below stay inside these ranges and needn't reach their ends.
There are 2 independent parts, one for each index of `groups`. The reference program is written for one: setup_inputs(seed, part) draws one part's arguments, and reference() takes and returns one part's arrays. A program takes and returns all parts, laid end to end along the dimension named above; an argument that names none is the same for every part. Nothing has to cross between parts.
All inputs are finite; a program needn't handle non-finite values.
Results may differ from the reference program's by a relative error of at most 0.03.
Values may be sent and summed in bfloat16 or wider, within the bound.
No kernel may reach another device: no remote copies, remote signals or barrier semaphores. Data moves between devices by JAX's collectives and lax.ppermute only.
A program may use at most 128 MiB of HBM per device.

```python
import jax
import jax.numpy as jnp
from jax import lax

D = 2048
HEAD_DIM = 128
LATENTS = 2048
MODS = 3
HEADS = 16
TOKENS = 4096


def latent_and_keys(key):
    base_queries = jnp.clip(jax.random.normal(jax.random.fold_in(key, 101), (LATENTS, D), jnp.float32), -5.0, 5.0)
    base_keys = jnp.clip(jax.random.normal(jax.random.fold_in(key, 102), (TOKENS, D), jnp.float32), -5.0, 5.0)
    return (base_queries, base_keys)


def draw_latent_queries(key, part):
    base_queries, base_keys = latent_and_keys(key)
    return (2.5 * base_queries).astype(jnp.bfloat16)


def draw_enc_keys(key, part):
    base_queries, base_keys = latent_and_keys(key)
    return base_keys.astype(jnp.bfloat16)


def draw_query_features(key, part):
    key = jax.random.fold_in(key, 3)
    base = jnp.clip(jax.random.normal(jax.random.fold_in(key, 7), (TOKENS, D), jnp.float32), -6.0, 6.0)
    return (2.0 * base).astype(jnp.bfloat16)


def touch_ends(entries, rng, low, top_value):
    longest = entries.shape.index(max(entries.shape))
    spots = []
    for shift in (0, 1):
        where = [jax.random.randint(jax.random.fold_in(rng, axis), (), 0, length) for axis, length in enumerate(entries.shape)]
        where[longest] = (where[longest] + shift) % entries.shape[longest]
        spots.append(tuple(where))
    return entries.at[spots[0]].set(low).at[spots[1]].set(top_value)


def block_scale(rng, dims, pieces, low, top_value):
    level = 1.0
    for dim, shards_of in pieces:
        draws = jax.random.uniform(jax.random.fold_in(jax.random.fold_in(rng, 6), dim), (shards_of,), jnp.float32, low / len(pieces), top_value / len(pieces))
        level = level * jnp.repeat(jnp.exp(draws), dims[dim] // shards_of).reshape((-1,) + (1,) * (len(dims) - 1 - dim))
    return level


def normal_values(own_key, shape, width, bound, shards=(), kind=jnp.bfloat16):
    loudness = block_scale(own_key, shape, shards, -0.22, 0.18) if shards else 1.0
    entries = jax.random.normal(own_key, shape, jnp.float32) * width * loudness
    return jnp.minimum(jnp.maximum(entries, -bound), bound).astype(kind)


def setup_inputs(seed: int = 0, part: int = 0) -> dict:
    key_list = jax.random.split(jax.random.key(seed), 15)
    part_keys = jax.random.split(jax.random.fold_in(key_list[14], part), 15)
    enc_keys = draw_enc_keys(jax.random.fold_in(jax.random.fold_in(key_list[14], part), 71), part)
    enc_values = normal_values(part_keys[1], (TOKENS, D), 1.0, 6.0, ((0, 8), (1, 2)))
    input_ids = touch_ends(jax.random.randint(part_keys[2], (TOKENS,), 0, MODS), jax.random.fold_in(part_keys[2], 1), 0, MODS - 1).astype(jnp.int32)
    latent_queries = draw_latent_queries(jax.random.fold_in(jax.random.fold_in(key_list[14], part), 71), part)
    latent_array = normal_values(part_keys[4], (LATENTS, D), 0.05, 0.29882812, ((0, 8),))
    w_out = normal_values(key_list[5], (D, D), D ** -0.5, 0.125, ((0, 2), (1, 8)))
    norm_gain = jnp.clip(1.0 + 0.18 * jax.random.normal(key_list[6], (D,), jnp.float32), 0.1, 1.9)
    w_key = normal_values(key_list[7], (D, D), D ** -0.5, 0.125, ((0, 8), (1, 2)))
    w_value = normal_values(key_list[8], (D, D), D ** -0.5, 0.125, ((0, 8), (1, 2)))
    query_features = draw_query_features(jax.random.fold_in(jax.random.fold_in(key_list[14], part), 71), part)
    query_ids = touch_ends(jax.random.randint(part_keys[10], (TOKENS,), 0, MODS), jax.random.fold_in(part_keys[10], 1), 0, MODS - 1).astype(jnp.int32)
    query_table = normal_values(key_list[11], (MODS, D), 1.0, 6.0, ((1, 2),))
    enc_bias = jnp.clip(jax.random.uniform(key_list[12], (MODS, HEADS), jnp.float32, -2.0, 2.0) * block_scale(key_list[12], (MODS, HEADS), ((1, 2),), -0.4, 0.0), -2.0, 2.0)
    query_counts = jax.random.randint(part_keys[13], (MODS,), TOKENS // 8, TOKENS // 3).astype(jnp.int32)
    return dict(enc_keys=enc_keys, enc_values=enc_values, input_ids=input_ids, latent_queries=latent_queries, latent_array=latent_array, w_out=w_out, norm_gain=norm_gain, w_key=w_key, w_value=w_value, query_features=query_features, query_ids=query_ids, query_table=query_table, enc_bias=enc_bias, query_counts=query_counts)


norm_eps = 1e-06

def head_slice(matrix, head_index):
    return lax.dynamic_slice_in_dim(matrix, (head_index * HEAD_DIM).astype(jnp.int32), HEAD_DIM, 1)

def attend_full(queries, keys, values, score_bias):
    scores = jnp.dot(queries, keys.T, preferred_element_type=jnp.float32) * HEAD_DIM ** (-0.5) + score_bias
    highest = lax.optimization_barrier(jnp.max(scores, axis=1, keepdims=True))
    weights = jnp.exp(scores - highest)
    totals = lax.optimization_barrier(jnp.sum(weights, axis=1, keepdims=True))
    return jnp.dot(weights.astype(jnp.bfloat16), values, preferred_element_type=jnp.float32) / totals

def reference(enc_keys, enc_values, input_ids, latent_queries, latent_array, w_out, norm_gain, w_key, w_value, query_features, query_ids, query_table, enc_bias, query_counts):
    heads = D // HEAD_DIM
    modality = jnp.arange(MODS, dtype=jnp.int32)
    in_onehot = (input_ids[:, None] == modality[None, :]).astype(jnp.float32)
    bias_rows = jnp.dot(in_onehot, enc_bias, precision=lax.Precision.HIGHEST)

    def encode_head(head_index):
        column = lax.dynamic_slice_in_dim(bias_rows, head_index.astype(jnp.int32), 1, 1)
        return attend_full(head_slice(latent_queries, head_index), head_slice(enc_keys, head_index), head_slice(enc_values, head_index), column.T)
    per_head = lax.map(encode_head, jnp.arange(heads, dtype=jnp.int32))
    attended = jnp.transpose(per_head, (1, 0, 2)).reshape(LATENTS, D).astype(jnp.bfloat16)
    updated = latent_array.astype(jnp.float32) + jnp.dot(attended, w_out, preferred_element_type=jnp.float32)
    mean_square = lax.optimization_barrier(jnp.mean(updated * updated, axis=1, keepdims=True))
    latents_out = updated * lax.rsqrt(mean_square + norm_eps) * norm_gain
    normed = latents_out.astype(jnp.bfloat16)
    latent_keys = jnp.dot(normed, w_key, preferred_element_type=jnp.float32).astype(jnp.bfloat16)
    latent_values = jnp.dot(normed, w_value, preferred_element_type=jnp.float32).astype(jnp.bfloat16)
    q_onehot = (query_ids[:, None] == modality[None, :]).astype(jnp.int32)
    lookup = jnp.dot(q_onehot.astype(jnp.bfloat16), query_table, preferred_element_type=jnp.float32)
    queries = (query_features.astype(jnp.float32) + lookup).astype(jnp.bfloat16)
    earlier_counts = jnp.cumsum(q_onehot, axis=0) - q_onehot
    ranked = lax.optimization_barrier(jnp.sum(earlier_counts * q_onehot, axis=1))
    limits = lax.optimization_barrier(jnp.sum(q_onehot * query_counts[None, :], axis=1))
    kept_rows = ranked < limits

    def decode_head(head_index):
        return attend_full(head_slice(queries, head_index), head_slice(latent_keys, head_index), head_slice(latent_values, head_index), 0.0)
    dec_heads = lax.map(decode_head, jnp.arange(heads, dtype=jnp.int32))
    dec_full = jnp.transpose(dec_heads, (1, 0, 2)).reshape(TOKENS, D)
    decoded = jnp.where(kept_rows[:, None], dec_full, 0.0)
    return (latents_out, decoded)
```

```python
import functools

import jax
import jax.numpy as jnp
from jax import lax
from jax.experimental import pallas as pl
from jax.experimental.pallas import tpu as pltpu
from jax.sharding import PartitionSpec as P

HEAD_DIM = 128


norm_eps = 1e-06


def prefix(shard, axis, combine, identity):
    peers, place = (lax.axis_size(axis), lax.axis_index(axis))
    everything = lax.all_gather(shard, axis)
    start = jnp.broadcast_to(jnp.asarray(identity, shard.dtype), shard.shape)

    def step(k, before):
        reached = k < place
        new = combine(before, everything[k])
        return jnp.where(reached, new, before)

    return lax.fori_loop(0, peers, step, start)


def plain_on_device(
    enc_keys,
    enc_values,
    input_ids,
    latent_queries,
    latent_array,
    w_out,
    norm_gain,
    w_key,
    w_value,
    query_features,
    query_ids,
    query_table,
    enc_bias,
    query_counts,
):
    tok_rows = enc_keys.shape[0]
    half_width = enc_keys.shape[1]
    local_heads = half_width // HEAD_DIM
    score_scale = HEAD_DIM ** (-0.5)
    modality = jnp.arange(enc_bias.shape[0], dtype=jnp.int32)
    in_onehot = (input_ids[:, None] == modality[None, :]).astype(jnp.float32)
    bias_rows = jnp.dot(in_onehot, enc_bias, precision=lax.Precision.HIGHEST)
    bias_heads = bias_rows.T[:, None, :]
    keys_split = enc_keys.reshape(tok_rows, local_heads, HEAD_DIM)
    values_split = enc_values.reshape(tok_rows, local_heads, HEAD_DIM)
    lat_total = latent_queries.shape[0]
    block_rows = min(512, lat_total)
    query_blocks = latent_queries.reshape(
        lat_total // block_rows, block_rows, local_heads, HEAD_DIM
    )

    def encode_block(block_queries):
        scores = (
            jnp.einsum(
                "nha,tha->hnt", block_queries, keys_split, preferred_element_type=jnp.float32
            )
            * score_scale
            + bias_heads
        )
        highest = jnp.max(scores, axis=2)
        weights = jnp.exp(scores - highest[:, :, None])
        totals = jnp.sum(weights, axis=2)
        summed = jnp.einsum(
            "hnt,tha->nha",
            weights.astype(jnp.bfloat16),
            values_split,
            preferred_element_type=jnp.float32,
        )
        return (highest.T, totals.T, summed.reshape(block_rows, half_width))

    block_max, block_tot, block_acc = lax.map(encode_block, query_blocks)
    row_highest = block_max.reshape(lat_total, local_heads)
    row_totals = block_tot.reshape(lat_total, local_heads)
    row_sums = block_acc.reshape(lat_total, half_width)
    own_rows = latent_array.shape[0]
    global_max = lax.pmax(row_highest, "pos")
    factor = jnp.exp(row_highest - global_max)
    scaled_sums = (row_sums.reshape(lat_total, local_heads, HEAD_DIM) * factor[:, :, None]).reshape(
        lat_total, half_width
    )
    totals, summed = (
        lax.psum_scatter(row_totals * factor, "pos", scatter_dimension=0, tiled=True),
        lax.psum_scatter(scaled_sums, "pos", scatter_dimension=0, tiled=True),
    )
    summed = summed.reshape(own_rows, local_heads, HEAD_DIM)
    attended = (summed / totals[:, :, None]).reshape(own_rows, half_width).astype(jnp.bfloat16)
    partial_value = jnp.dot(
        attended,
        lax.all_gather(w_out, "pos", axis=1, tiled=True),
        preferred_element_type=jnp.float32,
    )
    offset = lax.axis_index("head") * half_width
    projected = lax.psum(partial_value, "head")
    updated = latent_array.astype(jnp.float32) + projected
    mean_square = jnp.mean(updated * updated, axis=1, keepdims=True)
    normed_full = updated * lax.rsqrt(mean_square + norm_eps) * norm_gain
    normed = normed_full.astype(jnp.bfloat16)
    own_cols = lax.dynamic_slice_in_dim(normed_full, offset, half_width, 1)
    pieces = (
        lax.all_gather(w_key, "pos", axis=0, tiled=True),
        lax.all_gather(w_value, "pos", axis=0, tiled=True),
    )
    key_sum = jnp.dot(normed, pieces[0], preferred_element_type=jnp.float32)
    value_sum = jnp.dot(normed, pieces[1], preferred_element_type=jnp.float32)
    latent_keys = key_sum.astype(jnp.bfloat16)
    latent_values = value_sum.astype(jnp.bfloat16)
    q_onehot = (query_ids[:, None] == modality[None, :]).astype(jnp.int32)
    local_counts = jnp.sum(q_onehot, axis=0)
    before = prefix(
        local_counts, "pos", lambda earlier, later: earlier + later, jnp.zeros_like(local_counts)
    )
    within = jnp.cumsum(q_onehot, axis=0) - q_onehot
    ranked = jnp.sum((within + before[None, :]) * q_onehot, axis=1)
    limits = jnp.sum(q_onehot * query_counts[None, :], axis=1)
    kept_rows = ranked < limits
    lookup = jnp.dot(q_onehot.astype(jnp.bfloat16), query_table, preferred_element_type=jnp.float32)
    queries = (
        (query_features.astype(jnp.float32) + lookup)
        .astype(jnp.bfloat16)
        .reshape(tok_rows, local_heads, HEAD_DIM)
    )

    def fold_rows(running, key_rows, value_rows):
        running_max, running_tot, running_acc = running
        key_heads = key_rows.reshape(key_rows.shape[0], local_heads, HEAD_DIM)
        value_heads = value_rows.reshape(value_rows.shape[0], local_heads, HEAD_DIM)
        scores = (
            jnp.einsum("tha,rha->htr", queries, key_heads, preferred_element_type=jnp.float32)
            * score_scale
        )
        new_max = jnp.maximum(running_max, jnp.max(scores, axis=2))
        fade = jnp.exp(running_max - new_max)
        weights = jnp.exp(scores - new_max[:, :, None])
        new_tot = running_tot * fade + jnp.sum(weights, axis=2)
        new_acc = running_acc * fade[:, :, None] + jnp.einsum(
            "htr,rha->hta",
            weights.astype(jnp.bfloat16),
            value_heads,
            preferred_element_type=jnp.float32,
        )
        return (new_max, new_tot, new_acc)

    start_state = (
        jnp.full((local_heads, tok_rows), -jnp.inf, jnp.float32),
        jnp.zeros((local_heads, tok_rows), jnp.float32),
        jnp.zeros((local_heads, tok_rows, HEAD_DIM), jnp.float32),
    )
    running = start_state
    pieces = (
        lax.all_gather(latent_keys, "pos", axis=0, tiled=True),
        lax.all_gather(latent_values, "pos", axis=0, tiled=True),
    )
    row_count = pieces[0].shape[0]
    key_blocks = pieces[0].reshape(row_count // 512, 512, half_width)
    value_blocks = pieces[1].reshape(row_count // 512, 512, half_width)

    def scan_step(state, pair):
        return (fold_rows(state, pair[0], pair[1]), None)

    running, ignored = lax.scan(scan_step, running, (key_blocks, value_blocks))
    final_max, final_tot, final_acc = running
    dec_heads = final_acc / final_tot[:, :, None]
    dec_rows = jnp.transpose(dec_heads, (1, 0, 2)).reshape(tok_rows, half_width)
    decoded = jnp.where(kept_rows[:, None], dec_rows, 0.0)
    return (own_cols, decoded)


LANES = 128
NT = (((1,), (1,)), ((), ()))


def params(mib):
    return pltpu.CompilerParams(vmem_limit_bytes=mib << 20)


def cost(flops, nbytes, exps=0):
    return pl.CostEstimate(flops=int(flops), bytes_accessed=int(nbytes), transcendentals=int(exps))


def whole(shape):
    return pl.BlockSpec(shape, lambda *args: (0,) * len(shape))


def pack_lse(lse, lane, heads):
    high = lse.astype(jnp.bfloat16)
    rest = lse - high.astype(jnp.float32)
    mid = rest.astype(jnp.bfloat16)
    low = (rest - mid.astype(jnp.float32)).astype(jnp.bfloat16)
    picked = jnp.where(
        lane < heads,
        high.astype(jnp.float32),
        jnp.where(lane < 2 * heads, mid.astype(jnp.float32), low.astype(jnp.float32)),
    )
    return picked.astype(jnp.bfloat16)


def unpack_lse(stats, h, heads):
    return (
        stats[:, h : h + 1]
        + stats[:, heads + h : heads + h + 1]
        + stats[:, 2 * heads + h : 2 * heads + h + 1]
    )


def encode_kernel(heads, ids_ref, q_ref, k_ref, v_ref, bias_ref, out_ref):
    rows = q_ref.shape[0]
    width = heads * HEAD_DIM
    lane = lax.broadcasted_iota(jnp.int32, (rows, LANES), 1)
    lse_all = jnp.zeros((rows, LANES), jnp.float32)
    for h in range(heads):
        cols = slice(h * HEAD_DIM, (h + 1) * HEAD_DIM)
        scores = lax.dot_general(
            q_ref[:, cols], k_ref[:, cols], NT, preferred_element_type=jnp.float32
        )
        scores = scores * (HEAD_DIM**-0.5) + bias_ref[h : h + 1, :]
        highest = jnp.max(scores, axis=1, keepdims=True)
        weights = jnp.exp(scores - highest)
        totals = jnp.sum(weights, axis=1, keepdims=True)
        summed = jnp.dot(
            weights.astype(jnp.bfloat16), v_ref[:, cols], preferred_element_type=jnp.float32
        )
        out_ref[:, cols] = (summed * (1.0 / totals)).astype(jnp.bfloat16)
        lse_all = jnp.where(lane % heads == h, highest + jnp.log(totals), lse_all)
    out_ref[:, width:] = pack_lse(lse_all, lane, heads)


def encode(block, latent_queries, keys, values, bias, rows):
    tokens, width = keys.shape
    heads = width // HEAD_DIM
    grid_spec = pltpu.PrefetchScalarGridSpec(
        num_scalar_prefetch=1,
        grid=(1,),
        in_specs=[
            pl.BlockSpec((rows, width), lambda i, ids: (ids[0], 0)),
            whole((tokens, width)),
            whole((tokens, width)),
            whole((heads, tokens)),
        ],
        out_specs=whole((rows, width + LANES)),
    )
    return pl.pallas_call(
        functools.partial(encode_kernel, heads),
        grid_spec=grid_spec,
        out_shape=jax.ShapeDtypeStruct((rows, width + LANES), jnp.bfloat16),
        compiler_params=params(24),
        cost_estimate=cost(
            8 * rows * tokens * width, 4 * tokens * width + 4 * rows * width, heads * rows * tokens
        ),
        name="encode_rows",
    )(block.reshape(1), latent_queries, keys, values, bias)


def merge_parts(heads, refs, h):
    width = heads * HEAD_DIM
    lses = [unpack_lse(r[:, width:].astype(jnp.float32), h, heads) for r in refs]
    top = functools.reduce(jnp.maximum, lses)
    factors = [jnp.exp(v - top) for v in lses]
    total = functools.reduce(jnp.add, factors)
    inverse = 1.0 / total
    cols = slice(h * HEAD_DIM, (h + 1) * HEAD_DIM)
    merged = functools.reduce(
        jnp.add,
        [r[:, cols].astype(jnp.float32) * (f * inverse) for r, f in zip(refs, factors)],
    )
    return merged, top + jnp.log(total)


def merge_kernel(heads, a_ref, b_ref, out_ref):
    rows = a_ref.shape[0]
    lane = lax.broadcasted_iota(jnp.int32, (rows, LANES), 1)
    lse_all = jnp.zeros((rows, LANES), jnp.float32)
    for h in range(heads):
        merged, lse = merge_parts(heads, (a_ref, b_ref), h)
        out_ref[:, h * HEAD_DIM : (h + 1) * HEAD_DIM] = merged.astype(jnp.bfloat16)
        lse_all = jnp.where(lane % heads == h, lse, lse_all)
    out_ref[:, heads * HEAD_DIM :] = pack_lse(lse_all, lane, heads)


def merge(a, b):
    heads = (a.shape[1] - LANES) // HEAD_DIM
    return pl.pallas_call(
        functools.partial(merge_kernel, heads),
        out_shape=jax.ShapeDtypeStruct(a.shape, a.dtype),
        compiler_params=params(16),
        cost_estimate=cost(4 * a.size, 6 * a.size, 2 * a.shape[0] * heads),
        name="merge_rows",
    )(a, b)


def project_kernel(heads, count, slots, ids_ref, *refs):
    parts, w_refs, out_ref, att_ref = (
        refs[:count],
        refs[count : count + 2 * slots],
        refs[count + 2 * slots],
        refs[count + 2 * slots + 1],
    )
    for h in range(heads):
        merged, ignored = merge_parts(heads, parts, h)
        att_ref[:, h * HEAD_DIM : (h + 1) * HEAD_DIM] = merged.astype(jnp.bfloat16)
    depth, cols = w_refs[0].shape
    for j in range(slots):
        total = None
        for k in range(2):
            start = pl.multiple_of(ids_ref[slots + k] * depth, depth)
            term = jnp.dot(
                att_ref[:, pl.ds(start, depth)],
                w_refs[k * slots + j][...],
                preferred_element_type=jnp.float32,
            )
            total = term if total is None else total + term
        place = pl.multiple_of(ids_ref[j] * cols, cols)
        out_ref[:, pl.ds(place, cols)] = total


def project(ids, parts, w_slots):
    rows, packed = parts[0].shape
    width = packed - LANES
    slots = len(w_slots) // 2
    out_cols = slots * w_slots[0].shape[1]
    grid_spec = pltpu.PrefetchScalarGridSpec(
        num_scalar_prefetch=1,
        grid=(1,),
        in_specs=[whole(v.shape) for v in (*parts, *w_slots)],
        out_specs=whole((rows, out_cols)),
        scratch_shapes=[pltpu.VMEM((rows, width), jnp.bfloat16)],
    )
    return pl.pallas_call(
        functools.partial(project_kernel, width // HEAD_DIM, len(parts), slots),
        grid_spec=grid_spec,
        out_shape=jax.ShapeDtypeStruct((rows, out_cols), jnp.float32),
        compiler_params=params(32),
        cost_estimate=cost(2 * rows * width * out_cols, 2 * width * out_cols + 4 * rows * out_cols),
        name="project_rows",
    )(ids, *parts, *w_slots)


def norm_kernel(ids_ref, mine_ref, theirs_ref, latent_ref, gain_ref, out_ref, normed_ref, full_ref):
    updated = latent_ref[...].astype(jnp.float32) + (mine_ref[...] + theirs_ref[...])
    mean_square = jnp.mean(updated * updated, axis=1, keepdims=True)
    full_ref[...] = updated * lax.rsqrt(mean_square + norm_eps) * gain_ref[...]
    half = out_ref.shape[1]
    own = full_ref[:, pl.ds(pl.multiple_of(ids_ref[0] * half, half), half)]
    out_ref[...] = own
    normed_ref[...] = own.astype(jnp.bfloat16)


def normalise(place, mine, theirs, latent_array, gain):
    rows, width = mine.shape
    half = width // 2
    grid_spec = pltpu.PrefetchScalarGridSpec(
        num_scalar_prefetch=1,
        grid=(1,),
        in_specs=[whole((rows, width))] * 3 + [whole((1, width))],
        out_specs=[whole((rows, half))] * 2,
        scratch_shapes=[pltpu.VMEM((rows, width), jnp.float32)],
    )
    return pl.pallas_call(
        norm_kernel,
        grid_spec=grid_spec,
        out_shape=[
            jax.ShapeDtypeStruct((rows, half), jnp.float32),
            jax.ShapeDtypeStruct((rows, half), jnp.bfloat16),
        ],
        compiler_params=params(32),
        cost_estimate=cost(6 * rows * width, 13 * rows * width),
        name="norm_rows",
    )(place.reshape(1), mine, theirs, latent_array, gain)


def decode_kernel(slots, pieces, first, last, ids_ref, *refs):
    mine = refs[:pieces]
    theirs = refs[pieces : 2 * pieces]
    wk_ref, wv_ref, q_ref = refs[2 * pieces : 2 * pieces + 3]
    rest = list(refs[2 * pieces + 3 :])
    if not first:
        old_max_ref, old_acc_ref = rest[:2]
        rest = rest[2:]
    if last:
        kept_ref, out_ref = rest[:2]
        rest = rest[2:]
    else:
        max_ref, acc_ref = rest[:2]
        rest = rest[2:]
    plain_ref, slot_ref = rest
    half = mine[0].shape[1]
    rows = mine[0].shape[0]

    @pl.when(pl.program_id(0) == 0)
    def arrange():
        place = ids_ref[0]
        for r in range(pieces):
            band = slice(r * rows, (r + 1) * rows)
            plain_ref[band, pl.ds(pl.multiple_of(place * half, half), half)] = mine[r][...]
            plain_ref[band, pl.ds(pl.multiple_of((1 - place) * half, half), half)] = theirs[r][...]
        depth = 2 * half // slots
        for j in range(slots):
            start = pl.multiple_of(ids_ref[1 + j] * depth, depth)
            slot_ref[:, j * depth : (j + 1) * depth] = plain_ref[:, pl.ds(start, depth)]

    normed = slot_ref[...]
    keys = jnp.dot(normed, wk_ref[0], preferred_element_type=jnp.float32).astype(jnp.bfloat16)
    values = jnp.dot(normed, wv_ref[0], preferred_element_type=jnp.float32).astype(jnp.bfloat16)
    ones = jnp.ones((keys.shape[0], LANES), jnp.bfloat16)
    for h in range(keys.shape[1] // HEAD_DIM):
        cols = slice(h * HEAD_DIM, (h + 1) * HEAD_DIM)
        wide = slice(2 * h * HEAD_DIM, 2 * (h + 1) * HEAD_DIM)
        scores = lax.dot_general(
            q_ref[:, cols], keys[:, cols], NT, preferred_element_type=jnp.float32
        ) * (HEAD_DIM**-0.5)
        highest = jnp.max(scores, axis=1, keepdims=True)
        if not first:
            old_max = old_max_ref[:, cols]
            new_max = jnp.maximum(old_max, highest)
            highest = new_max[:, :1]
            fade = jnp.exp(old_max - new_max)
        weights = jnp.exp(scores - highest).astype(jnp.bfloat16)
        summed = jnp.dot(
            weights,
            jnp.concatenate([values[:, cols], ones], axis=1),
            preferred_element_type=jnp.float32,
        )
        acc, tot = summed[:, :HEAD_DIM], summed[:, HEAD_DIM:]
        if not first:
            old = old_acc_ref[:, wide]
            acc = acc + old[:, :HEAD_DIM] * fade
            tot = tot + old[:, HEAD_DIM:] * fade
        if last:
            out_ref[:, cols] = jnp.where(kept_ref[...] > 0.0, acc * (1.0 / tot), 0.0)
        else:
            if first:
                new_max = jnp.broadcast_to(highest, acc.shape)
            max_ref[:, cols] = new_max
            acc_ref[:, wide] = jnp.concatenate([acc, tot], axis=1)


def decode(ids, mine, theirs, weights, queries, state, kept):
    first, last = state is None, kept is not None
    tokens, width = queries.shape
    rows, half = mine[0].shape
    depth = weights.shape[1]
    slots = ids.shape[0] - 5
    pair = 2 * HEAD_DIM
    steps = width // pair
    pieces = len(mine)

    def pair_of(i, ids):
        return (0, ids[1 + slots + i])

    def wide_block():
        return pl.BlockSpec((tokens, 2 * pair), pair_of)

    def pair_block():
        return pl.BlockSpec((tokens, pair), pair_of)

    per = steps // 2
    in_specs = [whole((rows, half))] * (2 * pieces) + [
        pl.BlockSpec((1, depth, pair), lambda i, ids: (i // per, 0, i % per)),
        pl.BlockSpec((1, depth, pair), lambda i, ids: (i // per, 0, per + i % per)),
        pair_block(),
    ]
    args = [*mine, *theirs, weights, weights, queries]
    if not first:
        in_specs += [pair_block(), wide_block()]
        args += list(state)
    if last:
        in_specs += [whole(kept.shape)]
        args += [kept]
        out_specs = pair_block()
        out_shape = jax.ShapeDtypeStruct((tokens, width), jnp.float32)
    else:
        out_specs = [pair_block(), wide_block()]
        out_shape = [
            jax.ShapeDtypeStruct((tokens, width), jnp.float32),
            jax.ShapeDtypeStruct((tokens, 2 * width), jnp.float32),
        ]
    latents = rows * pieces
    grid_spec = pltpu.PrefetchScalarGridSpec(
        num_scalar_prefetch=1,
        grid=(steps,),
        in_specs=in_specs,
        out_specs=out_specs,
        scratch_shapes=[
            pltpu.VMEM((latents, 2 * half), jnp.bfloat16),
            pltpu.VMEM((latents, 2 * half), jnp.bfloat16),
        ],
    )
    return pl.pallas_call(
        functools.partial(decode_kernel, slots, pieces, first, last),
        grid_spec=grid_spec,
        out_shape=out_shape,
        compiler_params=params(48),
        cost_estimate=cost(
            4 * latents * depth * width + 8 * tokens * latents * width,
            4 * depth * width + 24 * tokens * width,
            tokens * latents * (width // HEAD_DIM),
        ),
        name="decode_rows",
    )(ids, *args)


def swap_perm(size):
    return [(i, i ^ 1) for i in range(size)]


def shift_perm(size, k):
    far = size // 2
    return [(((z + k) % far) * 2 + y, z * 2 + y) for z in range(far) for y in range(2)]


def far_order(far):
    return sorted(range(1, far), key=lambda k: -min(k, far - k))


def gather_near(shard, pos):
    got = {(0, 0): shard, (0, 1): lax.ppermute(shard, "pos", swap_perm(pos))}
    for k in far_order(pos // 2):
        got[(k, 0)] = lax.ppermute(shard, "pos", shift_perm(pos, k))
        got[(k, 1)] = lax.ppermute(got[(k, 0)], "pos", swap_perm(pos))
    return got


def fast_on_device(
    sizes,
    enc_keys,
    enc_values,
    input_ids,
    latent_queries,
    latent_array,
    w_out,
    norm_gain,
    w_key,
    w_value,
    query_features,
    query_ids,
    query_table,
    enc_bias,
    query_counts,
):
    groups, pos = sizes
    far = pos // 2
    g = lax.axis_index("groups")
    p = lax.axis_index("pos")
    place = lax.axis_index("head")
    z, y, x = p // 2, p % 2, g % 2
    rows = latent_array.shape[0]
    half_width = enc_keys.shape[1]
    modality = jnp.arange(enc_bias.shape[0], dtype=jnp.int32)
    slots = [(k, j) for k in range(far) for j in range(2)]
    slot_pos = [((z + k) % far) * 2 + (y ^ j) for k, j in slots]

    def share(shard):
        got = gather_near(shard, pos)
        near = [got[s] for s in slots]
        return near + [lax.ppermute(v, "groups", swap_perm(groups)) for v in near]

    out_depth = w_out.shape[0] // 2
    out_slots = share(lax.dynamic_slice_in_dim(w_out, x * out_depth, out_depth, 0))
    kv_cols = half_width // 2
    kv_shard = jnp.concatenate(
        [
            lax.dynamic_slice_in_dim(w_key, x * kv_cols, kv_cols, 1),
            lax.dynamic_slice_in_dim(w_value, x * kv_cols, kv_cols, 1),
        ],
        axis=1,
    )
    kv_slots = share(kv_shard)
    n = len(slots)
    kv_weights = jnp.stack(
        [jnp.concatenate(kv_slots[:n], axis=0), jnp.concatenate(kv_slots[n:], axis=0)]
    )

    in_onehot = (input_ids[:, None] == modality[None, :]).astype(jnp.float32)
    bias = jnp.dot(in_onehot, enc_bias, precision=lax.Precision.HIGHEST).T
    order = far_order(far) + [0]
    run = lambda block: encode(block, latent_queries, enc_keys, enc_values, bias, rows)
    sent, kept_parts = {}, {}
    for k in order:
        z_to = (z - k) % far
        sent[k] = lax.ppermute(run(z_to * 2 + (1 - y)), "pos", swap_perm(pos))
    for k in order:
        z_to = (z - k) % far
        kept_parts[k] = merge(run(z_to * 2 + y), sent[k])
    parts = [kept_parts[0]]
    for k in order[:-1]:
        parts.append(lax.ppermute(kept_parts[k], "pos", shift_perm(pos, k)))

    out_ids = jnp.stack(slot_pos + [x, 1 - x]).astype(jnp.int32)
    partial_value = project(out_ids, parts, out_slots)
    theirs = lax.ppermute(partial_value, "head", swap_perm(2))
    own_cols, normed = normalise(place, partial_value, theirs, latent_array, norm_gain[None, :])

    q_onehot = (query_ids[:, None] == modality[None, :]).astype(jnp.int32)
    local_counts = jnp.sum(q_onehot, axis=0)
    reached, step = local_counts, 1
    while step < pos:
        reached = reached + lax.ppermute(
            reached, "pos", [(i, i + step) for i in range(pos - step)]
        )
        step *= 2
    before = reached - local_counts
    within = jnp.cumsum(q_onehot, axis=0) - q_onehot
    ranked = jnp.sum((within + before[None, :]) * q_onehot, axis=1)
    limits = jnp.sum(q_onehot * query_counts[None, :], axis=1)
    kept = (ranked < limits).astype(jnp.float32)[:, None]
    lookup = jnp.dot(q_onehot.astype(jnp.bfloat16), query_table, preferred_element_type=jnp.float32)
    queries = (query_features.astype(jnp.float32) + lookup).astype(jnp.bfloat16)

    steps = half_width // (2 * HEAD_DIM)
    per = steps // 2
    pair_ids = [(x ^ (i // per)) * per + i % per for i in range(steps)]
    dec_ids = jnp.stack([place, *slot_pos, *pair_ids]).astype(jnp.int32)
    got = gather_near(normed, pos)
    state = None
    order = [0] + far_order(far)[1:] + far_order(far)[:1]
    for k in order:
        mine = [got[(k, 0)], got[(k, 1)]]
        others = [lax.ppermute(v, "head", swap_perm(2)) for v in mine]
        state = decode(
            dec_ids, mine, others, kv_weights, queries, state, kept if k == order[-1] else None
        )
    return (own_cols, state)


def on_device(sizes, *args):
    groups, pos, head = sizes
    w_key, w_out, half_width = args[7], args[5], args[0].shape[1]
    fits = (
        head == 2
        and groups % 2 == 0
        and pos % 2 == 0
        and pos > 2
        and half_width == 1024
        and w_key.shape[0] % 256 == 0
        and w_out.shape[1] % 256 == 0
        and args[4].shape[0] % 128 == 0
        and args[0].shape[0] % 128 == 0
    )
    if fits:
        return fast_on_device((groups, pos), *args)
    return plain_on_device(*args)


def solution(mesh):
    return jax.shard_map(
        functools.partial(on_device, tuple(mesh.shape[a] for a in ("groups", "pos", "head"))),
        mesh=mesh,
        in_specs=(
            P(("groups", "pos"), "head"),
            P(("groups", "pos"), "head"),
            P(("groups", "pos")),
            P("groups", "head"),
            P(("groups", "pos"), None),
            P("head", "pos"),
            P(),
            P("pos", "head"),
            P("pos", "head"),
            P(("groups", "pos"), "head"),
            P(("groups", "pos")),
            P(None, "head"),
            P(None, "head"),
            P("groups"),
        ),
        out_specs=(P(("groups", "pos"), "head"), P(("groups", "pos"), "head")),
        check_vma=False,
    )
```

```python
import functools

import jax
import jax.numpy as jnp
from jax import lax
from jax.experimental import pallas as pl
from jax.experimental.pallas import tpu as pltpu
from jax.sharding import PartitionSpec as P

HEAD_DIM = 128


norm_eps = 1e-06


def prefix(shard, axis, combine, identity):
    peers, place = (lax.axis_size(axis), lax.axis_index(axis))
    everything = lax.all_gather(shard, axis)
    start = jnp.broadcast_to(jnp.asarray(identity, shard.dtype), shard.shape)

    def step(k, before):
        reached = k < place
        new = combine(before, everything[k])
        return jnp.where(reached, new, before)

    return lax.fori_loop(0, peers, step, start)


def plain_on_device(
    enc_keys,
    enc_values,
    input_ids,
    latent_queries,
    latent_array,
    w_out,
    norm_gain,
    w_key,
    w_value,
    query_features,
    query_ids,
    query_table,
    enc_bias,
    query_counts,
):
    tok_rows = enc_keys.shape[0]
    half_width = enc_keys.shape[1]
    local_heads = half_width // HEAD_DIM
    score_scale = HEAD_DIM ** (-0.5)
    modality = jnp.arange(enc_bias.shape[0], dtype=jnp.int32)
    in_onehot = (input_ids[:, None] == modality[None, :]).astype(jnp.float32)
    bias_rows = jnp.dot(in_onehot, enc_bias, precision=lax.Precision.HIGHEST)
    bias_heads = bias_rows.T[:, None, :]
    keys_split = enc_keys.reshape(tok_rows, local_heads, HEAD_DIM)
    values_split = enc_values.reshape(tok_rows, local_heads, HEAD_DIM)
    lat_total = latent_queries.shape[0]
    block_rows = min(512, lat_total)
    query_blocks = latent_queries.reshape(
        lat_total // block_rows, block_rows, local_heads, HEAD_DIM
    )

    def encode_block(block_queries):
        scores = (
            jnp.einsum(
                "nha,tha->hnt", block_queries, keys_split, preferred_element_type=jnp.float32
            )
            * score_scale
            + bias_heads
        )
        highest = jnp.max(scores, axis=2)
        weights = jnp.exp(scores - highest[:, :, None])
        totals = jnp.sum(weights, axis=2)
        summed = jnp.einsum(
            "hnt,tha->nha",
            weights.astype(jnp.bfloat16),
            values_split,
            preferred_element_type=jnp.float32,
        )
        return (highest.T, totals.T, summed.reshape(block_rows, half_width))

    block_max, block_tot, block_acc = lax.map(encode_block, query_blocks)
    row_highest = block_max.reshape(lat_total, local_heads)
    row_totals = block_tot.reshape(lat_total, local_heads)
    row_sums = block_acc.reshape(lat_total, half_width)
    own_rows = latent_array.shape[0]
    global_max = lax.pmax(row_highest, "pos")
    factor = jnp.exp(row_highest - global_max)
    scaled_sums = (row_sums.reshape(lat_total, local_heads, HEAD_DIM) * factor[:, :, None]).reshape(
        lat_total, half_width
    )
    totals, summed = (
        lax.psum_scatter(row_totals * factor, "pos", scatter_dimension=0, tiled=True),
        lax.psum_scatter(scaled_sums, "pos", scatter_dimension=0, tiled=True),
    )
    summed = summed.reshape(own_rows, local_heads, HEAD_DIM)
    attended = (summed / totals[:, :, None]).reshape(own_rows, half_width).astype(jnp.bfloat16)
    partial_value = jnp.dot(
        attended,
        lax.all_gather(w_out, "pos", axis=1, tiled=True),
        preferred_element_type=jnp.float32,
    )
    offset = lax.axis_index("head") * half_width
    projected = lax.psum(partial_value, "head")
    updated = latent_array.astype(jnp.float32) + projected
    mean_square = jnp.mean(updated * updated, axis=1, keepdims=True)
    normed_full = updated * lax.rsqrt(mean_square + norm_eps) * norm_gain
    normed = normed_full.astype(jnp.bfloat16)
    own_cols = lax.dynamic_slice_in_dim(normed_full, offset, half_width, 1)
    pieces = (
        lax.all_gather(w_key, "pos", axis=0, tiled=True),
        lax.all_gather(w_value, "pos", axis=0, tiled=True),
    )
    key_sum = jnp.dot(normed, pieces[0], preferred_element_type=jnp.float32)
    value_sum = jnp.dot(normed, pieces[1], preferred_element_type=jnp.float32)
    latent_keys = key_sum.astype(jnp.bfloat16)
    latent_values = value_sum.astype(jnp.bfloat16)
    q_onehot = (query_ids[:, None] == modality[None, :]).astype(jnp.int32)
    local_counts = jnp.sum(q_onehot, axis=0)
    before = prefix(
        local_counts, "pos", lambda earlier, later: earlier + later, jnp.zeros_like(local_counts)
    )
    within = jnp.cumsum(q_onehot, axis=0) - q_onehot
    ranked = jnp.sum((within + before[None, :]) * q_onehot, axis=1)
    limits = jnp.sum(q_onehot * query_counts[None, :], axis=1)
    kept_rows = ranked < limits
    lookup = jnp.dot(q_onehot.astype(jnp.bfloat16), query_table, preferred_element_type=jnp.float32)
    queries = (
        (query_features.astype(jnp.float32) + lookup)
        .astype(jnp.bfloat16)
        .reshape(tok_rows, local_heads, HEAD_DIM)
    )

    def fold_rows(running, key_rows, value_rows):
        running_max, running_tot, running_acc = running
        key_heads = key_rows.reshape(key_rows.shape[0], local_heads, HEAD_DIM)
        value_heads = value_rows.reshape(value_rows.shape[0], local_heads, HEAD_DIM)
        scores = (
            jnp.einsum("tha,rha->htr", queries, key_heads, preferred_element_type=jnp.float32)
            * score_scale
        )
        new_max = jnp.maximum(running_max, jnp.max(scores, axis=2))
        fade = jnp.exp(running_max - new_max)
        weights = jnp.exp(scores - new_max[:, :, None])
        new_tot = running_tot * fade + jnp.sum(weights, axis=2)
        new_acc = running_acc * fade[:, :, None] + jnp.einsum(
            "htr,rha->hta",
            weights.astype(jnp.bfloat16),
            value_heads,
            preferred_element_type=jnp.float32,
        )
        return (new_max, new_tot, new_acc)

    start_state = (
        jnp.full((local_heads, tok_rows), -jnp.inf, jnp.float32),
        jnp.zeros((local_heads, tok_rows), jnp.float32),
        jnp.zeros((local_heads, tok_rows, HEAD_DIM), jnp.float32),
    )
    running = start_state
    pieces = (
        lax.all_gather(latent_keys, "pos", axis=0, tiled=True),
        lax.all_gather(latent_values, "pos", axis=0, tiled=True),
    )
    row_count = pieces[0].shape[0]
    key_blocks = pieces[0].reshape(row_count // 512, 512, half_width)
    value_blocks = pieces[1].reshape(row_count // 512, 512, half_width)

    def scan_step(state, pair):
        return (fold_rows(state, pair[0], pair[1]), None)

    running, ignored = lax.scan(scan_step, running, (key_blocks, value_blocks))
    final_max, final_tot, final_acc = running
    dec_heads = final_acc / final_tot[:, :, None]
    dec_rows = jnp.transpose(dec_heads, (1, 0, 2)).reshape(tok_rows, half_width)
    decoded = jnp.where(kept_rows[:, None], dec_rows, 0.0)
    return (own_cols, decoded)


LANES = 128
EXTRA = 16
LOG2E = 1.4426950408889634
EXP2_SCALE = LOG2E * HEAD_DIM**-0.5
NT = (((1,), (1,)), ((), ()))


def params(mib):
    return pltpu.CompilerParams(vmem_limit_bytes=mib << 20)


def cost(flops, nbytes, exps=0):
    return pl.CostEstimate(flops=int(flops), bytes_accessed=int(nbytes), transcendentals=int(exps))


def whole(shape):
    return pl.BlockSpec(shape, lambda *args: (0,) * len(shape))


def pack_kernel(k_ref, v_ref, extra_ref, out_ref):
    tokens = k_ref.shape[0]
    out_ref[:tokens, :HEAD_DIM] = k_ref[...]
    out_ref[:tokens, HEAD_DIM:] = v_ref[...]
    out_ref[tokens:, :] = extra_ref[...]


def pack(keys, values, extra):
    tokens, width = keys.shape
    heads = width // HEAD_DIM
    column = pl.BlockSpec((tokens, HEAD_DIM), lambda h: (0, h))
    block = (tokens + EXTRA, 2 * HEAD_DIM)
    return pl.pallas_call(
        pack_kernel,
        grid=(heads,),
        in_specs=[column, column, whole(extra.shape)],
        out_specs=pl.BlockSpec(block, lambda h: (h, 0)),
        out_shape=jax.ShapeDtypeStruct((heads * block[0], block[1]), keys.dtype),
        compiler_params=params(16),
        cost_estimate=cost(0, 8 * tokens * width),
        name="pack_heads",
    )(keys, values, extra)


def encode_kernel(pos, tokens, ids_ref, q_ref, kv_ref, bias_ref, out_ref):
    rows = q_ref.shape[0]
    head = ids_ref[0]
    queries = q_ref[...]
    ones = jnp.ones((tokens, LANES), jnp.bfloat16)
    row_bits = kv_ref.shape[1]
    top = jnp.full((rows, 1), -jnp.inf, jnp.float32)
    acc = jnp.zeros((rows, 2 * HEAD_DIM), jnp.float32)
    for j in range(pos):
        base = j * (tokens + EXTRA)
        band = slice(base, base + tokens)
        scores = lax.dot_general(
            queries, kv_ref[band, :HEAD_DIM], NT, preferred_element_type=jnp.float32
        )
        tail = kv_ref[base + tokens : base + tokens + EXTRA, :].astype(jnp.float32)
        kind = jnp.concatenate([tail[r : r + 1] for r in range(tokens // row_bits)], axis=1)
        bias = jnp.zeros_like(kind)
        for m in range(bias_ref.shape[0]):
            bias = jnp.where(kind == m, bias_ref[m, head] * LOG2E, bias)
        scores = scores * EXP2_SCALE + bias
        new_top = jnp.maximum(top, jnp.max(scores, axis=1, keepdims=True))
        weights = jnp.exp2(scores - new_top).astype(jnp.bfloat16)
        acc = acc * jnp.exp2(top - new_top) + jnp.dot(
            weights,
            jnp.concatenate([kv_ref[band, HEAD_DIM:], ones], axis=1),
            preferred_element_type=jnp.float32,
        )
        top = new_top
    out_ref[...] = (acc[:, :HEAD_DIM] / acc[:, HEAD_DIM:]).astype(jnp.bfloat16)


def encode(head, latent_queries, kv, enc_bias, pos):
    latents = latent_queries.shape[0]
    tokens = kv.shape[0] // pos - EXTRA
    rows = min(512, latents)
    grid_spec = pltpu.PrefetchScalarGridSpec(
        num_scalar_prefetch=1,
        grid=(latents // rows,),
        in_specs=[
            pl.BlockSpec((rows, HEAD_DIM), lambda i, ids: (i, ids[0])),
            whole(kv.shape),
            pl.BlockSpec(memory_space=pltpu.SMEM),
        ],
        out_specs=pl.BlockSpec((rows, HEAD_DIM), lambda i, ids: (i, 0)),
    )
    return pl.pallas_call(
        functools.partial(encode_kernel, pos, tokens),
        grid_spec=grid_spec,
        out_shape=jax.ShapeDtypeStruct((latents, HEAD_DIM), jnp.bfloat16),
        compiler_params=params(32),
        cost_estimate=cost(
            16 * latents * tokens * pos * HEAD_DIM, 2 * kv.size, latents * tokens * pos
        ),
        name="encode_head",
    )(head.reshape(1), latent_queries, kv, enc_bias)


def project_kernel(heads, att_in_ref, w_ref, out_ref, att_ref):
    rows = att_ref.shape[0]
    shares, depth, _ = w_ref.shape

    @pl.when(pl.program_id(0) == 0)
    def arrange():
        for h in range(heads):
            att_ref[:, h * HEAD_DIM : (h + 1) * HEAD_DIM] = att_in_ref[h * rows : (h + 1) * rows, :]

    total = None
    for k in range(shares):
        term = jnp.dot(
            att_ref[:, k * depth : (k + 1) * depth], w_ref[k], preferred_element_type=jnp.float32
        )
        total = term if total is None else total + term
    out_ref[...] = total


def project(attended, w_all, rows, depth):
    heads = attended.shape[0] // rows
    shares, long, cols = w_all.shape
    steps = long // depth
    return pl.pallas_call(
        functools.partial(project_kernel, heads),
        grid=(steps,),
        in_specs=[
            whole(attended.shape),
            pl.BlockSpec((shares, depth, cols), lambda i: (0, i, 0)),
        ],
        out_specs=pl.BlockSpec((rows, cols), lambda i: (0, i)),
        out_shape=jax.ShapeDtypeStruct((rows, steps * cols), jnp.float32),
        scratch_shapes=[pltpu.VMEM((rows, heads * HEAD_DIM), jnp.bfloat16)],
        compiler_params=params(32),
        cost_estimate=cost(2 * rows * w_all.size, 2 * w_all.size + 4 * rows * steps * cols),
        name="project_rows",
    )(attended, w_all)


def norm_kernel(
    shares, band, ids_ref, mine_ref, theirs_ref, latent_ref, gain_ref, out_ref, normed_ref, full_ref
):
    updated = latent_ref[...].astype(jnp.float32) + (mine_ref[...] + theirs_ref[...])
    mean_square = jnp.mean(updated * updated, axis=1, keepdims=True)
    full_ref[...] = updated * lax.rsqrt(mean_square + norm_eps) * gain_ref[...]
    half = out_ref.shape[1]
    own = full_ref[:, pl.ds(pl.multiple_of(ids_ref[0] * half, half), half)]
    out_ref[...] = own
    normed = own.astype(jnp.bfloat16)
    count = half // (shares * band)
    for i in range(count):
        for k in range(shares):
            source = (i * shares + k) * band
            target = (k * count + i) * band
            normed_ref[:, target : target + band] = normed[:, source : source + band]


def normalise(place, mine, theirs, latent_array, gain, shares, band):
    rows, width = mine.shape
    half = width // 2
    grid_spec = pltpu.PrefetchScalarGridSpec(
        num_scalar_prefetch=1,
        grid=(1,),
        in_specs=[whole((rows, width))] * 3 + [whole((1, width))],
        out_specs=[whole((rows, half))] * 2,
        scratch_shapes=[pltpu.VMEM((rows, width), jnp.float32)],
    )
    return pl.pallas_call(
        functools.partial(norm_kernel, shares, band),
        grid_spec=grid_spec,
        out_shape=[
            jax.ShapeDtypeStruct((rows, half), jnp.float32),
            jax.ShapeDtypeStruct((rows, half), jnp.bfloat16),
        ],
        compiler_params=params(32),
        cost_estimate=cost(6 * rows * width, 13 * rows * width),
        name="norm_rows",
    )(place.reshape(1), mine, theirs, latent_array, gain)


def decode_kernel(shares, pieces, first, last, ids_ref, *refs):
    mine = refs[:pieces]
    theirs = refs[pieces : 2 * pieces]
    wk_ref, wv_ref, q_ref = refs[2 * pieces : 2 * pieces + 3]
    rest = list(refs[2 * pieces + 3 :])
    if not first:
        old_max_ref, old_acc_ref = rest[:2]
        rest = rest[2:]
    if last:
        kept_ref, out_ref = rest[:2]
        rest = rest[2:]
    else:
        max_ref, acc_ref = rest[:2]
        rest = rest[2:]
    (normed_ref,) = rest
    rows, half = mine[0].shape
    part = half // shares

    @pl.when(pl.program_id(0) == 0)
    def arrange():
        for r in range(pieces):
            band = slice(r * rows, (r + 1) * rows)
            for k in range(shares):
                cols = slice(k * part, (k + 1) * part)
                for source, which in ((mine[r], ids_ref[0]), (theirs[r], 1 - ids_ref[0])):
                    start = pl.multiple_of(k * 2 * part + which * part, part)
                    normed_ref[band, pl.ds(start, part)] = source[:, cols]

    normed = normed_ref[...]
    keys = jnp.dot(normed, wk_ref[...], preferred_element_type=jnp.float32).astype(jnp.bfloat16)
    values = jnp.dot(normed, wv_ref[...], preferred_element_type=jnp.float32).astype(jnp.bfloat16)
    ones = jnp.ones((keys.shape[0], LANES), jnp.bfloat16)
    for h in range(keys.shape[1] // HEAD_DIM):
        cols = slice(h * HEAD_DIM, (h + 1) * HEAD_DIM)
        wide = slice(2 * h * HEAD_DIM, 2 * (h + 1) * HEAD_DIM)
        scores = lax.dot_general(
            q_ref[:, cols], keys[:, cols], NT, preferred_element_type=jnp.float32
        )
        scores = scores * EXP2_SCALE
        highest = jnp.max(scores, axis=1, keepdims=True)
        if not first:
            old_max = old_max_ref[:, cols]
            new_max = jnp.maximum(old_max, highest)
            highest = new_max[:, :1]
            fade = jnp.exp2(old_max - new_max)
        weights = jnp.exp2(scores - highest).astype(jnp.bfloat16)
        summed = jnp.dot(
            weights,
            jnp.concatenate([values[:, cols], ones], axis=1),
            preferred_element_type=jnp.float32,
        )
        acc, tot = summed[:, :HEAD_DIM], summed[:, HEAD_DIM:]
        if not first:
            old = old_acc_ref[:, wide]
            acc = acc + old[:, :HEAD_DIM] * fade
            tot = tot + old[:, HEAD_DIM:] * fade
        if last:
            out_ref[:, cols] = jnp.where(kept_ref[...] > 0.0, acc / tot, 0.0)
        else:
            if first:
                new_max = jnp.broadcast_to(highest, acc.shape)
            max_ref[:, cols] = new_max
            acc_ref[:, wide] = jnp.concatenate([acc, tot], axis=1)


def decode(place, mine, theirs, weights, queries, state, kept, shares):
    first, last = state is None, kept is not None
    tokens, width = queries.shape
    rows, half = mine[0].shape
    depth = weights.shape[0]
    pair = 2 * HEAD_DIM
    steps = width // pair
    pieces = len(mine)
    pair_block = pl.BlockSpec((tokens, pair), lambda i, ids: (0, i))
    wide_block = pl.BlockSpec((tokens, 2 * pair), lambda i, ids: (0, i))
    in_specs = [whole((rows, half))] * (2 * pieces) + [
        pl.BlockSpec((depth, pair), lambda i, ids: (0, i)),
        pl.BlockSpec((depth, pair), lambda i, ids: (0, steps + i)),
        pair_block,
    ]
    args = [*mine, *theirs, weights, weights, queries]
    if not first:
        in_specs += [pair_block, wide_block]
        args += list(state)
    if last:
        in_specs += [whole(kept.shape)]
        args += [kept]
        out_specs = pair_block
        out_shape = jax.ShapeDtypeStruct((tokens, width), jnp.float32)
    else:
        out_specs = [pair_block, wide_block]
        out_shape = [
            jax.ShapeDtypeStruct((tokens, width), jnp.float32),
            jax.ShapeDtypeStruct((tokens, 2 * width), jnp.float32),
        ]
    latents = rows * pieces
    grid_spec = pltpu.PrefetchScalarGridSpec(
        num_scalar_prefetch=1,
        grid=(steps,),
        in_specs=in_specs,
        out_specs=out_specs,
        scratch_shapes=[pltpu.VMEM((latents, 2 * half), jnp.bfloat16)],
    )
    return pl.pallas_call(
        functools.partial(decode_kernel, shares, pieces, first, last),
        grid_spec=grid_spec,
        out_shape=out_shape,
        compiler_params=params(48),
        cost_estimate=cost(
            4 * latents * depth * width + 16 * tokens * latents * width,
            4 * depth * width + 24 * tokens * width,
            tokens * latents * (width // HEAD_DIM),
        ),
        name="decode_rows",
    )(place.reshape(1), *args)


def swap_perm(size):
    return [(i, i ^ 1) for i in range(size)]


def shift_perm(size, k):
    far = size // 2
    return [(((z + k) % far) * 2 + y, z * 2 + y) for z in range(far) for y in range(2)]


def fast_on_device(
    sizes,
    enc_keys,
    enc_values,
    input_ids,
    latent_queries,
    latent_array,
    w_out,
    norm_gain,
    w_key,
    w_value,
    query_features,
    query_ids,
    query_table,
    enc_bias,
    query_counts,
):
    groups, pos = sizes
    far = pos // 2
    g = lax.axis_index("groups")
    p = lax.axis_index("pos")
    place = lax.axis_index("head")
    rows = latent_array.shape[0]
    tokens, half_width = enc_keys.shape
    heads = half_width // HEAD_DIM
    mods = enc_bias.shape[0]
    modality = jnp.arange(mods, dtype=jnp.int32)
    pair = 2 * HEAD_DIM

    def share(weight):
        depth = weight.shape[0] // groups
        own = lax.dynamic_slice_in_dim(weight, g * depth, depth, 0)
        return lax.all_gather(own, ("groups", "pos"), tiled=True), depth

    out_all, out_depth = share(w_out)
    out_all = out_all.reshape(groups, pos * out_depth, w_out.shape[1])
    kv_all, kv_depth = share(jnp.concatenate([w_key, w_value], axis=1))

    q_onehot = (query_ids[:, None] == modality[None, :]).astype(jnp.int32)
    local_counts = jnp.sum(q_onehot, axis=0)
    id_rows = tokens // pair
    counted = jnp.concatenate([local_counts // 16, local_counts % 16])
    extra = jnp.concatenate(
        [
            input_ids.reshape(id_rows, pair),
            jnp.pad(counted[None, :], ((0, EXTRA - id_rows - 1), (0, pair - 2 * mods))),
        ]
    ).astype(jnp.bfloat16)
    payload = pack(enc_keys, enc_values, extra)
    kv = lax.all_to_all(payload, "pos", 0, 0, tiled=True)
    attended = encode(p, latent_queries, kv, enc_bias, pos)
    attended = lax.all_to_all(attended, "pos", 0, 0, tiled=True)

    partial_value = project(attended, out_all, rows, out_depth)
    theirs = lax.ppermute(partial_value, "head", swap_perm(2))
    own_cols, normed = normalise(
        place, partial_value, theirs, latent_array, norm_gain[None, :], groups, kv_depth
    )

    counts = kv.reshape(pos, tokens + EXTRA, pair)[:, tokens + id_rows, : 2 * mods]
    counts = counts.astype(jnp.int32)
    counts = counts[:, :mods] * 16 + counts[:, mods:]
    earlier = jnp.arange(pos, dtype=jnp.int32)[:, None] < p
    before = jnp.sum(jnp.where(earlier, counts, 0), axis=0)
    within = jnp.cumsum(q_onehot, axis=0) - q_onehot
    ranked = jnp.sum((within + before[None, :]) * q_onehot, axis=1)
    limits = jnp.sum(q_onehot * query_counts[None, :], axis=1)
    kept = (ranked < limits).astype(jnp.float32)[:, None]
    lookup = jnp.dot(q_onehot.astype(jnp.bfloat16), query_table, preferred_element_type=jnp.float32)
    queries = (query_features.astype(jnp.float32) + lookup).astype(jnp.bfloat16)

    state = None
    shifts = sorted(range(far), key=lambda k: min(k, far - k))
    arrived = {0: normed}
    for k in shifts[1:]:
        arrived[k] = lax.ppermute(normed, "pos", shift_perm(pos, k))
    for k in shifts:
        mine = [arrived[k], lax.ppermute(arrived[k], "pos", swap_perm(pos))]
        others = [lax.ppermute(v, "head", swap_perm(2)) for v in mine]
        state = decode(
            place, mine, others, kv_all, queries, state, kept if k == shifts[-1] else None, groups
        )
    return (own_cols, state)


def on_device(sizes, *args):
    groups, pos, head = sizes
    enc_keys, latent_array, w_out, w_key = args[0], args[4], args[5], args[7]
    fits = (
        head == 2
        and pos % 2 == 0
        and pos > 2
        and enc_keys.shape[1] == pos * HEAD_DIM
        and enc_keys.shape[0] % (2 * HEAD_DIM) == 0
        and enc_keys.shape[0] < 2048
        and w_key.shape[0] % (LANES * groups) == 0
        and w_out.shape[0] % (LANES * groups) == 0
        and w_out.shape[1] % LANES == 0
        and latent_array.shape[0] % LANES == 0
    )
    if fits:
        return fast_on_device((groups, pos), *args)
    return plain_on_device(*args)


def solution(mesh):
    return jax.shard_map(
        functools.partial(on_device, tuple(mesh.shape[a] for a in ("groups", "pos", "head"))),
        mesh=mesh,
        in_specs=(
            P(("groups", "pos"), "head"),
            P(("groups", "pos"), "head"),
            P(("groups", "pos")),
            P("groups", "head"),
            P(("groups", "pos"), None),
            P("head", "pos"),
            P(),
            P("pos", "head"),
            P("pos", "head"),
            P(("groups", "pos"), "head"),
            P(("groups", "pos")),
            P(None, "head"),
            P(None, "head"),
            P("groups"),
        ),
        out_specs=(P(("groups", "pos"), "head"), P(("groups", "pos"), "head")),
        check_vma=False,
    )
```

```python
import functools

import jax
import jax.numpy as jnp
from jax import lax
from jax.experimental import pallas as pl
from jax.experimental.pallas import tpu as pltpu
from jax.sharding import PartitionSpec as P

HEAD_DIM = 128


norm_eps = 1e-06


def prefix(shard, axis, combine, identity):
    peers, place = (lax.axis_size(axis), lax.axis_index(axis))
    everything = lax.all_gather(shard, axis)
    start = jnp.broadcast_to(jnp.asarray(identity, shard.dtype), shard.shape)

    def step(k, before):
        reached = k < place
        new = combine(before, everything[k])
        return jnp.where(reached, new, before)

    return lax.fori_loop(0, peers, step, start)


def plain_on_device(
    enc_keys,
    enc_values,
    input_ids,
    latent_queries,
    latent_array,
    w_out,
    norm_gain,
    w_key,
    w_value,
    query_features,
    query_ids,
    query_table,
    enc_bias,
    query_counts,
):
    tok_rows = enc_keys.shape[0]
    half_width = enc_keys.shape[1]
    local_heads = half_width // HEAD_DIM
    score_scale = HEAD_DIM ** (-0.5)
    modality = jnp.arange(enc_bias.shape[0], dtype=jnp.int32)
    in_onehot = (input_ids[:, None] == modality[None, :]).astype(jnp.float32)
    bias_rows = jnp.dot(in_onehot, enc_bias, precision=lax.Precision.HIGHEST)
    bias_heads = bias_rows.T[:, None, :]
    keys_split = enc_keys.reshape(tok_rows, local_heads, HEAD_DIM)
    values_split = enc_values.reshape(tok_rows, local_heads, HEAD_DIM)
    lat_total = latent_queries.shape[0]
    block_rows = min(512, lat_total)
    query_blocks = latent_queries.reshape(
        lat_total // block_rows, block_rows, local_heads, HEAD_DIM
    )

    def encode_block(block_queries):
        scores = (
            jnp.einsum(
                "nha,tha->hnt", block_queries, keys_split, preferred_element_type=jnp.float32
            )
            * score_scale
            + bias_heads
        )
        highest = jnp.max(scores, axis=2)
        weights = jnp.exp(scores - highest[:, :, None])
        totals = jnp.sum(weights, axis=2)
        summed = jnp.einsum(
            "hnt,tha->nha",
            weights.astype(jnp.bfloat16),
            values_split,
            preferred_element_type=jnp.float32,
        )
        return (highest.T, totals.T, summed.reshape(block_rows, half_width))

    block_max, block_tot, block_acc = lax.map(encode_block, query_blocks)
    row_highest = block_max.reshape(lat_total, local_heads)
    row_totals = block_tot.reshape(lat_total, local_heads)
    row_sums = block_acc.reshape(lat_total, half_width)
    own_rows = latent_array.shape[0]
    global_max = lax.pmax(row_highest, "pos")
    factor = jnp.exp(row_highest - global_max)
    scaled_sums = (row_sums.reshape(lat_total, local_heads, HEAD_DIM) * factor[:, :, None]).reshape(
        lat_total, half_width
    )
    totals, summed = (
        lax.psum_scatter(row_totals * factor, "pos", scatter_dimension=0, tiled=True),
        lax.psum_scatter(scaled_sums, "pos", scatter_dimension=0, tiled=True),
    )
    summed = summed.reshape(own_rows, local_heads, HEAD_DIM)
    attended = (summed / totals[:, :, None]).reshape(own_rows, half_width).astype(jnp.bfloat16)
    partial_value = jnp.dot(
        attended,
        lax.all_gather(w_out, "pos", axis=1, tiled=True),
        preferred_element_type=jnp.float32,
    )
    offset = lax.axis_index("head") * half_width
    projected = lax.psum(partial_value, "head")
    updated = latent_array.astype(jnp.float32) + projected
    mean_square = jnp.mean(updated * updated, axis=1, keepdims=True)
    normed_full = updated * lax.rsqrt(mean_square + norm_eps) * norm_gain
    normed = normed_full.astype(jnp.bfloat16)
    own_cols = lax.dynamic_slice_in_dim(normed_full, offset, half_width, 1)
    pieces = (
        lax.all_gather(w_key, "pos", axis=0, tiled=True),
        lax.all_gather(w_value, "pos", axis=0, tiled=True),
    )
    key_sum = jnp.dot(normed, pieces[0], preferred_element_type=jnp.float32)
    value_sum = jnp.dot(normed, pieces[1], preferred_element_type=jnp.float32)
    latent_keys = key_sum.astype(jnp.bfloat16)
    latent_values = value_sum.astype(jnp.bfloat16)
    q_onehot = (query_ids[:, None] == modality[None, :]).astype(jnp.int32)
    local_counts = jnp.sum(q_onehot, axis=0)
    before = prefix(
        local_counts, "pos", lambda earlier, later: earlier + later, jnp.zeros_like(local_counts)
    )
    within = jnp.cumsum(q_onehot, axis=0) - q_onehot
    ranked = jnp.sum((within + before[None, :]) * q_onehot, axis=1)
    limits = jnp.sum(q_onehot * query_counts[None, :], axis=1)
    kept_rows = ranked < limits
    lookup = jnp.dot(q_onehot.astype(jnp.bfloat16), query_table, preferred_element_type=jnp.float32)
    queries = (
        (query_features.astype(jnp.float32) + lookup)
        .astype(jnp.bfloat16)
        .reshape(tok_rows, local_heads, HEAD_DIM)
    )

    def fold_rows(running, key_rows, value_rows):
        running_max, running_tot, running_acc = running
        key_heads = key_rows.reshape(key_rows.shape[0], local_heads, HEAD_DIM)
        value_heads = value_rows.reshape(value_rows.shape[0], local_heads, HEAD_DIM)
        scores = (
            jnp.einsum("tha,rha->htr", queries, key_heads, preferred_element_type=jnp.float32)
            * score_scale
        )
        new_max = jnp.maximum(running_max, jnp.max(scores, axis=2))
        fade = jnp.exp(running_max - new_max)
        weights = jnp.exp(scores - new_max[:, :, None])
        new_tot = running_tot * fade + jnp.sum(weights, axis=2)
        new_acc = running_acc * fade[:, :, None] + jnp.einsum(
            "htr,rha->hta",
            weights.astype(jnp.bfloat16),
            value_heads,
            preferred_element_type=jnp.float32,
        )
        return (new_max, new_tot, new_acc)

    start_state = (
        jnp.full((local_heads, tok_rows), -jnp.inf, jnp.float32),
        jnp.zeros((local_heads, tok_rows), jnp.float32),
        jnp.zeros((local_heads, tok_rows, HEAD_DIM), jnp.float32),
    )
    running = start_state
    pieces = (
        lax.all_gather(latent_keys, "pos", axis=0, tiled=True),
        lax.all_gather(latent_values, "pos", axis=0, tiled=True),
    )
    row_count = pieces[0].shape[0]
    key_blocks = pieces[0].reshape(row_count // 512, 512, half_width)
    value_blocks = pieces[1].reshape(row_count // 512, 512, half_width)

    def scan_step(state, pair):
        return (fold_rows(state, pair[0], pair[1]), None)

    running, ignored = lax.scan(scan_step, running, (key_blocks, value_blocks))
    final_max, final_tot, final_acc = running
    dec_heads = final_acc / final_tot[:, :, None]
    dec_rows = jnp.transpose(dec_heads, (1, 0, 2)).reshape(tok_rows, half_width)
    decoded = jnp.where(kept_rows[:, None], dec_rows, 0.0)
    return (own_cols, decoded)


LANES = 128
EXTRA = 16
LOG2E = 1.4426950408889634
EXP2_SCALE = LOG2E * HEAD_DIM**-0.5
NT = (((1,), (1,)), ((), ()))


def params(mib):
    return pltpu.CompilerParams(vmem_limit_bytes=mib << 20)


def cost(flops, nbytes, exps=0):
    return pl.CostEstimate(flops=int(flops), bytes_accessed=int(nbytes), transcendentals=int(exps))


def whole(shape):
    return pl.BlockSpec(shape, lambda *args: (0,) * len(shape))


def pack_kernel(k_ref, v_ref, extra_ref, out_ref):
    tokens = k_ref.shape[0]
    out_ref[:tokens, :HEAD_DIM] = k_ref[...]
    out_ref[:tokens, HEAD_DIM:] = v_ref[...]
    out_ref[tokens:, :] = extra_ref[...]


def pack(keys, values, extra):
    tokens, width = keys.shape
    heads = width // HEAD_DIM
    column = pl.BlockSpec((tokens, HEAD_DIM), lambda h: (0, h))
    block = (tokens + EXTRA, 2 * HEAD_DIM)
    return pl.pallas_call(
        pack_kernel,
        grid=(heads,),
        in_specs=[column, column, whole(extra.shape)],
        out_specs=pl.BlockSpec(block, lambda h: (h, 0)),
        out_shape=jax.ShapeDtypeStruct((heads * block[0], block[1]), keys.dtype),
        compiler_params=params(16),
        cost_estimate=cost(0, 8 * tokens * width),
        name="pack_heads",
    )(keys, values, extra)


def encode_kernel(pos, tokens, q_ref, kv_ref, bias_ref, out_ref):
    rows = q_ref.shape[0]
    queries = q_ref[...]
    ones = jnp.ones((tokens, LANES), jnp.bfloat16)
    row_bits = kv_ref.shape[1]
    top = jnp.full((rows, 1), -jnp.inf, jnp.float32)
    acc = jnp.zeros((rows, 2 * HEAD_DIM), jnp.float32)
    for j in range(pos):
        base = j * (tokens + EXTRA)
        band = slice(base, base + tokens)
        scores = lax.dot_general(
            queries, kv_ref[band, :HEAD_DIM], NT, preferred_element_type=jnp.float32
        )
        tail = kv_ref[base + tokens : base + tokens + EXTRA, :].astype(jnp.float32)
        kind = jnp.concatenate([tail[r : r + 1] for r in range(tokens // row_bits)], axis=1)
        bias = jnp.zeros_like(kind)
        for m in range(bias_ref.shape[0]):
            bias = jnp.where(kind == m, bias_ref[m] * LOG2E, bias)
        scores = scores * EXP2_SCALE + bias
        new_top = jnp.maximum(top, jnp.max(scores, axis=1, keepdims=True))
        weights = jnp.exp2(scores - new_top).astype(jnp.bfloat16)
        acc = acc * jnp.exp2(top - new_top) + jnp.dot(
            weights,
            jnp.concatenate([kv_ref[band, HEAD_DIM:], ones], axis=1),
            preferred_element_type=jnp.float32,
        )
        top = new_top
    out_ref[...] = (acc[:, :HEAD_DIM] / acc[:, HEAD_DIM:]).astype(jnp.bfloat16)


def encode(queries, kv, bias, pos):
    latents = queries.shape[0]
    tokens = kv.shape[0] // pos - EXTRA
    rows = min(512, latents)
    block = pl.BlockSpec((rows, HEAD_DIM), lambda i: (i, 0))
    return pl.pallas_call(
        functools.partial(encode_kernel, pos, tokens),
        grid=(latents // rows,),
        in_specs=[block, whole(kv.shape), pl.BlockSpec(memory_space=pltpu.SMEM)],
        out_specs=block,
        out_shape=jax.ShapeDtypeStruct((latents, HEAD_DIM), jnp.bfloat16),
        compiler_params=params(32),
        cost_estimate=cost(
            16 * latents * tokens * pos * HEAD_DIM, 2 * kv.size, latents * tokens * pos
        ),
        name="encode_head",
    )(queries, kv, bias)


def project_kernel(heads, slots, ids_ref, att_in_ref, *refs):
    w_refs, out_ref, att_ref = refs[:-2], refs[-2], refs[-1]
    rows = att_ref.shape[0]
    for h in range(heads):
        att_ref[:, h * HEAD_DIM : (h + 1) * HEAD_DIM] = att_in_ref[h * rows : (h + 1) * rows, :]
    depth = att_ref.shape[1] // 2
    cols = w_refs[0].shape[1]
    bands = [
        w.at[r * depth : (r + 1) * depth, :] for w in w_refs for r in range(w.shape[0] // depth)
    ]
    halves = []
    for k in range(2):
        start = pl.multiple_of(ids_ref[slots + k] * depth, depth)
        halves.append(att_ref[:, pl.ds(start, depth)])
    for j in range(slots):
        total = jnp.dot(halves[0], bands[j][...], preferred_element_type=jnp.float32) + jnp.dot(
            halves[1], bands[slots + j][...], preferred_element_type=jnp.float32
        )
        out_ref[:, pl.ds(pl.multiple_of(ids_ref[j] * cols, cols), cols)] = total


def project(ids, attended, weights, rows):
    slots = ids.shape[0] - 2
    heads = attended.shape[0] // rows
    out_cols = slots * weights[0].shape[1]
    width = heads * HEAD_DIM
    grid_spec = pltpu.PrefetchScalarGridSpec(
        num_scalar_prefetch=1,
        grid=(1,),
        in_specs=[whole(v.shape) for v in (attended, *weights)],
        out_specs=whole((rows, out_cols)),
        scratch_shapes=[pltpu.VMEM((rows, width), jnp.bfloat16)],
    )
    return pl.pallas_call(
        functools.partial(project_kernel, heads, slots),
        grid_spec=grid_spec,
        out_shape=jax.ShapeDtypeStruct((rows, out_cols), jnp.float32),
        compiler_params=params(32),
        cost_estimate=cost(2 * rows * width * out_cols, 2 * width * out_cols + 4 * rows * out_cols),
        name="project_rows",
    )(ids, attended, *weights)


def norm_kernel(
    shares, band, ids_ref, mine_ref, theirs_ref, latent_ref, gain_ref, out_ref, normed_ref, full_ref
):
    updated = latent_ref[...].astype(jnp.float32) + (mine_ref[...] + theirs_ref[...])
    mean_square = jnp.mean(updated * updated, axis=1, keepdims=True)
    full_ref[...] = updated * lax.rsqrt(mean_square + norm_eps) * gain_ref[...]
    half = out_ref.shape[1]
    own = full_ref[:, pl.ds(pl.multiple_of(ids_ref[0] * half, half), half)]
    out_ref[...] = own
    normed = own.astype(jnp.bfloat16)
    count = half // (shares * band)
    for i in range(count):
        for k in range(shares):
            source = (i * shares + k) * band
            target = (k * count + i) * band
            normed_ref[:, target : target + band] = normed[:, source : source + band]


def normalise(place, mine, theirs, latent_array, gain, shares, band):
    rows, width = mine.shape
    half = width // 2
    grid_spec = pltpu.PrefetchScalarGridSpec(
        num_scalar_prefetch=1,
        grid=(1,),
        in_specs=[whole((rows, width))] * 3 + [whole((1, width))],
        out_specs=[whole((rows, half))] * 2,
        scratch_shapes=[pltpu.VMEM((rows, width), jnp.float32)],
    )
    return pl.pallas_call(
        functools.partial(norm_kernel, shares, band),
        grid_spec=grid_spec,
        out_shape=[
            jax.ShapeDtypeStruct((rows, half), jnp.float32),
            jax.ShapeDtypeStruct((rows, half), jnp.bfloat16),
        ],
        compiler_params=params(32),
        cost_estimate=cost(6 * rows * width, 13 * rows * width),
        name="norm_rows",
    )(place.reshape(1), mine, theirs, latent_array, gain)


def decode_kernel(shares, pieces, first, last, ids_ref, *refs):
    mine = refs[:pieces]
    theirs = refs[pieces : 2 * pieces]
    wk_ref, wv_ref, q_ref = refs[2 * pieces : 2 * pieces + 3]
    rest = list(refs[2 * pieces + 3 :])
    if not first:
        old_max_ref, old_acc_ref = rest[:2]
        rest = rest[2:]
    if last:
        kept_ref, out_ref = rest[:2]
        rest = rest[2:]
    else:
        max_ref, acc_ref = rest[:2]
        rest = rest[2:]
    (normed_ref,) = rest
    rows, half = mine[0].shape
    part = half // shares

    @pl.when(pl.program_id(0) == 0)
    def arrange():
        for r in range(pieces):
            band = slice(r * rows, (r + 1) * rows)
            for k in range(shares):
                cols = slice(k * part, (k + 1) * part)
                for source, which in ((mine[r], ids_ref[0]), (theirs[r], 1 - ids_ref[0])):
                    start = pl.multiple_of(k * 2 * part + which * part, part)
                    normed_ref[band, pl.ds(start, part)] = source[:, cols]

    latents = normed_ref.shape[0]
    chunk = min(512, latents)
    ones = jnp.ones((chunk, LANES), jnp.bfloat16)
    heads = q_ref.shape[1] // HEAD_DIM
    tops = [None] * heads
    accs = [None] * heads
    for h in range(0 if first else heads):
        tops[h] = old_max_ref[:, h * HEAD_DIM : h * HEAD_DIM + 1]
        accs[h] = old_acc_ref[:, 2 * h * HEAD_DIM : 2 * (h + 1) * HEAD_DIM]
    for start in range(0, latents, chunk):
        normed = normed_ref[start : start + chunk, :]
        keys = jnp.dot(normed, wk_ref[...], preferred_element_type=jnp.float32)
        keys = keys.astype(jnp.bfloat16)
        values = jnp.dot(normed, wv_ref[...], preferred_element_type=jnp.float32)
        values = values.astype(jnp.bfloat16)
        for h in range(heads):
            cols = slice(h * HEAD_DIM, (h + 1) * HEAD_DIM)
            scores = lax.dot_general(
                q_ref[:, cols], keys[:, cols], NT, preferred_element_type=jnp.float32
            )
            scores = scores * EXP2_SCALE
            top = jnp.max(scores, axis=1, keepdims=True)
            if tops[h] is not None:
                top = jnp.maximum(top, tops[h])
            weights = jnp.exp2(scores - top).astype(jnp.bfloat16)
            summed = jnp.dot(
                weights,
                jnp.concatenate([values[:, cols], ones], axis=1),
                preferred_element_type=jnp.float32,
            )
            if tops[h] is not None:
                summed = summed + accs[h] * jnp.exp2(tops[h] - top)
            tops[h], accs[h] = top, summed
    for h in range(heads):
        cols = slice(h * HEAD_DIM, (h + 1) * HEAD_DIM)
        if last:
            result = accs[h][:, :HEAD_DIM] / accs[h][:, HEAD_DIM:]
            out_ref[:, cols] = jnp.where(kept_ref[...] > 0.0, result, 0.0)
        else:
            max_ref[:, cols] = jnp.broadcast_to(tops[h], (tops[h].shape[0], HEAD_DIM))
            acc_ref[:, 2 * h * HEAD_DIM : 2 * (h + 1) * HEAD_DIM] = accs[h]


def decode(place, mine, theirs, weights, queries, state, kept, shares):
    first, last = state is None, kept is not None
    tokens, width = queries.shape
    rows, half = mine[0].shape
    depth = weights.shape[0]
    pair = 2 * HEAD_DIM
    steps = width // pair
    pieces = len(mine)
    pair_block = pl.BlockSpec((tokens, pair), lambda i, ids: (0, i))
    wide_block = pl.BlockSpec((tokens, 2 * pair), lambda i, ids: (0, i))
    in_specs = [whole((rows, half))] * (2 * pieces) + [
        pl.BlockSpec((depth, pair), lambda i, ids: (0, i)),
        pl.BlockSpec((depth, pair), lambda i, ids: (0, steps + i)),
        pair_block,
    ]
    args = [*mine, *theirs, weights, weights, queries]
    if not first:
        in_specs += [pair_block, wide_block]
        args += list(state)
    if last:
        in_specs += [whole(kept.shape)]
        args += [kept]
        out_specs = pair_block
        out_shape = jax.ShapeDtypeStruct((tokens, width), jnp.float32)
    else:
        out_specs = [pair_block, wide_block]
        out_shape = [
            jax.ShapeDtypeStruct((tokens, width), jnp.float32),
            jax.ShapeDtypeStruct((tokens, 2 * width), jnp.float32),
        ]
    latents = rows * pieces
    grid_spec = pltpu.PrefetchScalarGridSpec(
        num_scalar_prefetch=1,
        grid=(steps,),
        in_specs=in_specs,
        out_specs=out_specs,
        scratch_shapes=[pltpu.VMEM((latents, 2 * half), jnp.bfloat16)],
    )
    return pl.pallas_call(
        functools.partial(decode_kernel, shares, pieces, first, last),
        grid_spec=grid_spec,
        out_shape=out_shape,
        compiler_params=params(48),
        cost_estimate=cost(
            4 * latents * depth * width + 16 * tokens * latents * width,
            4 * depth * width + 24 * tokens * width,
            tokens * latents * (width // HEAD_DIM),
        ),
        name="decode_rows",
    )(place.reshape(1), *args)


def swap_perm(size):
    return [(i, i ^ 1) for i in range(size)]


def shift_perm(size, k):
    far = size // 2
    return [(((z + k) % far) * 2 + y, z * 2 + y) for z in range(far) for y in range(2)]


def fast_on_device(
    sizes,
    enc_keys,
    enc_values,
    input_ids,
    latent_queries,
    latent_array,
    w_out,
    norm_gain,
    w_key,
    w_value,
    query_features,
    query_ids,
    query_table,
    enc_bias,
    query_counts,
):
    groups, pos = sizes
    far = pos // 2
    g = lax.axis_index("groups")
    p = lax.axis_index("pos")
    place = lax.axis_index("head")
    rows = latent_array.shape[0]
    tokens, half_width = enc_keys.shape
    heads = half_width // HEAD_DIM
    mods = enc_bias.shape[0]
    modality = jnp.arange(mods, dtype=jnp.int32)
    pair = 2 * HEAD_DIM

    out_depth = w_out.shape[0] // 2
    z, y, x = p // 2, p % 2, g % 2
    own = lax.dynamic_slice_in_dim(w_out, x * out_depth, out_depth, 0)
    column = [own] + [lax.ppermute(own, "pos", shift_perm(pos, k)) for k in range(1, far)]
    column = jnp.concatenate(column)
    across = lax.ppermute(column, "pos", swap_perm(pos))
    half = jnp.concatenate([column, across])
    out_bands = [half, lax.ppermute(half, "groups", swap_perm(groups))]
    slot_pos = [((z + k) % far) * 2 + (y ^ j) for j in range(2) for k in range(far)]
    out_ids = jnp.stack([*slot_pos, x, 1 - x]).astype(jnp.int32)

    kv_depth = w_key.shape[0] // groups
    kv_all = lax.all_gather(
        jnp.concatenate(
            [lax.dynamic_slice_in_dim(w, g * kv_depth, kv_depth, 0) for w in (w_key, w_value)],
            axis=1,
        ),
        ("groups", "pos"),
        tiled=True,
    )

    q_onehot = (query_ids[:, None] == modality[None, :]).astype(jnp.int32)
    local_counts = jnp.sum(q_onehot, axis=0)
    id_rows = tokens // pair
    counted = jnp.concatenate([local_counts // 16, local_counts % 16])
    extra = jnp.concatenate(
        [
            input_ids.reshape(id_rows, pair),
            jnp.pad(counted[None, :], ((0, EXTRA - id_rows - 1), (0, pair - 2 * mods))),
        ]
    ).astype(jnp.bfloat16)
    payload = pack(enc_keys, enc_values, extra)
    kv = lax.all_to_all(payload, "pos", 0, 0, tiled=True)
    head_queries = lax.dynamic_slice_in_dim(latent_queries, p * HEAD_DIM, HEAD_DIM, 1)
    head_bias = lax.dynamic_slice_in_dim(enc_bias, p, 1, 1)[:, 0]
    attended = encode(head_queries, kv, head_bias, pos)
    attended = lax.all_to_all(attended, "pos", 0, 0, tiled=True)

    partial_value = project(out_ids, attended, out_bands, rows)
    theirs = lax.ppermute(partial_value, "head", swap_perm(2))
    own_cols, normed = normalise(
        place, partial_value, theirs, latent_array, norm_gain[None, :], groups, kv_depth
    )

    counts = kv.reshape(pos, tokens + EXTRA, pair)[:, tokens + id_rows, : 2 * mods]
    counts = counts.astype(jnp.int32)
    counts = counts[:, :mods] * 16 + counts[:, mods:]
    earlier = jnp.arange(pos, dtype=jnp.int32)[:, None] < p
    before = jnp.sum(jnp.where(earlier, counts, 0), axis=0)
    within = jnp.cumsum(q_onehot, axis=0) - q_onehot
    ranked = jnp.sum((within + before[None, :]) * q_onehot, axis=1)
    limits = jnp.sum(q_onehot * query_counts[None, :], axis=1)
    kept = (ranked < limits).astype(jnp.float32)[:, None]
    lookup = jnp.dot(q_onehot.astype(jnp.bfloat16), query_table, preferred_element_type=jnp.float32)
    queries = (query_features.astype(jnp.float32) + lookup).astype(jnp.bfloat16)

    state = None
    shifts = sorted(range(far), key=lambda k: min(k, far - k))
    arrived = {0: normed}
    for k in shifts[1:]:
        arrived[k] = lax.ppermute(normed, "pos", shift_perm(pos, k))
    for turn in (shifts[:-1], shifts[-1:]):
        mine, others = [], []
        for k in turn:
            both = [arrived[k], lax.ppermute(arrived[k], "pos", swap_perm(pos))]
            mine += both
            others += [lax.ppermute(v, "head", swap_perm(2)) for v in both]
        last = turn[-1] == shifts[-1]
        state = decode(
            place, mine, others, kv_all, queries, state, kept if last else None, groups
        )
    return (own_cols, state)


def on_device(sizes, *args):
    groups, pos, head = sizes
    enc_keys, latent_array, w_out, w_key = args[0], args[4], args[5], args[7]
    fits = (
        head == 2
        and pos % 2 == 0
        and pos > 2
        and groups % 2 == 0
        and enc_keys.shape[1] == pos * HEAD_DIM
        and enc_keys.shape[0] % (2 * HEAD_DIM) == 0
        and enc_keys.shape[0] < 2048
        and w_key.shape[0] % (LANES * groups) == 0
        and w_out.shape[0] % (2 * LANES) == 0
        and w_out.shape[1] % LANES == 0
        and latent_array.shape[0] % LANES == 0
    )
    if fits:
        return fast_on_device((groups, pos), *args)
    return plain_on_device(*args)


def solution(mesh):
    return jax.shard_map(
        functools.partial(on_device, tuple(mesh.shape[a] for a in ("groups", "pos", "head"))),
        mesh=mesh,
        in_specs=(
            P(("groups", "pos"), "head"),
            P(("groups", "pos"), "head"),
            P(("groups", "pos")),
            P("groups", "head"),
            P(("groups", "pos"), None),
            P("head", "pos"),
            P(),
            P("pos", "head"),
            P("pos", "head"),
            P(("groups", "pos"), "head"),
            P(("groups", "pos")),
            P(None, "head"),
            P(None, "head"),
            P("groups"),
        ),
        out_specs=(P(("groups", "pos"), "head"), P(("groups", "pos"), "head")),
        check_vma=False,
    )
```

```python
import functools

import jax
import jax.numpy as jnp
from jax import lax
from jax.experimental import pallas as pl
from jax.experimental.pallas import tpu as pltpu
from jax.sharding import PartitionSpec as P

HEAD_DIM = 128


norm_eps = 1e-06


def prefix(shard, axis, combine, identity):
    peers, place = (lax.axis_size(axis), lax.axis_index(axis))
    everything = lax.all_gather(shard, axis)
    start = jnp.broadcast_to(jnp.asarray(identity, shard.dtype), shard.shape)

    def step(k, before):
        reached = k < place
        new = combine(before, everything[k])
        return jnp.where(reached, new, before)

    return lax.fori_loop(0, peers, step, start)


def plain_on_device(
    enc_keys,
    enc_values,
    input_ids,
    latent_queries,
    latent_array,
    w_out,
    norm_gain,
    w_key,
    w_value,
    query_features,
    query_ids,
    query_table,
    enc_bias,
    query_counts,
):
    tok_rows = enc_keys.shape[0]
    half_width = enc_keys.shape[1]
    local_heads = half_width // HEAD_DIM
    score_scale = HEAD_DIM ** (-0.5)
    modality = jnp.arange(enc_bias.shape[0], dtype=jnp.int32)
    in_onehot = (input_ids[:, None] == modality[None, :]).astype(jnp.float32)
    bias_rows = jnp.dot(in_onehot, enc_bias, precision=lax.Precision.HIGHEST)
    bias_heads = bias_rows.T[:, None, :]
    keys_split = enc_keys.reshape(tok_rows, local_heads, HEAD_DIM)
    values_split = enc_values.reshape(tok_rows, local_heads, HEAD_DIM)
    lat_total = latent_queries.shape[0]
    block_rows = min(512, lat_total)
    query_blocks = latent_queries.reshape(
        lat_total // block_rows, block_rows, local_heads, HEAD_DIM
    )

    def encode_block(block_queries):
        scores = (
            jnp.einsum(
                "nha,tha->hnt", block_queries, keys_split, preferred_element_type=jnp.float32
            )
            * score_scale
            + bias_heads
        )
        highest = jnp.max(scores, axis=2)
        weights = jnp.exp(scores - highest[:, :, None])
        totals = jnp.sum(weights, axis=2)
        summed = jnp.einsum(
            "hnt,tha->nha",
            weights.astype(jnp.bfloat16),
            values_split,
            preferred_element_type=jnp.float32,
        )
        return (highest.T, totals.T, summed.reshape(block_rows, half_width))

    block_max, block_tot, block_acc = lax.map(encode_block, query_blocks)
    row_highest = block_max.reshape(lat_total, local_heads)
    row_totals = block_tot.reshape(lat_total, local_heads)
    row_sums = block_acc.reshape(lat_total, half_width)
    own_rows = latent_array.shape[0]
    global_max = lax.pmax(row_highest, "pos")
    factor = jnp.exp(row_highest - global_max)
    scaled_sums = (row_sums.reshape(lat_total, local_heads, HEAD_DIM) * factor[:, :, None]).reshape(
        lat_total, half_width
    )
    totals, summed = (
        lax.psum_scatter(row_totals * factor, "pos", scatter_dimension=0, tiled=True),
        lax.psum_scatter(scaled_sums, "pos", scatter_dimension=0, tiled=True),
    )
    summed = summed.reshape(own_rows, local_heads, HEAD_DIM)
    attended = (summed / totals[:, :, None]).reshape(own_rows, half_width).astype(jnp.bfloat16)
    partial_value = jnp.dot(
        attended,
        lax.all_gather(w_out, "pos", axis=1, tiled=True),
        preferred_element_type=jnp.float32,
    )
    offset = lax.axis_index("head") * half_width
    projected = lax.psum(partial_value, "head")
    updated = latent_array.astype(jnp.float32) + projected
    mean_square = jnp.mean(updated * updated, axis=1, keepdims=True)
    normed_full = updated * lax.rsqrt(mean_square + norm_eps) * norm_gain
    normed = normed_full.astype(jnp.bfloat16)
    own_cols = lax.dynamic_slice_in_dim(normed_full, offset, half_width, 1)
    pieces = (
        lax.all_gather(w_key, "pos", axis=0, tiled=True),
        lax.all_gather(w_value, "pos", axis=0, tiled=True),
    )
    key_sum = jnp.dot(normed, pieces[0], preferred_element_type=jnp.float32)
    value_sum = jnp.dot(normed, pieces[1], preferred_element_type=jnp.float32)
    latent_keys = key_sum.astype(jnp.bfloat16)
    latent_values = value_sum.astype(jnp.bfloat16)
    q_onehot = (query_ids[:, None] == modality[None, :]).astype(jnp.int32)
    local_counts = jnp.sum(q_onehot, axis=0)
    before = prefix(
        local_counts, "pos", lambda earlier, later: earlier + later, jnp.zeros_like(local_counts)
    )
    within = jnp.cumsum(q_onehot, axis=0) - q_onehot
    ranked = jnp.sum((within + before[None, :]) * q_onehot, axis=1)
    limits = jnp.sum(q_onehot * query_counts[None, :], axis=1)
    kept_rows = ranked < limits
    lookup = jnp.dot(q_onehot.astype(jnp.bfloat16), query_table, preferred_element_type=jnp.float32)
    queries = (
        (query_features.astype(jnp.float32) + lookup)
        .astype(jnp.bfloat16)
        .reshape(tok_rows, local_heads, HEAD_DIM)
    )

    def fold_rows(running, key_rows, value_rows):
        running_max, running_tot, running_acc = running
        key_heads = key_rows.reshape(key_rows.shape[0], local_heads, HEAD_DIM)
        value_heads = value_rows.reshape(value_rows.shape[0], local_heads, HEAD_DIM)
        scores = (
            jnp.einsum("tha,rha->htr", queries, key_heads, preferred_element_type=jnp.float32)
            * score_scale
        )
        new_max = jnp.maximum(running_max, jnp.max(scores, axis=2))
        fade = jnp.exp(running_max - new_max)
        weights = jnp.exp(scores - new_max[:, :, None])
        new_tot = running_tot * fade + jnp.sum(weights, axis=2)
        new_acc = running_acc * fade[:, :, None] + jnp.einsum(
            "htr,rha->hta",
            weights.astype(jnp.bfloat16),
            value_heads,
            preferred_element_type=jnp.float32,
        )
        return (new_max, new_tot, new_acc)

    start_state = (
        jnp.full((local_heads, tok_rows), -jnp.inf, jnp.float32),
        jnp.zeros((local_heads, tok_rows), jnp.float32),
        jnp.zeros((local_heads, tok_rows, HEAD_DIM), jnp.float32),
    )
    running = start_state
    pieces = (
        lax.all_gather(latent_keys, "pos", axis=0, tiled=True),
        lax.all_gather(latent_values, "pos", axis=0, tiled=True),
    )
    row_count = pieces[0].shape[0]
    key_blocks = pieces[0].reshape(row_count // 512, 512, half_width)
    value_blocks = pieces[1].reshape(row_count // 512, 512, half_width)

    def scan_step(state, pair):
        return (fold_rows(state, pair[0], pair[1]), None)

    running, ignored = lax.scan(scan_step, running, (key_blocks, value_blocks))
    final_max, final_tot, final_acc = running
    dec_heads = final_acc / final_tot[:, :, None]
    dec_rows = jnp.transpose(dec_heads, (1, 0, 2)).reshape(tok_rows, half_width)
    decoded = jnp.where(kept_rows[:, None], dec_rows, 0.0)
    return (own_cols, decoded)


LANES = 128
EXTRA = 16
LOG2E = 1.4426950408889634
EXP2_SCALE = LOG2E * HEAD_DIM**-0.5
NT = (((1,), (1,)), ((), ()))


def params(mib):
    return pltpu.CompilerParams(vmem_limit_bytes=mib << 20)


def cost(flops, nbytes, exps=0):
    return pl.CostEstimate(flops=int(flops), bytes_accessed=int(nbytes), transcendentals=int(exps))


def whole(shape):
    return pl.BlockSpec(shape, lambda *args: (0,) * len(shape))


def pack_kernel(k_ref, v_ref, extra_ref, out_ref):
    tokens = k_ref.shape[0]
    out_ref[:tokens, :HEAD_DIM] = k_ref[...]
    out_ref[:tokens, HEAD_DIM:] = v_ref[...]
    out_ref[tokens:, :] = extra_ref[...]


def pack(keys, values, extra):
    tokens, width = keys.shape
    heads = width // HEAD_DIM
    column = pl.BlockSpec((tokens, HEAD_DIM), lambda h: (0, h))
    block = (tokens + EXTRA, 2 * HEAD_DIM)
    return pl.pallas_call(
        pack_kernel,
        grid=(heads,),
        in_specs=[column, column, whole(extra.shape)],
        out_specs=pl.BlockSpec(block, lambda h: (h, 0)),
        out_shape=jax.ShapeDtypeStruct((heads * block[0], block[1]), keys.dtype),
        compiler_params=params(16),
        cost_estimate=cost(0, 8 * tokens * width),
        name="pack_heads",
    )(keys, values, extra)


def encode_kernel(pos, tokens, q_ref, kv_ref, bias_ref, out_ref):
    rows = q_ref.shape[0]
    queries = q_ref[...]
    ones = jnp.ones((tokens, LANES), jnp.bfloat16)
    row_bits = kv_ref.shape[1]
    top = jnp.full((rows, 1), -jnp.inf, jnp.float32)
    acc = jnp.zeros((rows, 2 * HEAD_DIM), jnp.float32)
    for j in range(pos):
        base = j * (tokens + EXTRA)
        band = slice(base, base + tokens)
        scores = lax.dot_general(
            queries, kv_ref[band, :HEAD_DIM], NT, preferred_element_type=jnp.float32
        )
        tail = kv_ref[base + tokens : base + tokens + EXTRA, :].astype(jnp.float32)
        kind = jnp.concatenate([tail[r : r + 1] for r in range(tokens // row_bits)], axis=1)
        bias = jnp.zeros_like(kind)
        for m in range(bias_ref.shape[0]):
            bias = jnp.where(kind == m, bias_ref[m] * LOG2E, bias)
        scores = scores * EXP2_SCALE + bias
        new_top = jnp.maximum(top, jnp.max(scores, axis=1, keepdims=True))
        weights = jnp.exp2(scores - new_top).astype(jnp.bfloat16)
        acc = acc * jnp.exp2(top - new_top) + jnp.dot(
            weights,
            jnp.concatenate([kv_ref[band, HEAD_DIM:], ones], axis=1),
            preferred_element_type=jnp.float32,
        )
        top = new_top
    out_ref[...] = (acc[:, :HEAD_DIM] / acc[:, HEAD_DIM:]).astype(jnp.bfloat16)


def encode(queries, kv, bias, pos):
    latents = queries.shape[0]
    tokens = kv.shape[0] // pos - EXTRA
    rows = min(512, latents)
    block = pl.BlockSpec((rows, HEAD_DIM), lambda i: (i, 0))
    return pl.pallas_call(
        functools.partial(encode_kernel, pos, tokens),
        grid=(latents // rows,),
        in_specs=[block, whole(kv.shape), pl.BlockSpec(memory_space=pltpu.SMEM)],
        out_specs=block,
        out_shape=jax.ShapeDtypeStruct((latents, HEAD_DIM), jnp.bfloat16),
        compiler_params=params(32),
        cost_estimate=cost(
            16 * latents * tokens * pos * HEAD_DIM, 2 * kv.size, latents * tokens * pos
        ),
        name="encode_head",
    )(queries, kv, bias)


def project_kernel(heads, att_in_ref, w_ref, out_ref, att_ref):
    rows = att_ref.shape[0]
    shares, depth, _ = w_ref.shape

    @pl.when(pl.program_id(0) == 0)
    def arrange():
        for h in range(heads):
            att_ref[:, h * HEAD_DIM : (h + 1) * HEAD_DIM] = att_in_ref[h * rows : (h + 1) * rows, :]

    total = None
    for k in range(shares):
        term = jnp.dot(
            att_ref[:, k * depth : (k + 1) * depth], w_ref[k], preferred_element_type=jnp.float32
        )
        total = term if total is None else total + term
    out_ref[...] = total


def project(attended, w_all, rows, depth):
    heads = attended.shape[0] // rows
    shares, long, cols = w_all.shape
    steps = long // depth
    return pl.pallas_call(
        functools.partial(project_kernel, heads),
        grid=(steps,),
        in_specs=[
            whole(attended.shape),
            pl.BlockSpec((shares, depth, cols), lambda i: (0, i, 0)),
        ],
        out_specs=pl.BlockSpec((rows, cols), lambda i: (0, i)),
        out_shape=jax.ShapeDtypeStruct((rows, steps * cols), jnp.float32),
        scratch_shapes=[pltpu.VMEM((rows, heads * HEAD_DIM), jnp.bfloat16)],
        compiler_params=params(32),
        cost_estimate=cost(2 * rows * w_all.size, 2 * w_all.size + 4 * rows * steps * cols),
        name="project_rows",
    )(attended, w_all)


def norm_kernel(
    ids_ref, mine_ref, theirs_ref, latent_ref, gain_ref, out_ref, normed_ref, other_ref, full_ref
):
    updated = latent_ref[...].astype(jnp.float32) + (mine_ref[...] + theirs_ref[...])
    mean_square = jnp.mean(updated * updated, axis=1, keepdims=True)
    full_ref[...] = updated * lax.rsqrt(mean_square + norm_eps) * gain_ref[...]
    half = out_ref.shape[1]
    own = full_ref[:, pl.ds(pl.multiple_of(ids_ref[0] * half, half), half)]
    out_ref[...] = own
    normed_ref[...] = own.astype(jnp.bfloat16)
    other = full_ref[:, pl.ds(pl.multiple_of((1 - ids_ref[0]) * half, half), half)]
    other_ref[...] = other.astype(jnp.bfloat16)


def normalise(place, mine, theirs, latent_array, gain):
    rows, width = mine.shape
    half = width // 2
    grid_spec = pltpu.PrefetchScalarGridSpec(
        num_scalar_prefetch=1,
        grid=(1,),
        in_specs=[whole((rows, width))] * 3 + [whole((1, width))],
        out_specs=[whole((rows, half))] * 3,
        scratch_shapes=[pltpu.VMEM((rows, width), jnp.float32)],
    )
    return pl.pallas_call(
        norm_kernel,
        grid_spec=grid_spec,
        out_shape=[
            jax.ShapeDtypeStruct((rows, half), jnp.float32),
            jax.ShapeDtypeStruct((rows, half), jnp.bfloat16),
            jax.ShapeDtypeStruct((rows, half), jnp.bfloat16),
        ],
        compiler_params=params(32),
        cost_estimate=cost(6 * rows * width, 13 * rows * width),
        name="norm_rows",
    )(place.reshape(1), mine, theirs, latent_array, gain)


def latents_kernel(pieces, ids_ref, *refs):
    mine, theirs = refs[:pieces], refs[pieces : 2 * pieces]
    w_ref, out_ref, normed_ref = refs[2 * pieces :]
    rows, half = mine[0].shape
    slots = ids_ref.shape[0] - 1
    depth = 2 * half // slots

    @pl.when(pl.program_id(0) == 0)
    def arrange():
        for j in range(slots):
            at = ids_ref[1 + j]
            is_mine = at // (slots // 2) == ids_ref[0]
            start = pl.multiple_of((at % (slots // 2)) * depth, depth)
            for r in range(pieces):
                both = [v[r][:, pl.ds(start, depth)] for v in (mine, theirs)]
                normed_ref[r * rows : (r + 1) * rows, j * depth : (j + 1) * depth] = jnp.where(
                    is_mine, both[0], both[1]
                )

    out_ref[...] = jnp.dot(
        normed_ref[...], w_ref[...], preferred_element_type=jnp.float32
    ).astype(jnp.bfloat16)


def latent_keys_values(ids, mine, theirs, weights):
    pieces = len(mine)
    rows, half = mine[0].shape
    depth, width = weights.shape
    block = min(512, width)
    grid_spec = pltpu.PrefetchScalarGridSpec(
        num_scalar_prefetch=1,
        grid=(width // block,),
        in_specs=[whole((rows, half))] * (2 * pieces)
        + [pl.BlockSpec((depth, block), lambda i, ids: (0, i))],
        out_specs=pl.BlockSpec((rows * pieces, block), lambda i, ids: (0, i)),
        scratch_shapes=[pltpu.VMEM((rows * pieces, depth), jnp.bfloat16)],
    )
    return pl.pallas_call(
        functools.partial(latents_kernel, pieces),
        grid_spec=grid_spec,
        out_shape=jax.ShapeDtypeStruct((rows * pieces, width), jnp.bfloat16),
        compiler_params=params(40),
        cost_estimate=cost(2 * rows * pieces * depth * width, 2 * depth * width),
        name="latent_keys_values",
    )(ids, *mine, *theirs, weights)


def decode_kernel(first, last, *refs):
    q_ref, k_ref, v_ref = refs[:3]
    rest = refs[3:]
    if not first:
        old_max_ref, old_acc_ref = rest[:2]
        rest = rest[2:]
    latents = k_ref.shape[0]
    chunk = min(512, latents)
    ones = jnp.ones((chunk, LANES), jnp.bfloat16)
    for h in range(q_ref.shape[1] // HEAD_DIM):
        cols = slice(h * HEAD_DIM, (h + 1) * HEAD_DIM)
        wide = slice(2 * h * HEAD_DIM, 2 * (h + 1) * HEAD_DIM)
        if first:
            top, acc = None, None
        else:
            top, acc = old_max_ref[:, cols][:, :1], old_acc_ref[:, wide]
        for start in range(0, latents, chunk):
            band = slice(start, start + chunk)
            scores = lax.dot_general(
                q_ref[:, cols], k_ref[band, cols], NT, preferred_element_type=jnp.float32
            )
            scores = scores * EXP2_SCALE
            new_top = jnp.max(scores, axis=1, keepdims=True)
            if top is not None:
                new_top = jnp.maximum(top, new_top)
            weights = jnp.exp2(scores - new_top).astype(jnp.bfloat16)
            summed = jnp.dot(
                weights,
                jnp.concatenate([v_ref[band, cols], ones], axis=1),
                preferred_element_type=jnp.float32,
            )
            if top is not None:
                summed = summed + acc * jnp.exp2(top - new_top)
            top, acc = new_top, summed
        if last:
            (out_ref,) = rest
            out_ref[:, cols] = (acc[:, :HEAD_DIM] / acc[:, HEAD_DIM:]).astype(out_ref.dtype)
        else:
            max_ref, acc_ref = rest
            max_ref[:, cols] = jnp.broadcast_to(top, (top.shape[0], HEAD_DIM))
            acc_ref[:, wide] = acc


def decode(queries, keys_values, state, out_type):
    first, last = state is None, out_type is not None
    tokens, width = queries.shape
    latents = keys_values.shape[0]
    pair = min(2 * HEAD_DIM, width)
    steps = width // pair
    narrow = pl.BlockSpec((tokens, pair), lambda i: (0, i))
    wide = pl.BlockSpec((tokens, 2 * pair), lambda i: (0, i))
    in_specs = [
        narrow,
        pl.BlockSpec((latents, pair), lambda i: (0, i)),
        pl.BlockSpec((latents, pair), lambda i: (0, steps + i)),
    ]
    args = [queries, keys_values, keys_values]
    if not first:
        in_specs += [narrow, wide]
        args += list(state)
    if last:
        out_specs = narrow
        out_shape = jax.ShapeDtypeStruct((tokens, width), out_type)
    else:
        out_specs = [narrow, wide]
        out_shape = [
            jax.ShapeDtypeStruct((tokens, width), jnp.float32),
            jax.ShapeDtypeStruct((tokens, 2 * width), jnp.float32),
        ]
    return pl.pallas_call(
        functools.partial(decode_kernel, first, last),
        grid=(steps,),
        in_specs=in_specs,
        out_specs=out_specs,
        out_shape=out_shape,
        compiler_params=params(40),
        cost_estimate=cost(
            16 * tokens * latents * width,
            4 * latents * width + 16 * tokens * width,
            tokens * latents * (width // HEAD_DIM),
        ),
        name="decode_rows",
    )(*args)


def swap_perm(size):
    return [(i, i ^ 1) for i in range(size)]


def shift_perm(size, k):
    far = size // 2
    return [(((z + k) % far) * 2 + y, z * 2 + y) for z in range(far) for y in range(2)]


def fast_on_device(
    sizes,
    enc_keys,
    enc_values,
    input_ids,
    latent_queries,
    latent_array,
    w_out,
    norm_gain,
    w_key,
    w_value,
    query_features,
    query_ids,
    query_table,
    enc_bias,
    query_counts,
):
    groups, pos = sizes
    far = pos // 2
    g = lax.axis_index("groups")
    p = lax.axis_index("pos")
    place = lax.axis_index("head")
    rows = latent_array.shape[0]
    tokens, half_width = enc_keys.shape
    heads = half_width // HEAD_DIM
    mods = enc_bias.shape[0]
    modality = jnp.arange(mods, dtype=jnp.int32)
    pair = 2 * HEAD_DIM

    far, z, y, x = pos // 2, p // 2, p % 2, g % 2
    near = swap_perm(pos)

    out_depth = w_out.shape[0] // groups
    out_all = lax.all_gather(
        lax.dynamic_slice_in_dim(w_out, g * out_depth, out_depth, 0),
        ("groups", "pos"),
        tiled=True,
    ).reshape(groups, pos * out_depth, w_out.shape[1])

    part = half_width // 2

    def columns(arrays, which):
        return jnp.concatenate(
            [lax.dynamic_slice_in_dim(v, which * part, part, 1) for v in arrays], axis=1
        )

    kv_own = columns((w_key, w_value), y)
    kv_near = lax.ppermute(columns((w_key, w_value), 1 - y), "pos", near)

    q_onehot = (query_ids[:, None] == modality[None, :]).astype(jnp.int32)
    local_counts = jnp.sum(q_onehot, axis=0)
    id_rows = tokens // pair
    counted = jnp.concatenate([local_counts // 16, local_counts % 16])
    extra = jnp.concatenate(
        [
            input_ids.reshape(id_rows, pair),
            jnp.pad(counted[None, :], ((0, EXTRA - id_rows - 1), (0, pair - 2 * mods))),
        ]
    ).astype(jnp.bfloat16)
    payload = pack(enc_keys, enc_values, extra)
    kv = lax.all_to_all(payload, "pos", 0, 0, tiled=True)
    head_queries = lax.dynamic_slice_in_dim(latent_queries, p * HEAD_DIM, HEAD_DIM, 1)
    head_bias = lax.dynamic_slice_in_dim(enc_bias, p, 1, 1)[:, 0]
    kv_sent, kv = lax.optimization_barrier((jnp.where(x == 0, kv_own, kv_near), kv))
    kv_bands = [kv_own, kv_near]
    kv_at = [p, p ^ 1]
    shifts = sorted(range(far), key=lambda k: min(k, far - k))
    moved = {}
    for k in shifts[1:-1]:
        moved[k] = lax.ppermute(kv_sent, "pos", shift_perm(pos, k))
    attended = encode(head_queries, kv, head_bias, pos)
    attended, kv_sent, moved = lax.optimization_barrier((attended, kv_sent, moved))
    moved[shifts[-1]] = lax.ppermute(kv_sent, "pos", shift_perm(pos, shifts[-1]))
    attended = lax.all_to_all(attended, "pos", 0, 0, tiled=True)
    attended, moved = lax.optimization_barrier((attended, moved))

    partial_value = project(attended, out_all, rows, out_depth)
    theirs = lax.ppermute(partial_value, "head", swap_perm(2))
    own_cols, normed, normed_other = normalise(
        place, partial_value, theirs, latent_array, norm_gain[None, :]
    )
    for k in shifts[1:]:
        kv_bands += [moved[k], lax.ppermute(moved[k], "groups", swap_perm(groups))]
        there = ((z + k) % far) * 2
        kv_at += [there + (y ^ x), there + (1 - (y ^ x))]
    kv_weights = jnp.concatenate(kv_bands)
    kv_ids = jnp.stack([place, *kv_at]).astype(jnp.int32)

    counts = kv.reshape(pos, tokens + EXTRA, pair)[:, tokens + id_rows, : 2 * mods]
    counts = counts.astype(jnp.int32)
    counts = counts[:, :mods] * 16 + counts[:, mods:]
    earlier = jnp.arange(pos, dtype=jnp.int32)[:, None] < p
    before = jnp.sum(jnp.where(earlier, counts, 0), axis=0)
    within = jnp.cumsum(q_onehot, axis=0) - q_onehot
    ranked = jnp.sum((within + before[None, :]) * q_onehot, axis=1)
    limits = jnp.sum(q_onehot * query_counts[None, :], axis=1)
    kept = ranked < limits
    lookup = jnp.dot(q_onehot.astype(jnp.bfloat16), query_table, preferred_element_type=jnp.float32)
    queries = (query_features.astype(jnp.float32) + lookup).astype(jnp.bfloat16)

    own_queries = columns((queries,), y)
    near_queries = lax.ppermute(columns((queries,), 1 - y), "pos", near)

    def across(value):
        return lax.ppermute(value, "pos", near)

    def cores(values):
        return [lax.ppermute(v, "head", swap_perm(2)) for v in values]

    early = [lax.ppermute(normed, "pos", shift_perm(pos, k)) for k in shifts[1:-1]]
    first = [normed, across(normed), *early]
    first = lax.optimization_barrier(first)
    late = lax.ppermute(first[0], "pos", shift_perm(pos, shifts[-1]))
    first_other = [normed_other, *cores(first[1:])]
    second = [across(v) for v in first[2:]]
    keys_values = latent_keys_values(
        kv_ids, first + second, first_other + cores(second), kv_weights
    )
    near_state = decode(near_queries, keys_values, None, None)
    own_state = decode(own_queries, keys_values, None, None)
    late_near, near_state, own_state = lax.optimization_barrier(
        (across(late), near_state, own_state)
    )
    last = [late, late_near]
    last_other = cores(last)
    keys_values = latent_keys_values(kv_ids, last, last_other, kv_weights)
    near_state = decode(near_queries, keys_values, near_state, jnp.bfloat16)
    own_state = decode(own_queries, keys_values, own_state, jnp.float32)
    from_near = lax.ppermute(near_state, "pos", near).astype(jnp.float32)
    decoded = jnp.where(
        y == 0,
        jnp.concatenate([own_state, from_near], axis=1),
        jnp.concatenate([from_near, own_state], axis=1),
    )
    decoded = jnp.where(kept[:, None], decoded, 0.0)
    return (own_cols, decoded)


def on_device(sizes, *args):
    groups, pos, head = sizes
    enc_keys, latent_array, w_out, w_key = args[0], args[4], args[5], args[7]
    fits = (
        head == 2
        and pos % 2 == 0
        and pos > 2
        and groups % 2 == 0
        and enc_keys.shape[1] == pos * HEAD_DIM
        and enc_keys.shape[0] % (2 * HEAD_DIM) == 0
        and enc_keys.shape[0] < 2048
        and w_key.shape[0] % LANES == 0
        and w_out.shape[0] % (LANES * groups) == 0
        and w_out.shape[1] % LANES == 0
        and latent_array.shape[0] % LANES == 0
    )
    if fits:
        return fast_on_device((groups, pos), *args)
    return plain_on_device(*args)


def solution(mesh):
    return jax.shard_map(
        functools.partial(on_device, tuple(mesh.shape[a] for a in ("groups", "pos", "head"))),
        mesh=mesh,
        in_specs=(
            P(("groups", "pos"), "head"),
            P(("groups", "pos"), "head"),
            P(("groups", "pos")),
            P("groups", "head"),
            P(("groups", "pos"), None),
            P("head", "pos"),
            P(),
            P("pos", "head"),
            P("pos", "head"),
            P(("groups", "pos"), "head"),
            P(("groups", "pos")),
            P(None, "head"),
            P(None, "head"),
            P("groups"),
        ),
        out_specs=(P(("groups", "pos"), "head"), P(("groups", "pos"), "head")),
        check_vma=False,
    )
```

```python
import functools

import jax
import jax.numpy as jnp
from jax import lax
from jax.experimental import pallas as pl
from jax.experimental.pallas import tpu as pltpu
from jax.sharding import PartitionSpec as P

HEAD_DIM = 128


norm_eps = 1e-06


def prefix(shard, axis, combine, identity):
    peers, place = (lax.axis_size(axis), lax.axis_index(axis))
    everything = lax.all_gather(shard, axis)
    start = jnp.broadcast_to(jnp.asarray(identity, shard.dtype), shard.shape)

    def step(k, before):
        reached = k < place
        new = combine(before, everything[k])
        return jnp.where(reached, new, before)

    return lax.fori_loop(0, peers, step, start)


def plain_on_device(
    enc_keys,
    enc_values,
    input_ids,
    latent_queries,
    latent_array,
    w_out,
    norm_gain,
    w_key,
    w_value,
    query_features,
    query_ids,
    query_table,
    enc_bias,
    query_counts,
):
    tok_rows = enc_keys.shape[0]
    half_width = enc_keys.shape[1]
    local_heads = half_width // HEAD_DIM
    score_scale = HEAD_DIM ** (-0.5)
    modality = jnp.arange(enc_bias.shape[0], dtype=jnp.int32)
    in_onehot = (input_ids[:, None] == modality[None, :]).astype(jnp.float32)
    bias_rows = jnp.dot(in_onehot, enc_bias, precision=lax.Precision.HIGHEST)
    bias_heads = bias_rows.T[:, None, :]
    keys_split = enc_keys.reshape(tok_rows, local_heads, HEAD_DIM)
    values_split = enc_values.reshape(tok_rows, local_heads, HEAD_DIM)
    lat_total = latent_queries.shape[0]
    block_rows = min(512, lat_total)
    query_blocks = latent_queries.reshape(
        lat_total // block_rows, block_rows, local_heads, HEAD_DIM
    )

    def encode_block(block_queries):
        scores = (
            jnp.einsum(
                "nha,tha->hnt", block_queries, keys_split, preferred_element_type=jnp.float32
            )
            * score_scale
            + bias_heads
        )
        highest = jnp.max(scores, axis=2)
        weights = jnp.exp(scores - highest[:, :, None])
        totals = jnp.sum(weights, axis=2)
        summed = jnp.einsum(
            "hnt,tha->nha",
            weights.astype(jnp.bfloat16),
            values_split,
            preferred_element_type=jnp.float32,
        )
        return (highest.T, totals.T, summed.reshape(block_rows, half_width))

    block_max, block_tot, block_acc = lax.map(encode_block, query_blocks)
    row_highest = block_max.reshape(lat_total, local_heads)
    row_totals = block_tot.reshape(lat_total, local_heads)
    row_sums = block_acc.reshape(lat_total, half_width)
    own_rows = latent_array.shape[0]
    global_max = lax.pmax(row_highest, "pos")
    factor = jnp.exp(row_highest - global_max)
    scaled_sums = (row_sums.reshape(lat_total, local_heads, HEAD_DIM) * factor[:, :, None]).reshape(
        lat_total, half_width
    )
    totals, summed = (
        lax.psum_scatter(row_totals * factor, "pos", scatter_dimension=0, tiled=True),
        lax.psum_scatter(scaled_sums, "pos", scatter_dimension=0, tiled=True),
    )
    summed = summed.reshape(own_rows, local_heads, HEAD_DIM)
    attended = (summed / totals[:, :, None]).reshape(own_rows, half_width).astype(jnp.bfloat16)
    partial_value = jnp.dot(
        attended,
        lax.all_gather(w_out, "pos", axis=1, tiled=True),
        preferred_element_type=jnp.float32,
    )
    offset = lax.axis_index("head") * half_width
    projected = lax.psum(partial_value, "head")
    updated = latent_array.astype(jnp.float32) + projected
    mean_square = jnp.mean(updated * updated, axis=1, keepdims=True)
    normed_full = updated * lax.rsqrt(mean_square + norm_eps) * norm_gain
    normed = normed_full.astype(jnp.bfloat16)
    own_cols = lax.dynamic_slice_in_dim(normed_full, offset, half_width, 1)
    pieces = (
        lax.all_gather(w_key, "pos", axis=0, tiled=True),
        lax.all_gather(w_value, "pos", axis=0, tiled=True),
    )
    key_sum = jnp.dot(normed, pieces[0], preferred_element_type=jnp.float32)
    value_sum = jnp.dot(normed, pieces[1], preferred_element_type=jnp.float32)
    latent_keys = key_sum.astype(jnp.bfloat16)
    latent_values = value_sum.astype(jnp.bfloat16)
    q_onehot = (query_ids[:, None] == modality[None, :]).astype(jnp.int32)
    local_counts = jnp.sum(q_onehot, axis=0)
    before = prefix(
        local_counts, "pos", lambda earlier, later: earlier + later, jnp.zeros_like(local_counts)
    )
    within = jnp.cumsum(q_onehot, axis=0) - q_onehot
    ranked = jnp.sum((within + before[None, :]) * q_onehot, axis=1)
    limits = jnp.sum(q_onehot * query_counts[None, :], axis=1)
    kept_rows = ranked < limits
    lookup = jnp.dot(q_onehot.astype(jnp.bfloat16), query_table, preferred_element_type=jnp.float32)
    queries = (
        (query_features.astype(jnp.float32) + lookup)
        .astype(jnp.bfloat16)
        .reshape(tok_rows, local_heads, HEAD_DIM)
    )

    def fold_rows(running, key_rows, value_rows):
        running_max, running_tot, running_acc = running
        key_heads = key_rows.reshape(key_rows.shape[0], local_heads, HEAD_DIM)
        value_heads = value_rows.reshape(value_rows.shape[0], local_heads, HEAD_DIM)
        scores = (
            jnp.einsum("tha,rha->htr", queries, key_heads, preferred_element_type=jnp.float32)
            * score_scale
        )
        new_max = jnp.maximum(running_max, jnp.max(scores, axis=2))
        fade = jnp.exp(running_max - new_max)
        weights = jnp.exp(scores - new_max[:, :, None])
        new_tot = running_tot * fade + jnp.sum(weights, axis=2)
        new_acc = running_acc * fade[:, :, None] + jnp.einsum(
            "htr,rha->hta",
            weights.astype(jnp.bfloat16),
            value_heads,
            preferred_element_type=jnp.float32,
        )
        return (new_max, new_tot, new_acc)

    start_state = (
        jnp.full((local_heads, tok_rows), -jnp.inf, jnp.float32),
        jnp.zeros((local_heads, tok_rows), jnp.float32),
        jnp.zeros((local_heads, tok_rows, HEAD_DIM), jnp.float32),
    )
    running = start_state
    pieces = (
        lax.all_gather(latent_keys, "pos", axis=0, tiled=True),
        lax.all_gather(latent_values, "pos", axis=0, tiled=True),
    )
    row_count = pieces[0].shape[0]
    key_blocks = pieces[0].reshape(row_count // 512, 512, half_width)
    value_blocks = pieces[1].reshape(row_count // 512, 512, half_width)

    def scan_step(state, pair):
        return (fold_rows(state, pair[0], pair[1]), None)

    running, ignored = lax.scan(scan_step, running, (key_blocks, value_blocks))
    final_max, final_tot, final_acc = running
    dec_heads = final_acc / final_tot[:, :, None]
    dec_rows = jnp.transpose(dec_heads, (1, 0, 2)).reshape(tok_rows, half_width)
    decoded = jnp.where(kept_rows[:, None], dec_rows, 0.0)
    return (own_cols, decoded)


LANES = 128
EXTRA = 16
LOG2E = 1.4426950408889634
EXP2_SCALE = LOG2E * HEAD_DIM**-0.5
NT = (((1,), (1,)), ((), ()))


def params(mib):
    return pltpu.CompilerParams(vmem_limit_bytes=mib << 20)


def cost(flops, nbytes, exps=0):
    return pl.CostEstimate(flops=int(flops), bytes_accessed=int(nbytes), transcendentals=int(exps))


def whole(shape):
    return pl.BlockSpec(shape, lambda *args: (0,) * len(shape))


def pack_kernel(k_ref, v_ref, extra_ref, out_ref):
    tokens = k_ref.shape[0]
    out_ref[:tokens, :HEAD_DIM] = k_ref[...]
    out_ref[:tokens, HEAD_DIM:] = v_ref[...]
    out_ref[tokens:, :] = extra_ref[...]


def pack(keys, values, extra):
    tokens, width = keys.shape
    heads = width // HEAD_DIM
    column = pl.BlockSpec((tokens, HEAD_DIM), lambda h: (0, h))
    block = (tokens + EXTRA, 2 * HEAD_DIM)
    return pl.pallas_call(
        pack_kernel,
        grid=(heads,),
        in_specs=[column, column, whole(extra.shape)],
        out_specs=pl.BlockSpec(block, lambda h: (h, 0)),
        out_shape=jax.ShapeDtypeStruct((heads * block[0], block[1]), keys.dtype),
        compiler_params=params(16),
        cost_estimate=cost(0, 8 * tokens * width),
        name="pack_heads",
    )(keys, values, extra)


def encode_kernel(pos, tokens, q_ref, kv_ref, bias_ref, out_ref):
    rows = q_ref.shape[0]
    queries = q_ref[...]
    ones = jnp.ones((tokens, LANES), jnp.bfloat16)
    row_bits = kv_ref.shape[1]
    top = jnp.full((rows, 1), -jnp.inf, jnp.float32)
    acc = jnp.zeros((rows, 2 * HEAD_DIM), jnp.float32)
    for j in range(pos):
        base = j * (tokens + EXTRA)
        band = slice(base, base + tokens)
        scores = lax.dot_general(
            queries, kv_ref[band, :HEAD_DIM], NT, preferred_element_type=jnp.float32
        )
        tail = kv_ref[base + tokens : base + tokens + EXTRA, :].astype(jnp.float32)
        kind = jnp.concatenate([tail[r : r + 1] for r in range(tokens // row_bits)], axis=1)
        bias = jnp.zeros_like(kind)
        for m in range(bias_ref.shape[0]):
            bias = jnp.where(kind == m, bias_ref[m] * LOG2E, bias)
        scores = scores * EXP2_SCALE + bias
        new_top = jnp.maximum(top, jnp.max(scores, axis=1, keepdims=True))
        weights = jnp.exp2(scores - new_top).astype(jnp.bfloat16)
        acc = acc * jnp.exp2(top - new_top) + jnp.dot(
            weights,
            jnp.concatenate([kv_ref[band, HEAD_DIM:], ones], axis=1),
            preferred_element_type=jnp.float32,
        )
        top = new_top
    out_ref[...] = (acc[:, :HEAD_DIM] / acc[:, HEAD_DIM:]).astype(jnp.bfloat16)


def encode(queries, kv, bias, pos):
    latents = queries.shape[0]
    tokens = kv.shape[0] // pos - EXTRA
    rows = min(512, latents)
    block = pl.BlockSpec((rows, HEAD_DIM), lambda i: (i, 0))
    return pl.pallas_call(
        functools.partial(encode_kernel, pos, tokens),
        grid=(latents // rows,),
        in_specs=[block, whole(kv.shape), pl.BlockSpec(memory_space=pltpu.SMEM)],
        out_specs=block,
        out_shape=jax.ShapeDtypeStruct((latents, HEAD_DIM), jnp.bfloat16),
        compiler_params=params(32),
        cost_estimate=cost(
            16 * latents * tokens * pos * HEAD_DIM, 2 * kv.size, latents * tokens * pos
        ),
        name="encode_head",
    )(queries, kv, bias)


def project_kernel(heads, far, ids_ref, att_in_ref, *refs):
    w_refs, out_ref, att_ref = refs[:-2], refs[-2], refs[-1]
    rows = att_ref.shape[0]
    for h in range(heads):
        att_ref[:, h * HEAD_DIM : (h + 1) * HEAD_DIM] = att_in_ref[h * rows : (h + 1) * rows, :]
    cols = w_refs[0].shape[1]
    depth = att_ref.shape[1] // 2

    def place(slot, value):
        out_ref[:, pl.ds(pl.multiple_of(ids_ref[slot] * cols, cols), cols)] = value

    for slot in range(2):
        place(slot, jnp.dot(att_ref[...], w_refs[slot][...], preferred_element_type=jnp.float32))
    mine, theirs = [
        att_ref[:, pl.ds(pl.multiple_of(ids_ref[2 * far + k] * depth, depth), depth)]
        for k in range(2)
    ]
    for j in range(2):
        for k in range(far - 1):
            band = slice(k * depth, (k + 1) * depth)
            total = jnp.dot(
                mine, w_refs[2 + 2 * j][band, :], preferred_element_type=jnp.float32
            ) + jnp.dot(theirs, w_refs[3 + 2 * j][band, :], preferred_element_type=jnp.float32)
            place(2 + j * (far - 1) + k, total)


def project(ids, attended, weights, rows):
    heads = attended.shape[0] // rows
    far = (ids.shape[0] - 2) // 2
    width = heads * HEAD_DIM
    out_cols = 2 * far * weights[0].shape[1]
    grid_spec = pltpu.PrefetchScalarGridSpec(
        num_scalar_prefetch=1,
        grid=(1,),
        in_specs=[whole(v.shape) for v in (attended, *weights)],
        out_specs=whole((rows, out_cols)),
        scratch_shapes=[pltpu.VMEM((rows, width), jnp.bfloat16)],
    )
    return pl.pallas_call(
        functools.partial(project_kernel, heads, far),
        grid_spec=grid_spec,
        out_shape=jax.ShapeDtypeStruct((rows, out_cols), jnp.float32),
        compiler_params=params(32),
        cost_estimate=cost(2 * rows * width * out_cols, 2 * width * out_cols + 4 * rows * out_cols),
        name="project_rows",
    )(ids, attended, *weights)


def norm_kernel(
    ids_ref, mine_ref, theirs_ref, latent_ref, gain_ref, out_ref, normed_ref, other_ref, full_ref
):
    updated = latent_ref[...].astype(jnp.float32) + (mine_ref[...] + theirs_ref[...])
    mean_square = jnp.mean(updated * updated, axis=1, keepdims=True)
    full_ref[...] = updated * lax.rsqrt(mean_square + norm_eps) * gain_ref[...]
    half = out_ref.shape[1]
    own = full_ref[:, pl.ds(pl.multiple_of(ids_ref[0] * half, half), half)]
    out_ref[...] = own
    normed_ref[...] = own.astype(jnp.bfloat16)
    other = full_ref[:, pl.ds(pl.multiple_of((1 - ids_ref[0]) * half, half), half)]
    other_ref[...] = other.astype(jnp.bfloat16)


def normalise(place, mine, theirs, latent_array, gain):
    rows, width = mine.shape
    half = width // 2
    grid_spec = pltpu.PrefetchScalarGridSpec(
        num_scalar_prefetch=1,
        grid=(1,),
        in_specs=[whole((rows, width))] * 3 + [whole((1, width))],
        out_specs=[whole((rows, half))] * 3,
        scratch_shapes=[pltpu.VMEM((rows, width), jnp.float32)],
    )
    return pl.pallas_call(
        norm_kernel,
        grid_spec=grid_spec,
        out_shape=[
            jax.ShapeDtypeStruct((rows, half), jnp.float32),
            jax.ShapeDtypeStruct((rows, half), jnp.bfloat16),
            jax.ShapeDtypeStruct((rows, half), jnp.bfloat16),
        ],
        compiler_params=params(32),
        cost_estimate=cost(6 * rows * width, 13 * rows * width),
        name="norm_rows",
    )(place.reshape(1), mine, theirs, latent_array, gain)


def latents_kernel(pieces, ids_ref, *refs):
    mine, theirs = refs[:pieces], refs[pieces : 2 * pieces]
    w_refs, (out_ref, normed_ref, w_ref) = refs[2 * pieces : -3], refs[-3:]
    rows, half = mine[0].shape
    slots = ids_ref.shape[0] - 1
    depth = 2 * half // slots

    @pl.when(pl.program_id(0) == 0)
    def arrange():
        for j in range(slots):
            at = ids_ref[1 + j]
            is_mine = at // (slots // 2) == ids_ref[0]
            start = pl.multiple_of((at % (slots // 2)) * depth, depth)
            for r in range(pieces):
                both = [v[r][:, pl.ds(start, depth)] for v in (mine, theirs)]
                normed_ref[r * rows : (r + 1) * rows, j * depth : (j + 1) * depth] = jnp.where(
                    is_mine, both[0], both[1]
                )

    for j, band in enumerate(w_refs):
        w_ref[j * depth : (j + 1) * depth, :] = band[...]
    out_ref[...] = jnp.dot(
        normed_ref[...], w_ref[...], preferred_element_type=jnp.float32
    ).astype(jnp.bfloat16)


def latent_keys_values(ids, mine, theirs, bands):
    pieces = len(mine)
    rows, half = mine[0].shape
    depth, width = bands[0].shape
    block = min(512, width)
    total = depth * len(bands)
    grid_spec = pltpu.PrefetchScalarGridSpec(
        num_scalar_prefetch=1,
        grid=(width // block,),
        in_specs=[whole((rows, half))] * (2 * pieces)
        + [pl.BlockSpec((depth, block), lambda i, ids: (0, i))] * len(bands),
        out_specs=pl.BlockSpec((rows * pieces, block), lambda i, ids: (0, i)),
        scratch_shapes=[
            pltpu.VMEM((rows * pieces, total), jnp.bfloat16),
            pltpu.VMEM((total, block), jnp.bfloat16),
        ],
    )
    return pl.pallas_call(
        functools.partial(latents_kernel, pieces),
        grid_spec=grid_spec,
        out_shape=jax.ShapeDtypeStruct((rows * pieces, width), jnp.bfloat16),
        compiler_params=params(40),
        cost_estimate=cost(2 * rows * pieces * total * width, 2 * total * width),
        name="latent_keys_values",
    )(ids, *mine, *theirs, *bands)


def decode_kernel(first, last, *refs):
    q_ref, k_ref, v_ref = refs[:3]
    rest = refs[3:]
    if not first:
        old_max_ref, old_acc_ref = rest[:2]
        rest = rest[2:]
    latents = k_ref.shape[0]
    chunk = 512 if latents % 512 == 0 else 256 if latents % 256 == 0 else latents
    ones = jnp.ones((chunk, LANES), jnp.bfloat16)
    for h in range(q_ref.shape[1] // HEAD_DIM):
        cols = slice(h * HEAD_DIM, (h + 1) * HEAD_DIM)
        wide = slice(2 * h * HEAD_DIM, 2 * (h + 1) * HEAD_DIM)
        if first:
            top, acc = None, None
        else:
            top, acc = old_max_ref[:, cols][:, :1], old_acc_ref[:, wide]
        for start in range(0, latents, chunk):
            band = slice(start, start + chunk)
            scores = lax.dot_general(
                q_ref[:, cols], k_ref[band, cols], NT, preferred_element_type=jnp.float32
            )
            scores = scores * EXP2_SCALE
            new_top = jnp.max(scores, axis=1, keepdims=True)
            if top is not None:
                new_top = jnp.maximum(top, new_top)
            weights = jnp.exp2(scores - new_top).astype(jnp.bfloat16)
            summed = jnp.dot(
                weights,
                jnp.concatenate([v_ref[band, cols], ones], axis=1),
                preferred_element_type=jnp.float32,
            )
            if top is not None:
                summed = summed + acc * jnp.exp2(top - new_top)
            top, acc = new_top, summed
        if last:
            (out_ref,) = rest
            out_ref[:, cols] = (acc[:, :HEAD_DIM] / acc[:, HEAD_DIM:]).astype(out_ref.dtype)
        else:
            max_ref, acc_ref = rest
            max_ref[:, cols] = jnp.broadcast_to(top, (top.shape[0], HEAD_DIM))
            acc_ref[:, wide] = acc


def decode(queries, keys_values, state, out_type):
    first, last = state is None, out_type is not None
    tokens, width = queries.shape
    latents = keys_values.shape[0]
    pair = min(2 * HEAD_DIM, width)
    steps = width // pair
    narrow = pl.BlockSpec((tokens, pair), lambda i: (0, i))
    wide = pl.BlockSpec((tokens, 2 * pair), lambda i: (0, i))
    in_specs = [
        narrow,
        pl.BlockSpec((latents, pair), lambda i: (0, i)),
        pl.BlockSpec((latents, pair), lambda i: (0, steps + i)),
    ]
    args = [queries, keys_values, keys_values]
    if not first:
        in_specs += [narrow, wide]
        args += list(state)
    if last:
        out_specs = narrow
        out_shape = jax.ShapeDtypeStruct((tokens, width), out_type)
    else:
        out_specs = [narrow, wide]
        out_shape = [
            jax.ShapeDtypeStruct((tokens, width), jnp.float32),
            jax.ShapeDtypeStruct((tokens, 2 * width), jnp.float32),
        ]
    return pl.pallas_call(
        functools.partial(decode_kernel, first, last),
        grid=(steps,),
        in_specs=in_specs,
        out_specs=out_specs,
        out_shape=out_shape,
        compiler_params=params(40),
        cost_estimate=cost(
            16 * tokens * latents * width,
            4 * latents * width + 16 * tokens * width,
            tokens * latents * (width // HEAD_DIM),
        ),
        name="decode_rows",
    )(*args)


def swap_perm(size):
    return [(i, i ^ 1) for i in range(size)]


def shift_perm(size, k):
    far = size // 2
    return [(((z + k) % far) * 2 + y, z * 2 + y) for z in range(far) for y in range(2)]


def hop_perm(size, step, way):
    far = size // 2
    moves = [(z, z + 1) for z in range(step - 1, far - 1)]
    if way < 0:
        moves = [(far - 1 - a, far - 1 - b) for a, b in moves]
    return [(a * 2 + y, b * 2 + y) for a, b in moves for y in range(2)]


def fast_on_device(
    sizes,
    enc_keys,
    enc_values,
    input_ids,
    latent_queries,
    latent_array,
    w_out,
    norm_gain,
    w_key,
    w_value,
    query_features,
    query_ids,
    query_table,
    enc_bias,
    query_counts,
):
    groups, pos = sizes
    far = pos // 2
    p = lax.axis_index("pos")
    place = lax.axis_index("head")
    rows = latent_array.shape[0]
    tokens, half_width = enc_keys.shape
    heads = half_width // HEAD_DIM
    mods = enc_bias.shape[0]
    modality = jnp.arange(mods, dtype=jnp.int32)
    pair = 2 * HEAD_DIM

    far, z, y, x = pos // 2, p // 2, p % 2, lax.axis_index("groups") % 2
    near = swap_perm(pos)

    def over_groups(value):
        return lax.ppermute(value, "groups", swap_perm(groups))

    def over_near(value):
        return lax.ppermute(value, "pos", near)

    def over_far(value, k):
        return lax.ppermute(value, "pos", shift_perm(pos, k))

    shifts = sorted(range(far), key=lambda k: min(k, far - k))
    out_half = w_out.shape[0] // 2
    out_sent = lax.dynamic_slice_in_dim(w_out, x * out_half, out_half, 0)
    out_far = [over_far(out_sent, k) for k in shifts[1:]]
    out_near = over_near(w_out)
    out_ids = [p, p ^ 1]
    for j in range(2):
        out_ids += [((z + k) % far) * 2 + (y ^ j) for k in shifts[1:]]
    out_ids = jnp.stack([*out_ids, x, 1 - x]).astype(jnp.int32)

    part = half_width // 2

    def columns(arrays, which):
        return jnp.concatenate(
            [lax.dynamic_slice_in_dim(v, which * part, part, 1) for v in arrays], axis=1
        )

    kv_own = columns((w_key, w_value), y)
    kv_near = over_near(columns((w_key, w_value), 1 - y))
    lookup = jnp.dot(
        (query_ids[:, None] == modality[None, :]).astype(jnp.bfloat16),
        query_table,
        preferred_element_type=jnp.float32,
    )
    queries = (query_features.astype(jnp.float32) + lookup).astype(jnp.bfloat16)
    own_queries = columns((queries,), y)
    near_queries = over_near(columns((queries,), 1 - y))


    q_onehot = (query_ids[:, None] == modality[None, :]).astype(jnp.int32)
    local_counts = jnp.sum(q_onehot, axis=0)
    id_rows = tokens // pair
    counted = jnp.concatenate([local_counts // 16, local_counts % 16])
    extra = jnp.concatenate(
        [
            input_ids.reshape(id_rows, pair),
            jnp.pad(counted[None, :], ((0, EXTRA - id_rows - 1), (0, pair - 2 * mods))),
        ]
    ).astype(jnp.bfloat16)
    payload = pack(enc_keys, enc_values, extra)
    kv = lax.all_to_all(payload, "pos", 0, 0, tiled=True)
    head_queries = lax.dynamic_slice_in_dim(latent_queries, p * HEAD_DIM, HEAD_DIM, 1)
    head_bias = lax.dynamic_slice_in_dim(enc_bias, p, 1, 1)[:, 0]
    kv_sent = jnp.where(x == 0, kv_own, kv_near)
    kv, kv_sent, near_queries, out_far, out_near = lax.optimization_barrier(
        (kv, kv_sent, near_queries, out_far, out_near)
    )
    out_far = jnp.concatenate(out_far)
    out_bands = [out_far, over_near(out_far), over_groups(out_far)]

    def hop(step, pair):
        return [
            lax.ppermute(v, "pos", hop_perm(pos, step, way)) for v, way in zip(pair, (1, -1))
        ]

    hops = {1: hop(1, [kv_sent, kv_sent])}
    attended = encode(head_queries, kv, head_bias, pos)
    attended, hops[1], out_bands = lax.optimization_barrier((attended, hops[1], out_bands))
    out_far, out_across, out_other = out_bands
    out_bands = [w_out, out_near, out_far, out_other, out_across, over_near(out_other)]
    hops[2] = hop(2, hops[1])
    attended = lax.all_to_all(attended, "pos", 0, 0, tiled=True)
    attended, hops[2], out_bands = lax.optimization_barrier((attended, hops[2], out_bands))
    for step in range(3, far):
        hops[step] = hop(step, hops[step - 1])
    partial_value = project(out_ids, attended, out_bands, rows)
    theirs = lax.ppermute(partial_value, "head", swap_perm(2))
    theirs, hops = lax.optimization_barrier((theirs, hops))
    own_cols, normed, normed_other = normalise(
        place, partial_value, theirs, latent_array, norm_gain[None, :]
    )
    kv_bands = [kv_own, kv_near]
    kv_at = [p, p ^ 1]
    for k in range(1, far):
        moved = jnp.where(z + k < far, hops[k][1], hops[far - k][0])
        kv_bands += [moved, over_groups(moved)]
        there = ((z + k) % far) * 2
        kv_at += [there + (y ^ x), there + (1 - (y ^ x))]
    kv_ids = jnp.stack([place, *kv_at]).astype(jnp.int32)

    counts = kv.reshape(pos, tokens + EXTRA, pair)[:, tokens + id_rows, : 2 * mods]
    counts = counts.astype(jnp.int32)
    counts = counts[:, :mods] * 16 + counts[:, mods:]
    earlier = jnp.arange(pos, dtype=jnp.int32)[:, None] < p
    before = jnp.sum(jnp.where(earlier, counts, 0), axis=0)
    within = jnp.cumsum(q_onehot, axis=0) - q_onehot
    ranked = jnp.sum((within + before[None, :]) * q_onehot, axis=1)
    limits = jnp.sum(q_onehot * query_counts[None, :], axis=1)
    kept = ranked < limits
    def cores(values):
        return [lax.ppermute(v, "head", swap_perm(2)) for v in values]

    def fold(mine, other, states, types):
        keys_values = latent_keys_values(kv_ids, mine, other, kv_bands)
        return [
            decode(q, keys_values, state, kind)
            for q, state, kind in zip((near_queries, own_queries), states, types)
        ]

    first = [normed, over_near(normed), *[over_far(normed, k) for k in shifts[1:-1]]]
    first, kept = lax.optimization_barrier((first, kept))
    second = [over_far(first[0], shifts[-1]), *[over_near(v) for v in first[2:]]]
    states = fold(first, [normed_other, *cores(first[1:])], [None, None], [None, None])
    second, states = lax.optimization_barrier((second, states))
    last = over_near(second[0])
    states = fold(second, cores(second), states, [None, None])
    last, states = lax.optimization_barrier((last, states))
    near_state, own_state = fold([last], cores([last]), states, [jnp.bfloat16, jnp.float32])
    from_near = lax.ppermute(near_state, "pos", near).astype(jnp.float32)
    decoded = jnp.where(
        y == 0,
        jnp.concatenate([own_state, from_near], axis=1),
        jnp.concatenate([from_near, own_state], axis=1),
    )
    decoded = jnp.where(kept[:, None], decoded, 0.0)
    return (own_cols, decoded)


def on_device(sizes, *args):
    groups, pos, head = sizes
    enc_keys, latent_array, w_out, w_key = args[0], args[4], args[5], args[7]
    fits = (
        head == 2
        and pos % 2 == 0
        and pos > 2
        and groups % 2 == 0
        and enc_keys.shape[1] == pos * HEAD_DIM
        and enc_keys.shape[0] % (2 * HEAD_DIM) == 0
        and enc_keys.shape[0] < 2048
        and w_key.shape[0] % LANES == 0
        and w_out.shape[0] % (2 * LANES) == 0
        and w_out.shape[1] % LANES == 0
        and latent_array.shape[0] % LANES == 0
    )
    if fits:
        return fast_on_device((groups, pos), *args)
    return plain_on_device(*args)


def solution(mesh):
    return jax.shard_map(
        functools.partial(on_device, tuple(mesh.shape[a] for a in ("groups", "pos", "head"))),
        mesh=mesh,
        in_specs=(
            P(("groups", "pos"), "head"),
            P(("groups", "pos"), "head"),
            P(("groups", "pos")),
            P("groups", "head"),
            P(("groups", "pos"), None),
            P("head", "pos"),
            P(),
            P("pos", "head"),
            P("pos", "head"),
            P(("groups", "pos"), "head"),
            P(("groups", "pos")),
            P(None, "head"),
            P(None, "head"),
            P("groups"),
        ),
        out_specs=(P(("groups", "pos"), "head"), P(("groups", "pos"), "head")),
        check_vma=False,
    )
```

```python
import functools

import jax
import jax.numpy as jnp
from jax import lax
from jax.experimental import pallas as pl
from jax.experimental.pallas import tpu as pltpu
from jax.sharding import PartitionSpec as P

HEAD_DIM = 128


norm_eps = 1e-06


def prefix(shard, axis, combine, identity):
    peers, place = (lax.axis_size(axis), lax.axis_index(axis))
    everything = lax.all_gather(shard, axis)
    start = jnp.broadcast_to(jnp.asarray(identity, shard.dtype), shard.shape)

    def step(k, before):
        reached = k < place
        new = combine(before, everything[k])
        return jnp.where(reached, new, before)

    return lax.fori_loop(0, peers, step, start)


def plain_on_device(
    enc_keys,
    enc_values,
    input_ids,
    latent_queries,
    latent_array,
    w_out,
    norm_gain,
    w_key,
    w_value,
    query_features,
    query_ids,
    query_table,
    enc_bias,
    query_counts,
):
    tok_rows = enc_keys.shape[0]
    half_width = enc_keys.shape[1]
    local_heads = half_width // HEAD_DIM
    score_scale = HEAD_DIM ** (-0.5)
    modality = jnp.arange(enc_bias.shape[0], dtype=jnp.int32)
    in_onehot = (input_ids[:, None] == modality[None, :]).astype(jnp.float32)
    bias_rows = jnp.dot(in_onehot, enc_bias, precision=lax.Precision.HIGHEST)
    bias_heads = bias_rows.T[:, None, :]
    keys_split = enc_keys.reshape(tok_rows, local_heads, HEAD_DIM)
    values_split = enc_values.reshape(tok_rows, local_heads, HEAD_DIM)
    lat_total = latent_queries.shape[0]
    block_rows = min(512, lat_total)
    query_blocks = latent_queries.reshape(
        lat_total // block_rows, block_rows, local_heads, HEAD_DIM
    )

    def encode_block(block_queries):
        scores = (
            jnp.einsum(
                "nha,tha->hnt", block_queries, keys_split, preferred_element_type=jnp.float32
            )
            * score_scale
            + bias_heads
        )
        highest = jnp.max(scores, axis=2)
        weights = jnp.exp(scores - highest[:, :, None])
        totals = jnp.sum(weights, axis=2)
        summed = jnp.einsum(
            "hnt,tha->nha",
            weights.astype(jnp.bfloat16),
            values_split,
            preferred_element_type=jnp.float32,
        )
        return (highest.T, totals.T, summed.reshape(block_rows, half_width))

    block_max, block_tot, block_acc = lax.map(encode_block, query_blocks)
    row_highest = block_max.reshape(lat_total, local_heads)
    row_totals = block_tot.reshape(lat_total, local_heads)
    row_sums = block_acc.reshape(lat_total, half_width)
    own_rows = latent_array.shape[0]
    global_max = lax.pmax(row_highest, "pos")
    factor = jnp.exp(row_highest - global_max)
    scaled_sums = (row_sums.reshape(lat_total, local_heads, HEAD_DIM) * factor[:, :, None]).reshape(
        lat_total, half_width
    )
    totals, summed = (
        lax.psum_scatter(row_totals * factor, "pos", scatter_dimension=0, tiled=True),
        lax.psum_scatter(scaled_sums, "pos", scatter_dimension=0, tiled=True),
    )
    summed = summed.reshape(own_rows, local_heads, HEAD_DIM)
    attended = (summed / totals[:, :, None]).reshape(own_rows, half_width).astype(jnp.bfloat16)
    partial_value = jnp.dot(
        attended,
        lax.all_gather(w_out, "pos", axis=1, tiled=True),
        preferred_element_type=jnp.float32,
    )
    offset = lax.axis_index("head") * half_width
    projected = lax.psum(partial_value, "head")
    updated = latent_array.astype(jnp.float32) + projected
    mean_square = jnp.mean(updated * updated, axis=1, keepdims=True)
    normed_full = updated * lax.rsqrt(mean_square + norm_eps) * norm_gain
    normed = normed_full.astype(jnp.bfloat16)
    own_cols = lax.dynamic_slice_in_dim(normed_full, offset, half_width, 1)
    pieces = (
        lax.all_gather(w_key, "pos", axis=0, tiled=True),
        lax.all_gather(w_value, "pos", axis=0, tiled=True),
    )
    key_sum = jnp.dot(normed, pieces[0], preferred_element_type=jnp.float32)
    value_sum = jnp.dot(normed, pieces[1], preferred_element_type=jnp.float32)
    latent_keys = key_sum.astype(jnp.bfloat16)
    latent_values = value_sum.astype(jnp.bfloat16)
    q_onehot = (query_ids[:, None] == modality[None, :]).astype(jnp.int32)
    local_counts = jnp.sum(q_onehot, axis=0)
    before = prefix(
        local_counts, "pos", lambda earlier, later: earlier + later, jnp.zeros_like(local_counts)
    )
    within = jnp.cumsum(q_onehot, axis=0) - q_onehot
    ranked = jnp.sum((within + before[None, :]) * q_onehot, axis=1)
    limits = jnp.sum(q_onehot * query_counts[None, :], axis=1)
    kept_rows = ranked < limits
    lookup = jnp.dot(q_onehot.astype(jnp.bfloat16), query_table, preferred_element_type=jnp.float32)
    queries = (
        (query_features.astype(jnp.float32) + lookup)
        .astype(jnp.bfloat16)
        .reshape(tok_rows, local_heads, HEAD_DIM)
    )

    def fold_rows(running, key_rows, value_rows):
        running_max, running_tot, running_acc = running
        key_heads = key_rows.reshape(key_rows.shape[0], local_heads, HEAD_DIM)
        value_heads = value_rows.reshape(value_rows.shape[0], local_heads, HEAD_DIM)
        scores = (
            jnp.einsum("tha,rha->htr", queries, key_heads, preferred_element_type=jnp.float32)
            * score_scale
        )
        new_max = jnp.maximum(running_max, jnp.max(scores, axis=2))
        fade = jnp.exp(running_max - new_max)
        weights = jnp.exp(scores - new_max[:, :, None])
        new_tot = running_tot * fade + jnp.sum(weights, axis=2)
        new_acc = running_acc * fade[:, :, None] + jnp.einsum(
            "htr,rha->hta",
            weights.astype(jnp.bfloat16),
            value_heads,
            preferred_element_type=jnp.float32,
        )
        return (new_max, new_tot, new_acc)

    start_state = (
        jnp.full((local_heads, tok_rows), -jnp.inf, jnp.float32),
        jnp.zeros((local_heads, tok_rows), jnp.float32),
        jnp.zeros((local_heads, tok_rows, HEAD_DIM), jnp.float32),
    )
    running = start_state
    pieces = (
        lax.all_gather(latent_keys, "pos", axis=0, tiled=True),
        lax.all_gather(latent_values, "pos", axis=0, tiled=True),
    )
    row_count = pieces[0].shape[0]
    key_blocks = pieces[0].reshape(row_count // 512, 512, half_width)
    value_blocks = pieces[1].reshape(row_count // 512, 512, half_width)

    def scan_step(state, pair):
        return (fold_rows(state, pair[0], pair[1]), None)

    running, ignored = lax.scan(scan_step, running, (key_blocks, value_blocks))
    final_max, final_tot, final_acc = running
    dec_heads = final_acc / final_tot[:, :, None]
    dec_rows = jnp.transpose(dec_heads, (1, 0, 2)).reshape(tok_rows, half_width)
    decoded = jnp.where(kept_rows[:, None], dec_rows, 0.0)
    return (own_cols, decoded)


LANES = 128
EXTRA = 16
BIG = 56
LOG2E = 1.4426950408889634
EXP2_SCALE = LOG2E * HEAD_DIM**-0.5
NT = (((1,), (1,)), ((), ()))


def params(mib):
    return pltpu.CompilerParams(vmem_limit_bytes=mib << 20)


def cost(flops, nbytes, exps=0):
    return pl.CostEstimate(flops=int(flops), bytes_accessed=int(nbytes), transcendentals=int(exps))


def whole(shape):
    return pl.BlockSpec(shape, lambda *args: (0,) * len(shape))


def pack_kernel(k_ref, v_ref, extra_ref, out_ref):
    tokens = k_ref.shape[0]
    out_ref[:tokens, :HEAD_DIM] = k_ref[...]
    out_ref[:tokens, HEAD_DIM:] = v_ref[...]
    out_ref[tokens:, :] = extra_ref[...]


def pack(keys, values, extra):
    tokens, width = keys.shape
    heads = width // HEAD_DIM
    column = pl.BlockSpec((tokens, HEAD_DIM), lambda h: (0, h))
    block = (tokens + EXTRA, 2 * HEAD_DIM)
    return pl.pallas_call(
        pack_kernel,
        grid=(heads,),
        in_specs=[column, column, whole(extra.shape)],
        out_specs=pl.BlockSpec(block, lambda h: (h, 0)),
        out_shape=jax.ShapeDtypeStruct((heads * block[0], block[1]), keys.dtype),
        compiler_params=params(BIG),
        cost_estimate=cost(0, 8 * tokens * width),
        name="pack_heads",
    )(keys, values, extra)


def encode_kernel(pos, tokens, q_ref, kv_ref, bias_ref, out_ref):
    rows = q_ref.shape[0]
    queries = q_ref[...]
    ones = jnp.ones((tokens, LANES), jnp.bfloat16)
    row_bits = kv_ref.shape[1]
    top = jnp.full((rows, 1), -jnp.inf, jnp.float32)
    acc = jnp.zeros((rows, 2 * HEAD_DIM), jnp.float32)
    for j in range(pos):
        base = j * (tokens + EXTRA)
        band = slice(base, base + tokens)
        scores = lax.dot_general(
            queries, kv_ref[band, :HEAD_DIM], NT, preferred_element_type=jnp.float32
        )
        tail = kv_ref[base + tokens : base + tokens + EXTRA, :].astype(jnp.float32)
        kind = jnp.concatenate([tail[r : r + 1] for r in range(tokens // row_bits)], axis=1)
        bias = jnp.zeros_like(kind)
        for m in range(bias_ref.shape[0]):
            bias = jnp.where(kind == m, bias_ref[m] * LOG2E, bias)
        scores = scores * EXP2_SCALE + bias
        new_top = jnp.maximum(top, jnp.max(scores, axis=1, keepdims=True))
        weights = jnp.exp2(scores - new_top).astype(jnp.bfloat16)
        acc = acc * jnp.exp2(top - new_top) + jnp.dot(
            weights,
            jnp.concatenate([kv_ref[band, HEAD_DIM:], ones], axis=1),
            preferred_element_type=jnp.float32,
        )
        top = new_top
    out_ref[...] = (acc[:, :HEAD_DIM] / acc[:, HEAD_DIM:]).astype(jnp.bfloat16)


def encode(queries, kv, bias, pos):
    latents = queries.shape[0]
    tokens = kv.shape[0] // pos - EXTRA
    rows = min(512, latents)
    block = pl.BlockSpec((rows, HEAD_DIM), lambda i: (i, 0))
    return pl.pallas_call(
        functools.partial(encode_kernel, pos, tokens),
        grid=(latents // rows,),
        in_specs=[block, whole(kv.shape), pl.BlockSpec(memory_space=pltpu.SMEM)],
        out_specs=block,
        out_shape=jax.ShapeDtypeStruct((latents, HEAD_DIM), jnp.bfloat16),
        compiler_params=params(BIG),
        cost_estimate=cost(
            16 * latents * tokens * pos * HEAD_DIM, 2 * kv.size, latents * tokens * pos
        ),
        name="encode_head",
    )(queries, kv, bias)


def project_kernel(heads, far, ids_ref, att_in_ref, *refs):
    w_refs, out_ref, att_ref = refs[:-2], refs[-2], refs[-1]
    rows = att_ref.shape[0]
    for h in range(heads):
        att_ref[:, h * HEAD_DIM : (h + 1) * HEAD_DIM] = att_in_ref[h * rows : (h + 1) * rows, :]
    cols = w_refs[0].shape[1]
    depth = att_ref.shape[1] // 2

    def place(slot, value):
        out_ref[:, pl.ds(pl.multiple_of(ids_ref[slot] * cols, cols), cols)] = value

    for slot in range(2):
        place(slot, jnp.dot(att_ref[...], w_refs[slot][...], preferred_element_type=jnp.float32))
    mine, theirs = [
        att_ref[:, pl.ds(pl.multiple_of(ids_ref[2 * far + k] * depth, depth), depth)]
        for k in range(2)
    ]
    for j in range(2):
        for k in range(far - 1):
            band = slice(k * depth, (k + 1) * depth)
            total = jnp.dot(
                mine, w_refs[2 + 2 * j][band, :], preferred_element_type=jnp.float32
            ) + jnp.dot(theirs, w_refs[3 + 2 * j][band, :], preferred_element_type=jnp.float32)
            place(2 + j * (far - 1) + k, total)


def project(ids, attended, weights, rows):
    heads = attended.shape[0] // rows
    far = (ids.shape[0] - 2) // 2
    width = heads * HEAD_DIM
    out_cols = 2 * far * weights[0].shape[1]
    grid_spec = pltpu.PrefetchScalarGridSpec(
        num_scalar_prefetch=1,
        grid=(1,),
        in_specs=[whole(v.shape) for v in (attended, *weights)],
        out_specs=whole((rows, out_cols)),
        scratch_shapes=[pltpu.VMEM((rows, width), jnp.bfloat16)],
    )
    return pl.pallas_call(
        functools.partial(project_kernel, heads, far),
        grid_spec=grid_spec,
        out_shape=jax.ShapeDtypeStruct((rows, out_cols), jnp.float32),
        compiler_params=params(BIG),
        cost_estimate=cost(2 * rows * width * out_cols, 2 * width * out_cols + 4 * rows * out_cols),
        name="project_rows",
    )(ids, attended, *weights)


def norm_kernel(
    ids_ref, mine_ref, theirs_ref, latent_ref, gain_ref, out_ref, normed_ref, other_ref, full_ref
):
    updated = latent_ref[...].astype(jnp.float32) + (mine_ref[...] + theirs_ref[...])
    mean_square = jnp.mean(updated * updated, axis=1, keepdims=True)
    full_ref[...] = updated * lax.rsqrt(mean_square + norm_eps) * gain_ref[...]
    half = out_ref.shape[1]
    own = full_ref[:, pl.ds(pl.multiple_of(ids_ref[0] * half, half), half)]
    out_ref[...] = own
    normed_ref[...] = own.astype(jnp.bfloat16)
    other = full_ref[:, pl.ds(pl.multiple_of((1 - ids_ref[0]) * half, half), half)]
    other_ref[...] = other.astype(jnp.bfloat16)


def normalise(place, mine, theirs, latent_array, gain):
    rows, width = mine.shape
    half = width // 2
    grid_spec = pltpu.PrefetchScalarGridSpec(
        num_scalar_prefetch=1,
        grid=(1,),
        in_specs=[whole((rows, width))] * 3 + [whole((1, width))],
        out_specs=[whole((rows, half))] * 3,
        scratch_shapes=[pltpu.VMEM((rows, width), jnp.float32)],
    )
    return pl.pallas_call(
        norm_kernel,
        grid_spec=grid_spec,
        out_shape=[
            jax.ShapeDtypeStruct((rows, half), jnp.float32),
            jax.ShapeDtypeStruct((rows, half), jnp.bfloat16),
            jax.ShapeDtypeStruct((rows, half), jnp.bfloat16),
        ],
        compiler_params=params(BIG),
        cost_estimate=cost(6 * rows * width, 13 * rows * width),
        name="norm_rows",
    )(place.reshape(1), mine, theirs, latent_array, gain)


def latents_kernel(pieces, ids_ref, *refs):
    mine, theirs = refs[:pieces], refs[pieces : 2 * pieces]
    w_refs, (out_ref, normed_ref, w_ref) = refs[2 * pieces : -3], refs[-3:]
    rows, half = mine[0].shape
    slots = ids_ref.shape[0] - 1
    depth = 2 * half // slots

    @pl.when(pl.program_id(0) == 0)
    def arrange():
        for j in range(slots):
            at = ids_ref[1 + j]
            is_mine = at // (slots // 2) == ids_ref[0]
            start = pl.multiple_of((at % (slots // 2)) * depth, depth)
            for r in range(pieces):
                both = [v[r][:, pl.ds(start, depth)] for v in (mine, theirs)]
                normed_ref[r * rows : (r + 1) * rows, j * depth : (j + 1) * depth] = jnp.where(
                    is_mine, both[0], both[1]
                )

    for j, band in enumerate(w_refs):
        w_ref[j * depth : (j + 1) * depth, :] = band[...]
    out_ref[...] = jnp.dot(
        normed_ref[...], w_ref[...], preferred_element_type=jnp.float32
    ).astype(jnp.bfloat16)


def latent_keys_values(ids, mine, theirs, bands):
    pieces = len(mine)
    rows, half = mine[0].shape
    depth, width = bands[0].shape
    block = min(512, width)
    total = depth * len(bands)
    grid_spec = pltpu.PrefetchScalarGridSpec(
        num_scalar_prefetch=1,
        grid=(width // block,),
        in_specs=[whole((rows, half))] * (2 * pieces)
        + [pl.BlockSpec((depth, block), lambda i, ids: (0, i))] * len(bands),
        out_specs=pl.BlockSpec((rows * pieces, block), lambda i, ids: (0, i)),
        scratch_shapes=[
            pltpu.VMEM((rows * pieces, total), jnp.bfloat16),
            pltpu.VMEM((total, block), jnp.bfloat16),
        ],
    )
    return pl.pallas_call(
        functools.partial(latents_kernel, pieces),
        grid_spec=grid_spec,
        out_shape=jax.ShapeDtypeStruct((rows * pieces, width), jnp.bfloat16),
        compiler_params=params(BIG),
        cost_estimate=cost(2 * rows * pieces * total * width, 2 * total * width),
        name="latent_keys_values",
    )(ids, *mine, *theirs, *bands)


def row_chunks(lengths, size):
    chunks, open_chunk, room = [], [], size
    for i, length in enumerate(lengths):
        start = 0
        while start < length:
            take = min(room, length - start)
            open_chunk.append((i, start, start + take))
            start, room = start + take, room - take
            if room == 0:
                chunks.append(open_chunk)
                open_chunk, room = [], size
    return chunks + ([open_chunk] if open_chunk else [])


def decode_kernel(parts, q_ref, *refs):
    k_refs, v_refs, out_ref = refs[:parts], refs[parts : 2 * parts], refs[-1]

    def gathered(sources, chunk, cols):
        rows = [sources[i][start:stop, cols] for i, start, stop in chunk]
        return rows[0] if len(rows) == 1 else jnp.concatenate(rows)

    for h in range(q_ref.shape[1] // HEAD_DIM):
        cols = slice(h * HEAD_DIM, (h + 1) * HEAD_DIM)
        top = acc = None
        for chunk in row_chunks([k.shape[0] for k in k_refs], 512):
            keys, values = gathered(k_refs, chunk, cols), gathered(v_refs, chunk, cols)
            scores = lax.dot_general(q_ref[:, cols], keys, NT, preferred_element_type=jnp.float32)
            scores = scores * EXP2_SCALE
            new_top = jnp.max(scores, axis=1, keepdims=True)
            if top is not None:
                new_top = jnp.maximum(top, new_top)
            weights = jnp.exp2(scores - new_top).astype(jnp.bfloat16)
            summed = jnp.dot(
                weights,
                jnp.concatenate([values, jnp.ones((keys.shape[0], LANES), jnp.bfloat16)], axis=1),
                preferred_element_type=jnp.float32,
            )
            if top is not None:
                summed = summed + acc * jnp.exp2(top - new_top)
            top, acc = new_top, summed
        out_ref[:, cols] = (acc[:, :HEAD_DIM] / acc[:, HEAD_DIM:]).astype(out_ref.dtype)


def decode(queries, keys_values, out_type):
    tokens, width = queries.shape
    latents = sum(v.shape[0] for v in keys_values)
    pair = min(2 * HEAD_DIM, width)
    steps = width // pair
    narrow = pl.BlockSpec((tokens, pair), lambda i: (0, i))
    keys = [pl.BlockSpec((v.shape[0], pair), lambda i: (0, i)) for v in keys_values]
    values = [pl.BlockSpec((v.shape[0], pair), lambda i: (0, steps + i)) for v in keys_values]
    return pl.pallas_call(
        functools.partial(decode_kernel, len(keys_values)),
        grid=(steps,),
        in_specs=[narrow, *keys, *values],
        out_specs=narrow,
        out_shape=jax.ShapeDtypeStruct((tokens, width), out_type),
        compiler_params=params(BIG),
        cost_estimate=cost(
            16 * tokens * latents * width,
            4 * latents * width + 6 * tokens * width,
            tokens * latents * (width // HEAD_DIM),
        ),
        name="decode_rows",
    )(queries, *keys_values, *keys_values)


def swap_perm(size):
    return [(i, i ^ 1) for i in range(size)]


def hop_perm(size, step, way):
    far = size // 2
    moves = [(z, z + 1) for z in range(step - 1, far - 1)]
    if way < 0:
        moves = [(far - 1 - a, far - 1 - b) for a, b in moves]
    return [(a * 2 + y, b * 2 + y) for a, b in moves for y in range(2)]


def fast_on_device(
    sizes,
    enc_keys,
    enc_values,
    input_ids,
    latent_queries,
    latent_array,
    w_out,
    norm_gain,
    w_key,
    w_value,
    query_features,
    query_ids,
    query_table,
    enc_bias,
    query_counts,
):
    groups, pos = sizes
    far = pos // 2
    p = lax.axis_index("pos")
    place = lax.axis_index("head")
    rows = latent_array.shape[0]
    tokens, half_width = enc_keys.shape
    heads = half_width // HEAD_DIM
    mods = enc_bias.shape[0]
    modality = jnp.arange(mods, dtype=jnp.int32)
    pair = 2 * HEAD_DIM

    far, z, y, x = pos // 2, p // 2, p % 2, lax.axis_index("groups") % 2
    near = swap_perm(pos)

    def over_groups(value):
        return lax.ppermute(value, "groups", swap_perm(groups))

    def over_near(value):
        return lax.ppermute(value, "pos", near)

    def hop(step, pair):
        return [
            lax.ppermute(v, "pos", hop_perm(pos, step, way)) for v, way in zip(pair, (1, -1))
        ]

    def by_shift(hops, k):
        return jnp.where(z + k < far, hops[k][1], hops[far - k][0])

    out_half = w_out.shape[0] // 2
    out_sent = lax.dynamic_slice_in_dim(w_out, x * out_half, out_half, 0)
    out_hops = {0: [out_sent, out_sent]}
    for step in range(1, far):
        out_hops[step] = hop(step, out_hops[step - 1])
    out_near = over_near(w_out)
    out_ids = [p, p ^ 1]
    for j in range(2):
        out_ids += [((z + k) % far) * 2 + (y ^ j) for k in range(1, far)]
    out_ids = jnp.stack([*out_ids, x, 1 - x]).astype(jnp.int32)

    part = half_width // 2

    def columns(arrays, which):
        return jnp.concatenate(
            [lax.dynamic_slice_in_dim(v, which * part, part, 1) for v in arrays], axis=1
        )

    kv_own = columns((w_key, w_value), y)
    kv_near = over_near(columns((w_key, w_value), 1 - y))
    lookup = jnp.dot(
        (query_ids[:, None] == modality[None, :]).astype(jnp.bfloat16),
        query_table,
        preferred_element_type=jnp.float32,
    )
    queries = (query_features.astype(jnp.float32) + lookup).astype(jnp.bfloat16)
    own_queries = columns((queries,), y)
    near_queries = over_near(columns((queries,), 1 - y))


    q_onehot = (query_ids[:, None] == modality[None, :]).astype(jnp.int32)
    local_counts = jnp.sum(q_onehot, axis=0)
    id_rows = tokens // pair
    counted = jnp.concatenate([local_counts // 16, local_counts % 16])
    extra = jnp.concatenate(
        [
            input_ids.reshape(id_rows, pair),
            jnp.pad(counted[None, :], ((0, EXTRA - id_rows - 1), (0, pair - 2 * mods))),
        ]
    ).astype(jnp.bfloat16)
    payload = pack(enc_keys, enc_values, extra)
    kv = lax.all_to_all(payload, "pos", 0, 0, tiled=True)
    head_queries = lax.dynamic_slice_in_dim(latent_queries, p * HEAD_DIM, HEAD_DIM, 1)
    head_bias = lax.dynamic_slice_in_dim(enc_bias, p, 1, 1)[:, 0]
    def kept_queries():
        counts = kv.reshape(pos, tokens + EXTRA, pair)[:, tokens + id_rows, : 2 * mods]
        counts = counts.astype(jnp.int32)
        counts = counts[:, :mods] * 16 + counts[:, mods:]
        earlier = jnp.arange(pos, dtype=jnp.int32)[:, None] < p
        before = jnp.sum(jnp.where(earlier, counts, 0), axis=0)
        within = jnp.cumsum(q_onehot, axis=0) - q_onehot
        ranked = jnp.sum((within + before[None, :]) * q_onehot, axis=1)
        limits = jnp.sum(q_onehot * query_counts[None, :], axis=1)
        return ranked < limits

    kv_sent = jnp.where(x == 0, kv_own, kv_near)
    hops = {0: [kv_sent, kv_sent]}
    hops[1] = hop(1, hops[0])
    kv, hops, near_queries, out_hops, out_near = lax.optimization_barrier(
        (kv, hops, near_queries, out_hops, out_near)
    )
    out_far = jnp.concatenate([by_shift(out_hops, k) for k in range(1, far)])
    out_bands = [out_far, over_near(out_far), over_groups(out_far)]
    hops[2] = hop(2, hops[1])
    attended = encode(head_queries, kv, head_bias, pos)
    attended, hops, out_bands = lax.optimization_barrier((attended, hops, out_bands))
    out_far, out_across, out_other = out_bands
    out_bands = [w_out, out_near, out_far, out_other, out_across, over_near(out_other)]
    moved = {k: by_shift(hops, k) for k in range(1, far) if max(k, far - k) < 3}
    swapped = {k: over_groups(v) for k, v in moved.items()}
    for step in range(3, far):
        hops[step] = hop(step, hops[step - 1])
    attended = lax.all_to_all(attended, "pos", 0, 0, tiled=True)
    kept = kept_queries()
    attended, hops, out_bands, kept, swapped = lax.optimization_barrier(
        (attended, hops, out_bands, kept, swapped)
    )
    for k in range(1, far):
        if k not in moved:
            moved[k] = by_shift(hops, k)
            swapped[k] = over_groups(moved[k])
    partial_value = project(out_ids, attended, out_bands, rows)
    theirs = lax.ppermute(partial_value, "head", swap_perm(2))
    own_cols, normed, normed_other = normalise(
        place, partial_value, theirs, latent_array, norm_gain[None, :]
    )
    kv_bands = [kv_own, kv_near]
    kv_at = [p, p ^ 1]
    for k in range(1, far):
        kv_bands += [moved[k], swapped[k]]
        there = ((z + k) % far) * 2
        kv_at += [there + (y ^ x), there + (1 - (y ^ x))]
    kv_ids = jnp.stack([place, *kv_at]).astype(jnp.int32)

    def cores(values):
        return [lax.ppermute(v, "head", swap_perm(2)) for v in values]

    def fold(mine, other):
        return latent_keys_values(kv_ids, mine, other, kv_bands)

    def arrival(hops, j):
        picked = None
        for at in range(far):
            came = [
                (step, way)
                for step in range(1, far)
                for way in (1, 0)
                if (at + step < far if way else at >= step)
            ]
            step, way = came[j - 1]
            value = hops[step][way]
            picked = value if picked is None else jnp.where(z == at, value, picked)
        return picked

    came = {0: [normed, normed]}
    came[1] = hop(1, came[0])
    came, normed_near, kv_bands = lax.optimization_barrier((came, over_near(normed), kv_bands))
    mine, other = [normed, normed_near], [normed_other, *cores([normed_near])]
    keys_values = []
    for step in range(1, far):
        fresh = arrival(came, step)
        if step + 1 < far:
            came[step + 1] = hop(step + 1, came[step])
        fresh_near = over_near(fresh)
        mine.append(fresh)
        other += cores([fresh])
        if step > 1:
            keys_values.append(fold(mine, other))
            mine, other = [], []
        came, fresh_near, mine, other, keys_values = lax.optimization_barrier(
            (came, fresh_near, mine, other, keys_values)
        )
        mine.append(fresh_near)
        other += cores([fresh_near])
    keys_values.append(fold(mine, other))
    near_state = decode(near_queries, keys_values, jnp.bfloat16)
    own_state = decode(own_queries, keys_values, jnp.float32)
    from_near = lax.ppermute(near_state, "pos", near).astype(jnp.float32)
    decoded = jnp.where(
        y == 0,
        jnp.concatenate([own_state, from_near], axis=1),
        jnp.concatenate([from_near, own_state], axis=1),
    )
    decoded = jnp.where(kept[:, None], decoded, 0.0)
    return (own_cols, decoded)


def on_device(sizes, *args):
    groups, pos, head = sizes
    enc_keys, latent_array, w_out, w_key = args[0], args[4], args[5], args[7]
    fits = (
        head == 2
        and pos % 2 == 0
        and pos > 2
        and groups % 2 == 0
        and enc_keys.shape[1] == pos * HEAD_DIM
        and enc_keys.shape[0] % (2 * HEAD_DIM) == 0
        and enc_keys.shape[0] < 2048
        and w_key.shape[0] % LANES == 0
        and w_out.shape[0] % (2 * LANES) == 0
        and w_out.shape[1] % LANES == 0
        and latent_array.shape[0] % LANES == 0
    )
    if fits:
        return fast_on_device((groups, pos), *args)
    return plain_on_device(*args)


def solution(mesh):
    return jax.shard_map(
        functools.partial(on_device, tuple(mesh.shape[a] for a in ("groups", "pos", "head"))),
        mesh=mesh,
        in_specs=(
            P(("groups", "pos"), "head"),
            P(("groups", "pos"), "head"),
            P(("groups", "pos")),
            P("groups", "head"),
            P(("groups", "pos"), None),
            P("head", "pos"),
            P(),
            P("pos", "head"),
            P("pos", "head"),
            P(("groups", "pos"), "head"),
            P(("groups", "pos")),
            P(None, "head"),
            P(None, "head"),
            P("groups"),
        ),
        out_specs=(P(("groups", "pos"), "head"), P(("groups", "pos"), "head")),
        check_vma=False,
    )
```

```python
import functools

import jax
import jax.numpy as jnp
from jax import lax
from jax.experimental import pallas as pl
from jax.experimental.pallas import tpu as pltpu
from jax.sharding import PartitionSpec as P

HEAD_DIM = 128


norm_eps = 1e-06


def prefix(shard, axis, combine, identity):
    peers, place = (lax.axis_size(axis), lax.axis_index(axis))
    everything = lax.all_gather(shard, axis)
    start = jnp.broadcast_to(jnp.asarray(identity, shard.dtype), shard.shape)

    def step(k, before):
        reached = k < place
        new = combine(before, everything[k])
        return jnp.where(reached, new, before)

    return lax.fori_loop(0, peers, step, start)


def plain_on_device(
    enc_keys,
    enc_values,
    input_ids,
    latent_queries,
    latent_array,
    w_out,
    norm_gain,
    w_key,
    w_value,
    query_features,
    query_ids,
    query_table,
    enc_bias,
    query_counts,
):
    tok_rows = enc_keys.shape[0]
    half_width = enc_keys.shape[1]
    local_heads = half_width // HEAD_DIM
    score_scale = HEAD_DIM ** (-0.5)
    modality = jnp.arange(enc_bias.shape[0], dtype=jnp.int32)
    in_onehot = (input_ids[:, None] == modality[None, :]).astype(jnp.float32)
    bias_rows = jnp.dot(in_onehot, enc_bias, precision=lax.Precision.HIGHEST)
    bias_heads = bias_rows.T[:, None, :]
    keys_split = enc_keys.reshape(tok_rows, local_heads, HEAD_DIM)
    values_split = enc_values.reshape(tok_rows, local_heads, HEAD_DIM)
    lat_total = latent_queries.shape[0]
    block_rows = min(512, lat_total)
    query_blocks = latent_queries.reshape(
        lat_total // block_rows, block_rows, local_heads, HEAD_DIM
    )

    def encode_block(block_queries):
        scores = (
            jnp.einsum(
                "nha,tha->hnt", block_queries, keys_split, preferred_element_type=jnp.float32
            )
            * score_scale
            + bias_heads
        )
        highest = jnp.max(scores, axis=2)
        weights = jnp.exp(scores - highest[:, :, None])
        totals = jnp.sum(weights, axis=2)
        summed = jnp.einsum(
            "hnt,tha->nha",
            weights.astype(jnp.bfloat16),
            values_split,
            preferred_element_type=jnp.float32,
        )
        return (highest.T, totals.T, summed.reshape(block_rows, half_width))

    block_max, block_tot, block_acc = lax.map(encode_block, query_blocks)
    row_highest = block_max.reshape(lat_total, local_heads)
    row_totals = block_tot.reshape(lat_total, local_heads)
    row_sums = block_acc.reshape(lat_total, half_width)
    own_rows = latent_array.shape[0]
    global_max = lax.pmax(row_highest, "pos")
    factor = jnp.exp(row_highest - global_max)
    scaled_sums = (row_sums.reshape(lat_total, local_heads, HEAD_DIM) * factor[:, :, None]).reshape(
        lat_total, half_width
    )
    totals, summed = (
        lax.psum_scatter(row_totals * factor, "pos", scatter_dimension=0, tiled=True),
        lax.psum_scatter(scaled_sums, "pos", scatter_dimension=0, tiled=True),
    )
    summed = summed.reshape(own_rows, local_heads, HEAD_DIM)
    attended = (summed / totals[:, :, None]).reshape(own_rows, half_width).astype(jnp.bfloat16)
    partial_value = jnp.dot(
        attended,
        lax.all_gather(w_out, "pos", axis=1, tiled=True),
        preferred_element_type=jnp.float32,
    )
    offset = lax.axis_index("head") * half_width
    projected = lax.psum(partial_value, "head")
    updated = latent_array.astype(jnp.float32) + projected
    mean_square = jnp.mean(updated * updated, axis=1, keepdims=True)
    normed_full = updated * lax.rsqrt(mean_square + norm_eps) * norm_gain
    normed = normed_full.astype(jnp.bfloat16)
    own_cols = lax.dynamic_slice_in_dim(normed_full, offset, half_width, 1)
    pieces = (
        lax.all_gather(w_key, "pos", axis=0, tiled=True),
        lax.all_gather(w_value, "pos", axis=0, tiled=True),
    )
    key_sum = jnp.dot(normed, pieces[0], preferred_element_type=jnp.float32)
    value_sum = jnp.dot(normed, pieces[1], preferred_element_type=jnp.float32)
    latent_keys = key_sum.astype(jnp.bfloat16)
    latent_values = value_sum.astype(jnp.bfloat16)
    q_onehot = (query_ids[:, None] == modality[None, :]).astype(jnp.int32)
    local_counts = jnp.sum(q_onehot, axis=0)
    before = prefix(
        local_counts, "pos", lambda earlier, later: earlier + later, jnp.zeros_like(local_counts)
    )
    within = jnp.cumsum(q_onehot, axis=0) - q_onehot
    ranked = jnp.sum((within + before[None, :]) * q_onehot, axis=1)
    limits = jnp.sum(q_onehot * query_counts[None, :], axis=1)
    kept_rows = ranked < limits
    lookup = jnp.dot(q_onehot.astype(jnp.bfloat16), query_table, preferred_element_type=jnp.float32)
    queries = (
        (query_features.astype(jnp.float32) + lookup)
        .astype(jnp.bfloat16)
        .reshape(tok_rows, local_heads, HEAD_DIM)
    )

    def fold_rows(running, key_rows, value_rows):
        running_max, running_tot, running_acc = running
        key_heads = key_rows.reshape(key_rows.shape[0], local_heads, HEAD_DIM)
        value_heads = value_rows.reshape(value_rows.shape[0], local_heads, HEAD_DIM)
        scores = (
            jnp.einsum("tha,rha->htr", queries, key_heads, preferred_element_type=jnp.float32)
            * score_scale
        )
        new_max = jnp.maximum(running_max, jnp.max(scores, axis=2))
        fade = jnp.exp(running_max - new_max)
        weights = jnp.exp(scores - new_max[:, :, None])
        new_tot = running_tot * fade + jnp.sum(weights, axis=2)
        new_acc = running_acc * fade[:, :, None] + jnp.einsum(
            "htr,rha->hta",
            weights.astype(jnp.bfloat16),
            value_heads,
            preferred_element_type=jnp.float32,
        )
        return (new_max, new_tot, new_acc)

    start_state = (
        jnp.full((local_heads, tok_rows), -jnp.inf, jnp.float32),
        jnp.zeros((local_heads, tok_rows), jnp.float32),
        jnp.zeros((local_heads, tok_rows, HEAD_DIM), jnp.float32),
    )
    running = start_state
    pieces = (
        lax.all_gather(latent_keys, "pos", axis=0, tiled=True),
        lax.all_gather(latent_values, "pos", axis=0, tiled=True),
    )
    row_count = pieces[0].shape[0]
    key_blocks = pieces[0].reshape(row_count // 512, 512, half_width)
    value_blocks = pieces[1].reshape(row_count // 512, 512, half_width)

    def scan_step(state, pair):
        return (fold_rows(state, pair[0], pair[1]), None)

    running, ignored = lax.scan(scan_step, running, (key_blocks, value_blocks))
    final_max, final_tot, final_acc = running
    dec_heads = final_acc / final_tot[:, :, None]
    dec_rows = jnp.transpose(dec_heads, (1, 0, 2)).reshape(tok_rows, half_width)
    decoded = jnp.where(kept_rows[:, None], dec_rows, 0.0)
    return (own_cols, decoded)


LANES = 128
EXTRA = 16
BIG = 56
LOG2E = 1.4426950408889634
EXP2_SCALE = LOG2E * HEAD_DIM**-0.5
NT = (((1,), (1,)), ((), ()))


def params(mib):
    return pltpu.CompilerParams(vmem_limit_bytes=mib << 20)


def cost(flops, nbytes, exps=0):
    return pl.CostEstimate(flops=int(flops), bytes_accessed=int(nbytes), transcendentals=int(exps))


def whole(shape):
    return pl.BlockSpec(shape, lambda *args: (0,) * len(shape))


def encode_kernel(ids_ref, q_ref, k_ref, v_ref, extra_ref, near_ref, bias_ref, out_ref):
    rows, width = q_ref.shape
    tokens = k_ref.shape[0]
    heads = width // HEAD_DIM
    ones = jnp.ones((tokens, LANES), jnp.bfloat16)
    kinds = [
        extra_ref[...].astype(jnp.float32)[:1, :tokens],
        near_ref[tokens:, :].astype(jnp.float32)[:1, :tokens],
    ]
    lane = lax.broadcasted_iota(jnp.int32, (rows, LANES), 1)
    lse_all = jnp.zeros((rows, LANES), jnp.float32)
    for h in range(heads):
        cols = slice(h * HEAD_DIM, (h + 1) * HEAD_DIM)
        late = slice(width + h * HEAD_DIM, width + (h + 1) * HEAD_DIM)
        pairs = [
            (k_ref[:, cols], v_ref[:, cols]),
            (near_ref[:tokens, cols], near_ref[:tokens, late]),
        ]
        top = acc = None
        for (keys, values), kind in zip(pairs, kinds):
            bias = jnp.zeros_like(kind)
            for m in range(bias_ref.shape[0]):
                bias = jnp.where(kind == m, bias_ref[m, h] * LOG2E, bias)
            scores = lax.dot_general(q_ref[:, cols], keys, NT, preferred_element_type=jnp.float32)
            scores = scores * EXP2_SCALE + bias
            new_top = jnp.max(scores, axis=1, keepdims=True)
            if top is not None:
                new_top = jnp.maximum(top, new_top)
            weights = jnp.exp2(scores - new_top).astype(jnp.bfloat16)
            summed = jnp.dot(
                weights, jnp.concatenate([values, ones], axis=1), preferred_element_type=jnp.float32
            )
            if top is not None:
                summed = summed + acc * jnp.exp2(top - new_top)
            top, acc = new_top, summed
        totals = acc[:, HEAD_DIM:]
        out_ref[:rows, cols] = (acc[:, :HEAD_DIM] / totals).astype(jnp.bfloat16)
        lse_all = jnp.where(lane % heads == h, top + jnp.log2(totals), lse_all)
    lse = lse_all.T[:EXTRA, :]
    high = lse.astype(jnp.bfloat16).astype(jnp.float32)
    mid = (lse - high).astype(jnp.bfloat16).astype(jnp.float32)
    low = lse - high - mid
    row = lax.broadcasted_iota(jnp.int32, lse.shape, 0)
    terms = jnp.where(row < heads, high, jnp.where(row < 2 * heads, mid, low))
    out_ref[rows:, :] = terms.astype(jnp.bfloat16)


def encode(ids, queries, keys, values, extra, near, bias, rows):
    tokens = keys.shape[0]
    width = keys.shape[1] // 2
    half = pl.BlockSpec((tokens, width), lambda i, ids: (0, ids[1]))
    grid_spec = pltpu.PrefetchScalarGridSpec(
        num_scalar_prefetch=1,
        grid=(1,),
        in_specs=[
            pl.BlockSpec((rows, width), lambda i, ids: (ids[0], ids[1])),
            half,
            half,
            whole(extra.shape),
            whole(near.shape),
            pl.BlockSpec(memory_space=pltpu.SMEM),
        ],
        out_specs=whole((rows + EXTRA, width)),
    )
    return pl.pallas_call(
        encode_kernel,
        grid_spec=grid_spec,
        out_shape=jax.ShapeDtypeStruct((rows + EXTRA, width), jnp.bfloat16),
        compiler_params=params(32),
        cost_estimate=cost(16 * rows * tokens * width, 8 * tokens * width, rows * tokens * 8),
        name="encode_rows",
    )(ids, queries, keys, values, extra, near, bias)


def merge_kernel(count, ids_ref, *refs):
    parts, (mine_ref, near_ref, all_ref) = refs[:count], refs[count:]
    rows, width = all_ref.shape
    heads = width // HEAD_DIM
    stats = [v[rows:, :].astype(jnp.float32).T for v in parts]
    for h in range(heads):
        cols = slice(h * HEAD_DIM, (h + 1) * HEAD_DIM)
        lses = [
            s[:, h : h + 1] + s[:, heads + h : heads + h + 1] + s[:, 2 * heads + h : 2 * heads + h + 1]
            for s in stats
        ]
        top = functools.reduce(jnp.maximum, lses)
        factors = [jnp.exp2(v - top) for v in lses]
        inverse = 1.0 / functools.reduce(jnp.add, factors)
        merged = functools.reduce(
            jnp.add,
            [v[:rows, cols].astype(jnp.float32) * (f * inverse) for v, f in zip(parts, factors)],
        )
        all_ref[:, cols] = merged.astype(jnp.bfloat16)
    own = rows // 2
    mine_ref[...] = all_ref[pl.ds(pl.multiple_of(ids_ref[0] * own, own), own), :]
    near_ref[...] = all_ref[pl.ds(pl.multiple_of((1 - ids_ref[0]) * own, own), own), :]


def merge(which, parts):
    long, width = parts[0].shape
    rows = long - EXTRA
    grid_spec = pltpu.PrefetchScalarGridSpec(
        num_scalar_prefetch=1,
        grid=(1,),
        in_specs=[whole(v.shape) for v in parts],
        out_specs=[whole((rows // 2, width))] * 2,
        scratch_shapes=[pltpu.VMEM((rows, width), jnp.bfloat16)],
    )
    return pl.pallas_call(
        functools.partial(merge_kernel, len(parts)),
        grid_spec=grid_spec,
        out_shape=[jax.ShapeDtypeStruct((rows // 2, width), jnp.bfloat16)] * 2,
        compiler_params=params(32),
        cost_estimate=cost(8 * rows * width, 10 * rows * width),
        name="merge_rows",
    )(which.reshape(1), *parts)


def project_kernel(far, ids_ref, mine_ref, near_ref, *refs):
    w_ref, far_ref, far_other_ref, near_w_ref, near_other_ref, out_ref, att_ref = refs
    part = mine_ref.shape[1]
    first = ids_ref[2 * far]
    att_ref[:, pl.ds(pl.multiple_of(first * part, part), part)] = mine_ref[...]
    att_ref[:, pl.ds(pl.multiple_of((1 - first) * part, part), part)] = near_ref[...]
    cols = w_ref.shape[1]
    depth = att_ref.shape[1] // 2
    share = ids_ref[2 * far + 1]
    halves = [
        att_ref[:, pl.ds(pl.multiple_of(v * depth, depth), depth)] for v in (share, 1 - share)
    ]

    def place(slot, value):
        out_ref[:, pl.ds(pl.multiple_of(ids_ref[slot] * cols, cols), cols)] = value

    place(0, jnp.dot(att_ref[...], w_ref[...], preferred_element_type=jnp.float32))
    for slot in range(1, 2 * far):
        refs = (far_ref, far_other_ref) if slot < far else (near_w_ref, near_other_ref)
        start = (slot - 1 if slot < far else slot - far) * (depth + EXTRA)
        terms = [
            jnp.dot(v, w[start : start + depth, :], preferred_element_type=jnp.float32)
            for v, w in zip(halves, refs)
        ]
        place(slot, terms[0] + terms[1])


def project(ids, mine, near, weights):
    rows, part = mine.shape
    far = (ids.shape[0] - 2) // 2
    out_cols = 2 * far * weights[0].shape[1]
    grid_spec = pltpu.PrefetchScalarGridSpec(
        num_scalar_prefetch=1,
        grid=(1,),
        in_specs=[whole(v.shape) for v in (mine, near, *weights)],
        out_specs=whole((rows, out_cols)),
        scratch_shapes=[pltpu.VMEM((rows, 2 * part), jnp.bfloat16)],
    )
    return pl.pallas_call(
        functools.partial(project_kernel, far),
        grid_spec=grid_spec,
        out_shape=jax.ShapeDtypeStruct((rows, out_cols), jnp.float32),
        compiler_params=params(BIG),
        cost_estimate=cost(4 * rows * part * out_cols, 4 * part * out_cols + 4 * rows * out_cols),
        name="project_rows",
    )(ids, mine, near, *weights)


def norm_kernel(
    ids_ref, mine_ref, theirs_ref, latent_ref, gain_ref, out_ref, normed_ref, other_ref, full_ref
):
    updated = latent_ref[...].astype(jnp.float32) + (mine_ref[...] + theirs_ref[...])
    mean_square = jnp.mean(updated * updated, axis=1, keepdims=True)
    full_ref[...] = updated * lax.rsqrt(mean_square + norm_eps) * gain_ref[...]
    half = out_ref.shape[1]
    own = full_ref[:, pl.ds(pl.multiple_of(ids_ref[0] * half, half), half)]
    out_ref[...] = own
    normed_ref[...] = own.astype(jnp.bfloat16)
    other = full_ref[:, pl.ds(pl.multiple_of((1 - ids_ref[0]) * half, half), half)]
    other_ref[...] = other.astype(jnp.bfloat16)


def normalise(place, mine, theirs, latent_array, gain):
    rows, width = mine.shape
    half = width // 2
    grid_spec = pltpu.PrefetchScalarGridSpec(
        num_scalar_prefetch=1,
        grid=(1,),
        in_specs=[whole((rows, width))] * 3 + [whole((1, width))],
        out_specs=[whole((rows, half))] * 3,
        scratch_shapes=[pltpu.VMEM((rows, width), jnp.float32)],
    )
    return pl.pallas_call(
        norm_kernel,
        grid_spec=grid_spec,
        out_shape=[
            jax.ShapeDtypeStruct((rows, half), jnp.float32),
            jax.ShapeDtypeStruct((rows, half), jnp.bfloat16),
            jax.ShapeDtypeStruct((rows, half), jnp.bfloat16),
        ],
        compiler_params=params(BIG),
        cost_estimate=cost(6 * rows * width, 13 * rows * width),
        name="norm_rows",
    )(place.reshape(1), mine, theirs, latent_array, gain)


def latents_kernel(pieces, ids_ref, *refs):
    mine, theirs = refs[:pieces], refs[pieces : 2 * pieces]
    w_refs, (out_ref, normed_ref, w_ref) = refs[2 * pieces : -3], refs[-3:]
    rows, half = mine[0].shape
    slots = ids_ref.shape[0] - 1
    depth = 2 * half // slots

    @pl.when(pl.program_id(0) == 0)
    def arrange():
        for j in range(slots):
            at = ids_ref[1 + j]
            start = pl.multiple_of((at % (slots // 2)) * depth, depth)

            def copy(pieces):
                for r, piece in enumerate(pieces):
                    normed_ref[r * rows : (r + 1) * rows, j * depth : (j + 1) * depth] = piece[
                        :, pl.ds(start, depth)
                    ]

            is_mine = at // (slots // 2) == ids_ref[0]
            pl.when(is_mine)(functools.partial(copy, mine))
            pl.when(jnp.logical_not(is_mine))(functools.partial(copy, theirs))

    for j, band in enumerate(w_refs):
        w_ref[j * depth : (j + 1) * depth, :] = band[...]
    out_ref[...] = jnp.dot(
        normed_ref[...], w_ref[...], preferred_element_type=jnp.float32
    ).astype(jnp.bfloat16)


def latent_keys_values(ids, mine, theirs, bands):
    pieces = len(mine)
    rows, half = mine[0].shape
    depth, width = bands[0].shape
    block = min(512, width)
    total = depth * len(bands)
    grid_spec = pltpu.PrefetchScalarGridSpec(
        num_scalar_prefetch=1,
        grid=(width // block,),
        in_specs=[whole((rows, half))] * (2 * pieces)
        + [pl.BlockSpec((depth, block), lambda i, ids: (0, i))] * len(bands),
        out_specs=pl.BlockSpec((rows * pieces, block), lambda i, ids: (0, i)),
        scratch_shapes=[
            pltpu.VMEM((rows * pieces, total), jnp.bfloat16),
            pltpu.VMEM((total, block), jnp.bfloat16),
        ],
    )
    return pl.pallas_call(
        functools.partial(latents_kernel, pieces),
        grid_spec=grid_spec,
        out_shape=jax.ShapeDtypeStruct((rows * pieces, width), jnp.bfloat16),
        compiler_params=params(BIG),
        cost_estimate=cost(2 * rows * pieces * total * width, 2 * total * width),
        name="latent_keys_values",
    )(ids, *mine, *theirs, *bands)


def row_chunks(lengths, size):
    chunks, open_chunk, room = [], [], size
    for i, length in enumerate(lengths):
        start = 0
        while start < length:
            take = min(room, length - start)
            open_chunk.append((i, start, start + take))
            start, room = start + take, room - take
            if room == 0:
                chunks.append(open_chunk)
                open_chunk, room = [], size
    return chunks + ([open_chunk] if open_chunk else [])


def decode_kernel(parts, q_ref, *refs):
    k_refs, v_refs, out_ref = refs[:parts], refs[parts : 2 * parts], refs[-1]

    def gathered(sources, chunk, cols):
        rows = [sources[i][start:stop, cols] for i, start, stop in chunk]
        return rows[0] if len(rows) == 1 else jnp.concatenate(rows)

    for h in range(q_ref.shape[1] // HEAD_DIM):
        cols = slice(h * HEAD_DIM, (h + 1) * HEAD_DIM)
        top = acc = None
        for chunk in row_chunks([k.shape[0] for k in k_refs], 512):
            keys, values = gathered(k_refs, chunk, cols), gathered(v_refs, chunk, cols)
            scores = lax.dot_general(q_ref[:, cols], keys, NT, preferred_element_type=jnp.float32)
            scores = scores * EXP2_SCALE
            new_top = jnp.max(scores, axis=1, keepdims=True)
            if top is not None:
                new_top = jnp.maximum(top, new_top)
            weights = jnp.exp2(scores - new_top).astype(jnp.bfloat16)
            summed = jnp.dot(
                weights,
                jnp.concatenate([values, jnp.ones((keys.shape[0], LANES), jnp.bfloat16)], axis=1),
                preferred_element_type=jnp.float32,
            )
            if top is not None:
                summed = summed + acc * jnp.exp2(top - new_top)
            top, acc = new_top, summed
        out_ref[:, cols] = (acc[:, :HEAD_DIM] / acc[:, HEAD_DIM:]).astype(out_ref.dtype)


def decode(queries, keys_values, out_type):
    tokens, width = queries.shape
    latents = sum(v.shape[0] for v in keys_values)
    pair = min(2 * HEAD_DIM, width)
    steps = width // pair
    narrow = pl.BlockSpec((tokens, pair), lambda i: (0, i))
    keys = [pl.BlockSpec((v.shape[0], pair), lambda i: (0, i)) for v in keys_values]
    values = [pl.BlockSpec((v.shape[0], pair), lambda i: (0, steps + i)) for v in keys_values]
    return pl.pallas_call(
        functools.partial(decode_kernel, len(keys_values)),
        grid=(steps,),
        in_specs=[narrow, *keys, *values],
        out_specs=narrow,
        out_shape=jax.ShapeDtypeStruct((tokens, width), out_type),
        compiler_params=params(BIG),
        cost_estimate=cost(
            16 * tokens * latents * width,
            4 * latents * width + 6 * tokens * width,
            tokens * latents * (width // HEAD_DIM),
        ),
        name="decode_rows",
    )(queries, *keys_values, *keys_values)


def swap_perm(size):
    return [(i, i ^ 1) for i in range(size)]


def shift_perm(size, k):
    far = size // 2
    return [(((z + k) % far) * 2 + y, z * 2 + y) for z in range(far) for y in range(2)]


def hop_perm(size, step, way):
    far = size // 2
    moves = [(z, z + 1) for z in range(step - 1, far - 1)]
    if way < 0:
        moves = [(far - 1 - a, far - 1 - b) for a, b in moves]
    return [(a * 2 + y, b * 2 + y) for a, b in moves for y in range(2)]


def fast_on_device(
    sizes,
    enc_keys,
    enc_values,
    input_ids,
    latent_queries,
    latent_array,
    w_out,
    norm_gain,
    w_key,
    w_value,
    query_features,
    query_ids,
    query_table,
    enc_bias,
    query_counts,
):
    groups, pos = sizes
    p = lax.axis_index("pos")
    place = lax.axis_index("head")
    rows = latent_array.shape[0]
    tokens, half_width = enc_keys.shape
    heads = half_width // HEAD_DIM
    mods = enc_bias.shape[0]
    modality = jnp.arange(mods, dtype=jnp.int32)
    far, z, y, x = pos // 2, p // 2, p % 2, lax.axis_index("groups") % 2
    near = swap_perm(pos)

    def over_groups(value):
        return lax.ppermute(value, "groups", swap_perm(groups))

    def over_near(value):
        return lax.ppermute(value, "pos", near)

    def over_far(value, k):
        return lax.ppermute(value, "pos", shift_perm(pos, k))

    def hop(step, pair):
        return [
            lax.ppermute(v, "pos", hop_perm(pos, step, way)) for v, way in zip(pair, (1, -1))
        ]

    def by_shift(hops, k):
        return jnp.where(z + k < far, hops[k][1], hops[far - k][0])

    q_onehot = (query_ids[:, None] == modality[None, :]).astype(jnp.int32)
    local_counts = jnp.sum(q_onehot, axis=0)

    def columns(arrays, which):
        part = half_width // 2
        return jnp.concatenate(
            [lax.dynamic_slice_in_dim(v, which * part, part, 1) for v in arrays], axis=1
        )

    extra = jnp.pad(input_ids[None, :], ((0, EXTRA - 1), (0, half_width - tokens)))
    extra = extra.astype(jnp.bfloat16)
    near_inputs = over_near(
        jnp.concatenate([columns((enc_keys, enc_values), 1 - y), extra], axis=0)
    )

    out_half, out_cols = w_out.shape[0] // 2, w_out.shape[1]
    counted = jnp.concatenate([local_counts // 16, local_counts % 16])
    counted = jnp.pad(counted[None, :], ((0, EXTRA - 1), (0, out_cols - 2 * mods)))
    counted = counted.astype(jnp.bfloat16)

    def half_of_out(which):
        own = lax.dynamic_slice_in_dim(w_out, which * out_half, out_half, 0)
        return jnp.concatenate([own, counted])

    out_sent = half_of_out(x)
    out_far = [over_far(out_sent, k) for k in range(1, far)]
    places = [((z + k) % far) * 2 + (y ^ j) for j in range(2) for k in range(far)]
    kv_for_near = columns((w_key, w_value), 1 - y)
    near_inputs, out_far, out_sent, kv_for_near = lax.optimization_barrier(
        (near_inputs, out_far, out_sent, kv_for_near)
    )
    out_far = jnp.concatenate(out_far)
    out_near = over_near(jnp.concatenate([out_sent, out_far]))
    out_far_other = over_groups(out_far)

    kv_own = columns((w_key, w_value), y)
    kv_near = over_near(kv_for_near)

    ids = [jnp.stack([(z - k) % far, y]).astype(jnp.int32) for k in range(far)]
    head_bias = lax.dynamic_slice_in_dim(enc_bias, y * (heads // 2), heads // 2, 1)
    order = sorted(range(1, far), key=lambda k: -min(k, far - k)) + [0]
    results = {}
    for k in order:
        result = encode(
            ids[k], latent_queries, enc_keys, enc_values, extra, near_inputs, head_bias, 2 * rows
        )
        results[k], near_inputs = lax.optimization_barrier((result, near_inputs))
    parts = [over_far(results[k], k) for k in order[:-1]]
    result, out_far_other = lax.optimization_barrier((results[0], out_far_other))
    parts.append(result)
    out_near_other = over_near(jnp.concatenate([half_of_out(1 - x), out_far_other]))

    def kept_queries():
        far_counts = out_far.reshape(far - 1, out_half + EXTRA, out_cols)[:, out_half, : 2 * mods]
        near_counts = out_near.reshape(far, out_half + EXTRA, out_cols)[:, out_half, : 2 * mods]
        counts = jnp.concatenate([counted[:1, : 2 * mods], far_counts, near_counts])
        counts = counts.astype(jnp.int32)
        counts = counts[:, :mods] * 16 + counts[:, mods:]
        earlier = jnp.stack(places)[:, None] < p
        before = jnp.sum(jnp.where(earlier, counts, 0), axis=0)
        within = jnp.cumsum(q_onehot, axis=0) - q_onehot
        ranked = jnp.sum((within + before[None, :]) * q_onehot, axis=1)
        limits = jnp.sum(q_onehot * query_counts[None, :], axis=1)
        return ranked < limits

    parts, out_near, out_far_other, out_near_other, kv_near = lax.optimization_barrier(
        (parts, out_near, out_far_other, out_near_other, kv_near)
    )
    kv_sent = jnp.where(x == 0, kv_own, kv_near)
    hops = {0: [kv_sent, kv_sent]}
    hops[1] = hop(1, hops[0])
    attended, for_near = merge(y, parts)
    from_near = over_near(for_near)
    kept = kept_queries()
    from_near, hops, kept = lax.optimization_barrier((from_near, hops, kept))
    hops[2] = hop(2, hops[1])
    out_ids = jnp.stack([*places, y, x]).astype(jnp.int32)
    weights = [w_out, out_far, out_far_other, out_near, out_near_other]
    partial_value = project(out_ids, attended, from_near, weights)
    theirs = lax.ppermute(partial_value, "head", swap_perm(2))
    theirs, hops = lax.optimization_barrier((theirs, hops))
    own_cols, normed, normed_other = normalise(
        place, partial_value, theirs, latent_array, norm_gain[None, :]
    )
    lookup = jnp.dot(q_onehot.astype(jnp.bfloat16), query_table, preferred_element_type=jnp.float32)
    queries = (query_features.astype(jnp.float32) + lookup).astype(jnp.bfloat16)
    own_queries = columns((queries,), y)
    near_queries = over_near(columns((queries,), 1 - y))

    kv_at = [p, p ^ 1]
    for k in range(1, far):
        there = ((z + k) % far) * 2
        kv_at += [there + (y ^ x), there + (1 - (y ^ x))]
    kv_ids = jnp.stack([place, *kv_at]).astype(jnp.int32)

    def cores(values):
        return [lax.ppermute(v, "head", swap_perm(2)) for v in values]

    def fold(mine, other):
        return latent_keys_values(kv_ids, mine, other, kv_bands)

    def arrival(hops, j):
        picked = None
        for at in range(far):
            came = [
                (step, way)
                for step in range(1, far)
                for way in (1, 0)
                if (at + step < far if way else at >= step)
            ]
            step, way = came[j - 1]
            value = hops[step][way]
            picked = value if picked is None else jnp.where(z == at, value, picked)
        return picked

    came = {0: [normed, normed]}
    came[1] = hop(1, came[0])
    moved = {k: by_shift(hops, k) for k in range(1, far) if max(k, far - k) < 3}
    swapped = {k: over_groups(v) for k, v in moved.items()}
    for step in range(3, far):
        hops[step] = hop(step, hops[step - 1])
    came, normed_near, hops, swapped = lax.optimization_barrier(
        (came, over_near(normed), hops, swapped)
    )
    for k in range(1, far):
        if k not in moved:
            moved[k] = by_shift(hops, k)
            swapped[k] = over_groups(moved[k])
    kv_bands = [kv_own, kv_near]
    for k in range(1, far):
        kv_bands += [moved[k], swapped[k]]
    mine, other = [normed, normed_near], [normed_other, *cores([normed_near])]
    keys_values = []
    for step in range(1, far):
        fresh = arrival(came, step)
        if step + 1 < far:
            came[step + 1] = hop(step + 1, came[step])
        fresh_near = over_near(fresh)
        mine.append(fresh)
        other += cores([fresh])
        if step > 1:
            keys_values.append(fold(mine, other))
            mine, other = [], []
        came, fresh_near, mine, other, keys_values, near_queries = lax.optimization_barrier(
            (came, fresh_near, mine, other, keys_values, near_queries)
        )
        mine.append(fresh_near)
        other += cores([fresh_near])
    keys_values.append(fold(mine, other))
    near_state = decode(near_queries, keys_values, jnp.bfloat16)
    own_state = decode(own_queries, keys_values, jnp.float32)
    from_near = lax.ppermute(near_state, "pos", near).astype(jnp.float32)
    decoded = jnp.where(
        y == 0,
        jnp.concatenate([own_state, from_near], axis=1),
        jnp.concatenate([from_near, own_state], axis=1),
    )
    decoded = jnp.where(kept[:, None], decoded, 0.0)
    return (own_cols, decoded)


def on_device(sizes, *args):
    groups, pos, head = sizes
    enc_keys, latent_array, w_out, w_key = args[0], args[4], args[5], args[7]
    fits = (
        head == 2
        and pos % 2 == 0
        and pos > 2
        and groups % 2 == 0
        and enc_keys.shape[1] % (4 * HEAD_DIM) == 0
        and 3 * enc_keys.shape[1] <= 2 * HEAD_DIM * EXTRA
        and enc_keys.shape[0] % LANES == 0
        and enc_keys.shape[0] <= enc_keys.shape[1]
        and w_key.shape[0] % LANES == 0
        and w_out.shape[0] % (2 * LANES) == 0
        and w_out.shape[1] % LANES == 0
        and latent_array.shape[0] % LANES == 0
    )
    if fits:
        return fast_on_device((groups, pos), *args)
    return plain_on_device(*args)


def solution(mesh):
    return jax.shard_map(
        functools.partial(on_device, tuple(mesh.shape[a] for a in ("groups", "pos", "head"))),
        mesh=mesh,
        in_specs=(
            P(("groups", "pos"), "head"),
            P(("groups", "pos"), "head"),
            P(("groups", "pos")),
            P("groups", "head"),
            P(("groups", "pos"), None),
            P("head", "pos"),
            P(),
            P("pos", "head"),
            P("pos", "head"),
            P(("groups", "pos"), "head"),
            P(("groups", "pos")),
            P(None, "head"),
            P(None, "head"),
            P("groups"),
        ),
        out_specs=(P(("groups", "pos"), "head"), P(("groups", "pos"), "head")),
        check_vma=False,
    )
```

```python
import functools

import jax
import jax.numpy as jnp
from jax import lax
from jax.experimental import pallas as pl
from jax.experimental.pallas import tpu as pltpu
from jax.sharding import PartitionSpec as P

HEAD_DIM = 128


norm_eps = 1e-06


def prefix(shard, axis, combine, identity):
    peers, place = (lax.axis_size(axis), lax.axis_index(axis))
    everything = lax.all_gather(shard, axis)
    start = jnp.broadcast_to(jnp.asarray(identity, shard.dtype), shard.shape)

    def step(k, before):
        reached = k < place
        new = combine(before, everything[k])
        return jnp.where(reached, new, before)

    return lax.fori_loop(0, peers, step, start)


def plain_on_device(
    enc_keys,
    enc_values,
    input_ids,
    latent_queries,
    latent_array,
    w_out,
    norm_gain,
    w_key,
    w_value,
    query_features,
    query_ids,
    query_table,
    enc_bias,
    query_counts,
):
    tok_rows = enc_keys.shape[0]
    half_width = enc_keys.shape[1]
    local_heads = half_width // HEAD_DIM
    score_scale = HEAD_DIM ** (-0.5)
    modality = jnp.arange(enc_bias.shape[0], dtype=jnp.int32)
    in_onehot = (input_ids[:, None] == modality[None, :]).astype(jnp.float32)
    bias_rows = jnp.dot(in_onehot, enc_bias, precision=lax.Precision.HIGHEST)
    bias_heads = bias_rows.T[:, None, :]
    keys_split = enc_keys.reshape(tok_rows, local_heads, HEAD_DIM)
    values_split = enc_values.reshape(tok_rows, local_heads, HEAD_DIM)
    lat_total = latent_queries.shape[0]
    block_rows = min(512, lat_total)
    query_blocks = latent_queries.reshape(
        lat_total // block_rows, block_rows, local_heads, HEAD_DIM
    )

    def encode_block(block_queries):
        scores = (
            jnp.einsum(
                "nha,tha->hnt", block_queries, keys_split, preferred_element_type=jnp.float32
            )
            * score_scale
            + bias_heads
        )
        highest = jnp.max(scores, axis=2)
        weights = jnp.exp(scores - highest[:, :, None])
        totals = jnp.sum(weights, axis=2)
        summed = jnp.einsum(
            "hnt,tha->nha",
            weights.astype(jnp.bfloat16),
            values_split,
            preferred_element_type=jnp.float32,
        )
        return (highest.T, totals.T, summed.reshape(block_rows, half_width))

    block_max, block_tot, block_acc = lax.map(encode_block, query_blocks)
    row_highest = block_max.reshape(lat_total, local_heads)
    row_totals = block_tot.reshape(lat_total, local_heads)
    row_sums = block_acc.reshape(lat_total, half_width)
    own_rows = latent_array.shape[0]
    global_max = lax.pmax(row_highest, "pos")
    factor = jnp.exp(row_highest - global_max)
    scaled_sums = (row_sums.reshape(lat_total, local_heads, HEAD_DIM) * factor[:, :, None]).reshape(
        lat_total, half_width
    )
    totals, summed = (
        lax.psum_scatter(row_totals * factor, "pos", scatter_dimension=0, tiled=True),
        lax.psum_scatter(scaled_sums, "pos", scatter_dimension=0, tiled=True),
    )
    summed = summed.reshape(own_rows, local_heads, HEAD_DIM)
    attended = (summed / totals[:, :, None]).reshape(own_rows, half_width).astype(jnp.bfloat16)
    partial_value = jnp.dot(
        attended,
        lax.all_gather(w_out, "pos", axis=1, tiled=True),
        preferred_element_type=jnp.float32,
    )
    offset = lax.axis_index("head") * half_width
    projected = lax.psum(partial_value, "head")
    updated = latent_array.astype(jnp.float32) + projected
    mean_square = jnp.mean(updated * updated, axis=1, keepdims=True)
    normed_full = updated * lax.rsqrt(mean_square + norm_eps) * norm_gain
    normed = normed_full.astype(jnp.bfloat16)
    own_cols = lax.dynamic_slice_in_dim(normed_full, offset, half_width, 1)
    pieces = (
        lax.all_gather(w_key, "pos", axis=0, tiled=True),
        lax.all_gather(w_value, "pos", axis=0, tiled=True),
    )
    key_sum = jnp.dot(normed, pieces[0], preferred_element_type=jnp.float32)
    value_sum = jnp.dot(normed, pieces[1], preferred_element_type=jnp.float32)
    latent_keys = key_sum.astype(jnp.bfloat16)
    latent_values = value_sum.astype(jnp.bfloat16)
    q_onehot = (query_ids[:, None] == modality[None, :]).astype(jnp.int32)
    local_counts = jnp.sum(q_onehot, axis=0)
    before = prefix(
        local_counts, "pos", lambda earlier, later: earlier + later, jnp.zeros_like(local_counts)
    )
    within = jnp.cumsum(q_onehot, axis=0) - q_onehot
    ranked = jnp.sum((within + before[None, :]) * q_onehot, axis=1)
    limits = jnp.sum(q_onehot * query_counts[None, :], axis=1)
    kept_rows = ranked < limits
    lookup = jnp.dot(q_onehot.astype(jnp.bfloat16), query_table, preferred_element_type=jnp.float32)
    queries = (
        (query_features.astype(jnp.float32) + lookup)
        .astype(jnp.bfloat16)
        .reshape(tok_rows, local_heads, HEAD_DIM)
    )

    def fold_rows(running, key_rows, value_rows):
        running_max, running_tot, running_acc = running
        key_heads = key_rows.reshape(key_rows.shape[0], local_heads, HEAD_DIM)
        value_heads = value_rows.reshape(value_rows.shape[0], local_heads, HEAD_DIM)
        scores = (
            jnp.einsum("tha,rha->htr", queries, key_heads, preferred_element_type=jnp.float32)
            * score_scale
        )
        new_max = jnp.maximum(running_max, jnp.max(scores, axis=2))
        fade = jnp.exp(running_max - new_max)
        weights = jnp.exp(scores - new_max[:, :, None])
        new_tot = running_tot * fade + jnp.sum(weights, axis=2)
        new_acc = running_acc * fade[:, :, None] + jnp.einsum(
            "htr,rha->hta",
            weights.astype(jnp.bfloat16),
            value_heads,
            preferred_element_type=jnp.float32,
        )
        return (new_max, new_tot, new_acc)

    start_state = (
        jnp.full((local_heads, tok_rows), -jnp.inf, jnp.float32),
        jnp.zeros((local_heads, tok_rows), jnp.float32),
        jnp.zeros((local_heads, tok_rows, HEAD_DIM), jnp.float32),
    )
    running = start_state
    pieces = (
        lax.all_gather(latent_keys, "pos", axis=0, tiled=True),
        lax.all_gather(latent_values, "pos", axis=0, tiled=True),
    )
    row_count = pieces[0].shape[0]
    key_blocks = pieces[0].reshape(row_count // 512, 512, half_width)
    value_blocks = pieces[1].reshape(row_count // 512, 512, half_width)

    def scan_step(state, pair):
        return (fold_rows(state, pair[0], pair[1]), None)

    running, ignored = lax.scan(scan_step, running, (key_blocks, value_blocks))
    final_max, final_tot, final_acc = running
    dec_heads = final_acc / final_tot[:, :, None]
    dec_rows = jnp.transpose(dec_heads, (1, 0, 2)).reshape(tok_rows, half_width)
    decoded = jnp.where(kept_rows[:, None], dec_rows, 0.0)
    return (own_cols, decoded)


LANES = 128
EXTRA = 16
BIG = 56
LOG2E = 1.4426950408889634
EXP2_SCALE = LOG2E * HEAD_DIM**-0.5
NT = (((1,), (1,)), ((), ()))


def params(mib):
    return pltpu.CompilerParams(vmem_limit_bytes=mib << 20)


def cost(flops, nbytes, exps=0):
    return pl.CostEstimate(flops=int(flops), bytes_accessed=int(nbytes), transcendentals=int(exps))


def whole(shape):
    return pl.BlockSpec(shape, lambda *args: (0,) * len(shape))


def encode_kernel(ids_ref, q_ref, k_ref, v_ref, extra_ref, near_ref, bias_ref, out_ref):
    rows, width = q_ref.shape
    tokens = k_ref.shape[0]
    heads = width // HEAD_DIM
    ones = jnp.ones((tokens, LANES), jnp.bfloat16)
    kinds = [
        extra_ref[...].astype(jnp.float32)[:1, :tokens],
        near_ref[tokens:, :].astype(jnp.float32)[:1, :tokens],
    ]
    lane = lax.broadcasted_iota(jnp.int32, (rows, LANES), 1)
    lse_all = jnp.zeros((rows, LANES), jnp.float32)
    for h in range(heads):
        cols = slice(h * HEAD_DIM, (h + 1) * HEAD_DIM)
        late = slice(width + h * HEAD_DIM, width + (h + 1) * HEAD_DIM)
        pairs = [
            (k_ref[:, cols], v_ref[:, cols]),
            (near_ref[:tokens, cols], near_ref[:tokens, late]),
        ]
        top = acc = None
        for (keys, values), kind in zip(pairs, kinds):
            bias = jnp.zeros_like(kind)
            for m in range(bias_ref.shape[0]):
                bias = jnp.where(kind == m, bias_ref[m, h] * LOG2E, bias)
            scores = lax.dot_general(q_ref[:, cols], keys, NT, preferred_element_type=jnp.float32)
            scores = scores * EXP2_SCALE + bias
            new_top = jnp.max(scores, axis=1, keepdims=True)
            if top is not None:
                new_top = jnp.maximum(top, new_top)
            weights = jnp.exp2(scores - new_top).astype(jnp.bfloat16)
            summed = jnp.dot(
                weights, jnp.concatenate([values, ones], axis=1), preferred_element_type=jnp.float32
            )
            if top is not None:
                summed = summed + acc * jnp.exp2(top - new_top)
            top, acc = new_top, summed
        totals = acc[:, HEAD_DIM:]
        out_ref[:rows, cols] = (acc[:, :HEAD_DIM] / totals).astype(jnp.bfloat16)
        lse_all = jnp.where(lane % heads == h, top + jnp.log2(totals), lse_all)
    lse = lse_all.T[:EXTRA, :]
    high = lse.astype(jnp.bfloat16).astype(jnp.float32)
    mid = (lse - high).astype(jnp.bfloat16).astype(jnp.float32)
    low = lse - high - mid
    row = lax.broadcasted_iota(jnp.int32, lse.shape, 0)
    terms = jnp.where(row < heads, high, jnp.where(row < 2 * heads, mid, low))
    out_ref[rows:, :] = terms.astype(jnp.bfloat16)


def encode(which, queries, keys, values, extra, near, bias, rows):
    tokens = keys.shape[0]
    width = keys.shape[1] // 2
    blocks = queries.shape[0] // rows
    half = pl.BlockSpec((tokens, width), lambda i, ids: (0, ids[0]))
    grid_spec = pltpu.PrefetchScalarGridSpec(
        num_scalar_prefetch=1,
        grid=(blocks,),
        in_specs=[
            pl.BlockSpec((rows, width), lambda i, ids: (i, ids[0])),
            half,
            half,
            whole(extra.shape),
            whole(near.shape),
            pl.BlockSpec(memory_space=pltpu.SMEM),
        ],
        out_specs=pl.BlockSpec((rows + EXTRA, width), lambda i, ids: (i, 0)),
    )
    return pl.pallas_call(
        encode_kernel,
        grid_spec=grid_spec,
        out_shape=jax.ShapeDtypeStruct((blocks * (rows + EXTRA), width), jnp.bfloat16),
        compiler_params=params(32),
        cost_estimate=cost(
            16 * blocks * rows * tokens * width, 8 * tokens * width, blocks * rows * tokens * 8
        ),
        name="encode_rows",
    )(which.reshape(1), queries, keys, values, extra, near, bias)


def merge_kernel(count, ids_ref, parts_ref, mine_ref, near_ref, all_ref):
    rows, width = all_ref.shape
    long = rows + EXTRA
    parts = [parts_ref.at[i * long : (i + 1) * long, :] for i in range(count)]
    heads = width // HEAD_DIM
    stats = [v[rows:, :].astype(jnp.float32).T for v in parts]
    for h in range(heads):
        cols = slice(h * HEAD_DIM, (h + 1) * HEAD_DIM)
        lses = [
            s[:, h : h + 1] + s[:, heads + h : heads + h + 1] + s[:, 2 * heads + h : 2 * heads + h + 1]
            for s in stats
        ]
        top = functools.reduce(jnp.maximum, lses)
        factors = [jnp.exp2(v - top) for v in lses]
        inverse = 1.0 / functools.reduce(jnp.add, factors)
        merged = functools.reduce(
            jnp.add,
            [v[:rows, cols].astype(jnp.float32) * (f * inverse) for v, f in zip(parts, factors)],
        )
        all_ref[:, cols] = merged.astype(jnp.bfloat16)
    own = rows // 2
    mine_ref[...] = all_ref[pl.ds(pl.multiple_of(ids_ref[0] * own, own), own), :]
    near_ref[...] = all_ref[pl.ds(pl.multiple_of((1 - ids_ref[0]) * own, own), own), :]


def merge(which, parts, count):
    long, width = parts.shape[0] // count, parts.shape[1]
    rows = long - EXTRA
    grid_spec = pltpu.PrefetchScalarGridSpec(
        num_scalar_prefetch=1,
        grid=(1,),
        in_specs=[whole(parts.shape)],
        out_specs=[whole((rows // 2, width))] * 2,
        scratch_shapes=[pltpu.VMEM((rows, width), jnp.bfloat16)],
    )
    return pl.pallas_call(
        functools.partial(merge_kernel, count),
        grid_spec=grid_spec,
        out_shape=[jax.ShapeDtypeStruct((rows // 2, width), jnp.bfloat16)] * 2,
        compiler_params=params(32),
        cost_estimate=cost(8 * rows * width, 10 * rows * width),
        name="merge_rows",
    )(which.reshape(1), parts)


def project_kernel(far, ids_ref, mine_ref, near_ref, *refs):
    w_ref, far_ref, far_other_ref, near_w_ref, near_other_ref, out_ref, att_ref = refs
    part = mine_ref.shape[1]
    first = ids_ref[2 * far]
    att_ref[:, pl.ds(pl.multiple_of(first * part, part), part)] = mine_ref[...]
    att_ref[:, pl.ds(pl.multiple_of((1 - first) * part, part), part)] = near_ref[...]
    cols = w_ref.shape[1]
    depth = att_ref.shape[1] // 2
    share = ids_ref[2 * far + 1]
    halves = [
        att_ref[:, pl.ds(pl.multiple_of(v * depth, depth), depth)] for v in (share, 1 - share)
    ]

    def place(slot, value):
        out_ref[:, pl.ds(pl.multiple_of(ids_ref[slot] * cols, cols), cols)] = value

    place(0, jnp.dot(att_ref[...], w_ref[...], preferred_element_type=jnp.float32))
    for slot in range(1, 2 * far):
        refs = (far_ref, far_other_ref) if slot < far else (near_w_ref, near_other_ref)
        start = (slot - 1 if slot < far else slot - far) * (depth + EXTRA)
        terms = [
            jnp.dot(v, w[start : start + depth, :], preferred_element_type=jnp.float32)
            for v, w in zip(halves, refs)
        ]
        place(slot, terms[0] + terms[1])


def project(ids, mine, near, weights):
    rows, part = mine.shape
    far = (ids.shape[0] - 2) // 2
    out_cols = 2 * far * weights[0].shape[1]
    grid_spec = pltpu.PrefetchScalarGridSpec(
        num_scalar_prefetch=1,
        grid=(1,),
        in_specs=[whole(v.shape) for v in (mine, near, *weights)],
        out_specs=whole((rows, out_cols)),
        scratch_shapes=[pltpu.VMEM((rows, 2 * part), jnp.bfloat16)],
    )
    return pl.pallas_call(
        functools.partial(project_kernel, far),
        grid_spec=grid_spec,
        out_shape=jax.ShapeDtypeStruct((rows, out_cols), jnp.float32),
        compiler_params=params(BIG),
        cost_estimate=cost(4 * rows * part * out_cols, 4 * part * out_cols + 4 * rows * out_cols),
        name="project_rows",
    )(ids, mine, near, *weights)


def norm_kernel(
    ids_ref, mine_ref, theirs_ref, latent_ref, gain_ref, out_ref, normed_ref, other_ref, full_ref
):
    updated = latent_ref[...].astype(jnp.float32) + (mine_ref[...] + theirs_ref[...])
    mean_square = jnp.mean(updated * updated, axis=1, keepdims=True)
    full_ref[...] = updated * lax.rsqrt(mean_square + norm_eps) * gain_ref[...]
    half = out_ref.shape[1]
    own = full_ref[:, pl.ds(pl.multiple_of(ids_ref[0] * half, half), half)]
    out_ref[...] = own
    normed_ref[...] = own.astype(jnp.bfloat16)
    other = full_ref[:, pl.ds(pl.multiple_of((1 - ids_ref[0]) * half, half), half)]
    other_ref[...] = other.astype(jnp.bfloat16)


def normalise(place, mine, theirs, latent_array, gain):
    rows, width = mine.shape
    half = width // 2
    grid_spec = pltpu.PrefetchScalarGridSpec(
        num_scalar_prefetch=1,
        grid=(1,),
        in_specs=[whole((rows, width))] * 3 + [whole((1, width))],
        out_specs=[whole((rows, half))] * 3,
        scratch_shapes=[pltpu.VMEM((rows, width), jnp.float32)],
    )
    return pl.pallas_call(
        norm_kernel,
        grid_spec=grid_spec,
        out_shape=[
            jax.ShapeDtypeStruct((rows, half), jnp.float32),
            jax.ShapeDtypeStruct((rows, half), jnp.bfloat16),
            jax.ShapeDtypeStruct((rows, half), jnp.bfloat16),
        ],
        compiler_params=params(BIG),
        cost_estimate=cost(6 * rows * width, 13 * rows * width),
        name="norm_rows",
    )(place.reshape(1), mine, theirs, latent_array, gain)


def latents_kernel(pieces, ids_ref, *refs):
    mine, theirs = refs[:pieces], refs[pieces : 2 * pieces]
    w_refs, (out_ref, normed_ref, w_ref) = refs[2 * pieces : -3], refs[-3:]
    rows, half = mine[0].shape
    slots = ids_ref.shape[0] - 1
    depth = 2 * half // slots

    @pl.when(pl.program_id(0) == 0)
    def arrange():
        for j in range(slots):
            at = ids_ref[1 + j]
            start = pl.multiple_of((at % (slots // 2)) * depth, depth)

            def copy(pieces):
                for r, piece in enumerate(pieces):
                    normed_ref[r * rows : (r + 1) * rows, j * depth : (j + 1) * depth] = piece[
                        :, pl.ds(start, depth)
                    ]

            is_mine = at // (slots // 2) == ids_ref[0]
            pl.when(is_mine)(functools.partial(copy, mine))
            pl.when(jnp.logical_not(is_mine))(functools.partial(copy, theirs))

    for j, band in enumerate(w_refs):
        w_ref[j * depth : (j + 1) * depth, :] = band[...]
    out_ref[...] = jnp.dot(
        normed_ref[...], w_ref[...], preferred_element_type=jnp.float32
    ).astype(jnp.bfloat16)


def latent_keys_values(ids, mine, theirs, bands):
    pieces = len(mine)
    rows, half = mine[0].shape
    depth, width = bands[0].shape
    block = min(512, width)
    total = depth * len(bands)
    grid_spec = pltpu.PrefetchScalarGridSpec(
        num_scalar_prefetch=1,
        grid=(width // block,),
        in_specs=[whole((rows, half))] * (2 * pieces)
        + [pl.BlockSpec((depth, block), lambda i, ids: (0, i))] * len(bands),
        out_specs=pl.BlockSpec((rows * pieces, block), lambda i, ids: (0, i)),
        scratch_shapes=[
            pltpu.VMEM((rows * pieces, total), jnp.bfloat16),
            pltpu.VMEM((total, block), jnp.bfloat16),
        ],
    )
    return pl.pallas_call(
        functools.partial(latents_kernel, pieces),
        grid_spec=grid_spec,
        out_shape=jax.ShapeDtypeStruct((rows * pieces, width), jnp.bfloat16),
        compiler_params=params(BIG),
        cost_estimate=cost(2 * rows * pieces * total * width, 2 * total * width),
        name="latent_keys_values",
    )(ids, *mine, *theirs, *bands)


def row_chunks(lengths, size):
    chunks, open_chunk, room = [], [], size
    for i, length in enumerate(lengths):
        start = 0
        while start < length:
            take = min(room, length - start)
            open_chunk.append((i, start, start + take))
            start, room = start + take, room - take
            if room == 0:
                chunks.append(open_chunk)
                open_chunk, room = [], size
    return chunks + ([open_chunk] if open_chunk else [])


def decode_kernel(parts, q_ref, *refs):
    k_refs, v_refs, out_ref = refs[:parts], refs[parts : 2 * parts], refs[-1]

    def gathered(sources, chunk, cols):
        rows = [sources[i][start:stop, cols] for i, start, stop in chunk]
        return rows[0] if len(rows) == 1 else jnp.concatenate(rows)

    for h in range(q_ref.shape[1] // HEAD_DIM):
        cols = slice(h * HEAD_DIM, (h + 1) * HEAD_DIM)
        top = acc = None
        for chunk in row_chunks([k.shape[0] for k in k_refs], 512):
            keys, values = gathered(k_refs, chunk, cols), gathered(v_refs, chunk, cols)
            scores = lax.dot_general(q_ref[:, cols], keys, NT, preferred_element_type=jnp.float32)
            scores = scores * EXP2_SCALE
            new_top = jnp.max(scores, axis=1, keepdims=True)
            if top is not None:
                new_top = jnp.maximum(top, new_top)
            weights = jnp.exp2(scores - new_top).astype(jnp.bfloat16)
            summed = jnp.dot(
                weights,
                jnp.concatenate([values, jnp.ones((keys.shape[0], LANES), jnp.bfloat16)], axis=1),
                preferred_element_type=jnp.float32,
            )
            if top is not None:
                summed = summed + acc * jnp.exp2(top - new_top)
            top, acc = new_top, summed
        out_ref[:, cols] = (acc[:, :HEAD_DIM] / acc[:, HEAD_DIM:]).astype(out_ref.dtype)


def decode(queries, keys_values, out_type):
    tokens, width = queries.shape
    latents = sum(v.shape[0] for v in keys_values)
    pair = min(2 * HEAD_DIM, width)
    steps = width // pair
    narrow = pl.BlockSpec((tokens, pair), lambda i: (0, i))
    keys = [pl.BlockSpec((v.shape[0], pair), lambda i: (0, i)) for v in keys_values]
    values = [pl.BlockSpec((v.shape[0], pair), lambda i: (0, steps + i)) for v in keys_values]
    return pl.pallas_call(
        functools.partial(decode_kernel, len(keys_values)),
        grid=(steps,),
        in_specs=[narrow, *keys, *values],
        out_specs=narrow,
        out_shape=jax.ShapeDtypeStruct((tokens, width), out_type),
        compiler_params=params(BIG),
        cost_estimate=cost(
            16 * tokens * latents * width,
            4 * latents * width + 6 * tokens * width,
            tokens * latents * (width // HEAD_DIM),
        ),
        name="decode_rows",
    )(queries, *keys_values, *keys_values)


def swap_perm(size):
    return [(i, i ^ 1) for i in range(size)]


def shift_perm(size, k):
    far = size // 2
    return [(((z + k) % far) * 2 + y, z * 2 + y) for z in range(far) for y in range(2)]


def hop_perm(size, step, way):
    far = size // 2
    moves = [(z, z + 1) for z in range(step - 1, far - 1)]
    if way < 0:
        moves = [(far - 1 - a, far - 1 - b) for a, b in moves]
    return [(a * 2 + y, b * 2 + y) for a, b in moves for y in range(2)]


def fast_on_device(
    sizes,
    enc_keys,
    enc_values,
    input_ids,
    latent_queries,
    latent_array,
    w_out,
    norm_gain,
    w_key,
    w_value,
    query_features,
    query_ids,
    query_table,
    enc_bias,
    query_counts,
):
    groups, pos = sizes
    p = lax.axis_index("pos")
    place = lax.axis_index("head")
    rows = latent_array.shape[0]
    tokens, half_width = enc_keys.shape
    heads = half_width // HEAD_DIM
    mods = enc_bias.shape[0]
    modality = jnp.arange(mods, dtype=jnp.int32)
    far, z, y, x = pos // 2, p // 2, p % 2, lax.axis_index("groups") % 2
    near = swap_perm(pos)

    def over_groups(value):
        return lax.ppermute(value, "groups", swap_perm(groups))

    def over_near(value):
        return lax.ppermute(value, "pos", near)

    def over_far(value, k):
        return lax.ppermute(value, "pos", shift_perm(pos, k))

    def hop(step, pair):
        return [
            lax.ppermute(v, "pos", hop_perm(pos, step, way)) for v, way in zip(pair, (1, -1))
        ]

    def by_shift(hops, k):
        return jnp.where(z + k < far, hops[k][1], hops[far - k][0])

    q_onehot = (query_ids[:, None] == modality[None, :]).astype(jnp.int32)
    local_counts = jnp.sum(q_onehot, axis=0)

    def columns(arrays, which):
        part = half_width // 2
        return jnp.concatenate(
            [lax.dynamic_slice_in_dim(v, which * part, part, 1) for v in arrays], axis=1
        )

    extra = jnp.pad(input_ids[None, :], ((0, EXTRA - 1), (0, half_width - tokens)))
    extra = extra.astype(jnp.bfloat16)
    near_inputs = over_near(
        jnp.concatenate([columns((enc_keys, enc_values), 1 - y), extra], axis=0)
    )

    out_half, out_cols = w_out.shape[0] // 2, w_out.shape[1]
    counted = jnp.concatenate([local_counts // 16, local_counts % 16])
    counted = jnp.pad(counted[None, :], ((0, EXTRA - 1), (0, out_cols - 2 * mods)))
    counted = counted.astype(jnp.bfloat16)

    def half_of_out(which):
        own = lax.dynamic_slice_in_dim(w_out, which * out_half, out_half, 0)
        return jnp.concatenate([own, counted])

    out_sent = half_of_out(x)
    out_far = [over_far(out_sent, k) for k in range(1, far)]
    places = [((z + k) % far) * 2 + (y ^ j) for j in range(2) for k in range(far)]
    kv_for_near = columns((w_key, w_value), 1 - y)
    near_inputs, out_far, out_sent, kv_for_near = lax.optimization_barrier(
        (near_inputs, out_far, out_sent, kv_for_near)
    )
    out_far = jnp.concatenate(out_far)
    out_far_other = over_groups(out_far)

    kv_own = columns((w_key, w_value), y)
    kv_near = over_near(kv_for_near)

    head_bias = lax.dynamic_slice_in_dim(enc_bias, y * (heads // 2), heads // 2, 1)
    parts = encode(
        y, latent_queries, enc_keys, enc_values, extra, near_inputs, head_bias, 2 * rows
    )
    kv_near, out_sent, _ = lax.optimization_barrier((kv_near, out_sent, parts))
    kv_sent = jnp.where(x == 0, kv_own, kv_near)
    hops = {0: [kv_sent, kv_sent]}
    hops[1] = hop(1, hops[0])
    out_near = over_near(jnp.concatenate([out_sent, out_far]))
    out_near_other = over_near(jnp.concatenate([half_of_out(1 - x), out_far_other]))
    columns_of_slice = [[2 * i + j for i in range(far)] for j in range(2)]
    parts = lax.all_to_all(parts, "pos", 0, 0, axis_index_groups=columns_of_slice, tiled=True)

    def kept_queries():
        far_counts = out_far.reshape(far - 1, out_half + EXTRA, out_cols)[:, out_half, : 2 * mods]
        near_counts = out_near.reshape(far, out_half + EXTRA, out_cols)[:, out_half, : 2 * mods]
        counts = jnp.concatenate([counted[:1, : 2 * mods], far_counts, near_counts])
        counts = counts.astype(jnp.int32)
        counts = counts[:, :mods] * 16 + counts[:, mods:]
        earlier = jnp.stack(places)[:, None] < p
        before = jnp.sum(jnp.where(earlier, counts, 0), axis=0)
        within = jnp.cumsum(q_onehot, axis=0) - q_onehot
        ranked = jnp.sum((within + before[None, :]) * q_onehot, axis=1)
        limits = jnp.sum(q_onehot * query_counts[None, :], axis=1)
        return ranked < limits

    parts, out_near, out_far_other, out_near_other, hops = lax.optimization_barrier(
        (parts, out_near, out_far_other, out_near_other, hops)
    )
    hops[2] = hop(2, hops[1])
    attended, for_near = merge(y, parts, far)
    from_near = over_near(for_near)
    kept = kept_queries()
    from_near, hops, kept = lax.optimization_barrier((from_near, hops, kept))
    for step in range(3, far):
        hops[step] = hop(step, hops[step - 1])
    out_ids = jnp.stack([*places, y, x]).astype(jnp.int32)
    weights = [w_out, out_far, out_far_other, out_near, out_near_other]
    partial_value = project(out_ids, attended, from_near, weights)
    theirs = lax.ppermute(partial_value, "head", swap_perm(2))
    theirs, hops = lax.optimization_barrier((theirs, hops))
    own_cols, normed, normed_other = normalise(
        place, partial_value, theirs, latent_array, norm_gain[None, :]
    )
    lookup = jnp.dot(q_onehot.astype(jnp.bfloat16), query_table, preferred_element_type=jnp.float32)
    queries = (query_features.astype(jnp.float32) + lookup).astype(jnp.bfloat16)
    own_queries = columns((queries,), y)
    near_queries = over_near(columns((queries,), 1 - y))

    kv_at = [p, p ^ 1]
    for k in range(1, far):
        there = ((z + k) % far) * 2
        kv_at += [there + (y ^ x), there + (1 - (y ^ x))]
    kv_ids = jnp.stack([place, *kv_at]).astype(jnp.int32)

    def cores(values):
        return [lax.ppermute(v, "head", swap_perm(2)) for v in values]

    def fold(mine, other):
        return latent_keys_values(kv_ids, mine, other, kv_bands)

    def arrival(hops, j):
        picked = None
        for at in range(far):
            came = [
                (step, way)
                for step in range(1, far)
                for way in (1, 0)
                if (at + step < far if way else at >= step)
            ]
            step, way = came[j - 1]
            value = hops[step][way]
            picked = value if picked is None else jnp.where(z == at, value, picked)
        return picked

    came = {0: [normed, normed]}
    came[1] = hop(1, came[0])
    moved = {k: by_shift(hops, k) for k in range(1, far)}
    swapped = {k: over_groups(v) for k, v in moved.items()}
    came, normed_near, moved = lax.optimization_barrier((came, over_near(normed), moved))
    mine, other = [normed, normed_near], [normed_other, *cores([normed_near])]
    keys_values = []
    for step in range(1, far):
        fresh = arrival(came, step)
        if step + 1 < far:
            came[step + 1] = hop(step + 1, came[step])
        fresh_near = over_near(fresh)
        mine.append(fresh)
        other += cores([fresh])
        if step > 1:
            keys_values.append(fold(mine, other))
            mine, other = [], []
        came, fresh_near, mine, other, keys_values, swapped, near_queries = (
            lax.optimization_barrier(
                (came, fresh_near, mine, other, keys_values, swapped, near_queries)
            )
        )
        kv_bands = [kv_own, kv_near]
        for k in range(1, far):
            kv_bands += [moved[k], swapped[k]]
        mine.append(fresh_near)
        other += cores([fresh_near])
    keys_values.append(fold(mine, other))
    near_state = decode(near_queries, keys_values, jnp.bfloat16)
    own_state = decode(own_queries, keys_values, jnp.float32)
    from_near = lax.ppermute(near_state, "pos", near).astype(jnp.float32)
    decoded = jnp.where(
        y == 0,
        jnp.concatenate([own_state, from_near], axis=1),
        jnp.concatenate([from_near, own_state], axis=1),
    )
    decoded = jnp.where(kept[:, None], decoded, 0.0)
    return (own_cols, decoded)


def on_device(sizes, *args):
    groups, pos, head = sizes
    enc_keys, latent_array, w_out, w_key = args[0], args[4], args[5], args[7]
    fits = (
        head == 2
        and pos % 2 == 0
        and pos > 2
        and groups % 2 == 0
        and enc_keys.shape[1] % (4 * HEAD_DIM) == 0
        and 3 * enc_keys.shape[1] <= 2 * HEAD_DIM * EXTRA
        and enc_keys.shape[0] % LANES == 0
        and enc_keys.shape[0] <= enc_keys.shape[1]
        and w_key.shape[0] % LANES == 0
        and w_out.shape[0] % (2 * LANES) == 0
        and w_out.shape[1] % LANES == 0
        and latent_array.shape[0] % LANES == 0
    )
    if fits:
        return fast_on_device((groups, pos), *args)
    return plain_on_device(*args)


def solution(mesh):
    return jax.shard_map(
        functools.partial(on_device, tuple(mesh.shape[a] for a in ("groups", "pos", "head"))),
        mesh=mesh,
        in_specs=(
            P(("groups", "pos"), "head"),
            P(("groups", "pos"), "head"),
            P(("groups", "pos")),
            P("groups", "head"),
            P(("groups", "pos"), None),
            P("head", "pos"),
            P(),
            P("pos", "head"),
            P("pos", "head"),
            P(("groups", "pos"), "head"),
            P(("groups", "pos")),
            P(None, "head"),
            P(None, "head"),
            P("groups"),
        ),
        out_specs=(P(("groups", "pos"), "head"), P(("groups", "pos"), "head")),
        check_vma=False,
    )
```

```python
import functools

import jax
import jax.numpy as jnp
from jax import lax
from jax.experimental import pallas as pl
from jax.experimental.pallas import tpu as pltpu
from jax.sharding import PartitionSpec as P

HEAD_DIM = 128


norm_eps = 1e-06


def prefix(shard, axis, combine, identity):
    peers, place = (lax.axis_size(axis), lax.axis_index(axis))
    everything = lax.all_gather(shard, axis)
    start = jnp.broadcast_to(jnp.asarray(identity, shard.dtype), shard.shape)

    def step(k, before):
        reached = k < place
        new = combine(before, everything[k])
        return jnp.where(reached, new, before)

    return lax.fori_loop(0, peers, step, start)


def plain_on_device(
    enc_keys,
    enc_values,
    input_ids,
    latent_queries,
    latent_array,
    w_out,
    norm_gain,
    w_key,
    w_value,
    query_features,
    query_ids,
    query_table,
    enc_bias,
    query_counts,
):
    tok_rows = enc_keys.shape[0]
    half_width = enc_keys.shape[1]
    local_heads = half_width // HEAD_DIM
    score_scale = HEAD_DIM ** (-0.5)
    modality = jnp.arange(enc_bias.shape[0], dtype=jnp.int32)
    in_onehot = (input_ids[:, None] == modality[None, :]).astype(jnp.float32)
    bias_rows = jnp.dot(in_onehot, enc_bias, precision=lax.Precision.HIGHEST)
    bias_heads = bias_rows.T[:, None, :]
    keys_split = enc_keys.reshape(tok_rows, local_heads, HEAD_DIM)
    values_split = enc_values.reshape(tok_rows, local_heads, HEAD_DIM)
    lat_total = latent_queries.shape[0]
    block_rows = min(512, lat_total)
    query_blocks = latent_queries.reshape(
        lat_total // block_rows, block_rows, local_heads, HEAD_DIM
    )

    def encode_block(block_queries):
        scores = (
            jnp.einsum(
                "nha,tha->hnt", block_queries, keys_split, preferred_element_type=jnp.float32
            )
            * score_scale
            + bias_heads
        )
        highest = jnp.max(scores, axis=2)
        weights = jnp.exp(scores - highest[:, :, None])
        totals = jnp.sum(weights, axis=2)
        summed = jnp.einsum(
            "hnt,tha->nha",
            weights.astype(jnp.bfloat16),
            values_split,
            preferred_element_type=jnp.float32,
        )
        return (highest.T, totals.T, summed.reshape(block_rows, half_width))

    block_max, block_tot, block_acc = lax.map(encode_block, query_blocks)
    row_highest = block_max.reshape(lat_total, local_heads)
    row_totals = block_tot.reshape(lat_total, local_heads)
    row_sums = block_acc.reshape(lat_total, half_width)
    own_rows = latent_array.shape[0]
    global_max = lax.pmax(row_highest, "pos")
    factor = jnp.exp(row_highest - global_max)
    scaled_sums = (row_sums.reshape(lat_total, local_heads, HEAD_DIM) * factor[:, :, None]).reshape(
        lat_total, half_width
    )
    totals, summed = (
        lax.psum_scatter(row_totals * factor, "pos", scatter_dimension=0, tiled=True),
        lax.psum_scatter(scaled_sums, "pos", scatter_dimension=0, tiled=True),
    )
    summed = summed.reshape(own_rows, local_heads, HEAD_DIM)
    attended = (summed / totals[:, :, None]).reshape(own_rows, half_width).astype(jnp.bfloat16)
    partial_value = jnp.dot(
        attended,
        lax.all_gather(w_out, "pos", axis=1, tiled=True),
        preferred_element_type=jnp.float32,
    )
    offset = lax.axis_index("head") * half_width
    projected = lax.psum(partial_value, "head")
    updated = latent_array.astype(jnp.float32) + projected
    mean_square = jnp.mean(updated * updated, axis=1, keepdims=True)
    normed_full = updated * lax.rsqrt(mean_square + norm_eps) * norm_gain
    normed = normed_full.astype(jnp.bfloat16)
    own_cols = lax.dynamic_slice_in_dim(normed_full, offset, half_width, 1)
    pieces = (
        lax.all_gather(w_key, "pos", axis=0, tiled=True),
        lax.all_gather(w_value, "pos", axis=0, tiled=True),
    )
    key_sum = jnp.dot(normed, pieces[0], preferred_element_type=jnp.float32)
    value_sum = jnp.dot(normed, pieces[1], preferred_element_type=jnp.float32)
    latent_keys = key_sum.astype(jnp.bfloat16)
    latent_values = value_sum.astype(jnp.bfloat16)
    q_onehot = (query_ids[:, None] == modality[None, :]).astype(jnp.int32)
    local_counts = jnp.sum(q_onehot, axis=0)
    before = prefix(
        local_counts, "pos", lambda earlier, later: earlier + later, jnp.zeros_like(local_counts)
    )
    within = jnp.cumsum(q_onehot, axis=0) - q_onehot
    ranked = jnp.sum((within + before[None, :]) * q_onehot, axis=1)
    limits = jnp.sum(q_onehot * query_counts[None, :], axis=1)
    kept_rows = ranked < limits
    lookup = jnp.dot(q_onehot.astype(jnp.bfloat16), query_table, preferred_element_type=jnp.float32)
    queries = (
        (query_features.astype(jnp.float32) + lookup)
        .astype(jnp.bfloat16)
        .reshape(tok_rows, local_heads, HEAD_DIM)
    )

    def fold_rows(running, key_rows, value_rows):
        running_max, running_tot, running_acc = running
        key_heads = key_rows.reshape(key_rows.shape[0], local_heads, HEAD_DIM)
        value_heads = value_rows.reshape(value_rows.shape[0], local_heads, HEAD_DIM)
        scores = (
            jnp.einsum("tha,rha->htr", queries, key_heads, preferred_element_type=jnp.float32)
            * score_scale
        )
        new_max = jnp.maximum(running_max, jnp.max(scores, axis=2))
        fade = jnp.exp(running_max - new_max)
        weights = jnp.exp(scores - new_max[:, :, None])
        new_tot = running_tot * fade + jnp.sum(weights, axis=2)
        new_acc = running_acc * fade[:, :, None] + jnp.einsum(
            "htr,rha->hta",
            weights.astype(jnp.bfloat16),
            value_heads,
            preferred_element_type=jnp.float32,
        )
        return (new_max, new_tot, new_acc)

    start_state = (
        jnp.full((local_heads, tok_rows), -jnp.inf, jnp.float32),
        jnp.zeros((local_heads, tok_rows), jnp.float32),
        jnp.zeros((local_heads, tok_rows, HEAD_DIM), jnp.float32),
    )
    running = start_state
    pieces = (
        lax.all_gather(latent_keys, "pos", axis=0, tiled=True),
        lax.all_gather(latent_values, "pos", axis=0, tiled=True),
    )
    row_count = pieces[0].shape[0]
    key_blocks = pieces[0].reshape(row_count // 512, 512, half_width)
    value_blocks = pieces[1].reshape(row_count // 512, 512, half_width)

    def scan_step(state, pair):
        return (fold_rows(state, pair[0], pair[1]), None)

    running, ignored = lax.scan(scan_step, running, (key_blocks, value_blocks))
    final_max, final_tot, final_acc = running
    dec_heads = final_acc / final_tot[:, :, None]
    dec_rows = jnp.transpose(dec_heads, (1, 0, 2)).reshape(tok_rows, half_width)
    decoded = jnp.where(kept_rows[:, None], dec_rows, 0.0)
    return (own_cols, decoded)


LANES = 128
EXTRA = 16
BIG = 56
LOG2E = 1.4426950408889634
EXP2_SCALE = LOG2E * HEAD_DIM**-0.5
NT = (((1,), (1,)), ((), ()))


def params(mib):
    return pltpu.CompilerParams(vmem_limit_bytes=mib << 20)


def cost(flops, nbytes, exps=0):
    return pl.CostEstimate(flops=int(flops), bytes_accessed=int(nbytes), transcendentals=int(exps))


def whole(shape):
    return pl.BlockSpec(shape, lambda *args: (0,) * len(shape))


def encode_kernel(ids_ref, q_ref, k_ref, v_ref, extra_ref, near_ref, bias_ref, out_ref):
    rows, width = q_ref.shape
    tokens = k_ref.shape[0]
    heads = width // HEAD_DIM
    ones = jnp.ones((tokens, LANES), jnp.bfloat16)
    kinds = [
        extra_ref[...].astype(jnp.float32)[:1, :tokens],
        near_ref[tokens:, :].astype(jnp.float32)[:1, :tokens],
    ]
    lane = lax.broadcasted_iota(jnp.int32, (rows, LANES), 1)
    lse_all = jnp.zeros((rows, LANES), jnp.float32)
    for h in range(heads):
        cols = slice(h * HEAD_DIM, (h + 1) * HEAD_DIM)
        late = slice(width + h * HEAD_DIM, width + (h + 1) * HEAD_DIM)
        pairs = [
            (k_ref[:, cols], v_ref[:, cols]),
            (near_ref[:tokens, cols], near_ref[:tokens, late]),
        ]
        top = acc = None
        for (keys, values), kind in zip(pairs, kinds):
            bias = jnp.zeros_like(kind)
            for m in range(bias_ref.shape[0]):
                bias = jnp.where(kind == m, bias_ref[m, h] * LOG2E, bias)
            scores = lax.dot_general(q_ref[:, cols], keys, NT, preferred_element_type=jnp.float32)
            scores = scores * EXP2_SCALE + bias
            new_top = jnp.max(scores, axis=1, keepdims=True)
            if top is not None:
                new_top = jnp.maximum(top, new_top)
            weights = jnp.exp2(scores - new_top).astype(jnp.bfloat16)
            summed = jnp.dot(
                weights, jnp.concatenate([values, ones], axis=1), preferred_element_type=jnp.float32
            )
            if top is not None:
                summed = summed + acc * jnp.exp2(top - new_top)
            top, acc = new_top, summed
        totals = acc[:, HEAD_DIM:]
        out_ref[:rows, cols] = (acc[:, :HEAD_DIM] / totals).astype(jnp.bfloat16)
        lse_all = jnp.where(lane % heads == h, top + jnp.log2(totals), lse_all)
    lse = lse_all.T[:EXTRA, :]
    high = lse.astype(jnp.bfloat16).astype(jnp.float32)
    mid = (lse - high).astype(jnp.bfloat16).astype(jnp.float32)
    low = lse - high - mid
    row = lax.broadcasted_iota(jnp.int32, lse.shape, 0)
    terms = jnp.where(row < heads, high, jnp.where(row < 2 * heads, mid, low))
    out_ref[rows:, :] = terms.astype(jnp.bfloat16)


def encode(which, queries, keys, values, extra, near, bias, rows):
    tokens = keys.shape[0]
    width = keys.shape[1] // 2
    blocks = queries.shape[0] // rows
    half = pl.BlockSpec((tokens, width), lambda i, ids: (0, ids[0]))
    grid_spec = pltpu.PrefetchScalarGridSpec(
        num_scalar_prefetch=1,
        grid=(blocks,),
        in_specs=[
            pl.BlockSpec((rows, width), lambda i, ids: (i, ids[0])),
            half,
            half,
            whole(extra.shape),
            whole(near.shape),
            pl.BlockSpec(memory_space=pltpu.SMEM),
        ],
        out_specs=pl.BlockSpec((rows + EXTRA, width), lambda i, ids: (i, 0)),
    )
    return pl.pallas_call(
        encode_kernel,
        grid_spec=grid_spec,
        out_shape=jax.ShapeDtypeStruct((blocks * (rows + EXTRA), width), jnp.bfloat16),
        compiler_params=params(BIG),
        cost_estimate=cost(
            16 * blocks * rows * tokens * width, 8 * tokens * width, blocks * rows * tokens * 8
        ),
        name="encode_rows",
    )(which.reshape(1), queries, keys, values, extra, near, bias)


def merge_kernel(count, ids_ref, parts_ref, mine_ref, near_ref, all_ref):
    rows, width = all_ref.shape
    long = rows + EXTRA
    parts = [parts_ref.at[i * long : (i + 1) * long, :] for i in range(count)]
    heads = width // HEAD_DIM
    stats = [v[rows:, :].astype(jnp.float32).T for v in parts]
    for h in range(heads):
        cols = slice(h * HEAD_DIM, (h + 1) * HEAD_DIM)
        lses = [
            s[:, h : h + 1] + s[:, heads + h : heads + h + 1] + s[:, 2 * heads + h : 2 * heads + h + 1]
            for s in stats
        ]
        top = functools.reduce(jnp.maximum, lses)
        factors = [jnp.exp2(v - top) for v in lses]
        inverse = 1.0 / functools.reduce(jnp.add, factors)
        merged = functools.reduce(
            jnp.add,
            [v[:rows, cols].astype(jnp.float32) * (f * inverse) for v, f in zip(parts, factors)],
        )
        all_ref[:, cols] = merged.astype(jnp.bfloat16)
    own = rows // 2
    mine_ref[...] = all_ref[pl.ds(pl.multiple_of(ids_ref[0] * own, own), own), :]
    near_ref[...] = all_ref[pl.ds(pl.multiple_of((1 - ids_ref[0]) * own, own), own), :]


def merge(which, parts, count):
    long, width = parts.shape[0] // count, parts.shape[1]
    rows = long - EXTRA
    grid_spec = pltpu.PrefetchScalarGridSpec(
        num_scalar_prefetch=1,
        grid=(1,),
        in_specs=[whole(parts.shape)],
        out_specs=[whole((rows // 2, width))] * 2,
        scratch_shapes=[pltpu.VMEM((rows, width), jnp.bfloat16)],
    )
    return pl.pallas_call(
        functools.partial(merge_kernel, count),
        grid_spec=grid_spec,
        out_shape=[jax.ShapeDtypeStruct((rows // 2, width), jnp.bfloat16)] * 2,
        compiler_params=params(32),
        cost_estimate=cost(8 * rows * width, 10 * rows * width),
        name="merge_rows",
    )(which.reshape(1), parts)


def project_kernel(far, ids_ref, mine_ref, near_ref, *refs):
    w_ref, far_ref, far_other_ref, near_w_ref, near_other_ref, out_ref, att_ref = refs
    part = mine_ref.shape[1]
    first = ids_ref[2 * far]
    att_ref[:, pl.ds(pl.multiple_of(first * part, part), part)] = mine_ref[...]
    att_ref[:, pl.ds(pl.multiple_of((1 - first) * part, part), part)] = near_ref[...]
    cols = w_ref.shape[1]
    depth = att_ref.shape[1] // 2
    share = ids_ref[2 * far + 1]
    halves = [
        att_ref[:, pl.ds(pl.multiple_of(v * depth, depth), depth)] for v in (share, 1 - share)
    ]

    def place(slot, value):
        out_ref[:, pl.ds(pl.multiple_of(ids_ref[slot] * cols, cols), cols)] = value

    place(0, jnp.dot(att_ref[...], w_ref[...], preferred_element_type=jnp.float32))
    for slot in range(1, 2 * far):
        refs = (far_ref, far_other_ref) if slot < far else (near_w_ref, near_other_ref)
        start = (slot - 1 if slot < far else slot - far) * (depth + EXTRA)
        terms = [
            jnp.dot(v, w[start : start + depth, :], preferred_element_type=jnp.float32)
            for v, w in zip(halves, refs)
        ]
        place(slot, terms[0] + terms[1])


def project(ids, mine, near, weights):
    rows, part = mine.shape
    far = (ids.shape[0] - 2) // 2
    out_cols = 2 * far * weights[0].shape[1]
    grid_spec = pltpu.PrefetchScalarGridSpec(
        num_scalar_prefetch=1,
        grid=(1,),
        in_specs=[whole(v.shape) for v in (mine, near, *weights)],
        out_specs=whole((rows, out_cols)),
        scratch_shapes=[pltpu.VMEM((rows, 2 * part), jnp.bfloat16)],
    )
    return pl.pallas_call(
        functools.partial(project_kernel, far),
        grid_spec=grid_spec,
        out_shape=jax.ShapeDtypeStruct((rows, out_cols), jnp.float32),
        compiler_params=params(BIG),
        cost_estimate=cost(4 * rows * part * out_cols, 4 * part * out_cols + 4 * rows * out_cols),
        name="project_rows",
    )(ids, mine, near, *weights)


def norm_kernel(
    ids_ref, mine_ref, theirs_ref, latent_ref, gain_ref, out_ref, normed_ref, other_ref, full_ref
):
    updated = latent_ref[...].astype(jnp.float32) + (mine_ref[...] + theirs_ref[...])
    mean_square = jnp.mean(updated * updated, axis=1, keepdims=True)
    full_ref[...] = updated * lax.rsqrt(mean_square + norm_eps) * gain_ref[...]
    half = out_ref.shape[1]
    own = full_ref[:, pl.ds(pl.multiple_of(ids_ref[0] * half, half), half)]
    out_ref[...] = own
    normed_ref[...] = own.astype(jnp.bfloat16)
    other = full_ref[:, pl.ds(pl.multiple_of((1 - ids_ref[0]) * half, half), half)]
    other_ref[...] = other.astype(jnp.bfloat16)


def normalise(place, mine, theirs, latent_array, gain):
    rows, width = mine.shape
    half = width // 2
    grid_spec = pltpu.PrefetchScalarGridSpec(
        num_scalar_prefetch=1,
        grid=(1,),
        in_specs=[whole((rows, width))] * 3 + [whole((1, width))],
        out_specs=[whole((rows, half))] * 3,
        scratch_shapes=[pltpu.VMEM((rows, width), jnp.float32)],
    )
    return pl.pallas_call(
        norm_kernel,
        grid_spec=grid_spec,
        out_shape=[
            jax.ShapeDtypeStruct((rows, half), jnp.float32),
            jax.ShapeDtypeStruct((rows, half), jnp.bfloat16),
            jax.ShapeDtypeStruct((rows, half), jnp.bfloat16),
        ],
        compiler_params=params(BIG),
        cost_estimate=cost(6 * rows * width, 13 * rows * width),
        name="norm_rows",
    )(place.reshape(1), mine, theirs, latent_array, gain)


def latents_kernel(pieces, ids_ref, *refs):
    mine, theirs = refs[:pieces], refs[pieces : 2 * pieces]
    w_refs, (out_ref, normed_ref, w_ref) = refs[2 * pieces : -3], refs[-3:]
    rows, half = mine[0].shape
    slots = ids_ref.shape[0] - 1
    depth = 2 * half // slots

    @pl.when(pl.program_id(0) == 0)
    def arrange():
        for j in range(slots):
            at = ids_ref[1 + j]
            start = pl.multiple_of((at % (slots // 2)) * depth, depth)

            def copy(pieces):
                for r, piece in enumerate(pieces):
                    normed_ref[r * rows : (r + 1) * rows, j * depth : (j + 1) * depth] = piece[
                        :, pl.ds(start, depth)
                    ]

            is_mine = at // (slots // 2) == ids_ref[0]
            pl.when(is_mine)(functools.partial(copy, mine))
            pl.when(jnp.logical_not(is_mine))(functools.partial(copy, theirs))

    start = 0
    for band in w_refs:
        w_ref[start : start + band.shape[0], :] = band[...]
        start += band.shape[0]
    out_ref[...] = jnp.dot(
        normed_ref[...], w_ref[...], preferred_element_type=jnp.float32
    ).astype(jnp.bfloat16)


def latent_keys_values(ids, mine, theirs, bands):
    pieces = len(mine)
    rows, half = mine[0].shape
    width = bands[0].shape[1]
    block = min(512, width)
    total = sum(band.shape[0] for band in bands)
    grid_spec = pltpu.PrefetchScalarGridSpec(
        num_scalar_prefetch=1,
        grid=(width // block,),
        in_specs=[whole((rows, half))] * (2 * pieces)
        + [pl.BlockSpec((band.shape[0], block), lambda i, ids: (0, i)) for band in bands],
        out_specs=pl.BlockSpec((rows * pieces, block), lambda i, ids: (0, i)),
        scratch_shapes=[
            pltpu.VMEM((rows * pieces, total), jnp.bfloat16),
            pltpu.VMEM((total, block), jnp.bfloat16),
        ],
    )
    return pl.pallas_call(
        functools.partial(latents_kernel, pieces),
        grid_spec=grid_spec,
        out_shape=jax.ShapeDtypeStruct((rows * pieces, width), jnp.bfloat16),
        compiler_params=params(BIG),
        cost_estimate=cost(2 * rows * pieces * total * width, 2 * total * width),
        name="latent_keys_values",
    )(ids, *mine, *theirs, *bands)


def row_chunks(lengths, size):
    chunks, open_chunk, room = [], [], size
    for i, length in enumerate(lengths):
        start = 0
        while start < length:
            take = min(room, length - start)
            open_chunk.append((i, start, start + take))
            start, room = start + take, room - take
            if room == 0:
                chunks.append(open_chunk)
                open_chunk, room = [], size
    return chunks + ([open_chunk] if open_chunk else [])


def decode_kernel(parts, first, last, q_ref, *refs):
    k_refs, v_refs, rest = refs[:parts], refs[parts : 2 * parts], refs[2 * parts :]

    def gathered(sources, chunk, cols):
        rows = [sources[i][start:stop, cols] for i, start, stop in chunk]
        return rows[0] if len(rows) == 1 else jnp.concatenate(rows)

    for h in range(q_ref.shape[1] // HEAD_DIM):
        cols = slice(h * HEAD_DIM, (h + 1) * HEAD_DIM)
        wide = slice(2 * h * HEAD_DIM, 2 * (h + 1) * HEAD_DIM)
        top = acc = None
        if not first:
            top, acc = rest[0][:, cols][:, :1], rest[1][:, wide]
        for chunk in row_chunks([k.shape[0] for k in k_refs], 512):
            keys, values = gathered(k_refs, chunk, cols), gathered(v_refs, chunk, cols)
            scores = lax.dot_general(q_ref[:, cols], keys, NT, preferred_element_type=jnp.float32)
            scores = scores * EXP2_SCALE
            new_top = jnp.max(scores, axis=1, keepdims=True)
            if top is not None:
                new_top = jnp.maximum(top, new_top)
            weights = jnp.exp2(scores - new_top).astype(jnp.bfloat16)
            summed = jnp.dot(
                weights,
                jnp.concatenate([values, jnp.ones((keys.shape[0], LANES), jnp.bfloat16)], axis=1),
                preferred_element_type=jnp.float32,
            )
            if top is not None:
                summed = summed + acc * jnp.exp2(top - new_top)
            top, acc = new_top, summed
        if last:
            out_ref = rest[-1]
            out_ref[:, cols] = (acc[:, :HEAD_DIM] / acc[:, HEAD_DIM:]).astype(out_ref.dtype)
        else:
            rest[-2][:, cols] = jnp.broadcast_to(top, (top.shape[0], HEAD_DIM))
            rest[-1][:, wide] = acc


def decode(queries, keys_values, state, out_type):
    first, last = state is None, out_type is not None
    tokens, width = queries.shape
    latents = sum(v.shape[0] for v in keys_values)
    pair = min(2 * HEAD_DIM, width)
    steps = width // pair
    narrow = pl.BlockSpec((tokens, pair), lambda i: (0, i))
    wide = pl.BlockSpec((tokens, 2 * pair), lambda i: (0, i))
    keys = [pl.BlockSpec((v.shape[0], pair), lambda i: (0, i)) for v in keys_values]
    values = [pl.BlockSpec((v.shape[0], pair), lambda i: (0, steps + i)) for v in keys_values]
    if last:
        out_specs, out_shape = narrow, jax.ShapeDtypeStruct((tokens, width), out_type)
    else:
        out_specs = [narrow, wide]
        out_shape = [
            jax.ShapeDtypeStruct((tokens, n * width), jnp.float32) for n in (1, 2)
        ]
    return pl.pallas_call(
        functools.partial(decode_kernel, len(keys_values), first, last),
        grid=(steps,),
        in_specs=[narrow, *keys, *values, *([] if first else [narrow, wide])],
        out_specs=out_specs,
        out_shape=out_shape,
        compiler_params=params(BIG),
        cost_estimate=cost(
            16 * tokens * latents * width,
            4 * latents * width + 6 * tokens * width,
            tokens * latents * (width // HEAD_DIM),
        ),
        name="decode_rows",
    )(queries, *keys_values, *keys_values, *([] if first else state))


def swap_perm(size):
    return [(i, i ^ 1) for i in range(size)]


def shift_perm(size, k):
    far = size // 2
    return [(((z + k) % far) * 2 + y, z * 2 + y) for z in range(far) for y in range(2)]


def hop_perm(size, step, way):
    far = size // 2
    moves = [(z, z + 1) for z in range(step - 1, far - 1)]
    if way < 0:
        moves = [(far - 1 - a, far - 1 - b) for a, b in moves]
    return [(a * 2 + y, b * 2 + y) for a, b in moves for y in range(2)]


def fast_on_device(
    sizes,
    enc_keys,
    enc_values,
    input_ids,
    latent_queries,
    latent_array,
    w_out,
    norm_gain,
    w_key,
    w_value,
    query_features,
    query_ids,
    query_table,
    enc_bias,
    query_counts,
):
    groups, pos = sizes
    p = lax.axis_index("pos")
    place = lax.axis_index("head")
    rows = latent_array.shape[0]
    tokens, half_width = enc_keys.shape
    heads = half_width // HEAD_DIM
    mods = enc_bias.shape[0]
    modality = jnp.arange(mods, dtype=jnp.int32)
    far, z, y, x = pos // 2, p // 2, p % 2, lax.axis_index("groups") % 2
    near = swap_perm(pos)

    def over_groups(value):
        return lax.ppermute(value, "groups", swap_perm(groups))

    def over_near(value):
        return lax.ppermute(value, "pos", near)

    def over_far(value, k):
        return lax.ppermute(value, "pos", shift_perm(pos, k))

    def hop(step, pair):
        return [
            lax.ppermute(v, "pos", hop_perm(pos, step, way)) for v, way in zip(pair, (1, -1))
        ]

    def by_shift(hops, k):
        return jnp.where(z + k < far, hops[k][1], hops[far - k][0])

    q_onehot = (query_ids[:, None] == modality[None, :]).astype(jnp.int32)
    local_counts = jnp.sum(q_onehot, axis=0)

    def columns(arrays, which):
        part = half_width // 2
        return jnp.concatenate(
            [lax.dynamic_slice_in_dim(v, which * part, part, 1) for v in arrays], axis=1
        )

    extra = jnp.pad(input_ids[None, :], ((0, EXTRA - 1), (0, half_width - tokens)))
    extra = extra.astype(jnp.bfloat16)
    near_inputs = over_near(
        jnp.concatenate([columns((enc_keys, enc_values), 1 - y), extra], axis=0)
    )

    out_half, out_cols = w_out.shape[0] // 2, w_out.shape[1]
    counted = jnp.concatenate([local_counts // 16, local_counts % 16])
    counted = jnp.pad(counted[None, :], ((0, EXTRA - 1), (0, out_cols - 2 * mods)))
    counted = counted.astype(jnp.bfloat16)

    def half_of_out(which):
        own = lax.dynamic_slice_in_dim(w_out, which * out_half, out_half, 0)
        return jnp.concatenate([own, counted])

    out_sent = half_of_out(x)
    out_far = [over_far(out_sent, k) for k in range(1, far)]
    places = [((z + k) % far) * 2 + (y ^ j) for j in range(2) for k in range(far)]
    kv_for_near = columns((w_key, w_value), 1 - y)
    near_inputs, out_far, out_sent, kv_for_near = lax.optimization_barrier(
        (near_inputs, out_far, out_sent, kv_for_near)
    )
    out_far = jnp.concatenate(out_far)
    out_far_other = over_groups(out_far)

    kv_own = columns((w_key, w_value), y)
    kv_near = over_near(kv_for_near)

    head_bias = lax.dynamic_slice_in_dim(enc_bias, y * (heads // 2), heads // 2, 1)
    parts = encode(
        y, latent_queries, enc_keys, enc_values, extra, near_inputs, head_bias, 2 * rows
    )
    kv_near, out_sent, _ = lax.optimization_barrier((kv_near, out_sent, parts))
    kv_sent = jnp.where(x == 0, kv_own, kv_near)
    hops = {0: [kv_sent, kv_sent]}
    hops[1] = hop(1, hops[0])
    out_near = over_near(jnp.concatenate([out_sent, out_far]))
    out_near_other = over_near(jnp.concatenate([half_of_out(1 - x), out_far_other]))
    columns_of_slice = [[2 * i + j for i in range(far)] for j in range(2)]
    parts = lax.all_to_all(parts, "pos", 0, 0, axis_index_groups=columns_of_slice, tiled=True)

    def kept_queries():
        far_counts = out_far.reshape(far - 1, out_half + EXTRA, out_cols)[:, out_half, : 2 * mods]
        near_counts = out_near.reshape(far, out_half + EXTRA, out_cols)[:, out_half, : 2 * mods]
        counts = jnp.concatenate([counted[:1, : 2 * mods], far_counts, near_counts])
        counts = counts.astype(jnp.int32)
        counts = counts[:, :mods] * 16 + counts[:, mods:]
        earlier = jnp.stack(places)[:, None] < p
        before = jnp.sum(jnp.where(earlier, counts, 0), axis=0)
        within = jnp.cumsum(q_onehot, axis=0) - q_onehot
        ranked = jnp.sum((within + before[None, :]) * q_onehot, axis=1)
        limits = jnp.sum(q_onehot * query_counts[None, :], axis=1)
        return ranked < limits

    parts, out_near, out_far_other, out_near_other, hops = lax.optimization_barrier(
        (parts, out_near, out_far_other, out_near_other, hops)
    )
    hops[2] = hop(2, hops[1])
    attended, for_near = merge(y, parts, far)
    from_near = over_near(for_near)
    kept = kept_queries()
    from_near, kept = lax.optimization_barrier((from_near, kept))
    out_ids = jnp.stack([*places, y, x]).astype(jnp.int32)
    weights = [w_out, out_far, out_far_other, out_near, out_near_other]
    partial_value = project(out_ids, attended, from_near, weights)
    partial_value, hops = lax.optimization_barrier((partial_value, hops))
    for step in range(3, far):
        hops[step] = hop(step, hops[step - 1])
    theirs = lax.ppermute(partial_value, "head", swap_perm(2))
    own_cols, normed, normed_other = normalise(
        place, partial_value, theirs, latent_array, norm_gain[None, :]
    )
    lookup = jnp.dot(q_onehot.astype(jnp.bfloat16), query_table, preferred_element_type=jnp.float32)
    queries = (query_features.astype(jnp.float32) + lookup).astype(jnp.bfloat16)
    own_queries = columns((queries,), y)
    near_queries = over_near(columns((queries,), 1 - y))

    kv_at = [p, p ^ 1]
    for other in (x, 1 - x):
        kv_at += [((z + k) % far) * 2 + (y ^ other) for k in range(1, far)]
    kv_ids = jnp.stack([place, *kv_at]).astype(jnp.int32)

    def cores(values):
        return [lax.ppermute(v, "head", swap_perm(2)) for v in values]

    def fold(mine, other):
        return latent_keys_values(kv_ids, mine, other, kv_bands)

    def arrival(hops, j):
        picked = None
        for at in range(far):
            came = [
                (step, way)
                for step in range(1, far)
                for way in (1, 0)
                if (at + step < far if way else at >= step)
            ]
            step, way = came[j - 1]
            value = hops[step][way]
            picked = value if picked is None else jnp.where(z == at, value, picked)
        return picked

    came = {0: [normed, normed]}
    came[1] = hop(1, came[0])
    normed_near = over_near(normed)
    came, hops = lax.optimization_barrier((came, hops))
    kv_moved = jnp.concatenate([by_shift(hops, k) for k in range(1, far)])
    kv_bands = [kv_own, kv_near, kv_moved, over_groups(kv_moved)]
    mine, other = [normed, normed_near], [normed_other, *cores([normed_near])]
    keys_values, near_state = [], None
    for step in range(1, far):
        fresh = arrival(came, step)
        if step + 1 < far:
            came[step + 1] = hop(step + 1, came[step])
        fresh_near = over_near(fresh)
        mine.append(fresh)
        other += cores([fresh])
        if step > 1:
            keys_values.append(fold(mine, other))
            mine, other = [], []
        if step == 2 and far > 3:
            near_state = decode(near_queries, keys_values, None, None)
        if step + 1 < far:
            came, keys_values, near_state = lax.optimization_barrier(
                (came, keys_values, near_state)
            )
        else:
            fresh_near, keys_values = lax.optimization_barrier((fresh_near, keys_values))
        mine.append(fresh_near)
        other += cores([fresh_near])
    keys_values.append(fold(mine, other))
    own_state = decode(own_queries, keys_values, None, jnp.float32)
    if far > 3:
        near_state = decode(near_queries, keys_values[1:], near_state, jnp.bfloat16)
    else:
        near_state = decode(near_queries, keys_values, None, jnp.bfloat16)
    from_near = lax.ppermute(near_state, "pos", near).astype(jnp.float32)
    decoded = jnp.where(
        y == 0,
        jnp.concatenate([own_state, from_near], axis=1),
        jnp.concatenate([from_near, own_state], axis=1),
    )
    decoded = jnp.where(kept[:, None], decoded, 0.0)
    return (own_cols, decoded)


def on_device(sizes, *args):
    groups, pos, head = sizes
    enc_keys, latent_array, w_out, w_key = args[0], args[4], args[5], args[7]
    fits = (
        head == 2
        and pos % 2 == 0
        and pos > 2
        and groups % 2 == 0
        and enc_keys.shape[1] % (4 * HEAD_DIM) == 0
        and 3 * enc_keys.shape[1] <= 2 * HEAD_DIM * EXTRA
        and enc_keys.shape[0] % LANES == 0
        and enc_keys.shape[0] <= enc_keys.shape[1]
        and w_key.shape[0] % LANES == 0
        and w_out.shape[0] % (2 * LANES) == 0
        and w_out.shape[1] % LANES == 0
        and latent_array.shape[0] % LANES == 0
    )
    if fits:
        return fast_on_device((groups, pos), *args)
    return plain_on_device(*args)


def solution(mesh):
    return jax.shard_map(
        functools.partial(on_device, tuple(mesh.shape[a] for a in ("groups", "pos", "head"))),
        mesh=mesh,
        in_specs=(
            P(("groups", "pos"), "head"),
            P(("groups", "pos"), "head"),
            P(("groups", "pos")),
            P("groups", "head"),
            P(("groups", "pos"), None),
            P("head", "pos"),
            P(),
            P("pos", "head"),
            P("pos", "head"),
            P(("groups", "pos"), "head"),
            P(("groups", "pos")),
            P(None, "head"),
            P(None, "head"),
            P("groups"),
        ),
        out_specs=(P(("groups", "pos"), "head"), P(("groups", "pos"), "head")),
        check_vma=False,
    )
```

```python
import functools

import jax
import jax.numpy as jnp
from jax import lax
from jax.experimental import pallas as pl
from jax.experimental.pallas import tpu as pltpu
from jax.sharding import PartitionSpec as P

HEAD_DIM = 128


norm_eps = 1e-06


def prefix(shard, axis, combine, identity):
    peers, place = (lax.axis_size(axis), lax.axis_index(axis))
    everything = lax.all_gather(shard, axis)
    start = jnp.broadcast_to(jnp.asarray(identity, shard.dtype), shard.shape)

    def step(k, before):
        reached = k < place
        new = combine(before, everything[k])
        return jnp.where(reached, new, before)

    return lax.fori_loop(0, peers, step, start)


def plain_on_device(
    enc_keys,
    enc_values,
    input_ids,
    latent_queries,
    latent_array,
    w_out,
    norm_gain,
    w_key,
    w_value,
    query_features,
    query_ids,
    query_table,
    enc_bias,
    query_counts,
):
    tok_rows = enc_keys.shape[0]
    half_width = enc_keys.shape[1]
    local_heads = half_width // HEAD_DIM
    score_scale = HEAD_DIM ** (-0.5)
    modality = jnp.arange(enc_bias.shape[0], dtype=jnp.int32)
    in_onehot = (input_ids[:, None] == modality[None, :]).astype(jnp.float32)
    bias_rows = jnp.dot(in_onehot, enc_bias, precision=lax.Precision.HIGHEST)
    bias_heads = bias_rows.T[:, None, :]
    keys_split = enc_keys.reshape(tok_rows, local_heads, HEAD_DIM)
    values_split = enc_values.reshape(tok_rows, local_heads, HEAD_DIM)
    lat_total = latent_queries.shape[0]
    block_rows = min(512, lat_total)
    query_blocks = latent_queries.reshape(
        lat_total // block_rows, block_rows, local_heads, HEAD_DIM
    )

    def encode_block(block_queries):
        scores = (
            jnp.einsum(
                "nha,tha->hnt", block_queries, keys_split, preferred_element_type=jnp.float32
            )
            * score_scale
            + bias_heads
        )
        highest = jnp.max(scores, axis=2)
        weights = jnp.exp(scores - highest[:, :, None])
        totals = jnp.sum(weights, axis=2)
        summed = jnp.einsum(
            "hnt,tha->nha",
            weights.astype(jnp.bfloat16),
            values_split,
            preferred_element_type=jnp.float32,
        )
        return (highest.T, totals.T, summed.reshape(block_rows, half_width))

    block_max, block_tot, block_acc = lax.map(encode_block, query_blocks)
    row_highest = block_max.reshape(lat_total, local_heads)
    row_totals = block_tot.reshape(lat_total, local_heads)
    row_sums = block_acc.reshape(lat_total, half_width)
    own_rows = latent_array.shape[0]
    global_max = lax.pmax(row_highest, "pos")
    factor = jnp.exp(row_highest - global_max)
    scaled_sums = (row_sums.reshape(lat_total, local_heads, HEAD_DIM) * factor[:, :, None]).reshape(
        lat_total, half_width
    )
    totals, summed = (
        lax.psum_scatter(row_totals * factor, "pos", scatter_dimension=0, tiled=True),
        lax.psum_scatter(scaled_sums, "pos", scatter_dimension=0, tiled=True),
    )
    summed = summed.reshape(own_rows, local_heads, HEAD_DIM)
    attended = (summed / totals[:, :, None]).reshape(own_rows, half_width).astype(jnp.bfloat16)
    partial_value = jnp.dot(
        attended,
        lax.all_gather(w_out, "pos", axis=1, tiled=True),
        preferred_element_type=jnp.float32,
    )
    offset = lax.axis_index("head") * half_width
    projected = lax.psum(partial_value, "head")
    updated = latent_array.astype(jnp.float32) + projected
    mean_square = jnp.mean(updated * updated, axis=1, keepdims=True)
    normed_full = updated * lax.rsqrt(mean_square + norm_eps) * norm_gain
    normed = normed_full.astype(jnp.bfloat16)
    own_cols = lax.dynamic_slice_in_dim(normed_full, offset, half_width, 1)
    pieces = (
        lax.all_gather(w_key, "pos", axis=0, tiled=True),
        lax.all_gather(w_value, "pos", axis=0, tiled=True),
    )
    key_sum = jnp.dot(normed, pieces[0], preferred_element_type=jnp.float32)
    value_sum = jnp.dot(normed, pieces[1], preferred_element_type=jnp.float32)
    latent_keys = key_sum.astype(jnp.bfloat16)
    latent_values = value_sum.astype(jnp.bfloat16)
    q_onehot = (query_ids[:, None] == modality[None, :]).astype(jnp.int32)
    local_counts = jnp.sum(q_onehot, axis=0)
    before = prefix(
        local_counts, "pos", lambda earlier, later: earlier + later, jnp.zeros_like(local_counts)
    )
    within = jnp.cumsum(q_onehot, axis=0) - q_onehot
    ranked = jnp.sum((within + before[None, :]) * q_onehot, axis=1)
    limits = jnp.sum(q_onehot * query_counts[None, :], axis=1)
    kept_rows = ranked < limits
    lookup = jnp.dot(q_onehot.astype(jnp.bfloat16), query_table, preferred_element_type=jnp.float32)
    queries = (
        (query_features.astype(jnp.float32) + lookup)
        .astype(jnp.bfloat16)
        .reshape(tok_rows, local_heads, HEAD_DIM)
    )

    def fold_rows(running, key_rows, value_rows):
        running_max, running_tot, running_acc = running
        key_heads = key_rows.reshape(key_rows.shape[0], local_heads, HEAD_DIM)
        value_heads = value_rows.reshape(value_rows.shape[0], local_heads, HEAD_DIM)
        scores = (
            jnp.einsum("tha,rha->htr", queries, key_heads, preferred_element_type=jnp.float32)
            * score_scale
        )
        new_max = jnp.maximum(running_max, jnp.max(scores, axis=2))
        fade = jnp.exp(running_max - new_max)
        weights = jnp.exp(scores - new_max[:, :, None])
        new_tot = running_tot * fade + jnp.sum(weights, axis=2)
        new_acc = running_acc * fade[:, :, None] + jnp.einsum(
            "htr,rha->hta",
            weights.astype(jnp.bfloat16),
            value_heads,
            preferred_element_type=jnp.float32,
        )
        return (new_max, new_tot, new_acc)

    start_state = (
        jnp.full((local_heads, tok_rows), -jnp.inf, jnp.float32),
        jnp.zeros((local_heads, tok_rows), jnp.float32),
        jnp.zeros((local_heads, tok_rows, HEAD_DIM), jnp.float32),
    )
    running = start_state
    pieces = (
        lax.all_gather(latent_keys, "pos", axis=0, tiled=True),
        lax.all_gather(latent_values, "pos", axis=0, tiled=True),
    )
    row_count = pieces[0].shape[0]
    key_blocks = pieces[0].reshape(row_count // 512, 512, half_width)
    value_blocks = pieces[1].reshape(row_count // 512, 512, half_width)

    def scan_step(state, pair):
        return (fold_rows(state, pair[0], pair[1]), None)

    running, ignored = lax.scan(scan_step, running, (key_blocks, value_blocks))
    final_max, final_tot, final_acc = running
    dec_heads = final_acc / final_tot[:, :, None]
    dec_rows = jnp.transpose(dec_heads, (1, 0, 2)).reshape(tok_rows, half_width)
    decoded = jnp.where(kept_rows[:, None], dec_rows, 0.0)
    return (own_cols, decoded)


LANES = 128
EXTRA = 16
BIG = 56
LOG2E = 1.4426950408889634
EXP2_SCALE = LOG2E * HEAD_DIM**-0.5
NT = (((1,), (1,)), ((), ()))


def params(mib):
    return pltpu.CompilerParams(vmem_limit_bytes=mib << 20)


def cost(flops, nbytes, exps=0):
    return pl.CostEstimate(flops=int(flops), bytes_accessed=int(nbytes), transcendentals=int(exps))


def whole(shape):
    return pl.BlockSpec(shape, lambda *args: (0,) * len(shape))


def encode_kernel(ids_ref, q_ref, k_ref, v_ref, extra_ref, near_ref, bias_ref, out_ref):
    rows, width = q_ref.shape
    tokens = k_ref.shape[0]
    heads = width // HEAD_DIM
    ones = jnp.ones((tokens, LANES), jnp.bfloat16)
    kinds = [
        extra_ref[...].astype(jnp.float32)[:1, :tokens],
        near_ref[tokens:, :].astype(jnp.float32)[:1, :tokens],
    ]
    lane = lax.broadcasted_iota(jnp.int32, (rows, LANES), 1)
    lse_all = jnp.zeros((rows, LANES), jnp.float32)
    for h in range(heads):
        cols = slice(h * HEAD_DIM, (h + 1) * HEAD_DIM)
        late = slice(width + h * HEAD_DIM, width + (h + 1) * HEAD_DIM)
        pairs = [
            (k_ref[:, cols], v_ref[:, cols]),
            (near_ref[:tokens, cols], near_ref[:tokens, late]),
        ]
        top = acc = None
        for (keys, values), kind in zip(pairs, kinds):
            bias = jnp.zeros_like(kind)
            for m in range(bias_ref.shape[0]):
                bias = jnp.where(kind == m, bias_ref[m, h] * LOG2E, bias)
            scores = lax.dot_general(q_ref[:, cols], keys, NT, preferred_element_type=jnp.float32)
            scores = scores * EXP2_SCALE + bias
            new_top = jnp.max(scores, axis=1, keepdims=True)
            if top is not None:
                new_top = jnp.maximum(top, new_top)
            weights = jnp.exp2(scores - new_top).astype(jnp.bfloat16)
            summed = jnp.dot(
                weights, jnp.concatenate([values, ones], axis=1), preferred_element_type=jnp.float32
            )
            if top is not None:
                summed = summed + acc * jnp.exp2(top - new_top)
            top, acc = new_top, summed
        totals = acc[:, HEAD_DIM:]
        out_ref[:rows, cols] = (acc[:, :HEAD_DIM] / totals).astype(jnp.bfloat16)
        lse_all = jnp.where(lane % heads == h, top + jnp.log2(totals), lse_all)
    lse = lse_all.T[:EXTRA, :]
    high = lse.astype(jnp.bfloat16).astype(jnp.float32)
    mid = (lse - high).astype(jnp.bfloat16).astype(jnp.float32)
    low = lse - high - mid
    row = lax.broadcasted_iota(jnp.int32, lse.shape, 0)
    terms = jnp.where(row < heads, high, jnp.where(row < 2 * heads, mid, low))
    out_ref[rows:, :] = terms.astype(jnp.bfloat16)


def encode(which, queries, keys, values, extra, near, bias, rows):
    tokens = keys.shape[0]
    width = keys.shape[1] // 2
    blocks = queries.shape[0] // rows
    half = pl.BlockSpec((tokens, width), lambda i, ids: (0, ids[0]))
    grid_spec = pltpu.PrefetchScalarGridSpec(
        num_scalar_prefetch=1,
        grid=(blocks,),
        in_specs=[
            pl.BlockSpec((rows, width), lambda i, ids: (i, ids[0])),
            half,
            half,
            whole(extra.shape),
            whole(near.shape),
            pl.BlockSpec(memory_space=pltpu.SMEM),
        ],
        out_specs=pl.BlockSpec((rows + EXTRA, width), lambda i, ids: (i, 0)),
    )
    return pl.pallas_call(
        encode_kernel,
        grid_spec=grid_spec,
        out_shape=jax.ShapeDtypeStruct((blocks * (rows + EXTRA), width), jnp.bfloat16),
        compiler_params=params(BIG),
        cost_estimate=cost(
            16 * blocks * rows * tokens * width, 8 * tokens * width, blocks * rows * tokens * 8
        ),
        name="encode_rows",
    )(which.reshape(1), queries, keys, values, extra, near, bias)


def merge_kernel(count, ids_ref, parts_ref, mine_ref, near_ref, all_ref):
    rows, width = all_ref.shape
    long = rows + EXTRA
    parts = [parts_ref.at[i * long : (i + 1) * long, :] for i in range(count)]
    heads = width // HEAD_DIM
    stats = [v[rows:, :].astype(jnp.float32).T for v in parts]
    for h in range(heads):
        cols = slice(h * HEAD_DIM, (h + 1) * HEAD_DIM)
        lses = [
            s[:, h : h + 1] + s[:, heads + h : heads + h + 1] + s[:, 2 * heads + h : 2 * heads + h + 1]
            for s in stats
        ]
        top = functools.reduce(jnp.maximum, lses)
        factors = [jnp.exp2(v - top) for v in lses]
        inverse = 1.0 / functools.reduce(jnp.add, factors)
        merged = functools.reduce(
            jnp.add,
            [v[:rows, cols].astype(jnp.float32) * (f * inverse) for v, f in zip(parts, factors)],
        )
        all_ref[:, cols] = merged.astype(jnp.bfloat16)
    own = rows // 2
    mine_ref[...] = all_ref[pl.ds(pl.multiple_of(ids_ref[0] * own, own), own), :]
    near_ref[...] = all_ref[pl.ds(pl.multiple_of((1 - ids_ref[0]) * own, own), own), :]


def merge(which, parts, count):
    long, width = parts.shape[0] // count, parts.shape[1]
    rows = long - EXTRA
    grid_spec = pltpu.PrefetchScalarGridSpec(
        num_scalar_prefetch=1,
        grid=(1,),
        in_specs=[whole(parts.shape)],
        out_specs=[whole((rows // 2, width))] * 2,
        scratch_shapes=[pltpu.VMEM((rows, width), jnp.bfloat16)],
    )
    return pl.pallas_call(
        functools.partial(merge_kernel, count),
        grid_spec=grid_spec,
        out_shape=[jax.ShapeDtypeStruct((rows // 2, width), jnp.bfloat16)] * 2,
        compiler_params=params(32),
        cost_estimate=cost(8 * rows * width, 10 * rows * width),
        name="merge_rows",
    )(which.reshape(1), parts)


def project_kernel(far, ids_ref, mine_ref, near_ref, *refs):
    w_ref, far_ref, far_other_ref, near_w_ref, near_other_ref, out_ref, att_ref = refs
    part = mine_ref.shape[1]
    first = ids_ref[2 * far]
    att_ref[:, pl.ds(pl.multiple_of(first * part, part), part)] = mine_ref[...]
    att_ref[:, pl.ds(pl.multiple_of((1 - first) * part, part), part)] = near_ref[...]
    cols = w_ref.shape[1]
    depth = att_ref.shape[1] // 2
    share = ids_ref[2 * far + 1]
    halves = [
        att_ref[:, pl.ds(pl.multiple_of(v * depth, depth), depth)] for v in (share, 1 - share)
    ]

    def place(slot, value):
        out_ref[:, pl.ds(pl.multiple_of(ids_ref[slot] * cols, cols), cols)] = value

    place(0, jnp.dot(att_ref[...], w_ref[...], preferred_element_type=jnp.float32))
    for slot in range(1, 2 * far):
        refs = (far_ref, far_other_ref) if slot < far else (near_w_ref, near_other_ref)
        start = (slot - 1 if slot < far else slot - far) * (depth + EXTRA)
        terms = [
            jnp.dot(v, w[start : start + depth, :], preferred_element_type=jnp.float32)
            for v, w in zip(halves, refs)
        ]
        place(slot, terms[0] + terms[1])


def project(ids, mine, near, weights):
    rows, part = mine.shape
    far = (ids.shape[0] - 2) // 2
    out_cols = 2 * far * weights[0].shape[1]
    grid_spec = pltpu.PrefetchScalarGridSpec(
        num_scalar_prefetch=1,
        grid=(1,),
        in_specs=[whole(v.shape) for v in (mine, near, *weights)],
        out_specs=whole((rows, out_cols)),
        scratch_shapes=[pltpu.VMEM((rows, 2 * part), jnp.bfloat16)],
    )
    return pl.pallas_call(
        functools.partial(project_kernel, far),
        grid_spec=grid_spec,
        out_shape=jax.ShapeDtypeStruct((rows, out_cols), jnp.float32),
        compiler_params=params(BIG),
        cost_estimate=cost(4 * rows * part * out_cols, 4 * part * out_cols + 4 * rows * out_cols),
        name="project_rows",
    )(ids, mine, near, *weights)


def norm_kernel(
    ids_ref, mine_ref, theirs_ref, latent_ref, gain_ref, out_ref, normed_ref, other_ref, full_ref
):
    updated = latent_ref[...].astype(jnp.float32) + (mine_ref[...] + theirs_ref[...])
    mean_square = jnp.mean(updated * updated, axis=1, keepdims=True)
    full_ref[...] = updated * lax.rsqrt(mean_square + norm_eps) * gain_ref[...]
    half = out_ref.shape[1]
    own = full_ref[:, pl.ds(pl.multiple_of(ids_ref[0] * half, half), half)]
    out_ref[...] = own
    normed_ref[...] = own.astype(jnp.bfloat16)
    other = full_ref[:, pl.ds(pl.multiple_of((1 - ids_ref[0]) * half, half), half)]
    other_ref[...] = other.astype(jnp.bfloat16)


def normalise(place, mine, theirs, latent_array, gain):
    rows, width = mine.shape
    half = width // 2
    grid_spec = pltpu.PrefetchScalarGridSpec(
        num_scalar_prefetch=1,
        grid=(1,),
        in_specs=[whole((rows, width))] * 3 + [whole((1, width))],
        out_specs=[whole((rows, half))] * 3,
        scratch_shapes=[pltpu.VMEM((rows, width), jnp.float32)],
    )
    return pl.pallas_call(
        norm_kernel,
        grid_spec=grid_spec,
        out_shape=[
            jax.ShapeDtypeStruct((rows, half), jnp.float32),
            jax.ShapeDtypeStruct((rows, half), jnp.bfloat16),
            jax.ShapeDtypeStruct((rows, half), jnp.bfloat16),
        ],
        compiler_params=params(BIG),
        cost_estimate=cost(6 * rows * width, 13 * rows * width),
        name="norm_rows",
    )(place.reshape(1), mine, theirs, latent_array, gain)


def latents_kernel(pieces, ids_ref, *refs):
    mine, theirs = refs[:pieces], refs[pieces : 2 * pieces]
    w_refs, (out_ref, normed_ref, w_ref) = refs[2 * pieces : -3], refs[-3:]
    rows, half = mine[0].shape
    slots = ids_ref.shape[0] - 1
    depth = 2 * half // slots

    @pl.when(pl.program_id(0) == 0)
    def arrange():
        for j in range(slots):
            at = ids_ref[1 + j]
            start = pl.multiple_of((at % (slots // 2)) * depth, depth)

            def copy(pieces):
                for r, piece in enumerate(pieces):
                    normed_ref[r * rows : (r + 1) * rows, j * depth : (j + 1) * depth] = piece[
                        :, pl.ds(start, depth)
                    ]

            is_mine = at // (slots // 2) == ids_ref[0]
            pl.when(is_mine)(functools.partial(copy, mine))
            pl.when(jnp.logical_not(is_mine))(functools.partial(copy, theirs))

    start = 0
    for band in w_refs:
        w_ref[start : start + band.shape[0], :] = band[...]
        start += band.shape[0]
    out_ref[...] = jnp.dot(
        normed_ref[...], w_ref[...], preferred_element_type=jnp.float32
    ).astype(jnp.bfloat16)


def latent_keys_values(ids, mine, theirs, bands):
    pieces = len(mine)
    rows, half = mine[0].shape
    width = bands[0].shape[1]
    block = min(512, width)
    total = sum(band.shape[0] for band in bands)
    grid_spec = pltpu.PrefetchScalarGridSpec(
        num_scalar_prefetch=1,
        grid=(width // block,),
        in_specs=[whole((rows, half))] * (2 * pieces)
        + [pl.BlockSpec((band.shape[0], block), lambda i, ids: (0, i)) for band in bands],
        out_specs=pl.BlockSpec((rows * pieces, block), lambda i, ids: (0, i)),
        scratch_shapes=[
            pltpu.VMEM((rows * pieces, total), jnp.bfloat16),
            pltpu.VMEM((total, block), jnp.bfloat16),
        ],
    )
    return pl.pallas_call(
        functools.partial(latents_kernel, pieces),
        grid_spec=grid_spec,
        out_shape=jax.ShapeDtypeStruct((rows * pieces, width), jnp.bfloat16),
        compiler_params=params(BIG),
        cost_estimate=cost(2 * rows * pieces * total * width, 2 * total * width),
        name="latent_keys_values",
    )(ids, *mine, *theirs, *bands)


def row_chunks(lengths, size):
    chunks, open_chunk, room = [], [], size
    for i, length in enumerate(lengths):
        start = 0
        while start < length:
            take = min(room, length - start)
            open_chunk.append((i, start, start + take))
            start, room = start + take, room - take
            if room == 0:
                chunks.append(open_chunk)
                open_chunk, room = [], size
    return chunks + ([open_chunk] if open_chunk else [])


def decode_kernel(parts, q_ref, *refs):
    k_refs, v_refs, out_ref = refs[:parts], refs[parts : 2 * parts], refs[-1]

    def gathered(sources, chunk, cols):
        rows = [sources[i][start:stop, cols] for i, start, stop in chunk]
        return rows[0] if len(rows) == 1 else jnp.concatenate(rows)

    for h in range(q_ref.shape[1] // HEAD_DIM):
        cols = slice(h * HEAD_DIM, (h + 1) * HEAD_DIM)
        top = acc = None
        for chunk in row_chunks([k.shape[0] for k in k_refs], 512):
            keys, values = gathered(k_refs, chunk, cols), gathered(v_refs, chunk, cols)
            scores = lax.dot_general(q_ref[:, cols], keys, NT, preferred_element_type=jnp.float32)
            scores = scores * EXP2_SCALE
            new_top = jnp.max(scores, axis=1, keepdims=True)
            if top is not None:
                new_top = jnp.maximum(top, new_top)
            weights = jnp.exp2(scores - new_top).astype(jnp.bfloat16)
            summed = jnp.dot(
                weights,
                jnp.concatenate([values, jnp.ones((keys.shape[0], LANES), jnp.bfloat16)], axis=1),
                preferred_element_type=jnp.float32,
            )
            if top is not None:
                summed = summed + acc * jnp.exp2(top - new_top)
            top, acc = new_top, summed
        out_ref[:, cols] = (acc[:, :HEAD_DIM] / acc[:, HEAD_DIM:]).astype(out_ref.dtype)


def decode(queries, keys_values, out_type):
    tokens, width = queries.shape
    latents = sum(v.shape[0] for v in keys_values)
    pair = min(2 * HEAD_DIM, width)
    steps = width // pair
    narrow = pl.BlockSpec((tokens, pair), lambda i: (0, i))
    keys = [pl.BlockSpec((v.shape[0], pair), lambda i: (0, i)) for v in keys_values]
    values = [pl.BlockSpec((v.shape[0], pair), lambda i: (0, steps + i)) for v in keys_values]
    return pl.pallas_call(
        functools.partial(decode_kernel, len(keys_values)),
        grid=(steps,),
        in_specs=[narrow, *keys, *values],
        out_specs=narrow,
        out_shape=jax.ShapeDtypeStruct((tokens, width), out_type),
        compiler_params=params(BIG),
        cost_estimate=cost(
            16 * tokens * latents * width,
            4 * latents * width + 6 * tokens * width,
            tokens * latents * (width // HEAD_DIM),
        ),
        name="decode_rows",
    )(queries, *keys_values, *keys_values)


def swap_perm(size):
    return [(i, i ^ 1) for i in range(size)]


def shift_perm(size, k):
    far = size // 2
    return [(((z + k) % far) * 2 + y, z * 2 + y) for z in range(far) for y in range(2)]


def hop_perm(size, step, way):
    far = size // 2
    moves = [(z, z + 1) for z in range(step - 1, far - 1)]
    if way < 0:
        moves = [(far - 1 - a, far - 1 - b) for a, b in moves]
    return [(a * 2 + y, b * 2 + y) for a, b in moves for y in range(2)]


def fast_on_device(
    sizes,
    enc_keys,
    enc_values,
    input_ids,
    latent_queries,
    latent_array,
    w_out,
    norm_gain,
    w_key,
    w_value,
    query_features,
    query_ids,
    query_table,
    enc_bias,
    query_counts,
):
    groups, pos = sizes
    p = lax.axis_index("pos")
    place = lax.axis_index("head")
    rows = latent_array.shape[0]
    tokens, half_width = enc_keys.shape
    heads = half_width // HEAD_DIM
    mods = enc_bias.shape[0]
    modality = jnp.arange(mods, dtype=jnp.int32)
    far, z, y, x = pos // 2, p // 2, p % 2, lax.axis_index("groups") % 2
    near = swap_perm(pos)

    def over_groups(value):
        return lax.ppermute(value, "groups", swap_perm(groups))

    def over_near(value):
        return lax.ppermute(value, "pos", near)

    def over_far(value, k):
        return lax.ppermute(value, "pos", shift_perm(pos, k))

    def hop(step, pair):
        return [
            lax.ppermute(v, "pos", hop_perm(pos, step, way)) for v, way in zip(pair, (1, -1))
        ]

    def by_shift(hops, k):
        return jnp.where(z + k < far, hops[k][1], hops[far - k][0])

    q_onehot = (query_ids[:, None] == modality[None, :]).astype(jnp.int32)
    local_counts = jnp.sum(q_onehot, axis=0)

    def columns(arrays, which):
        part = half_width // 2
        return jnp.concatenate(
            [lax.dynamic_slice_in_dim(v, which * part, part, 1) for v in arrays], axis=1
        )

    extra = jnp.pad(input_ids[None, :], ((0, EXTRA - 1), (0, half_width - tokens)))
    extra = extra.astype(jnp.bfloat16)
    near_inputs = over_near(
        jnp.concatenate([columns((enc_keys, enc_values), 1 - y), extra], axis=0)
    )

    out_half, out_cols = w_out.shape[0] // 2, w_out.shape[1]
    counted = jnp.concatenate([local_counts // 16, local_counts % 16])
    counted = jnp.pad(counted[None, :], ((0, EXTRA - 1), (0, out_cols - 2 * mods)))
    counted = counted.astype(jnp.bfloat16)

    def half_of_out(which):
        own = lax.dynamic_slice_in_dim(w_out, which * out_half, out_half, 0)
        return jnp.concatenate([own, counted])

    out_sent = half_of_out(x)
    out_far = [over_far(out_sent, k) for k in range(1, far)]
    places = [((z + k) % far) * 2 + (y ^ j) for j in range(2) for k in range(far)]
    kv_for_near = columns((w_key, w_value), 1 - y)
    near_inputs, out_far, out_sent, kv_for_near = lax.optimization_barrier(
        (near_inputs, out_far, out_sent, kv_for_near)
    )
    out_far = jnp.concatenate(out_far)
    out_far_other = over_groups(out_far)

    kv_own = columns((w_key, w_value), y)
    kv_near = over_near(kv_for_near)

    head_bias = lax.dynamic_slice_in_dim(enc_bias, y * (heads // 2), heads // 2, 1)
    parts = encode(
        y, latent_queries, enc_keys, enc_values, extra, near_inputs, head_bias, 2 * rows
    )
    kv_near, out_sent, parts = lax.optimization_barrier((kv_near, out_sent, parts))
    kv_sent = jnp.where(x == 0, kv_own, kv_near)
    hops = {0: [kv_sent, kv_sent]}
    hops[1] = hop(1, hops[0])
    early = [k for k in range(1, far) if max(k, far - k) < 3]
    rest = [k for k in range(1, far) if k not in early]
    out_near = over_near(jnp.concatenate([out_sent, out_far]))
    out_near_other = over_near(jnp.concatenate([half_of_out(1 - x), out_far_other]))
    columns_of_slice = [[2 * i + j for i in range(far)] for j in range(2)]
    parts = lax.all_to_all(parts, "pos", 0, 0, axis_index_groups=columns_of_slice, tiled=True)

    def kept_queries():
        far_counts = out_far.reshape(far - 1, out_half + EXTRA, out_cols)[:, out_half, : 2 * mods]
        near_counts = out_near.reshape(far, out_half + EXTRA, out_cols)[:, out_half, : 2 * mods]
        counts = jnp.concatenate([counted[:1, : 2 * mods], far_counts, near_counts])
        counts = counts.astype(jnp.int32)
        counts = counts[:, :mods] * 16 + counts[:, mods:]
        earlier = jnp.stack(places)[:, None] < p
        before = jnp.sum(jnp.where(earlier, counts, 0), axis=0)
        within = jnp.cumsum(q_onehot, axis=0) - q_onehot
        ranked = jnp.sum((within + before[None, :]) * q_onehot, axis=1)
        limits = jnp.sum(q_onehot * query_counts[None, :], axis=1)
        return ranked < limits

    lookup = jnp.dot(q_onehot.astype(jnp.bfloat16), query_table, preferred_element_type=jnp.float32)
    queries = (query_features.astype(jnp.float32) + lookup).astype(jnp.bfloat16)
    own_queries = columns((queries,), y)
    near_queries = over_near(columns((queries,), 1 - y))

    parts, out_near, out_far_other, out_near_other, hops, near_queries = lax.optimization_barrier(
        (parts, out_near, out_far_other, out_near_other, hops, near_queries)
    )
    attended, for_near = merge(y, parts, far)
    for_near, hops = lax.optimization_barrier((for_near, hops))
    hops[2] = hop(2, hops[1])
    from_near = over_near(for_near)
    kept = kept_queries()
    out_ids = jnp.stack([*places, y, x]).astype(jnp.int32)
    weights = [w_out, out_far, out_far_other, out_near, out_near_other]
    partial_value = project(out_ids, attended, from_near, weights)
    partial_value, hops = lax.optimization_barrier((partial_value, hops))
    kv_bands = [kv_own, kv_near]
    for k in early:
        kv_moved = by_shift(hops, k)
        kv_bands += [kv_moved, over_groups(kv_moved)]
    for step in range(3, far):
        hops[step] = hop(step, hops[step - 1])
    theirs = lax.ppermute(partial_value, "head", swap_perm(2))
    own_cols, normed, normed_other = normalise(
        place, partial_value, theirs, latent_array, norm_gain[None, :]
    )
    kv_at = [p, p ^ 1]
    for k in early + rest:
        kv_at += [((z + k) % far) * 2 + (y ^ other) for other in (x, 1 - x)]
    kv_ids = jnp.stack([place, *kv_at]).astype(jnp.int32)

    def cores(values):
        return [lax.ppermute(v, "head", swap_perm(2)) for v in values]

    def fold(mine, other):
        return latent_keys_values(kv_ids, mine, other, kv_bands)

    def arrival(hops, j):
        picked = None
        for at in range(far):
            came = [
                (step, way)
                for step in range(1, far)
                for way in (1, 0)
                if (at + step < far if way else at >= step)
            ]
            step, way = came[j - 1]
            value = hops[step][way]
            picked = value if picked is None else jnp.where(z == at, value, picked)
        return picked

    came = {0: [normed, normed]}
    came[1] = hop(1, came[0])
    normed_near = over_near(normed)
    came, hops, kv_bands, kept = lax.optimization_barrier((came, hops, kv_bands, kept))
    mine, other = [normed, normed_near], [normed_other]
    for step in range(1, far):
        fresh = arrival(came, step)
        fresh_near = over_near(fresh)
        if step + 1 < far:
            came[step + 1] = hop(step + 1, came[step])
            k = rest[step - 1]
            kv_moved = by_shift(hops, k)
            kv_bands += [kv_moved, over_groups(kv_moved)]
            came, mine, kv_bands, fresh, fresh_near = lax.optimization_barrier(
                (came, mine, kv_bands, fresh, fresh_near)
            )
            other += cores(mine[-1:] + [fresh])
            mine += [fresh, fresh_near]
    mine, other, fresh = lax.optimization_barrier((mine, other, fresh))
    keys_values = [fold(mine[:-1], other)]
    last = [mine[-1], fresh]
    keys_values.append(fold(last, cores(last)))
    fresh_near, keys_values = lax.optimization_barrier((fresh_near, keys_values))
    keys_values.append(fold([fresh_near], cores([fresh_near])))
    near_state = decode(near_queries, keys_values, jnp.bfloat16)
    own_state = decode(own_queries, keys_values, jnp.float32)
    from_near = lax.ppermute(near_state, "pos", near).astype(jnp.float32)
    decoded = jnp.where(
        y == 0,
        jnp.concatenate([own_state, from_near], axis=1),
        jnp.concatenate([from_near, own_state], axis=1),
    )
    decoded = jnp.where(kept[:, None], decoded, 0.0)
    return (own_cols, decoded)


def on_device(sizes, *args):
    groups, pos, head = sizes
    enc_keys, latent_array, w_out, w_key = args[0], args[4], args[5], args[7]
    fits = (
        head == 2
        and pos % 2 == 0
        and pos > 4
        and groups % 2 == 0
        and enc_keys.shape[1] % (4 * HEAD_DIM) == 0
        and 3 * enc_keys.shape[1] <= 2 * HEAD_DIM * EXTRA
        and enc_keys.shape[0] % LANES == 0
        and enc_keys.shape[0] <= enc_keys.shape[1]
        and w_key.shape[0] % LANES == 0
        and w_out.shape[0] % (2 * LANES) == 0
        and w_out.shape[1] % LANES == 0
        and latent_array.shape[0] % LANES == 0
    )
    if fits:
        return fast_on_device((groups, pos), *args)
    return plain_on_device(*args)


def solution(mesh):
    return jax.shard_map(
        functools.partial(on_device, tuple(mesh.shape[a] for a in ("groups", "pos", "head"))),
        mesh=mesh,
        in_specs=(
            P(("groups", "pos"), "head"),
            P(("groups", "pos"), "head"),
            P(("groups", "pos")),
            P("groups", "head"),
            P(("groups", "pos"), None),
            P("head", "pos"),
            P(),
            P("pos", "head"),
            P("pos", "head"),
            P(("groups", "pos"), "head"),
            P(("groups", "pos")),
            P(None, "head"),
            P(None, "head"),
            P("groups"),
        ),
        out_specs=(P(("groups", "pos"), "head"), P(("groups", "pos"), "head")),
        check_vma=False,
    )
```

```python
import functools

import jax
import jax.numpy as jnp
from jax import lax
from jax.experimental import pallas as pl
from jax.experimental.pallas import tpu as pltpu
from jax.sharding import PartitionSpec as P

HEAD_DIM = 128


norm_eps = 1e-06


def prefix(shard, axis, combine, identity):
    peers, place = (lax.axis_size(axis), lax.axis_index(axis))
    everything = lax.all_gather(shard, axis)
    start = jnp.broadcast_to(jnp.asarray(identity, shard.dtype), shard.shape)

    def step(k, before):
        reached = k < place
        new = combine(before, everything[k])
        return jnp.where(reached, new, before)

    return lax.fori_loop(0, peers, step, start)


def plain_on_device(
    enc_keys,
    enc_values,
    input_ids,
    latent_queries,
    latent_array,
    w_out,
    norm_gain,
    w_key,
    w_value,
    query_features,
    query_ids,
    query_table,
    enc_bias,
    query_counts,
):
    tok_rows = enc_keys.shape[0]
    half_width = enc_keys.shape[1]
    local_heads = half_width // HEAD_DIM
    score_scale = HEAD_DIM ** (-0.5)
    modality = jnp.arange(enc_bias.shape[0], dtype=jnp.int32)
    in_onehot = (input_ids[:, None] == modality[None, :]).astype(jnp.float32)
    bias_rows = jnp.dot(in_onehot, enc_bias, precision=lax.Precision.HIGHEST)
    bias_heads = bias_rows.T[:, None, :]
    keys_split = enc_keys.reshape(tok_rows, local_heads, HEAD_DIM)
    values_split = enc_values.reshape(tok_rows, local_heads, HEAD_DIM)
    lat_total = latent_queries.shape[0]
    block_rows = min(512, lat_total)
    query_blocks = latent_queries.reshape(
        lat_total // block_rows, block_rows, local_heads, HEAD_DIM
    )

    def encode_block(block_queries):
        scores = (
            jnp.einsum(
                "nha,tha->hnt", block_queries, keys_split, preferred_element_type=jnp.float32
            )
            * score_scale
            + bias_heads
        )
        highest = jnp.max(scores, axis=2)
        weights = jnp.exp(scores - highest[:, :, None])
        totals = jnp.sum(weights, axis=2)
        summed = jnp.einsum(
            "hnt,tha->nha",
            weights.astype(jnp.bfloat16),
            values_split,
            preferred_element_type=jnp.float32,
        )
        return (highest.T, totals.T, summed.reshape(block_rows, half_width))

    block_max, block_tot, block_acc = lax.map(encode_block, query_blocks)
    row_highest = block_max.reshape(lat_total, local_heads)
    row_totals = block_tot.reshape(lat_total, local_heads)
    row_sums = block_acc.reshape(lat_total, half_width)
    own_rows = latent_array.shape[0]
    global_max = lax.pmax(row_highest, "pos")
    factor = jnp.exp(row_highest - global_max)
    scaled_sums = (row_sums.reshape(lat_total, local_heads, HEAD_DIM) * factor[:, :, None]).reshape(
        lat_total, half_width
    )
    totals, summed = (
        lax.psum_scatter(row_totals * factor, "pos", scatter_dimension=0, tiled=True),
        lax.psum_scatter(scaled_sums, "pos", scatter_dimension=0, tiled=True),
    )
    summed = summed.reshape(own_rows, local_heads, HEAD_DIM)
    attended = (summed / totals[:, :, None]).reshape(own_rows, half_width).astype(jnp.bfloat16)
    partial_value = jnp.dot(
        attended,
        lax.all_gather(w_out, "pos", axis=1, tiled=True),
        preferred_element_type=jnp.float32,
    )
    offset = lax.axis_index("head") * half_width
    projected = lax.psum(partial_value, "head")
    updated = latent_array.astype(jnp.float32) + projected
    mean_square = jnp.mean(updated * updated, axis=1, keepdims=True)
    normed_full = updated * lax.rsqrt(mean_square + norm_eps) * norm_gain
    normed = normed_full.astype(jnp.bfloat16)
    own_cols = lax.dynamic_slice_in_dim(normed_full, offset, half_width, 1)
    pieces = (
        lax.all_gather(w_key, "pos", axis=0, tiled=True),
        lax.all_gather(w_value, "pos", axis=0, tiled=True),
    )
    key_sum = jnp.dot(normed, pieces[0], preferred_element_type=jnp.float32)
    value_sum = jnp.dot(normed, pieces[1], preferred_element_type=jnp.float32)
    latent_keys = key_sum.astype(jnp.bfloat16)
    latent_values = value_sum.astype(jnp.bfloat16)
    q_onehot = (query_ids[:, None] == modality[None, :]).astype(jnp.int32)
    local_counts = jnp.sum(q_onehot, axis=0)
    before = prefix(
        local_counts, "pos", lambda earlier, later: earlier + later, jnp.zeros_like(local_counts)
    )
    within = jnp.cumsum(q_onehot, axis=0) - q_onehot
    ranked = jnp.sum((within + before[None, :]) * q_onehot, axis=1)
    limits = jnp.sum(q_onehot * query_counts[None, :], axis=1)
    kept_rows = ranked < limits
    lookup = jnp.dot(q_onehot.astype(jnp.bfloat16), query_table, preferred_element_type=jnp.float32)
    queries = (
        (query_features.astype(jnp.float32) + lookup)
        .astype(jnp.bfloat16)
        .reshape(tok_rows, local_heads, HEAD_DIM)
    )

    def fold_rows(running, key_rows, value_rows):
        running_max, running_tot, running_acc = running
        key_heads = key_rows.reshape(key_rows.shape[0], local_heads, HEAD_DIM)
        value_heads = value_rows.reshape(value_rows.shape[0], local_heads, HEAD_DIM)
        scores = (
            jnp.einsum("tha,rha->htr", queries, key_heads, preferred_element_type=jnp.float32)
            * score_scale
        )
        new_max = jnp.maximum(running_max, jnp.max(scores, axis=2))
        fade = jnp.exp(running_max - new_max)
        weights = jnp.exp(scores - new_max[:, :, None])
        new_tot = running_tot * fade + jnp.sum(weights, axis=2)
        new_acc = running_acc * fade[:, :, None] + jnp.einsum(
            "htr,rha->hta",
            weights.astype(jnp.bfloat16),
            value_heads,
            preferred_element_type=jnp.float32,
        )
        return (new_max, new_tot, new_acc)

    start_state = (
        jnp.full((local_heads, tok_rows), -jnp.inf, jnp.float32),
        jnp.zeros((local_heads, tok_rows), jnp.float32),
        jnp.zeros((local_heads, tok_rows, HEAD_DIM), jnp.float32),
    )
    running = start_state
    pieces = (
        lax.all_gather(latent_keys, "pos", axis=0, tiled=True),
        lax.all_gather(latent_values, "pos", axis=0, tiled=True),
    )
    row_count = pieces[0].shape[0]
    key_blocks = pieces[0].reshape(row_count // 512, 512, half_width)
    value_blocks = pieces[1].reshape(row_count // 512, 512, half_width)

    def scan_step(state, pair):
        return (fold_rows(state, pair[0], pair[1]), None)

    running, ignored = lax.scan(scan_step, running, (key_blocks, value_blocks))
    final_max, final_tot, final_acc = running
    dec_heads = final_acc / final_tot[:, :, None]
    dec_rows = jnp.transpose(dec_heads, (1, 0, 2)).reshape(tok_rows, half_width)
    decoded = jnp.where(kept_rows[:, None], dec_rows, 0.0)
    return (own_cols, decoded)


LANES = 128
EXTRA = 16
BIG = 56
LOG2E = 1.4426950408889634
EXP2_SCALE = LOG2E * HEAD_DIM**-0.5
NT = (((1,), (1,)), ((), ()))


def params(mib):
    return pltpu.CompilerParams(vmem_limit_bytes=mib << 20)


def cost(flops, nbytes, exps=0):
    return pl.CostEstimate(flops=int(flops), bytes_accessed=int(nbytes), transcendentals=int(exps))


def whole(shape):
    return pl.BlockSpec(shape, lambda *args: (0,) * len(shape))


def encode_kernel(ids_ref, q_ref, k_ref, v_ref, extra_ref, near_ref, bias_ref, out_ref):
    rows, width = q_ref.shape
    tokens = k_ref.shape[0]
    heads = width // HEAD_DIM
    ones = jnp.ones((tokens, LANES), jnp.bfloat16)
    kinds = [
        extra_ref[...].astype(jnp.float32)[:1, :tokens],
        near_ref[tokens:, :].astype(jnp.float32)[:1, :tokens],
    ]
    lane = lax.broadcasted_iota(jnp.int32, (rows, LANES), 1)
    lse_all = jnp.zeros((rows, LANES), jnp.float32)
    for h in range(heads):
        cols = slice(h * HEAD_DIM, (h + 1) * HEAD_DIM)
        late = slice(width + h * HEAD_DIM, width + (h + 1) * HEAD_DIM)
        pairs = [
            (k_ref[:, cols], v_ref[:, cols]),
            (near_ref[:tokens, cols], near_ref[:tokens, late]),
        ]
        top = acc = None
        for (keys, values), kind in zip(pairs, kinds):
            bias = jnp.zeros_like(kind)
            for m in range(bias_ref.shape[0]):
                bias = jnp.where(kind == m, bias_ref[m, h] * LOG2E, bias)
            scores = lax.dot_general(q_ref[:, cols], keys, NT, preferred_element_type=jnp.float32)
            scores = scores * EXP2_SCALE + bias
            new_top = jnp.max(scores, axis=1, keepdims=True)
            if top is not None:
                new_top = jnp.maximum(top, new_top)
            weights = jnp.exp2(scores - new_top).astype(jnp.bfloat16)
            summed = jnp.dot(
                weights, jnp.concatenate([values, ones], axis=1), preferred_element_type=jnp.float32
            )
            if top is not None:
                summed = summed + acc * jnp.exp2(top - new_top)
            top, acc = new_top, summed
        totals = acc[:, HEAD_DIM:]
        out_ref[:rows, cols] = (acc[:, :HEAD_DIM] / totals).astype(jnp.bfloat16)
        lse_all = jnp.where(lane % heads == h, top + jnp.log2(totals), lse_all)
    lse = lse_all.T[:EXTRA, :]
    high = lse.astype(jnp.bfloat16).astype(jnp.float32)
    mid = (lse - high).astype(jnp.bfloat16).astype(jnp.float32)
    low = lse - high - mid
    row = lax.broadcasted_iota(jnp.int32, lse.shape, 0)
    terms = jnp.where(row < heads, high, jnp.where(row < 2 * heads, mid, low))
    out_ref[rows:, :] = terms.astype(jnp.bfloat16)


def encode(which, queries, keys, values, extra, near, bias, rows):
    tokens = keys.shape[0]
    width = keys.shape[1] // 2
    blocks = queries.shape[0] // rows
    half = pl.BlockSpec((tokens, width), lambda i, ids: (0, ids[0]))
    grid_spec = pltpu.PrefetchScalarGridSpec(
        num_scalar_prefetch=1,
        grid=(blocks,),
        in_specs=[
            pl.BlockSpec((rows, width), lambda i, ids: (i, ids[0])),
            half,
            half,
            whole(extra.shape),
            whole(near.shape),
            pl.BlockSpec(memory_space=pltpu.SMEM),
        ],
        out_specs=pl.BlockSpec((rows + EXTRA, width), lambda i, ids: (i, 0)),
    )
    return pl.pallas_call(
        encode_kernel,
        grid_spec=grid_spec,
        out_shape=jax.ShapeDtypeStruct((blocks * (rows + EXTRA), width), jnp.bfloat16),
        compiler_params=params(BIG),
        cost_estimate=cost(
            16 * blocks * rows * tokens * width, 8 * tokens * width, blocks * rows * tokens * 8
        ),
        name="encode_rows",
    )(which.reshape(1), queries, keys, values, extra, near, bias)


def merge_kernel(count, ids_ref, parts_ref, mine_ref, near_ref, all_ref):
    rows, width = all_ref.shape
    long = rows + EXTRA
    parts = [parts_ref.at[i * long : (i + 1) * long, :] for i in range(count)]
    heads = width // HEAD_DIM
    stats = [v[rows:, :].astype(jnp.float32).T for v in parts]
    for h in range(heads):
        cols = slice(h * HEAD_DIM, (h + 1) * HEAD_DIM)
        lses = [
            s[:, h : h + 1] + s[:, heads + h : heads + h + 1] + s[:, 2 * heads + h : 2 * heads + h + 1]
            for s in stats
        ]
        top = functools.reduce(jnp.maximum, lses)
        factors = [jnp.exp2(v - top) for v in lses]
        inverse = 1.0 / functools.reduce(jnp.add, factors)
        merged = functools.reduce(
            jnp.add,
            [v[:rows, cols].astype(jnp.float32) * (f * inverse) for v, f in zip(parts, factors)],
        )
        all_ref[:, cols] = merged.astype(jnp.bfloat16)
    own = rows // 2
    mine_ref[...] = all_ref[pl.ds(pl.multiple_of(ids_ref[0] * own, own), own), :]
    near_ref[...] = all_ref[pl.ds(pl.multiple_of((1 - ids_ref[0]) * own, own), own), :]


def merge(which, parts, count):
    long, width = parts.shape[0] // count, parts.shape[1]
    rows = long - EXTRA
    grid_spec = pltpu.PrefetchScalarGridSpec(
        num_scalar_prefetch=1,
        grid=(1,),
        in_specs=[whole(parts.shape)],
        out_specs=[whole((rows // 2, width))] * 2,
        scratch_shapes=[pltpu.VMEM((rows, width), jnp.bfloat16)],
    )
    return pl.pallas_call(
        functools.partial(merge_kernel, count),
        grid_spec=grid_spec,
        out_shape=[jax.ShapeDtypeStruct((rows // 2, width), jnp.bfloat16)] * 2,
        compiler_params=params(32),
        cost_estimate=cost(8 * rows * width, 10 * rows * width),
        name="merge_rows",
    )(which.reshape(1), parts)


def project_kernel(far, ids_ref, mine_ref, near_ref, *refs):
    w_ref, far_ref, far_other_ref, near_w_ref, near_other_ref, out_ref, att_ref = refs
    part = mine_ref.shape[1]
    first = ids_ref[2 * far]
    att_ref[:, pl.ds(pl.multiple_of(first * part, part), part)] = mine_ref[...]
    att_ref[:, pl.ds(pl.multiple_of((1 - first) * part, part), part)] = near_ref[...]
    cols = w_ref.shape[1]
    depth = att_ref.shape[1] // 2
    share = ids_ref[2 * far + 1]
    halves = [
        att_ref[:, pl.ds(pl.multiple_of(v * depth, depth), depth)] for v in (share, 1 - share)
    ]

    def place(slot, value):
        out_ref[:, pl.ds(pl.multiple_of(ids_ref[slot] * cols, cols), cols)] = value

    for slot, own_ref in ((0, w_ref), (far, near_w_ref)):
        own = own_ref[: 2 * depth, :]
        place(slot, jnp.dot(att_ref[...], own, preferred_element_type=jnp.float32))
    for k in range(far - 1):
        start = k * (depth + EXTRA)
        band = slice(start, start + depth)
        near_band = slice(start + 2 * depth + EXTRA, start + 3 * depth + EXTRA)
        for slot, weights in (
            (1 + k, (far_ref[band, :], far_other_ref[band, :])),
            (far + 1 + k, (near_w_ref[near_band, :], near_other_ref[band, :])),
        ):
            terms = [
                jnp.dot(v, w, preferred_element_type=jnp.float32) for v, w in zip(halves, weights)
            ]
            place(slot, terms[0] + terms[1])


def project(ids, mine, near, weights):
    rows, part = mine.shape
    far = (ids.shape[0] - 2) // 2
    out_cols = 2 * far * weights[0].shape[1]
    grid_spec = pltpu.PrefetchScalarGridSpec(
        num_scalar_prefetch=1,
        grid=(1,),
        in_specs=[whole(v.shape) for v in (mine, near, *weights)],
        out_specs=whole((rows, out_cols)),
        scratch_shapes=[pltpu.VMEM((rows, 2 * part), jnp.bfloat16)],
    )
    return pl.pallas_call(
        functools.partial(project_kernel, far),
        grid_spec=grid_spec,
        out_shape=jax.ShapeDtypeStruct((rows, out_cols), jnp.float32),
        compiler_params=params(BIG),
        cost_estimate=cost(4 * rows * part * out_cols, 4 * part * out_cols + 4 * rows * out_cols),
        name="project_rows",
    )(ids, mine, near, *weights)


def norm_kernel(
    ids_ref, mine_ref, theirs_ref, latent_ref, gain_ref, out_ref, normed_ref, other_ref, full_ref
):
    updated = latent_ref[...].astype(jnp.float32) + (mine_ref[...] + theirs_ref[...])
    mean_square = jnp.mean(updated * updated, axis=1, keepdims=True)
    full_ref[...] = updated * lax.rsqrt(mean_square + norm_eps) * gain_ref[...]
    half = out_ref.shape[1]
    own = full_ref[:, pl.ds(pl.multiple_of(ids_ref[0] * half, half), half)]
    out_ref[...] = own
    normed_ref[...] = own.astype(jnp.bfloat16)
    other = full_ref[:, pl.ds(pl.multiple_of((1 - ids_ref[0]) * half, half), half)]
    other_ref[...] = other.astype(jnp.bfloat16)


def normalise(place, mine, theirs, latent_array, gain):
    rows, width = mine.shape
    half = width // 2
    grid_spec = pltpu.PrefetchScalarGridSpec(
        num_scalar_prefetch=1,
        grid=(1,),
        in_specs=[whole((rows, width))] * 3 + [whole((1, width))],
        out_specs=[whole((rows, half))] * 3,
        scratch_shapes=[pltpu.VMEM((rows, width), jnp.float32)],
    )
    return pl.pallas_call(
        norm_kernel,
        grid_spec=grid_spec,
        out_shape=[
            jax.ShapeDtypeStruct((rows, half), jnp.float32),
            jax.ShapeDtypeStruct((rows, half), jnp.bfloat16),
            jax.ShapeDtypeStruct((rows, half), jnp.bfloat16),
        ],
        compiler_params=params(BIG),
        cost_estimate=cost(6 * rows * width, 13 * rows * width),
        name="norm_rows",
    )(place.reshape(1), mine, theirs, latent_array, gain)


def latents_kernel(pieces, ids_ref, *refs):
    mine, theirs = refs[:pieces], refs[pieces : 2 * pieces]
    w_refs, (out_ref, normed_ref, w_ref) = refs[2 * pieces : -3], refs[-3:]
    rows, half = mine[0].shape
    slots = ids_ref.shape[0] - 1
    depth = 2 * half // slots

    @pl.when(pl.program_id(0) == 0)
    def arrange():
        for j in range(slots):
            at = ids_ref[1 + j]
            start = pl.multiple_of((at % (slots // 2)) * depth, depth)

            def copy(pieces):
                for r, piece in enumerate(pieces):
                    normed_ref[r * rows : (r + 1) * rows, j * depth : (j + 1) * depth] = piece[
                        :, pl.ds(start, depth)
                    ]

            is_mine = at // (slots // 2) == ids_ref[0]
            pl.when(is_mine)(functools.partial(copy, mine))
            pl.when(jnp.logical_not(is_mine))(functools.partial(copy, theirs))

    start, block = 0, w_ref.shape[1]
    for band in w_refs:
        columns = pl.ds(pl.multiple_of(pl.program_id(0) * block, block), block)
        w_ref[start : start + band.shape[0], :] = band[:, columns]
        start += band.shape[0]
    out_ref[...] = jnp.dot(
        normed_ref[...], w_ref[...], preferred_element_type=jnp.float32
    ).astype(jnp.bfloat16)


def latent_keys_values(ids, mine, theirs, bands):
    pieces = len(mine)
    rows, half = mine[0].shape
    width = bands[0].shape[1]
    block = min(512, width)
    total = sum(band.shape[0] for band in bands)
    grid_spec = pltpu.PrefetchScalarGridSpec(
        num_scalar_prefetch=1,
        grid=(width // block,),
        in_specs=[pl.BlockSpec(memory_space=pltpu.VMEM)] * (2 * pieces + len(bands)),
        out_specs=pl.BlockSpec((rows * pieces, block), lambda i, ids: (0, i)),
        scratch_shapes=[
            pltpu.VMEM((rows * pieces, total), jnp.bfloat16),
            pltpu.VMEM((total, block), jnp.bfloat16),
        ],
    )
    return pl.pallas_call(
        functools.partial(latents_kernel, pieces),
        grid_spec=grid_spec,
        out_shape=jax.ShapeDtypeStruct((rows * pieces, width), jnp.bfloat16),
        compiler_params=params(24),
        cost_estimate=cost(2 * rows * pieces * total * width, 2 * total * width),
        name="latent_keys_values",
    )(ids, *mine, *theirs, *bands)


def row_chunks(lengths, size):
    chunks, open_chunk, room = [], [], size
    for i, length in enumerate(lengths):
        start = 0
        while start < length:
            take = min(room, length - start)
            open_chunk.append((i, start, start + take))
            start, room = start + take, room - take
            if room == 0:
                chunks.append(open_chunk)
                open_chunk, room = [], size
    return chunks + ([open_chunk] if open_chunk else [])


def decode_kernel(parts, q_ref, *refs):
    k_refs, v_refs, out_ref = refs[:parts], refs[parts : 2 * parts], refs[-1]

    def gathered(sources, chunk, cols):
        rows = [sources[i][start:stop, cols] for i, start, stop in chunk]
        return rows[0] if len(rows) == 1 else jnp.concatenate(rows)

    for h in range(q_ref.shape[1] // HEAD_DIM):
        cols = slice(h * HEAD_DIM, (h + 1) * HEAD_DIM)
        top = acc = None
        for chunk in row_chunks([k.shape[0] for k in k_refs], 512):
            keys, values = gathered(k_refs, chunk, cols), gathered(v_refs, chunk, cols)
            scores = lax.dot_general(q_ref[:, cols], keys, NT, preferred_element_type=jnp.float32)
            scores = scores * EXP2_SCALE
            new_top = jnp.max(scores, axis=1, keepdims=True)
            if top is not None:
                new_top = jnp.maximum(top, new_top)
            weights = jnp.exp2(scores - new_top).astype(jnp.bfloat16)
            summed = jnp.dot(
                weights,
                jnp.concatenate([values, jnp.ones((keys.shape[0], LANES), jnp.bfloat16)], axis=1),
                preferred_element_type=jnp.float32,
            )
            if top is not None:
                summed = summed + acc * jnp.exp2(top - new_top)
            top, acc = new_top, summed
        out_ref[:, cols] = (acc[:, :HEAD_DIM] / acc[:, HEAD_DIM:]).astype(out_ref.dtype)


def decode(queries, keys_values, out_type):
    tokens, width = queries.shape
    latents = sum(v.shape[0] for v in keys_values)
    pair = min(2 * HEAD_DIM, width)
    steps = width // pair
    narrow = pl.BlockSpec((tokens, pair), lambda i: (0, i))
    keys = [pl.BlockSpec((v.shape[0], pair), lambda i: (0, i)) for v in keys_values]
    values = [pl.BlockSpec((v.shape[0], pair), lambda i: (0, steps + i)) for v in keys_values]
    return pl.pallas_call(
        functools.partial(decode_kernel, len(keys_values)),
        grid=(steps,),
        in_specs=[narrow, *keys, *values],
        out_specs=narrow,
        out_shape=jax.ShapeDtypeStruct((tokens, width), out_type),
        compiler_params=params(BIG),
        cost_estimate=cost(
            16 * tokens * latents * width,
            4 * latents * width + 6 * tokens * width,
            tokens * latents * (width // HEAD_DIM),
        ),
        name="decode_rows",
    )(queries, *keys_values, *keys_values)


def swap_perm(size):
    return [(i, i ^ 1) for i in range(size)]


def shift_perm(size, k):
    far = size // 2
    return [(((z + k) % far) * 2 + y, z * 2 + y) for z in range(far) for y in range(2)]


def hop_perm(size, step, way):
    far = size // 2
    moves = [(z, z + 1) for z in range(step - 1, far - 1)]
    if way < 0:
        moves = [(far - 1 - a, far - 1 - b) for a, b in moves]
    return [(a * 2 + y, b * 2 + y) for a, b in moves for y in range(2)]


def fast_on_device(
    sizes,
    enc_keys,
    enc_values,
    input_ids,
    latent_queries,
    latent_array,
    w_out,
    norm_gain,
    w_key,
    w_value,
    query_features,
    query_ids,
    query_table,
    enc_bias,
    query_counts,
):
    groups, pos = sizes
    p = lax.axis_index("pos")
    place = lax.axis_index("head")
    rows = latent_array.shape[0]
    tokens, half_width = enc_keys.shape
    heads = half_width // HEAD_DIM
    mods = enc_bias.shape[0]
    modality = jnp.arange(mods, dtype=jnp.int32)
    far, z, y, x = pos // 2, p // 2, p % 2, lax.axis_index("groups") % 2
    near = swap_perm(pos)

    def over_groups(value):
        return lax.ppermute(value, "groups", swap_perm(groups))

    def over_near(value):
        return lax.ppermute(value, "pos", near)

    def over_far(value, k):
        return lax.ppermute(value, "pos", shift_perm(pos, k))

    def hop(step, pair):
        return [
            lax.ppermute(v, "pos", hop_perm(pos, step, way)) for v, way in zip(pair, (1, -1))
        ]

    def by_shift(hops, k):
        return jnp.where(z + k < far, hops[k][1], hops[far - k][0])

    q_onehot = (query_ids[:, None] == modality[None, :]).astype(jnp.int32)
    local_counts = jnp.sum(q_onehot, axis=0)

    def columns(arrays, which):
        part = half_width // 2
        return jnp.concatenate(
            [lax.dynamic_slice_in_dim(v, which * part, part, 1) for v in arrays], axis=1
        )

    extra = jnp.pad(input_ids[None, :], ((0, EXTRA - 1), (0, half_width - tokens)))
    extra = extra.astype(jnp.bfloat16)
    near_inputs = over_near(
        jnp.concatenate([columns((enc_keys, enc_values), 1 - y), extra], axis=0)
    )

    out_half, out_cols = w_out.shape[0] // 2, w_out.shape[1]
    counted = jnp.concatenate([local_counts // 16, local_counts % 16])
    counted = jnp.pad(counted[None, :], ((0, EXTRA - 1), (0, out_cols - 2 * mods)))
    counted = counted.astype(jnp.bfloat16)

    out_sent = jnp.concatenate(
        [lax.dynamic_slice_in_dim(w_out, x * out_half, out_half, 0), counted]
    )
    out_far = [over_far(out_sent, k) for k in range(1, far)]
    places = [((z + k) % far) * 2 + (y ^ j) for j in range(2) for k in range(far)]
    kv_for_near = columns((w_key, w_value), 1 - y)
    near_inputs, out_far, kv_for_near = lax.optimization_barrier(
        (near_inputs, out_far, kv_for_near)
    )
    out_far = jnp.concatenate(out_far)
    out_far_other = over_groups(out_far)

    kv_own = columns((w_key, w_value), y)
    kv_near = over_near(kv_for_near)

    head_bias = lax.dynamic_slice_in_dim(enc_bias, y * (heads // 2), heads // 2, 1)
    parts = encode(
        y, latent_queries, enc_keys, enc_values, extra, near_inputs, head_bias, 2 * rows
    )
    kv_near, out_far, parts = lax.optimization_barrier((kv_near, out_far, parts))
    kv_sent = jnp.where(x == 0, kv_own, kv_near)
    hops = {0: [kv_sent, kv_sent]}
    hops[1] = hop(1, hops[0])
    early = [k for k in range(1, far) if max(k, far - k) < 3]
    rest = [k for k in range(1, far) if k not in early]
    out_near = over_near(jnp.concatenate([w_out, counted, out_far]))
    out_near_other = over_groups(out_near[w_out.shape[0] + EXTRA :])
    columns_of_slice = [[2 * i + j for i in range(far)] for j in range(2)]
    parts = lax.all_to_all(parts, "pos", 0, 0, axis_index_groups=columns_of_slice, tiled=True)

    def kept_queries():
        far_counts = out_far.reshape(far - 1, out_half + EXTRA, out_cols)[:, out_half, : 2 * mods]
        near_counts = out_near.reshape(-1, EXTRA, out_cols)[:, 0, : 2 * mods]
        at = [w_out.shape[0] // EXTRA]
        at += [at[0] + k * (out_half // EXTRA + 1) for k in range(1, far)]
        near_counts = jnp.concatenate([near_counts[i : i + 1] for i in at])
        counts = jnp.concatenate([counted[:1, : 2 * mods], far_counts, near_counts])
        counts = counts.astype(jnp.int32)
        counts = counts[:, :mods] * 16 + counts[:, mods:]
        earlier = jnp.stack(places)[:, None] < p
        before = jnp.sum(jnp.where(earlier, counts, 0), axis=0)
        within = jnp.cumsum(q_onehot, axis=0) - q_onehot
        ranked = jnp.sum((within + before[None, :]) * q_onehot, axis=1)
        limits = jnp.sum(q_onehot * query_counts[None, :], axis=1)
        return ranked < limits

    lookup = jnp.dot(q_onehot.astype(jnp.bfloat16), query_table, preferred_element_type=jnp.float32)
    queries = (query_features.astype(jnp.float32) + lookup).astype(jnp.bfloat16)
    own_queries = columns((queries,), y)
    near_queries = over_near(columns((queries,), 1 - y))

    parts, out_near, out_far_other, out_near_other, hops, near_queries = lax.optimization_barrier(
        (parts, out_near, out_far_other, out_near_other, hops, near_queries)
    )
    attended, for_near = merge(y, parts, far)
    for_near, hops = lax.optimization_barrier((for_near, hops))
    hops[2] = hop(2, hops[1])
    from_near = over_near(for_near)
    kept = kept_queries()
    out_ids = jnp.stack([*places, y, x]).astype(jnp.int32)
    weights = [w_out, out_far, out_far_other, out_near, out_near_other]
    partial_value = project(out_ids, attended, from_near, weights)
    partial_value, hops = lax.optimization_barrier((partial_value, hops))
    kv_bands = [kv_own, kv_near]
    for k in early:
        kv_moved = by_shift(hops, k)
        kv_bands += [kv_moved, over_groups(kv_moved)]
    for step in range(3, far):
        hops[step] = hop(step, hops[step - 1])
    theirs = lax.ppermute(partial_value, "head", swap_perm(2))
    own_cols, normed, normed_other = normalise(
        place, partial_value, theirs, latent_array, norm_gain[None, :]
    )
    kv_at = [p, p ^ 1]
    for k in early + rest:
        kv_at += [((z + k) % far) * 2 + (y ^ other) for other in (x, 1 - x)]
    kv_ids = jnp.stack([place, *kv_at]).astype(jnp.int32)

    def cores(values):
        return [lax.ppermute(v, "head", swap_perm(2)) for v in values]

    def fold(mine, other):
        return latent_keys_values(kv_ids, mine, other, kv_bands)

    def arrival(hops, j):
        picked = None
        for at in range(far):
            came = [
                (step, way)
                for step in range(1, far)
                for way in (1, 0)
                if (at + step < far if way else at >= step)
            ]
            step, way = came[j - 1]
            value = hops[step][way]
            picked = value if picked is None else jnp.where(z == at, value, picked)
        return picked

    came = {0: [normed, normed]}
    came[1] = hop(1, came[0])
    normed_near = over_near(normed)
    came, hops, kv_bands, kept = lax.optimization_barrier((came, hops, kv_bands, kept))
    mine, other, keys_values = [normed, normed_near], [normed_other], []
    for step in range(1, far):
        fresh = arrival(came, step)
        fresh_near = over_near(fresh)
        if step + 1 < far:
            came[step + 1] = hop(step + 1, came[step])
            k = rest[step - 1]
            kv_moved = by_shift(hops, k)
            kv_bands += [kv_moved, over_groups(kv_moved)]
            if step > 1:
                keys_values.append(fold(mine, other))
                mine, other = [], []
            came, mine, other, kv_bands, keys_values, fresh, fresh_near = (
                lax.optimization_barrier(
                    (came, mine, other, kv_bands, keys_values, fresh, fresh_near)
                )
            )
            if step == 1:
                mine += [fresh, fresh_near]
                other += cores(mine[1:])
            else:
                mine += [fresh, fresh_near]
                other += cores([fresh, fresh_near])
    keys_values.append(fold([*mine, fresh], [*other, *cores([fresh])]))
    fresh_near, keys_values = lax.optimization_barrier((fresh_near, keys_values))
    keys_values.append(fold([fresh_near], cores([fresh_near])))
    near_state = decode(near_queries, keys_values, jnp.bfloat16)
    own_state = decode(own_queries, keys_values, jnp.float32)
    from_near = lax.ppermute(near_state, "pos", near).astype(jnp.float32)
    decoded = jnp.where(
        y == 0,
        jnp.concatenate([own_state, from_near], axis=1),
        jnp.concatenate([from_near, own_state], axis=1),
    )
    decoded = jnp.where(kept[:, None], decoded, 0.0)
    return (own_cols, decoded)


def on_device(sizes, *args):
    groups, pos, head = sizes
    enc_keys, latent_array, w_out, w_key = args[0], args[4], args[5], args[7]
    fits = (
        head == 2
        and pos % 2 == 0
        and pos > 4
        and groups % 2 == 0
        and enc_keys.shape[1] % (4 * HEAD_DIM) == 0
        and 3 * enc_keys.shape[1] <= 2 * HEAD_DIM * EXTRA
        and enc_keys.shape[0] % LANES == 0
        and enc_keys.shape[0] <= enc_keys.shape[1]
        and w_key.shape[0] % LANES == 0
        and w_out.shape[0] % (2 * LANES) == 0
        and w_out.shape[1] % LANES == 0
        and latent_array.shape[0] % LANES == 0
    )
    if fits:
        return fast_on_device((groups, pos), *args)
    return plain_on_device(*args)


def solution(mesh):
    return jax.shard_map(
        functools.partial(on_device, tuple(mesh.shape[a] for a in ("groups", "pos", "head"))),
        mesh=mesh,
        in_specs=(
            P(("groups", "pos"), "head"),
            P(("groups", "pos"), "head"),
            P(("groups", "pos")),
            P("groups", "head"),
            P(("groups", "pos"), None),
            P("head", "pos"),
            P(),
            P("pos", "head"),
            P("pos", "head"),
            P(("groups", "pos"), "head"),
            P(("groups", "pos")),
            P(None, "head"),
            P(None, "head"),
            P("groups"),
        ),
        out_specs=(P(("groups", "pos"), "head"), P(("groups", "pos"), "head")),
        check_vma=False,
    )
```

```python
import functools

import jax
import jax.numpy as jnp
from jax import lax
from jax.experimental import pallas as pl
from jax.experimental.pallas import tpu as pltpu
from jax.sharding import PartitionSpec as P

HEAD_DIM = 128


norm_eps = 1e-06


def prefix(shard, axis, combine, identity):
    peers, place = (lax.axis_size(axis), lax.axis_index(axis))
    everything = lax.all_gather(shard, axis)
    start = jnp.broadcast_to(jnp.asarray(identity, shard.dtype), shard.shape)

    def step(k, before):
        reached = k < place
        new = combine(before, everything[k])
        return jnp.where(reached, new, before)

    return lax.fori_loop(0, peers, step, start)


def plain_on_device(
    enc_keys,
    enc_values,
    input_ids,
    latent_queries,
    latent_array,
    w_out,
    norm_gain,
    w_key,
    w_value,
    query_features,
    query_ids,
    query_table,
    enc_bias,
    query_counts,
):
    tok_rows = enc_keys.shape[0]
    half_width = enc_keys.shape[1]
    local_heads = half_width // HEAD_DIM
    score_scale = HEAD_DIM ** (-0.5)
    modality = jnp.arange(enc_bias.shape[0], dtype=jnp.int32)
    in_onehot = (input_ids[:, None] == modality[None, :]).astype(jnp.float32)
    bias_rows = jnp.dot(in_onehot, enc_bias, precision=lax.Precision.HIGHEST)
    bias_heads = bias_rows.T[:, None, :]
    keys_split = enc_keys.reshape(tok_rows, local_heads, HEAD_DIM)
    values_split = enc_values.reshape(tok_rows, local_heads, HEAD_DIM)
    lat_total = latent_queries.shape[0]
    block_rows = min(512, lat_total)
    query_blocks = latent_queries.reshape(
        lat_total // block_rows, block_rows, local_heads, HEAD_DIM
    )

    def encode_block(block_queries):
        scores = (
            jnp.einsum(
                "nha,tha->hnt", block_queries, keys_split, preferred_element_type=jnp.float32
            )
            * score_scale
            + bias_heads
        )
        highest = jnp.max(scores, axis=2)
        weights = jnp.exp(scores - highest[:, :, None])
        totals = jnp.sum(weights, axis=2)
        summed = jnp.einsum(
            "hnt,tha->nha",
            weights.astype(jnp.bfloat16),
            values_split,
            preferred_element_type=jnp.float32,
        )
        return (highest.T, totals.T, summed.reshape(block_rows, half_width))

    block_max, block_tot, block_acc = lax.map(encode_block, query_blocks)
    row_highest = block_max.reshape(lat_total, local_heads)
    row_totals = block_tot.reshape(lat_total, local_heads)
    row_sums = block_acc.reshape(lat_total, half_width)
    own_rows = latent_array.shape[0]
    global_max = lax.pmax(row_highest, "pos")
    factor = jnp.exp(row_highest - global_max)
    scaled_sums = (row_sums.reshape(lat_total, local_heads, HEAD_DIM) * factor[:, :, None]).reshape(
        lat_total, half_width
    )
    totals, summed = (
        lax.psum_scatter(row_totals * factor, "pos", scatter_dimension=0, tiled=True),
        lax.psum_scatter(scaled_sums, "pos", scatter_dimension=0, tiled=True),
    )
    summed = summed.reshape(own_rows, local_heads, HEAD_DIM)
    attended = (summed / totals[:, :, None]).reshape(own_rows, half_width).astype(jnp.bfloat16)
    partial_value = jnp.dot(
        attended,
        lax.all_gather(w_out, "pos", axis=1, tiled=True),
        preferred_element_type=jnp.float32,
    )
    offset = lax.axis_index("head") * half_width
    projected = lax.psum(partial_value, "head")
    updated = latent_array.astype(jnp.float32) + projected
    mean_square = jnp.mean(updated * updated, axis=1, keepdims=True)
    normed_full = updated * lax.rsqrt(mean_square + norm_eps) * norm_gain
    normed = normed_full.astype(jnp.bfloat16)
    own_cols = lax.dynamic_slice_in_dim(normed_full, offset, half_width, 1)
    pieces = (
        lax.all_gather(w_key, "pos", axis=0, tiled=True),
        lax.all_gather(w_value, "pos", axis=0, tiled=True),
    )
    key_sum = jnp.dot(normed, pieces[0], preferred_element_type=jnp.float32)
    value_sum = jnp.dot(normed, pieces[1], preferred_element_type=jnp.float32)
    latent_keys = key_sum.astype(jnp.bfloat16)
    latent_values = value_sum.astype(jnp.bfloat16)
    q_onehot = (query_ids[:, None] == modality[None, :]).astype(jnp.int32)
    local_counts = jnp.sum(q_onehot, axis=0)
    before = prefix(
        local_counts, "pos", lambda earlier, later: earlier + later, jnp.zeros_like(local_counts)
    )
    within = jnp.cumsum(q_onehot, axis=0) - q_onehot
    ranked = jnp.sum((within + before[None, :]) * q_onehot, axis=1)
    limits = jnp.sum(q_onehot * query_counts[None, :], axis=1)
    kept_rows = ranked < limits
    lookup = jnp.dot(q_onehot.astype(jnp.bfloat16), query_table, preferred_element_type=jnp.float32)
    queries = (
        (query_features.astype(jnp.float32) + lookup)
        .astype(jnp.bfloat16)
        .reshape(tok_rows, local_heads, HEAD_DIM)
    )

    def fold_rows(running, key_rows, value_rows):
        running_max, running_tot, running_acc = running
        key_heads = key_rows.reshape(key_rows.shape[0], local_heads, HEAD_DIM)
        value_heads = value_rows.reshape(value_rows.shape[0], local_heads, HEAD_DIM)
        scores = (
            jnp.einsum("tha,rha->htr", queries, key_heads, preferred_element_type=jnp.float32)
            * score_scale
        )
        new_max = jnp.maximum(running_max, jnp.max(scores, axis=2))
        fade = jnp.exp(running_max - new_max)
        weights = jnp.exp(scores - new_max[:, :, None])
        new_tot = running_tot * fade + jnp.sum(weights, axis=2)
        new_acc = running_acc * fade[:, :, None] + jnp.einsum(
            "htr,rha->hta",
            weights.astype(jnp.bfloat16),
            value_heads,
            preferred_element_type=jnp.float32,
        )
        return (new_max, new_tot, new_acc)

    start_state = (
        jnp.full((local_heads, tok_rows), -jnp.inf, jnp.float32),
        jnp.zeros((local_heads, tok_rows), jnp.float32),
        jnp.zeros((local_heads, tok_rows, HEAD_DIM), jnp.float32),
    )
    running = start_state
    pieces = (
        lax.all_gather(latent_keys, "pos", axis=0, tiled=True),
        lax.all_gather(latent_values, "pos", axis=0, tiled=True),
    )
    row_count = pieces[0].shape[0]
    key_blocks = pieces[0].reshape(row_count // 512, 512, half_width)
    value_blocks = pieces[1].reshape(row_count // 512, 512, half_width)

    def scan_step(state, pair):
        return (fold_rows(state, pair[0], pair[1]), None)

    running, ignored = lax.scan(scan_step, running, (key_blocks, value_blocks))
    final_max, final_tot, final_acc = running
    dec_heads = final_acc / final_tot[:, :, None]
    dec_rows = jnp.transpose(dec_heads, (1, 0, 2)).reshape(tok_rows, half_width)
    decoded = jnp.where(kept_rows[:, None], dec_rows, 0.0)
    return (own_cols, decoded)


LANES = 128
EXTRA = 16
BIG = 56
LOG2E = 1.4426950408889634
EXP2_SCALE = LOG2E * HEAD_DIM**-0.5
NT = (((1,), (1,)), ((), ()))


def params(mib):
    return pltpu.CompilerParams(vmem_limit_bytes=mib << 20)


def cost(flops, nbytes, exps=0):
    return pl.CostEstimate(flops=int(flops), bytes_accessed=int(nbytes), transcendentals=int(exps))


def whole(shape):
    return pl.BlockSpec(shape, lambda *args: (0,) * len(shape))


def stats_of(ref, heads):
    long = ref.shape[0]
    terms = ref[long - EXTRA : long, :].astype(jnp.float32).T
    return [
        terms[:, h : h + 1] + terms[:, heads + h : heads + h + 1] + terms[:, 2 * heads + h : 2 * heads + h + 1]
        for h in range(heads)
    ]


def encode_kernel(count, ids_ref, q_ref, k_ref, v_ref, extra_ref, bias_ref, *refs):
    out_ref = refs[-1]
    rows, width = q_ref.shape
    tokens = k_ref.shape[0]
    heads = width // HEAD_DIM
    ones = jnp.ones((tokens, LANES), jnp.bfloat16)
    kind = extra_ref[...].astype(jnp.float32)[:1, :tokens]
    lane = lax.broadcasted_iota(jnp.int32, (rows, LANES), 1)
    lse_all = jnp.zeros((rows, LANES), jnp.float32)
    earlier = stats_of(refs[0], heads) if len(refs) > 1 else None
    for h in range(heads):
        cols = slice(h * HEAD_DIM, (h + 1) * HEAD_DIM)
        bias = jnp.zeros_like(kind)
        for m in range(count):
            bias = jnp.where(kind == m, bias_ref[m, h] * LOG2E, bias)
        scores = lax.dot_general(
            q_ref[:, cols], k_ref[:, cols], NT, preferred_element_type=jnp.float32
        )
        scores = scores * EXP2_SCALE + bias
        top = jnp.max(scores, axis=1, keepdims=True)
        if earlier is not None:
            top = jnp.maximum(top, earlier[h])
        weights = jnp.exp2(scores - top).astype(jnp.bfloat16)
        acc = jnp.dot(
            weights,
            jnp.concatenate([v_ref[:, cols], ones], axis=1),
            preferred_element_type=jnp.float32,
        )
        summed, totals = acc[:, :HEAD_DIM], acc[:, HEAD_DIM:]
        if earlier is not None:
            fade = jnp.exp2(earlier[h] - top)
            summed = summed + refs[0][:rows, cols].astype(jnp.float32) * fade
            totals = totals + fade
        out_ref[:rows, cols] = (summed / totals).astype(jnp.bfloat16)
        lse_all = jnp.where(lane % heads == h, top + jnp.log2(totals), lse_all)
    lse = lse_all.T[:EXTRA, :]
    high = lse.astype(jnp.bfloat16).astype(jnp.float32)
    mid = (lse - high).astype(jnp.bfloat16).astype(jnp.float32)
    low = lse - high - mid
    row = lax.broadcasted_iota(jnp.int32, lse.shape, 0)
    terms = jnp.where(row < heads, high, jnp.where(row < 2 * heads, mid, low))
    out_ref[rows:, :] = terms.astype(jnp.bfloat16)


def encode(which, queries, keys, values, extra, bias, rows, earlier=None):
    tokens = extra.shape[1] // 2
    width = queries.shape[1] // 2
    blocks = queries.shape[0] // rows
    packed = pl.BlockSpec((rows + EXTRA, width), lambda i, ids: (i, 0))
    grid_spec = pltpu.PrefetchScalarGridSpec(
        num_scalar_prefetch=1,
        grid=(blocks,),
        in_specs=[
            pl.BlockSpec((rows, width), lambda i, ids: (i, ids[0])),
            pl.BlockSpec((tokens, width), lambda i, ids: (0, ids[1])),
            pl.BlockSpec((tokens, width), lambda i, ids: (0, ids[2])),
            pl.BlockSpec((EXTRA, extra.shape[1]), lambda i, ids: (ids[3], 0)),
            pl.BlockSpec(memory_space=pltpu.SMEM),
            *([] if earlier is None else [packed]),
        ],
        out_specs=packed,
    )
    return pl.pallas_call(
        functools.partial(encode_kernel, bias.shape[0]),
        grid_spec=grid_spec,
        out_shape=jax.ShapeDtypeStruct((blocks * (rows + EXTRA), width), jnp.bfloat16),
        compiler_params=params(BIG),
        cost_estimate=cost(
            8 * blocks * rows * tokens * width, 8 * tokens * width, blocks * rows * tokens * 4
        ),
        name="encode_rows",
    )(which, queries, keys, values, extra, bias, *([] if earlier is None else [earlier]))


def merge_kernel(count, ids_ref, parts_ref, mine_ref, near_ref, all_ref):
    rows, width = all_ref.shape
    long = rows + EXTRA
    parts = [parts_ref.at[i * long : (i + 1) * long, :] for i in range(count)]
    heads = width // HEAD_DIM
    stats = [stats_of(v, heads) for v in parts]
    for h in range(heads):
        cols = slice(h * HEAD_DIM, (h + 1) * HEAD_DIM)
        lses = [s[h] for s in stats]
        top = functools.reduce(jnp.maximum, lses)
        factors = [jnp.exp2(v - top) for v in lses]
        inverse = 1.0 / functools.reduce(jnp.add, factors)
        merged = functools.reduce(
            jnp.add,
            [v[:rows, cols].astype(jnp.float32) * (f * inverse) for v, f in zip(parts, factors)],
        )
        all_ref[:, cols] = merged.astype(jnp.bfloat16)
    own = rows // 2
    mine_ref[...] = all_ref[pl.ds(pl.multiple_of(ids_ref[0] * own, own), own), :]
    near_ref[...] = all_ref[pl.ds(pl.multiple_of((1 - ids_ref[0]) * own, own), own), :]


def merge(which, parts, count):
    long, width = parts.shape[0] // count, parts.shape[1]
    rows = long - EXTRA
    grid_spec = pltpu.PrefetchScalarGridSpec(
        num_scalar_prefetch=1,
        grid=(1,),
        in_specs=[whole(parts.shape)],
        out_specs=[whole((rows // 2, width))] * 2,
        scratch_shapes=[pltpu.VMEM((rows, width), jnp.bfloat16)],
    )
    return pl.pallas_call(
        functools.partial(merge_kernel, count),
        grid_spec=grid_spec,
        out_shape=[jax.ShapeDtypeStruct((rows // 2, width), jnp.bfloat16)] * 2,
        compiler_params=params(32),
        cost_estimate=cost(8 * rows * width, 10 * rows * width),
        name="merge_rows",
    )(which.reshape(1), parts)


def project_kernel(far, ids_ref, mine_ref, near_ref, *refs):
    w_ref, far_ref, far_other_ref, near_w_ref, near_other_ref, out_ref, att_ref = refs
    part = mine_ref.shape[1]
    first = ids_ref[2 * far]
    att_ref[:, pl.ds(pl.multiple_of(first * part, part), part)] = mine_ref[...]
    att_ref[:, pl.ds(pl.multiple_of((1 - first) * part, part), part)] = near_ref[...]
    cols = w_ref.shape[1]
    depth = att_ref.shape[1] // 2
    share = ids_ref[2 * far + 1]
    halves = [
        att_ref[:, pl.ds(pl.multiple_of(v * depth, depth), depth)] for v in (share, 1 - share)
    ]

    def place(slot, value):
        out_ref[:, pl.ds(pl.multiple_of(ids_ref[slot] * cols, cols), cols)] = value

    for slot, own_ref in ((0, w_ref), (far, near_w_ref)):
        own = own_ref[: 2 * depth, :]
        place(slot, jnp.dot(att_ref[...], own, preferred_element_type=jnp.float32))
    for k in range(far - 1):
        start = k * (depth + EXTRA)
        band = slice(start, start + depth)
        near_band = slice(start + 2 * depth + EXTRA, start + 3 * depth + EXTRA)
        for slot, weights in (
            (1 + k, (far_ref[band, :], far_other_ref[band, :])),
            (far + 1 + k, (near_w_ref[near_band, :], near_other_ref[band, :])),
        ):
            terms = [
                jnp.dot(v, w, preferred_element_type=jnp.float32) for v, w in zip(halves, weights)
            ]
            place(slot, terms[0] + terms[1])


def project(ids, mine, near, weights):
    rows, part = mine.shape
    far = (ids.shape[0] - 2) // 2
    out_cols = 2 * far * weights[0].shape[1]
    grid_spec = pltpu.PrefetchScalarGridSpec(
        num_scalar_prefetch=1,
        grid=(1,),
        in_specs=[whole(v.shape) for v in (mine, near, *weights)],
        out_specs=whole((rows, out_cols)),
        scratch_shapes=[pltpu.VMEM((rows, 2 * part), jnp.bfloat16)],
    )
    return pl.pallas_call(
        functools.partial(project_kernel, far),
        grid_spec=grid_spec,
        out_shape=jax.ShapeDtypeStruct((rows, out_cols), jnp.float32),
        compiler_params=params(BIG),
        cost_estimate=cost(4 * rows * part * out_cols, 4 * part * out_cols + 4 * rows * out_cols),
        name="project_rows",
    )(ids, mine, near, *weights)


def norm_kernel(
    ids_ref, mine_ref, theirs_ref, latent_ref, gain_ref, out_ref, normed_ref, other_ref, full_ref
):
    updated = latent_ref[...].astype(jnp.float32) + (mine_ref[...] + theirs_ref[...])
    mean_square = jnp.mean(updated * updated, axis=1, keepdims=True)
    full_ref[...] = updated * lax.rsqrt(mean_square + norm_eps) * gain_ref[...]
    half = out_ref.shape[1]
    own = full_ref[:, pl.ds(pl.multiple_of(ids_ref[0] * half, half), half)]
    out_ref[...] = own
    normed_ref[...] = own.astype(jnp.bfloat16)
    other = full_ref[:, pl.ds(pl.multiple_of((1 - ids_ref[0]) * half, half), half)]
    other_ref[...] = other.astype(jnp.bfloat16)


def normalise(place, mine, theirs, latent_array, gain):
    rows, width = mine.shape
    half = width // 2
    grid_spec = pltpu.PrefetchScalarGridSpec(
        num_scalar_prefetch=1,
        grid=(1,),
        in_specs=[whole((rows, width))] * 3 + [whole((1, width))],
        out_specs=[whole((rows, half))] * 3,
        scratch_shapes=[pltpu.VMEM((rows, width), jnp.float32)],
    )
    return pl.pallas_call(
        norm_kernel,
        grid_spec=grid_spec,
        out_shape=[
            jax.ShapeDtypeStruct((rows, half), jnp.float32),
            jax.ShapeDtypeStruct((rows, half), jnp.bfloat16),
            jax.ShapeDtypeStruct((rows, half), jnp.bfloat16),
        ],
        compiler_params=params(BIG),
        cost_estimate=cost(6 * rows * width, 13 * rows * width),
        name="norm_rows",
    )(place.reshape(1), mine, theirs, latent_array, gain)


def latents_kernel(pieces, ids_ref, *refs):
    mine, theirs = refs[:pieces], refs[pieces : 2 * pieces]
    w_refs, (out_ref, normed_ref, w_ref) = refs[2 * pieces : -3], refs[-3:]
    half = mine[0].shape[1]
    slots = ids_ref.shape[0] - 1
    depth = 2 * half // slots

    @pl.when(pl.program_id(0) == 0)
    def arrange():
        for j in range(slots):
            at = ids_ref[1 + j]
            start = pl.multiple_of((at % (slots // 2)) * depth, depth)

            def copy(pieces):
                row = 0
                for piece in pieces:
                    band = slice(row, row + piece.shape[0])
                    row += piece.shape[0]
                    normed_ref[band, j * depth : (j + 1) * depth] = piece[:, pl.ds(start, depth)]

            is_mine = at // (slots // 2) == ids_ref[0]
            pl.when(is_mine)(functools.partial(copy, mine))
            pl.when(jnp.logical_not(is_mine))(functools.partial(copy, theirs))

    start, block = 0, w_ref.shape[1]
    for band in w_refs:
        columns = pl.ds(pl.multiple_of(pl.program_id(0) * block, block), block)
        w_ref[start : start + band.shape[0], :] = band[:, columns]
        start += band.shape[0]
    out_ref[...] = jnp.dot(
        normed_ref[...], w_ref[...], preferred_element_type=jnp.float32
    ).astype(jnp.bfloat16)


def latent_keys_values(ids, mine, theirs, bands):
    pieces = len(mine)
    rows = sum(v.shape[0] for v in mine)
    width = bands[0].shape[1]
    block = min(512, width)
    total = sum(band.shape[0] for band in bands)
    grid_spec = pltpu.PrefetchScalarGridSpec(
        num_scalar_prefetch=1,
        grid=(width // block,),
        in_specs=[pl.BlockSpec(memory_space=pltpu.VMEM)] * (2 * pieces + len(bands)),
        out_specs=pl.BlockSpec((rows, block), lambda i, ids: (0, i)),
        scratch_shapes=[
            pltpu.VMEM((rows, total), jnp.bfloat16),
            pltpu.VMEM((total, block), jnp.bfloat16),
        ],
    )
    return pl.pallas_call(
        functools.partial(latents_kernel, pieces),
        grid_spec=grid_spec,
        out_shape=jax.ShapeDtypeStruct((rows, width), jnp.bfloat16),
        compiler_params=params(24),
        cost_estimate=cost(2 * rows * total * width, 2 * total * width),
        name="latent_keys_values",
    )(ids, *mine, *theirs, *bands)


def row_chunks(lengths, size):
    chunks, open_chunk, room = [], [], size
    for i, length in enumerate(lengths):
        start = 0
        while start < length:
            take = min(room, length - start)
            open_chunk.append((i, start, start + take))
            start, room = start + take, room - take
            if room == 0:
                chunks.append(open_chunk)
                open_chunk, room = [], size
    return chunks + ([open_chunk] if open_chunk else [])


def decode_kernel(parts, q_ref, *refs):
    k_refs, v_refs, out_ref = refs[:parts], refs[parts : 2 * parts], refs[-1]

    def gathered(sources, chunk, cols):
        rows = [sources[i][start:stop, cols] for i, start, stop in chunk]
        return rows[0] if len(rows) == 1 else jnp.concatenate(rows)

    for h in range(q_ref.shape[1] // HEAD_DIM):
        cols = slice(h * HEAD_DIM, (h + 1) * HEAD_DIM)
        top = acc = None
        for chunk in row_chunks([k.shape[0] for k in k_refs], 512):
            keys, values = gathered(k_refs, chunk, cols), gathered(v_refs, chunk, cols)
            scores = lax.dot_general(q_ref[:, cols], keys, NT, preferred_element_type=jnp.float32)
            scores = scores * EXP2_SCALE
            new_top = jnp.max(scores, axis=1, keepdims=True)
            if top is not None:
                new_top = jnp.maximum(top, new_top)
            weights = jnp.exp2(scores - new_top).astype(jnp.bfloat16)
            summed = jnp.dot(
                weights,
                jnp.concatenate([values, jnp.ones((keys.shape[0], LANES), jnp.bfloat16)], axis=1),
                preferred_element_type=jnp.float32,
            )
            if top is not None:
                summed = summed + acc * jnp.exp2(top - new_top)
            top, acc = new_top, summed
        out_ref[:, cols] = (acc[:, :HEAD_DIM] / acc[:, HEAD_DIM:]).astype(out_ref.dtype)


def decode(queries, keys_values, out_type):
    tokens, width = queries.shape
    latents = sum(v.shape[0] for v in keys_values)
    pair = min(2 * HEAD_DIM, width)
    steps = width // pair
    narrow = pl.BlockSpec((tokens, pair), lambda i: (0, i))
    keys = [pl.BlockSpec((v.shape[0], pair), lambda i: (0, i)) for v in keys_values]
    values = [pl.BlockSpec((v.shape[0], pair), lambda i: (0, steps + i)) for v in keys_values]
    return pl.pallas_call(
        functools.partial(decode_kernel, len(keys_values)),
        grid=(steps,),
        in_specs=[narrow, *keys, *values],
        out_specs=narrow,
        out_shape=jax.ShapeDtypeStruct((tokens, width), out_type),
        compiler_params=params(BIG),
        cost_estimate=cost(
            16 * tokens * latents * width,
            4 * latents * width + 6 * tokens * width,
            tokens * latents * (width // HEAD_DIM),
        ),
        name="decode_rows",
    )(queries, *keys_values, *keys_values)


def swap_perm(size):
    return [(i, i ^ 1) for i in range(size)]


def shift_perm(size, k):
    far = size // 2
    return [(((z + k) % far) * 2 + y, z * 2 + y) for z in range(far) for y in range(2)]


def hop_perm(size, step, way):
    far = size // 2
    moves = [(z, z + 1) for z in range(step - 1, far - 1)]
    if way < 0:
        moves = [(far - 1 - a, far - 1 - b) for a, b in moves]
    return [(a * 2 + y, b * 2 + y) for a, b in moves for y in range(2)]


def fast_on_device(
    sizes,
    enc_keys,
    enc_values,
    input_ids,
    latent_queries,
    latent_array,
    w_out,
    norm_gain,
    w_key,
    w_value,
    query_features,
    query_ids,
    query_table,
    enc_bias,
    query_counts,
):
    groups, pos = sizes
    p = lax.axis_index("pos")
    place = lax.axis_index("head")
    rows = latent_array.shape[0]
    tokens, half_width = enc_keys.shape
    heads = half_width // HEAD_DIM
    mods = enc_bias.shape[0]
    modality = jnp.arange(mods, dtype=jnp.int32)
    far, z, y, x = pos // 2, p // 2, p % 2, lax.axis_index("groups") % 2
    near = swap_perm(pos)

    def over_groups(value):
        return lax.ppermute(value, "groups", swap_perm(groups))

    def over_near(value):
        return lax.ppermute(value, "pos", near)

    def over_far(value, k):
        return lax.ppermute(value, "pos", shift_perm(pos, k))

    def hop(step, pair):
        return [
            lax.ppermute(v, "pos", hop_perm(pos, step, way)) for v, way in zip(pair, (1, -1))
        ]

    def by_shift(hops, k):
        return jnp.where(z + k < far, hops[k][1], hops[far - k][0])

    q_onehot = (query_ids[:, None] == modality[None, :]).astype(jnp.int32)
    local_counts = jnp.sum(q_onehot, axis=0)

    def columns(arrays, which):
        part = half_width // 2
        return jnp.concatenate(
            [lax.dynamic_slice_in_dim(v, which * part, part, 1) for v in arrays], axis=1
        )

    extra = jnp.pad(input_ids[None, :], ((0, EXTRA - 1), (0, half_width - tokens)))
    extra = extra.astype(jnp.bfloat16)
    near_inputs = over_near(
        jnp.concatenate([columns((enc_keys, enc_values), 1 - y), extra], axis=0)
    )

    out_half, out_cols = w_out.shape[0] // 2, w_out.shape[1]
    counted = jnp.concatenate([local_counts // 16, local_counts % 16])
    counted = jnp.pad(counted[None, :], ((0, EXTRA - 1), (0, out_cols - 2 * mods)))
    counted = counted.astype(jnp.bfloat16)

    out_sent = jnp.concatenate(
        [lax.dynamic_slice_in_dim(w_out, x * out_half, out_half, 0), counted]
    )
    out_far = [over_far(out_sent, k) for k in range(1, far)]
    places = [((z + k) % far) * 2 + (y ^ j) for j in range(2) for k in range(far)]
    kv_for_near = columns((w_key, w_value), 1 - y)
    head_bias = lax.dynamic_slice_in_dim(enc_bias, y * (heads // 2), heads // 2, 1)
    which = jnp.stack([y, y, y, 0 * y]).astype(jnp.int32)
    parts = encode(which, latent_queries, enc_keys, enc_values, extra, head_bias, 2 * rows)
    near_inputs, out_far, kv_for_near, parts = lax.optimization_barrier(
        (near_inputs, out_far, kv_for_near, parts)
    )

    kv_own = columns((w_key, w_value), y)
    kv_near = over_near(kv_for_near)

    which = jnp.stack([y, 0 * y, 0 * y + 1, 0 * y + tokens // EXTRA]).astype(jnp.int32)
    parts = encode(
        which,
        latent_queries,
        near_inputs,
        near_inputs,
        near_inputs,
        head_bias,
        2 * rows,
        parts,
    )
    kv_near, out_far, parts = lax.optimization_barrier((kv_near, out_far, parts))
    kv_sent = jnp.where(x == 0, kv_own, kv_near)
    hops = {0: [kv_sent, kv_sent]}
    hops[1] = hop(1, hops[0])
    early = [k for k in range(1, far) if max(k, far - k) < 3]
    rest = [k for k in range(1, far) if k not in early]
    out_far = jnp.concatenate(out_far)
    out_far_other = over_groups(out_far)
    out_near = over_near(jnp.concatenate([w_out, counted, out_far]))
    out_near, hops = lax.optimization_barrier((out_near, hops))
    out_near_other = over_groups(out_near[w_out.shape[0] + EXTRA :])
    columns_of_slice = [[2 * i + j for i in range(far)] for j in range(2)]
    parts = lax.all_to_all(parts, "pos", 0, 0, axis_index_groups=columns_of_slice, tiled=True)

    def kept_queries():
        far_counts = out_far.reshape(far - 1, out_half + EXTRA, out_cols)[:, out_half, : 2 * mods]
        near_counts = out_near.reshape(-1, EXTRA, out_cols)[:, 0, : 2 * mods]
        at = [w_out.shape[0] // EXTRA]
        at += [at[0] + k * (out_half // EXTRA + 1) for k in range(1, far)]
        near_counts = jnp.concatenate([near_counts[i : i + 1] for i in at])
        counts = jnp.concatenate([counted[:1, : 2 * mods], far_counts, near_counts])
        counts = counts.astype(jnp.int32)
        counts = counts[:, :mods] * 16 + counts[:, mods:]
        earlier = jnp.stack(places)[:, None] < p
        before = jnp.sum(jnp.where(earlier, counts, 0), axis=0)
        within = jnp.cumsum(q_onehot, axis=0) - q_onehot
        ranked = jnp.sum((within + before[None, :]) * q_onehot, axis=1)
        limits = jnp.sum(q_onehot * query_counts[None, :], axis=1)
        return ranked < limits

    lookup = jnp.dot(q_onehot.astype(jnp.bfloat16), query_table, preferred_element_type=jnp.float32)
    queries = (query_features.astype(jnp.float32) + lookup).astype(jnp.bfloat16)
    own_queries = columns((queries,), y)
    near_queries = over_near(columns((queries,), 1 - y))

    parts, out_near, out_far_other, out_near_other, hops, near_queries = lax.optimization_barrier(
        (parts, out_near, out_far_other, out_near_other, hops, near_queries)
    )
    attended, for_near = merge(y, parts, far)
    for_near, hops = lax.optimization_barrier((for_near, hops))
    hops[2] = hop(2, hops[1])
    from_near = over_near(for_near)
    kept = kept_queries()
    out_ids = jnp.stack([*places, y, x]).astype(jnp.int32)
    weights = [w_out, out_far, out_far_other, out_near, out_near_other]
    partial_value = project(out_ids, attended, from_near, weights)
    partial_value, hops = lax.optimization_barrier((partial_value, hops))
    kv_bands = [kv_own, kv_near]
    for k in early:
        kv_moved = by_shift(hops, k)
        kv_bands += [kv_moved, over_groups(kv_moved)]
    for step in range(3, far):
        hops[step] = hop(step, hops[step - 1])
    theirs = lax.ppermute(partial_value, "head", swap_perm(2))
    own_cols, normed, normed_other = normalise(
        place, partial_value, theirs, latent_array, norm_gain[None, :]
    )
    kv_at = [p, p ^ 1]
    for k in early + rest:
        kv_at += [((z + k) % far) * 2 + (y ^ other) for other in (x, 1 - x)]
    kv_ids = jnp.stack([place, *kv_at]).astype(jnp.int32)

    def cores(values):
        return [lax.ppermute(v, "head", swap_perm(2)) for v in values]

    def fold(mine, other):
        return latent_keys_values(kv_ids, mine, other, kv_bands)

    def arrival(hops, j):
        picked = None
        for at in range(far):
            came = [
                (step, way)
                for step in range(1, far)
                for way in (1, 0)
                if (at + step < far if way else at >= step)
            ]
            step, way = came[j - 1]
            value = hops[step][way]
            picked = value if picked is None else jnp.where(z == at, value, picked)
        return picked

    came = {0: [normed, normed]}
    came[1] = hop(1, came[0])
    normed_near = over_near(normed)
    came, hops, kv_bands, kept = lax.optimization_barrier((came, hops, kv_bands, kept))
    mine, other, keys_values = [normed, normed_near], [normed_other], []
    for step in range(1, far):
        fresh = arrival(came, step)
        fresh_near = over_near(fresh)
        if step + 1 < far:
            came[step + 1] = hop(step + 1, came[step])
            kv_moved = by_shift(hops, rest[step - 1])
            kv_bands += [kv_moved, over_groups(kv_moved)]
            if step > 1:
                keys_values.append(fold(mine, other))
                mine, other = [], []
            came, mine, other, kv_bands, keys_values, fresh, fresh_near = (
                lax.optimization_barrier(
                    (came, mine, other, kv_bands, keys_values, fresh, fresh_near)
                )
            )
            if step == 1:
                mine = [normed, jnp.concatenate([normed_near, fresh, fresh_near])]
                other = [normed_other, *cores(mine[1:])]
            else:
                mine += [fresh, fresh_near]
    mine = [jnp.concatenate([*mine, fresh])]
    keys_values.append(fold(mine, cores(mine)))
    fresh_near, keys_values = lax.optimization_barrier((fresh_near, keys_values))
    keys_values.append(fold([fresh_near], cores([fresh_near])))
    near_state = decode(near_queries, keys_values, jnp.bfloat16)
    own_state = decode(own_queries, keys_values, jnp.float32)
    from_near = over_near(near_state).astype(jnp.float32)
    decoded = jnp.where(
        y == 0,
        jnp.concatenate([own_state, from_near], axis=1),
        jnp.concatenate([from_near, own_state], axis=1),
    )
    decoded = jnp.where(kept[:, None], decoded, 0.0)
    return (own_cols, decoded)


def on_device(sizes, *args):
    groups, pos, head = sizes
    enc_keys, latent_array, w_out, w_key = args[0], args[4], args[5], args[7]
    fits = (
        head == 2
        and pos % 2 == 0
        and pos > 4
        and groups % 2 == 0
        and enc_keys.shape[1] % (4 * HEAD_DIM) == 0
        and 3 * enc_keys.shape[1] <= 2 * HEAD_DIM * EXTRA
        and enc_keys.shape[0] % LANES == 0
        and enc_keys.shape[0] <= enc_keys.shape[1]
        and w_key.shape[0] % LANES == 0
        and w_out.shape[0] % (2 * LANES) == 0
        and w_out.shape[1] % LANES == 0
        and latent_array.shape[0] % LANES == 0
    )
    if fits:
        return fast_on_device((groups, pos), *args)
    return plain_on_device(*args)


def solution(mesh):
    return jax.shard_map(
        functools.partial(on_device, tuple(mesh.shape[a] for a in ("groups", "pos", "head"))),
        mesh=mesh,
        in_specs=(
            P(("groups", "pos"), "head"),
            P(("groups", "pos"), "head"),
            P(("groups", "pos")),
            P("groups", "head"),
            P(("groups", "pos"), None),
            P("head", "pos"),
            P(),
            P("pos", "head"),
            P("pos", "head"),
            P(("groups", "pos"), "head"),
            P(("groups", "pos")),
            P(None, "head"),
            P(None, "head"),
            P("groups"),
        ),
        out_specs=(P(("groups", "pos"), "head"), P(("groups", "pos"), "head")),
        check_vma=False,
    )
```

```python
import functools

import jax
import jax.numpy as jnp
from jax import lax
from jax.experimental import pallas as pl
from jax.experimental.pallas import tpu as pltpu
from jax.sharding import PartitionSpec as P

HEAD_DIM = 128


norm_eps = 1e-06


def prefix(shard, axis, combine, identity):
    peers, place = (lax.axis_size(axis), lax.axis_index(axis))
    everything = lax.all_gather(shard, axis)
    start = jnp.broadcast_to(jnp.asarray(identity, shard.dtype), shard.shape)

    def step(k, before):
        reached = k < place
        new = combine(before, everything[k])
        return jnp.where(reached, new, before)

    return lax.fori_loop(0, peers, step, start)


def plain_on_device(
    enc_keys,
    enc_values,
    input_ids,
    latent_queries,
    latent_array,
    w_out,
    norm_gain,
    w_key,
    w_value,
    query_features,
    query_ids,
    query_table,
    enc_bias,
    query_counts,
):
    tok_rows = enc_keys.shape[0]
    half_width = enc_keys.shape[1]
    local_heads = half_width // HEAD_DIM
    score_scale = HEAD_DIM ** (-0.5)
    modality = jnp.arange(enc_bias.shape[0], dtype=jnp.int32)
    in_onehot = (input_ids[:, None] == modality[None, :]).astype(jnp.float32)
    bias_rows = jnp.dot(in_onehot, enc_bias, precision=lax.Precision.HIGHEST)
    bias_heads = bias_rows.T[:, None, :]
    keys_split = enc_keys.reshape(tok_rows, local_heads, HEAD_DIM)
    values_split = enc_values.reshape(tok_rows, local_heads, HEAD_DIM)
    lat_total = latent_queries.shape[0]
    block_rows = min(512, lat_total)
    query_blocks = latent_queries.reshape(
        lat_total // block_rows, block_rows, local_heads, HEAD_DIM
    )

    def encode_block(block_queries):
        scores = (
            jnp.einsum(
                "nha,tha->hnt", block_queries, keys_split, preferred_element_type=jnp.float32
            )
            * score_scale
            + bias_heads
        )
        highest = jnp.max(scores, axis=2)
        weights = jnp.exp(scores - highest[:, :, None])
        totals = jnp.sum(weights, axis=2)
        summed = jnp.einsum(
            "hnt,tha->nha",
            weights.astype(jnp.bfloat16),
            values_split,
            preferred_element_type=jnp.float32,
        )
        return (highest.T, totals.T, summed.reshape(block_rows, half_width))

    block_max, block_tot, block_acc = lax.map(encode_block, query_blocks)
    row_highest = block_max.reshape(lat_total, local_heads)
    row_totals = block_tot.reshape(lat_total, local_heads)
    row_sums = block_acc.reshape(lat_total, half_width)
    own_rows = latent_array.shape[0]
    global_max = lax.pmax(row_highest, "pos")
    factor = jnp.exp(row_highest - global_max)
    scaled_sums = (row_sums.reshape(lat_total, local_heads, HEAD_DIM) * factor[:, :, None]).reshape(
        lat_total, half_width
    )
    totals, summed = (
        lax.psum_scatter(row_totals * factor, "pos", scatter_dimension=0, tiled=True),
        lax.psum_scatter(scaled_sums, "pos", scatter_dimension=0, tiled=True),
    )
    summed = summed.reshape(own_rows, local_heads, HEAD_DIM)
    attended = (summed / totals[:, :, None]).reshape(own_rows, half_width).astype(jnp.bfloat16)
    partial_value = jnp.dot(
        attended,
        lax.all_gather(w_out, "pos", axis=1, tiled=True),
        preferred_element_type=jnp.float32,
    )
    offset = lax.axis_index("head") * half_width
    projected = lax.psum(partial_value, "head")
    updated = latent_array.astype(jnp.float32) + projected
    mean_square = jnp.mean(updated * updated, axis=1, keepdims=True)
    normed_full = updated * lax.rsqrt(mean_square + norm_eps) * norm_gain
    normed = normed_full.astype(jnp.bfloat16)
    own_cols = lax.dynamic_slice_in_dim(normed_full, offset, half_width, 1)
    pieces = (
        lax.all_gather(w_key, "pos", axis=0, tiled=True),
        lax.all_gather(w_value, "pos", axis=0, tiled=True),
    )
    key_sum = jnp.dot(normed, pieces[0], preferred_element_type=jnp.float32)
    value_sum = jnp.dot(normed, pieces[1], preferred_element_type=jnp.float32)
    latent_keys = key_sum.astype(jnp.bfloat16)
    latent_values = value_sum.astype(jnp.bfloat16)
    q_onehot = (query_ids[:, None] == modality[None, :]).astype(jnp.int32)
    local_counts = jnp.sum(q_onehot, axis=0)
    before = prefix(
        local_counts, "pos", lambda earlier, later: earlier + later, jnp.zeros_like(local_counts)
    )
    within = jnp.cumsum(q_onehot, axis=0) - q_onehot
    ranked = jnp.sum((within + before[None, :]) * q_onehot, axis=1)
    limits = jnp.sum(q_onehot * query_counts[None, :], axis=1)
    kept_rows = ranked < limits
    lookup = jnp.dot(q_onehot.astype(jnp.bfloat16), query_table, preferred_element_type=jnp.float32)
    queries = (
        (query_features.astype(jnp.float32) + lookup)
        .astype(jnp.bfloat16)
        .reshape(tok_rows, local_heads, HEAD_DIM)
    )

    def fold_rows(running, key_rows, value_rows):
        running_max, running_tot, running_acc = running
        key_heads = key_rows.reshape(key_rows.shape[0], local_heads, HEAD_DIM)
        value_heads = value_rows.reshape(value_rows.shape[0], local_heads, HEAD_DIM)
        scores = (
            jnp.einsum("tha,rha->htr", queries, key_heads, preferred_element_type=jnp.float32)
            * score_scale
        )
        new_max = jnp.maximum(running_max, jnp.max(scores, axis=2))
        fade = jnp.exp(running_max - new_max)
        weights = jnp.exp(scores - new_max[:, :, None])
        new_tot = running_tot * fade + jnp.sum(weights, axis=2)
        new_acc = running_acc * fade[:, :, None] + jnp.einsum(
            "htr,rha->hta",
            weights.astype(jnp.bfloat16),
            value_heads,
            preferred_element_type=jnp.float32,
        )
        return (new_max, new_tot, new_acc)

    start_state = (
        jnp.full((local_heads, tok_rows), -jnp.inf, jnp.float32),
        jnp.zeros((local_heads, tok_rows), jnp.float32),
        jnp.zeros((local_heads, tok_rows, HEAD_DIM), jnp.float32),
    )
    running = start_state
    pieces = (
        lax.all_gather(latent_keys, "pos", axis=0, tiled=True),
        lax.all_gather(latent_values, "pos", axis=0, tiled=True),
    )
    row_count = pieces[0].shape[0]
    key_blocks = pieces[0].reshape(row_count // 512, 512, half_width)
    value_blocks = pieces[1].reshape(row_count // 512, 512, half_width)

    def scan_step(state, pair):
        return (fold_rows(state, pair[0], pair[1]), None)

    running, ignored = lax.scan(scan_step, running, (key_blocks, value_blocks))
    final_max, final_tot, final_acc = running
    dec_heads = final_acc / final_tot[:, :, None]
    dec_rows = jnp.transpose(dec_heads, (1, 0, 2)).reshape(tok_rows, half_width)
    decoded = jnp.where(kept_rows[:, None], dec_rows, 0.0)
    return (own_cols, decoded)


LANES = 128
EXTRA = 16
BIG = 56
LOG2E = 1.4426950408889634
EXP2_SCALE = LOG2E * HEAD_DIM**-0.5
NT = (((1,), (1,)), ((), ()))


def params(mib):
    return pltpu.CompilerParams(vmem_limit_bytes=mib << 20)


def cost(flops, nbytes, exps=0):
    return pl.CostEstimate(flops=int(flops), bytes_accessed=int(nbytes), transcendentals=int(exps))


def whole(shape):
    return pl.BlockSpec(shape, lambda *args: (0,) * len(shape))


def stats_of(ref, heads):
    long = ref.shape[0]
    terms = ref[long - EXTRA : long, :].astype(jnp.float32).T
    return [
        terms[:, h : h + 1] + terms[:, heads + h : heads + h + 1] + terms[:, 2 * heads + h : 2 * heads + h + 1]
        for h in range(heads)
    ]


def encode_kernel(count, ids_ref, q_ref, k_ref, v_ref, extra_ref, bias_ref, *refs):
    out_ref = refs[-1]
    rows, width = q_ref.shape
    tokens = k_ref.shape[0]
    heads = width // HEAD_DIM
    ones = jnp.ones((tokens, LANES), jnp.bfloat16)
    kind = extra_ref[...].astype(jnp.float32)[:1, :tokens]
    lane = lax.broadcasted_iota(jnp.int32, (rows, LANES), 1)
    lse_all = jnp.zeros((rows, LANES), jnp.float32)
    earlier = None
    if len(refs) > 1:
        earlier = [
            jnp.max(jnp.broadcast_to(v, (rows, LANES)), axis=1, keepdims=True)
            for v in stats_of(refs[0], heads)
        ]
    for h in range(heads):
        cols = slice(h * HEAD_DIM, (h + 1) * HEAD_DIM)
        bias = jnp.zeros_like(kind)
        for m in range(count):
            bias = jnp.where(kind == m, bias_ref[m, h] * LOG2E, bias)
        scores = lax.dot_general(
            q_ref[:, cols], k_ref[:, cols], NT, preferred_element_type=jnp.float32
        )
        scores = scores * EXP2_SCALE + bias
        top = jnp.max(scores, axis=1, keepdims=True)
        if earlier is not None:
            top = jnp.maximum(top, earlier[h])
        weights = jnp.exp2(scores - top).astype(jnp.bfloat16)
        acc = jnp.dot(
            weights,
            jnp.concatenate([v_ref[:, cols], ones], axis=1),
            preferred_element_type=jnp.float32,
        )
        summed, totals = acc[:, :HEAD_DIM], acc[:, HEAD_DIM:]
        if earlier is not None:
            fade = jnp.exp2(earlier[h] - top)
            summed = summed + refs[0][:rows, cols].astype(jnp.float32) * fade
            totals = totals + fade
        out_ref[:rows, cols] = (summed / totals).astype(jnp.bfloat16)
        lse_all = jnp.where(lane % heads == h, top + jnp.log2(totals), lse_all)
    lse = lse_all.T[:EXTRA, :]
    high = lse.astype(jnp.bfloat16).astype(jnp.float32)
    mid = (lse - high).astype(jnp.bfloat16).astype(jnp.float32)
    low = lse - high - mid
    row = lax.broadcasted_iota(jnp.int32, lse.shape, 0)
    terms = jnp.where(row < heads, high, jnp.where(row < 2 * heads, mid, low))
    out_ref[rows:, :] = terms.astype(jnp.bfloat16)


def encode(which, queries, keys, values, extra, bias, rows, earlier=None):
    tokens = extra.shape[1] // 2
    width = queries.shape[1] // 2
    blocks = queries.shape[0] // rows
    packed = pl.BlockSpec((rows + EXTRA, width), lambda i, ids: (i, 0))
    grid_spec = pltpu.PrefetchScalarGridSpec(
        num_scalar_prefetch=1,
        grid=(blocks,),
        in_specs=[
            pl.BlockSpec((rows, width), lambda i, ids: (i, ids[0])),
            pl.BlockSpec((tokens, width), lambda i, ids: (0, ids[1])),
            pl.BlockSpec((tokens, width), lambda i, ids: (0, ids[2])),
            pl.BlockSpec((EXTRA, extra.shape[1]), lambda i, ids: (ids[3], 0)),
            pl.BlockSpec(memory_space=pltpu.SMEM),
            *([] if earlier is None else [packed]),
        ],
        out_specs=packed,
    )
    return pl.pallas_call(
        functools.partial(encode_kernel, bias.shape[0]),
        grid_spec=grid_spec,
        out_shape=jax.ShapeDtypeStruct((blocks * (rows + EXTRA), width), jnp.bfloat16),
        compiler_params=params(BIG),
        cost_estimate=cost(
            8 * blocks * rows * tokens * width, 8 * tokens * width, blocks * rows * tokens * 4
        ),
        name="encode_rows",
    )(which, queries, keys, values, extra, bias, *([] if earlier is None else [earlier]))


def merge_kernel(count, ids_ref, parts_ref, mine_ref, near_ref, all_ref):
    rows, width = all_ref.shape
    long = rows + EXTRA
    parts = [parts_ref.at[i * long : (i + 1) * long, :] for i in range(count)]
    heads = width // HEAD_DIM
    stats = [stats_of(v, heads) for v in parts]
    for h in range(heads):
        cols = slice(h * HEAD_DIM, (h + 1) * HEAD_DIM)
        lses = [s[h] for s in stats]
        top = functools.reduce(jnp.maximum, lses)
        factors = [jnp.exp2(v - top) for v in lses]
        inverse = 1.0 / functools.reduce(jnp.add, factors)
        merged = functools.reduce(
            jnp.add,
            [v[:rows, cols].astype(jnp.float32) * (f * inverse) for v, f in zip(parts, factors)],
        )
        all_ref[:, cols] = merged.astype(jnp.bfloat16)
    own = rows // 2
    mine_ref[...] = all_ref[pl.ds(pl.multiple_of(ids_ref[0] * own, own), own), :]
    near_ref[...] = all_ref[pl.ds(pl.multiple_of((1 - ids_ref[0]) * own, own), own), :]


def merge(which, parts, count):
    long, width = parts.shape[0] // count, parts.shape[1]
    rows = long - EXTRA
    grid_spec = pltpu.PrefetchScalarGridSpec(
        num_scalar_prefetch=1,
        grid=(1,),
        in_specs=[whole(parts.shape)],
        out_specs=[whole((rows // 2, width))] * 2,
        scratch_shapes=[pltpu.VMEM((rows, width), jnp.bfloat16)],
    )
    return pl.pallas_call(
        functools.partial(merge_kernel, count),
        grid_spec=grid_spec,
        out_shape=[jax.ShapeDtypeStruct((rows // 2, width), jnp.bfloat16)] * 2,
        compiler_params=params(32),
        cost_estimate=cost(8 * rows * width, 10 * rows * width),
        name="merge_rows",
    )(which.reshape(1), parts)


def project_kernel(far, ids_ref, mine_ref, near_ref, *refs):
    w_ref, far_ref, far_other_ref, near_w_ref, near_other_ref, out_ref, att_ref = refs
    part = mine_ref.shape[1]
    first = ids_ref[2 * far]
    att_ref[:, pl.ds(pl.multiple_of(first * part, part), part)] = mine_ref[...]
    att_ref[:, pl.ds(pl.multiple_of((1 - first) * part, part), part)] = near_ref[...]
    cols = w_ref.shape[1]
    depth = att_ref.shape[1] // 2
    share = ids_ref[2 * far + 1]
    halves = [
        att_ref[:, pl.ds(pl.multiple_of(v * depth, depth), depth)] for v in (share, 1 - share)
    ]

    def place(slot, value):
        out_ref[:, pl.ds(pl.multiple_of(ids_ref[slot] * cols, cols), cols)] = value

    for slot, own_ref in ((0, w_ref), (far, near_w_ref)):
        own = own_ref[: 2 * depth, :]
        place(slot, jnp.dot(att_ref[...], own, preferred_element_type=jnp.float32))
    for k in range(far - 1):
        start = k * (depth + EXTRA)
        band = slice(start, start + depth)
        near_band = slice(start + 2 * depth + EXTRA, start + 3 * depth + EXTRA)
        for slot, weights in (
            (1 + k, (far_ref[band, :], far_other_ref[band, :])),
            (far + 1 + k, (near_w_ref[near_band, :], near_other_ref[band, :])),
        ):
            terms = [
                jnp.dot(v, w, preferred_element_type=jnp.float32) for v, w in zip(halves, weights)
            ]
            place(slot, terms[0] + terms[1])


def project(ids, mine, near, weights):
    rows, part = mine.shape
    far = (ids.shape[0] - 2) // 2
    out_cols = 2 * far * weights[0].shape[1]
    grid_spec = pltpu.PrefetchScalarGridSpec(
        num_scalar_prefetch=1,
        grid=(1,),
        in_specs=[whole(v.shape) for v in (mine, near, *weights)],
        out_specs=whole((rows, out_cols)),
        scratch_shapes=[pltpu.VMEM((rows, 2 * part), jnp.bfloat16)],
    )
    return pl.pallas_call(
        functools.partial(project_kernel, far),
        grid_spec=grid_spec,
        out_shape=jax.ShapeDtypeStruct((rows, out_cols), jnp.float32),
        compiler_params=params(BIG),
        cost_estimate=cost(4 * rows * part * out_cols, 4 * part * out_cols + 4 * rows * out_cols),
        name="project_rows",
    )(ids, mine, near, *weights)


def norm_kernel(
    ids_ref, mine_ref, theirs_ref, latent_ref, gain_ref, out_ref, normed_ref, other_ref, full_ref
):
    updated = latent_ref[...].astype(jnp.float32) + (mine_ref[...] + theirs_ref[...])
    mean_square = jnp.mean(updated * updated, axis=1, keepdims=True)
    full_ref[...] = updated * lax.rsqrt(mean_square + norm_eps) * gain_ref[...]
    half = out_ref.shape[1]
    own = full_ref[:, pl.ds(pl.multiple_of(ids_ref[0] * half, half), half)]
    out_ref[...] = own
    normed_ref[...] = own.astype(jnp.bfloat16)
    other = full_ref[:, pl.ds(pl.multiple_of((1 - ids_ref[0]) * half, half), half)]
    other_ref[...] = other.astype(jnp.bfloat16)


def normalise(place, mine, theirs, latent_array, gain):
    rows, width = mine.shape
    half = width // 2
    grid_spec = pltpu.PrefetchScalarGridSpec(
        num_scalar_prefetch=1,
        grid=(1,),
        in_specs=[whole((rows, width))] * 3 + [whole((1, width))],
        out_specs=[whole((rows, half))] * 3,
        scratch_shapes=[pltpu.VMEM((rows, width), jnp.float32)],
    )
    return pl.pallas_call(
        norm_kernel,
        grid_spec=grid_spec,
        out_shape=[
            jax.ShapeDtypeStruct((rows, half), jnp.float32),
            jax.ShapeDtypeStruct((rows, half), jnp.bfloat16),
            jax.ShapeDtypeStruct((rows, half), jnp.bfloat16),
        ],
        compiler_params=params(BIG),
        cost_estimate=cost(6 * rows * width, 13 * rows * width),
        name="norm_rows",
    )(place.reshape(1), mine, theirs, latent_array, gain)


def latents_kernel(pieces, ids_ref, *refs):
    mine, theirs = refs[:pieces], refs[pieces : 2 * pieces]
    w_refs, (out_ref, normed_ref, w_ref) = refs[2 * pieces : -3], refs[-3:]
    half = mine[0].shape[1]
    slots = ids_ref.shape[0] - 1
    depth = 2 * half // slots

    @pl.when(pl.program_id(0) == 0)
    def arrange():
        for j in range(slots):
            at = ids_ref[1 + j]
            start = pl.multiple_of((at % (slots // 2)) * depth, depth)

            def copy(pieces):
                row = 0
                for piece in pieces:
                    band = slice(row, row + piece.shape[0])
                    row += piece.shape[0]
                    normed_ref[band, j * depth : (j + 1) * depth] = piece[:, pl.ds(start, depth)]

            is_mine = at // (slots // 2) == ids_ref[0]
            pl.when(is_mine)(functools.partial(copy, mine))
            pl.when(jnp.logical_not(is_mine))(functools.partial(copy, theirs))

    start, block = 0, w_ref.shape[1]
    for band in w_refs:
        columns = pl.ds(pl.multiple_of(pl.program_id(0) * block, block), block)
        w_ref[start : start + band.shape[0], :] = band[:, columns]
        start += band.shape[0]
    out_ref[...] = jnp.dot(
        normed_ref[...], w_ref[...], preferred_element_type=jnp.float32
    ).astype(jnp.bfloat16)


def latent_keys_values(ids, mine, theirs, bands):
    pieces = len(mine)
    rows = sum(v.shape[0] for v in mine)
    width = bands[0].shape[1]
    block = min(512, width)
    total = sum(band.shape[0] for band in bands)
    grid_spec = pltpu.PrefetchScalarGridSpec(
        num_scalar_prefetch=1,
        grid=(width // block,),
        in_specs=[pl.BlockSpec(memory_space=pltpu.VMEM)] * (2 * pieces + len(bands)),
        out_specs=pl.BlockSpec((rows, block), lambda i, ids: (0, i)),
        scratch_shapes=[
            pltpu.VMEM((rows, total), jnp.bfloat16),
            pltpu.VMEM((total, block), jnp.bfloat16),
        ],
    )
    return pl.pallas_call(
        functools.partial(latents_kernel, pieces),
        grid_spec=grid_spec,
        out_shape=jax.ShapeDtypeStruct((rows, width), jnp.bfloat16),
        compiler_params=params(24),
        cost_estimate=cost(2 * rows * total * width, 2 * total * width),
        name="latent_keys_values",
    )(ids, *mine, *theirs, *bands)


def row_chunks(lengths, size):
    chunks, open_chunk, room = [], [], size
    for i, length in enumerate(lengths):
        start = 0
        while start < length:
            take = min(room, length - start)
            open_chunk.append((i, start, start + take))
            start, room = start + take, room - take
            if room == 0:
                chunks.append(open_chunk)
                open_chunk, room = [], size
    return chunks + ([open_chunk] if open_chunk else [])


def decode_kernel(parts, q_ref, *refs):
    k_refs, v_refs, out_ref = refs[:parts], refs[parts : 2 * parts], refs[-1]

    def gathered(sources, chunk, cols):
        rows = [sources[i][start:stop, cols] for i, start, stop in chunk]
        return rows[0] if len(rows) == 1 else jnp.concatenate(rows)

    for h in range(q_ref.shape[1] // HEAD_DIM):
        cols = slice(h * HEAD_DIM, (h + 1) * HEAD_DIM)
        top = acc = None
        for chunk in row_chunks([k.shape[0] for k in k_refs], 512):
            keys, values = gathered(k_refs, chunk, cols), gathered(v_refs, chunk, cols)
            scores = lax.dot_general(q_ref[:, cols], keys, NT, preferred_element_type=jnp.float32)
            scores = scores * EXP2_SCALE
            new_top = jnp.max(scores, axis=1, keepdims=True)
            if top is not None:
                new_top = jnp.maximum(top, new_top)
            weights = jnp.exp2(scores - new_top).astype(jnp.bfloat16)
            summed = jnp.dot(
                weights,
                jnp.concatenate([values, jnp.ones((keys.shape[0], LANES), jnp.bfloat16)], axis=1),
                preferred_element_type=jnp.float32,
            )
            if top is not None:
                summed = summed + acc * jnp.exp2(top - new_top)
            top, acc = new_top, summed
        out_ref[:, cols] = (acc[:, :HEAD_DIM] / acc[:, HEAD_DIM:]).astype(out_ref.dtype)


def decode(queries, keys_values, out_type):
    tokens, width = queries.shape
    latents = sum(v.shape[0] for v in keys_values)
    pair = min(2 * HEAD_DIM, width)
    steps = width // pair
    narrow = pl.BlockSpec((tokens, pair), lambda i: (0, i))
    keys = [pl.BlockSpec((v.shape[0], pair), lambda i: (0, i)) for v in keys_values]
    values = [pl.BlockSpec((v.shape[0], pair), lambda i: (0, steps + i)) for v in keys_values]
    return pl.pallas_call(
        functools.partial(decode_kernel, len(keys_values)),
        grid=(steps,),
        in_specs=[narrow, *keys, *values],
        out_specs=narrow,
        out_shape=jax.ShapeDtypeStruct((tokens, width), out_type),
        compiler_params=params(BIG),
        cost_estimate=cost(
            16 * tokens * latents * width,
            4 * latents * width + 6 * tokens * width,
            tokens * latents * (width // HEAD_DIM),
        ),
        name="decode_rows",
    )(queries, *keys_values, *keys_values)


def swap_perm(size):
    return [(i, i ^ 1) for i in range(size)]


def shift_perm(size, k):
    far = size // 2
    return [(((z + k) % far) * 2 + y, z * 2 + y) for z in range(far) for y in range(2)]


def hop_perm(size, step, way):
    far = size // 2
    moves = [(z, z + 1) for z in range(step - 1, far - 1)]
    if way < 0:
        moves = [(far - 1 - a, far - 1 - b) for a, b in moves]
    return [(a * 2 + y, b * 2 + y) for a, b in moves for y in range(2)]


def fast_on_device(
    sizes,
    enc_keys,
    enc_values,
    input_ids,
    latent_queries,
    latent_array,
    w_out,
    norm_gain,
    w_key,
    w_value,
    query_features,
    query_ids,
    query_table,
    enc_bias,
    query_counts,
):
    groups, pos = sizes
    p = lax.axis_index("pos")
    place = lax.axis_index("head")
    rows = latent_array.shape[0]
    tokens, half_width = enc_keys.shape
    heads = half_width // HEAD_DIM
    mods = enc_bias.shape[0]
    modality = jnp.arange(mods, dtype=jnp.int32)
    far, z, y, x = pos // 2, p // 2, p % 2, lax.axis_index("groups") % 2
    near = swap_perm(pos)

    def over_groups(value):
        return lax.ppermute(value, "groups", swap_perm(groups))

    def over_near(value):
        return lax.ppermute(value, "pos", near)

    def over_far(value, k):
        return lax.ppermute(value, "pos", shift_perm(pos, k))

    def hop(step, pair):
        return [
            lax.ppermute(v, "pos", hop_perm(pos, step, way)) for v, way in zip(pair, (1, -1))
        ]

    def by_shift(hops, k):
        return jnp.where(z + k < far, hops[k][1], hops[far - k][0])

    q_onehot = (query_ids[:, None] == modality[None, :]).astype(jnp.int32)
    local_counts = jnp.sum(q_onehot, axis=0)

    def columns(arrays, which):
        part = half_width // 2
        return jnp.concatenate(
            [lax.dynamic_slice_in_dim(v, which * part, part, 1) for v in arrays], axis=1
        )

    extra = jnp.pad(input_ids[None, :], ((0, EXTRA - 1), (0, half_width - tokens)))
    extra = extra.astype(jnp.bfloat16)
    near_inputs = over_near(
        jnp.concatenate([columns((enc_keys, enc_values), 1 - y), extra], axis=0)
    )

    out_half, out_cols = w_out.shape[0] // 2, w_out.shape[1]
    counted = jnp.concatenate([local_counts // 16, local_counts % 16])
    counted = jnp.pad(counted[None, :], ((0, EXTRA - 1), (0, out_cols - 2 * mods)))
    counted = counted.astype(jnp.bfloat16)

    out_sent = jnp.concatenate(
        [lax.dynamic_slice_in_dim(w_out, x * out_half, out_half, 0), counted]
    )
    out_far = [over_far(out_sent, k) for k in range(1, far)]
    places = [((z + k) % far) * 2 + (y ^ j) for j in range(2) for k in range(far)]
    kv_for_near = columns((w_key, w_value), 1 - y)
    head_bias = lax.dynamic_slice_in_dim(enc_bias, y * (heads // 2), heads // 2, 1)
    which = jnp.stack([y, y, y, 0 * y]).astype(jnp.int32)
    parts = encode(which, latent_queries, enc_keys, enc_values, extra, head_bias, 2 * rows)
    kv_own = columns((w_key, w_value), y)
    kv_near, out_far, parts = lax.optimization_barrier((over_near(kv_for_near), out_far, parts))
    kv_sent = jnp.where(x == 0, kv_own, kv_near)
    hops = {0: [kv_sent, kv_sent]}
    hops[1] = hop(1, hops[0])
    early = [k for k in range(1, far) if max(k, far - k) < 3]
    rest = [k for k in range(1, far) if k not in early]
    near_inputs, hops, parts = lax.optimization_barrier((near_inputs, hops, parts))

    which = jnp.stack([y, 0 * y, 0 * y + 1, 0 * y + tokens // EXTRA]).astype(jnp.int32)
    parts = encode(
        which,
        latent_queries,
        near_inputs,
        near_inputs,
        near_inputs,
        head_bias,
        2 * rows,
        parts,
    )
    out_far, parts = lax.optimization_barrier((out_far, parts))
    out_far = jnp.concatenate(out_far)
    out_far_other = over_groups(out_far)
    out_near = over_near(jnp.concatenate([w_out, counted, out_far]))
    out_near_other = over_groups(out_near[w_out.shape[0] + EXTRA :])
    columns_of_slice = [[2 * i + j for i in range(far)] for j in range(2)]
    parts = lax.all_to_all(parts, "pos", 0, 0, axis_index_groups=columns_of_slice, tiled=True)

    def kept_queries():
        far_counts = out_far.reshape(far - 1, out_half + EXTRA, out_cols)[:, out_half, : 2 * mods]
        near_counts = out_near.reshape(-1, EXTRA, out_cols)[:, 0, : 2 * mods]
        at = [w_out.shape[0] // EXTRA]
        at += [at[0] + k * (out_half // EXTRA + 1) for k in range(1, far)]
        near_counts = jnp.concatenate([near_counts[i : i + 1] for i in at])
        counts = jnp.concatenate([counted[:1, : 2 * mods], far_counts, near_counts])
        counts = counts.astype(jnp.int32)
        counts = counts[:, :mods] * 16 + counts[:, mods:]
        earlier = jnp.stack(places)[:, None] < p
        before = jnp.sum(jnp.where(earlier, counts, 0), axis=0)
        within = jnp.cumsum(q_onehot, axis=0) - q_onehot
        ranked = jnp.sum((within + before[None, :]) * q_onehot, axis=1)
        limits = jnp.sum(q_onehot * query_counts[None, :], axis=1)
        return ranked < limits

    lookup = jnp.dot(q_onehot.astype(jnp.bfloat16), query_table, preferred_element_type=jnp.float32)
    queries = (query_features.astype(jnp.float32) + lookup).astype(jnp.bfloat16)
    own_queries = columns((queries,), y)
    near_queries = over_near(columns((queries,), 1 - y))

    parts, out_near, out_far_other, out_near_other, hops, near_queries = lax.optimization_barrier(
        (parts, out_near, out_far_other, out_near_other, hops, near_queries)
    )
    attended, for_near = merge(y, parts, far)
    for_near, hops = lax.optimization_barrier((for_near, hops))
    hops[2] = hop(2, hops[1])
    from_near = over_near(for_near)
    kept = kept_queries()
    out_ids = jnp.stack([*places, y, x]).astype(jnp.int32)
    weights = [w_out, out_far, out_far_other, out_near, out_near_other]
    partial_value = project(out_ids, attended, from_near, weights)
    partial_value, hops = lax.optimization_barrier((partial_value, hops))
    kv_bands = [kv_own, kv_near]
    for k in early:
        kv_moved = by_shift(hops, k)
        kv_bands += [kv_moved, over_groups(kv_moved)]
    for step in range(3, far):
        hops[step] = hop(step, hops[step - 1])
    theirs = lax.ppermute(partial_value, "head", swap_perm(2))
    own_cols, normed, normed_other = normalise(
        place, partial_value, theirs, latent_array, norm_gain[None, :]
    )
    kv_at = [p, p ^ 1]
    for k in early + rest:
        kv_at += [((z + k) % far) * 2 + (y ^ other) for other in (x, 1 - x)]
    kv_ids = jnp.stack([place, *kv_at]).astype(jnp.int32)

    def cores(values):
        return [lax.ppermute(v, "head", swap_perm(2)) for v in values]

    def fold(mine, other):
        return latent_keys_values(kv_ids, mine, other, kv_bands)

    def arrival(hops, j):
        picked = None
        for at in range(far):
            came = [
                (step, way)
                for step in range(1, far)
                for way in (1, 0)
                if (at + step < far if way else at >= step)
            ]
            step, way = came[j - 1]
            value = hops[step][way]
            picked = value if picked is None else jnp.where(z == at, value, picked)
        return picked

    came = {0: [normed, normed]}
    came[1] = hop(1, came[0])
    normed_near = over_near(normed)
    hops, _ = lax.optimization_barrier((hops, normed))

    def add_band(k):
        moved = by_shift(hops, k)
        return [*kv_bands, moved, over_groups(moved)]

    kv_bands = add_band(rest[0])
    came, kv_bands, kept, normed_near = lax.optimization_barrier(
        (came, kv_bands, kept, normed_near)
    )
    mine, other, keys_values = [normed, normed_near], [normed_other], []
    for step in range(1, far):
        fresh = arrival(came, step)
        fresh_near = over_near(fresh)
        if step + 1 < far:
            came[step + 1] = hop(step + 1, came[step])
            if step == 1:
                other += cores([normed_near])
            if step < len(rest):
                kv_bands = add_band(rest[step])
            if step > 1:
                keys_values.append(fold(mine, other))
                mine, other = [], []
            came, mine, other, kv_bands, keys_values, fresh, fresh_near = (
                lax.optimization_barrier(
                    (came, mine, other, kv_bands, keys_values, fresh, fresh_near)
                )
            )
            mine += [fresh, fresh_near]
            other += cores([fresh, fresh_near])
    keys_values.append(fold([*mine, fresh], [*other, *cores([fresh])]))
    fresh_near, keys_values = lax.optimization_barrier((fresh_near, keys_values))
    keys_values.append(fold([fresh_near], cores([fresh_near])))
    near_state = decode(near_queries, keys_values, jnp.bfloat16)
    own_state = decode(own_queries, keys_values, jnp.float32)
    from_near = over_near(near_state).astype(jnp.float32)
    decoded = jnp.where(
        y == 0,
        jnp.concatenate([own_state, from_near], axis=1),
        jnp.concatenate([from_near, own_state], axis=1),
    )
    decoded = jnp.where(kept[:, None], decoded, 0.0)
    return (own_cols, decoded)


def on_device(sizes, *args):
    groups, pos, head = sizes
    enc_keys, latent_array, w_out, w_key = args[0], args[4], args[5], args[7]
    fits = (
        head == 2
        and pos % 2 == 0
        and pos > 4
        and groups % 2 == 0
        and enc_keys.shape[1] % (4 * HEAD_DIM) == 0
        and 3 * enc_keys.shape[1] <= 2 * HEAD_DIM * EXTRA
        and enc_keys.shape[0] % LANES == 0
        and enc_keys.shape[0] <= enc_keys.shape[1]
        and w_key.shape[0] % LANES == 0
        and w_out.shape[0] % (2 * LANES) == 0
        and w_out.shape[1] % LANES == 0
        and latent_array.shape[0] % LANES == 0
    )
    if fits:
        return fast_on_device((groups, pos), *args)
    return plain_on_device(*args)


def solution(mesh):
    return jax.shard_map(
        functools.partial(on_device, tuple(mesh.shape[a] for a in ("groups", "pos", "head"))),
        mesh=mesh,
        in_specs=(
            P(("groups", "pos"), "head"),
            P(("groups", "pos"), "head"),
            P(("groups", "pos")),
            P("groups", "head"),
            P(("groups", "pos"), None),
            P("head", "pos"),
            P(),
            P("pos", "head"),
            P("pos", "head"),
            P(("groups", "pos"), "head"),
            P(("groups", "pos")),
            P(None, "head"),
            P(None, "head"),
            P("groups"),
        ),
        out_specs=(P(("groups", "pos"), "head"), P(("groups", "pos"), "head")),
        check_vma=False,
    )
```

```python
import functools

import jax
import jax.numpy as jnp
from jax import lax
from jax.experimental import pallas as pl
from jax.experimental.pallas import tpu as pltpu
from jax.sharding import PartitionSpec as P

HEAD_DIM = 128


norm_eps = 1e-06


def prefix(shard, axis, combine, identity):
    peers, place = (lax.axis_size(axis), lax.axis_index(axis))
    everything = lax.all_gather(shard, axis)
    start = jnp.broadcast_to(jnp.asarray(identity, shard.dtype), shard.shape)

    def step(k, before):
        reached = k < place
        new = combine(before, everything[k])
        return jnp.where(reached, new, before)

    return lax.fori_loop(0, peers, step, start)


def plain_on_device(
    enc_keys,
    enc_values,
    input_ids,
    latent_queries,
    latent_array,
    w_out,
    norm_gain,
    w_key,
    w_value,
    query_features,
    query_ids,
    query_table,
    enc_bias,
    query_counts,
):
    tok_rows = enc_keys.shape[0]
    half_width = enc_keys.shape[1]
    local_heads = half_width // HEAD_DIM
    score_scale = HEAD_DIM ** (-0.5)
    modality = jnp.arange(enc_bias.shape[0], dtype=jnp.int32)
    in_onehot = (input_ids[:, None] == modality[None, :]).astype(jnp.float32)
    bias_rows = jnp.dot(in_onehot, enc_bias, precision=lax.Precision.HIGHEST)
    bias_heads = bias_rows.T[:, None, :]
    keys_split = enc_keys.reshape(tok_rows, local_heads, HEAD_DIM)
    values_split = enc_values.reshape(tok_rows, local_heads, HEAD_DIM)
    lat_total = latent_queries.shape[0]
    block_rows = min(512, lat_total)
    query_blocks = latent_queries.reshape(
        lat_total // block_rows, block_rows, local_heads, HEAD_DIM
    )

    def encode_block(block_queries):
        scores = (
            jnp.einsum(
                "nha,tha->hnt", block_queries, keys_split, preferred_element_type=jnp.float32
            )
            * score_scale
            + bias_heads
        )
        highest = jnp.max(scores, axis=2)
        weights = jnp.exp(scores - highest[:, :, None])
        totals = jnp.sum(weights, axis=2)
        summed = jnp.einsum(
            "hnt,tha->nha",
            weights.astype(jnp.bfloat16),
            values_split,
            preferred_element_type=jnp.float32,
        )
        return (highest.T, totals.T, summed.reshape(block_rows, half_width))

    block_max, block_tot, block_acc = lax.map(encode_block, query_blocks)
    row_highest = block_max.reshape(lat_total, local_heads)
    row_totals = block_tot.reshape(lat_total, local_heads)
    row_sums = block_acc.reshape(lat_total, half_width)
    own_rows = latent_array.shape[0]
    global_max = lax.pmax(row_highest, "pos")
    factor = jnp.exp(row_highest - global_max)
    scaled_sums = (row_sums.reshape(lat_total, local_heads, HEAD_DIM) * factor[:, :, None]).reshape(
        lat_total, half_width
    )
    totals, summed = (
        lax.psum_scatter(row_totals * factor, "pos", scatter_dimension=0, tiled=True),
        lax.psum_scatter(scaled_sums, "pos", scatter_dimension=0, tiled=True),
    )
    summed = summed.reshape(own_rows, local_heads, HEAD_DIM)
    attended = (summed / totals[:, :, None]).reshape(own_rows, half_width).astype(jnp.bfloat16)
    partial_value = jnp.dot(
        attended,
        lax.all_gather(w_out, "pos", axis=1, tiled=True),
        preferred_element_type=jnp.float32,
    )
    offset = lax.axis_index("head") * half_width
    projected = lax.psum(partial_value, "head")
    updated = latent_array.astype(jnp.float32) + projected
    mean_square = jnp.mean(updated * updated, axis=1, keepdims=True)
    normed_full = updated * lax.rsqrt(mean_square + norm_eps) * norm_gain
    normed = normed_full.astype(jnp.bfloat16)
    own_cols = lax.dynamic_slice_in_dim(normed_full, offset, half_width, 1)
    pieces = (
        lax.all_gather(w_key, "pos", axis=0, tiled=True),
        lax.all_gather(w_value, "pos", axis=0, tiled=True),
    )
    key_sum = jnp.dot(normed, pieces[0], preferred_element_type=jnp.float32)
    value_sum = jnp.dot(normed, pieces[1], preferred_element_type=jnp.float32)
    latent_keys = key_sum.astype(jnp.bfloat16)
    latent_values = value_sum.astype(jnp.bfloat16)
    q_onehot = (query_ids[:, None] == modality[None, :]).astype(jnp.int32)
    local_counts = jnp.sum(q_onehot, axis=0)
    before = prefix(
        local_counts, "pos", lambda earlier, later: earlier + later, jnp.zeros_like(local_counts)
    )
    within = jnp.cumsum(q_onehot, axis=0) - q_onehot
    ranked = jnp.sum((within + before[None, :]) * q_onehot, axis=1)
    limits = jnp.sum(q_onehot * query_counts[None, :], axis=1)
    kept_rows = ranked < limits
    lookup = jnp.dot(q_onehot.astype(jnp.bfloat16), query_table, preferred_element_type=jnp.float32)
    queries = (
        (query_features.astype(jnp.float32) + lookup)
        .astype(jnp.bfloat16)
        .reshape(tok_rows, local_heads, HEAD_DIM)
    )

    def fold_rows(running, key_rows, value_rows):
        running_max, running_tot, running_acc = running
        key_heads = key_rows.reshape(key_rows.shape[0], local_heads, HEAD_DIM)
        value_heads = value_rows.reshape(value_rows.shape[0], local_heads, HEAD_DIM)
        scores = (
            jnp.einsum("tha,rha->htr", queries, key_heads, preferred_element_type=jnp.float32)
            * score_scale
        )
        new_max = jnp.maximum(running_max, jnp.max(scores, axis=2))
        fade = jnp.exp(running_max - new_max)
        weights = jnp.exp(scores - new_max[:, :, None])
        new_tot = running_tot * fade + jnp.sum(weights, axis=2)
        new_acc = running_acc * fade[:, :, None] + jnp.einsum(
            "htr,rha->hta",
            weights.astype(jnp.bfloat16),
            value_heads,
            preferred_element_type=jnp.float32,
        )
        return (new_max, new_tot, new_acc)

    start_state = (
        jnp.full((local_heads, tok_rows), -jnp.inf, jnp.float32),
        jnp.zeros((local_heads, tok_rows), jnp.float32),
        jnp.zeros((local_heads, tok_rows, HEAD_DIM), jnp.float32),
    )
    running = start_state
    pieces = (
        lax.all_gather(latent_keys, "pos", axis=0, tiled=True),
        lax.all_gather(latent_values, "pos", axis=0, tiled=True),
    )
    row_count = pieces[0].shape[0]
    key_blocks = pieces[0].reshape(row_count // 512, 512, half_width)
    value_blocks = pieces[1].reshape(row_count // 512, 512, half_width)

    def scan_step(state, pair):
        return (fold_rows(state, pair[0], pair[1]), None)

    running, ignored = lax.scan(scan_step, running, (key_blocks, value_blocks))
    final_max, final_tot, final_acc = running
    dec_heads = final_acc / final_tot[:, :, None]
    dec_rows = jnp.transpose(dec_heads, (1, 0, 2)).reshape(tok_rows, half_width)
    decoded = jnp.where(kept_rows[:, None], dec_rows, 0.0)
    return (own_cols, decoded)


LANES = 128
EXTRA = 16
BIG = 56
LOG2E = 1.4426950408889634
EXP2_SCALE = LOG2E * HEAD_DIM**-0.5
NT = (((1,), (1,)), ((), ()))


def params(mib):
    return pltpu.CompilerParams(vmem_limit_bytes=mib << 20)


def cost(flops, nbytes, exps=0):
    return pl.CostEstimate(flops=int(flops), bytes_accessed=int(nbytes), transcendentals=int(exps))


def whole(shape):
    return pl.BlockSpec(shape, lambda *args: (0,) * len(shape))


def encode_kernel(ids_ref, q_ref, k_ref, v_ref, extra_ref, near_ref, bias_ref, out_ref):
    rows, width = q_ref.shape
    tokens = k_ref.shape[0]
    heads = width // HEAD_DIM
    ones = jnp.ones((tokens, LANES), jnp.bfloat16)
    kinds = [
        extra_ref[...].astype(jnp.float32)[:1, :tokens],
        near_ref[tokens:, :].astype(jnp.float32)[:1, :tokens],
    ]
    lane = lax.broadcasted_iota(jnp.int32, (rows, LANES), 1)
    lse_all = jnp.zeros((rows, LANES), jnp.float32)
    for h in range(heads):
        cols = slice(h * HEAD_DIM, (h + 1) * HEAD_DIM)
        late = slice(width + h * HEAD_DIM, width + (h + 1) * HEAD_DIM)
        pairs = [
            (k_ref[:, cols], v_ref[:, cols]),
            (near_ref[:tokens, cols], near_ref[:tokens, late]),
        ]
        top = acc = None
        for (keys, values), kind in zip(pairs, kinds):
            bias = jnp.zeros_like(kind)
            for m in range(bias_ref.shape[0]):
                bias = jnp.where(kind == m, bias_ref[m, h] * LOG2E, bias)
            scores = lax.dot_general(q_ref[:, cols], keys, NT, preferred_element_type=jnp.float32)
            scores = scores * EXP2_SCALE + bias
            new_top = jnp.max(scores, axis=1, keepdims=True)
            if top is not None:
                new_top = jnp.maximum(top, new_top)
            weights = jnp.exp2(scores - new_top).astype(jnp.bfloat16)
            summed = jnp.dot(
                weights, jnp.concatenate([values, ones], axis=1), preferred_element_type=jnp.float32
            )
            if top is not None:
                summed = summed + acc * jnp.exp2(top - new_top)
            top, acc = new_top, summed
        totals = acc[:, HEAD_DIM:]
        out_ref[:rows, cols] = (acc[:, :HEAD_DIM] / totals).astype(jnp.bfloat16)
        lse_all = jnp.where(lane % heads == h, top + jnp.log2(totals), lse_all)
    lse = lse_all.T[:EXTRA, :]
    high = lse.astype(jnp.bfloat16).astype(jnp.float32)
    mid = (lse - high).astype(jnp.bfloat16).astype(jnp.float32)
    low = lse - high - mid
    row = lax.broadcasted_iota(jnp.int32, lse.shape, 0)
    terms = jnp.where(row < heads, high, jnp.where(row < 2 * heads, mid, low))
    out_ref[rows:, :] = terms.astype(jnp.bfloat16)


def encode(which, queries, keys, values, extra, near, bias, rows):
    tokens = keys.shape[0]
    width = keys.shape[1] // 2
    blocks = queries.shape[0] // rows
    half = pl.BlockSpec((tokens, width), lambda i, ids: (0, ids[0]))
    grid_spec = pltpu.PrefetchScalarGridSpec(
        num_scalar_prefetch=1,
        grid=(blocks,),
        in_specs=[
            pl.BlockSpec((rows, width), lambda i, ids: (i, ids[0])),
            half,
            half,
            whole(extra.shape),
            whole(near.shape),
            pl.BlockSpec(memory_space=pltpu.SMEM),
        ],
        out_specs=pl.BlockSpec((rows + EXTRA, width), lambda i, ids: (i, 0)),
    )
    return pl.pallas_call(
        encode_kernel,
        grid_spec=grid_spec,
        out_shape=jax.ShapeDtypeStruct((blocks * (rows + EXTRA), width), jnp.bfloat16),
        compiler_params=params(BIG),
        cost_estimate=cost(
            16 * blocks * rows * tokens * width, 8 * tokens * width, blocks * rows * tokens * 8
        ),
        name="encode_rows",
    )(which.reshape(1), queries, keys, values, extra, near, bias)


def merge_kernel(count, ids_ref, parts_ref, mine_ref, near_ref, all_ref):
    rows, width = all_ref.shape
    long = rows + EXTRA
    parts = [parts_ref.at[i * long : (i + 1) * long, :] for i in range(count)]
    heads = width // HEAD_DIM
    stats = [v[rows:, :].astype(jnp.float32).T for v in parts]
    for h in range(heads):
        cols = slice(h * HEAD_DIM, (h + 1) * HEAD_DIM)
        lses = [
            s[:, h : h + 1] + s[:, heads + h : heads + h + 1] + s[:, 2 * heads + h : 2 * heads + h + 1]
            for s in stats
        ]
        top = functools.reduce(jnp.maximum, lses)
        factors = [jnp.exp2(v - top) for v in lses]
        inverse = 1.0 / functools.reduce(jnp.add, factors)
        merged = functools.reduce(
            jnp.add,
            [v[:rows, cols].astype(jnp.float32) * (f * inverse) for v, f in zip(parts, factors)],
        )
        all_ref[:, cols] = merged.astype(jnp.bfloat16)
    own = rows // 2
    mine_ref[...] = all_ref[pl.ds(pl.multiple_of(ids_ref[0] * own, own), own), :]
    near_ref[...] = all_ref[pl.ds(pl.multiple_of((1 - ids_ref[0]) * own, own), own), :]


def merge(which, parts, count):
    long, width = parts.shape[0] // count, parts.shape[1]
    rows = long - EXTRA
    grid_spec = pltpu.PrefetchScalarGridSpec(
        num_scalar_prefetch=1,
        grid=(1,),
        in_specs=[whole(parts.shape)],
        out_specs=[whole((rows // 2, width))] * 2,
        scratch_shapes=[pltpu.VMEM((rows, width), jnp.bfloat16)],
    )
    return pl.pallas_call(
        functools.partial(merge_kernel, count),
        grid_spec=grid_spec,
        out_shape=[jax.ShapeDtypeStruct((rows // 2, width), jnp.bfloat16)] * 2,
        compiler_params=params(32),
        cost_estimate=cost(8 * rows * width, 10 * rows * width),
        name="merge_rows",
    )(which.reshape(1), parts)


def project_kernel(far, ids_ref, mine_ref, near_ref, *refs):
    w_ref, far_ref, far_other_ref, near_w_ref, near_other_ref, out_ref, att_ref = refs
    part = mine_ref.shape[1]
    first = ids_ref[2 * far]
    att_ref[:, pl.ds(pl.multiple_of(first * part, part), part)] = mine_ref[...]
    att_ref[:, pl.ds(pl.multiple_of((1 - first) * part, part), part)] = near_ref[...]
    cols = w_ref.shape[1]
    depth = att_ref.shape[1] // 2
    share = ids_ref[2 * far + 1]
    halves = [
        att_ref[:, pl.ds(pl.multiple_of(v * depth, depth), depth)] for v in (share, 1 - share)
    ]

    def place(slot, value):
        out_ref[:, pl.ds(pl.multiple_of(ids_ref[slot] * cols, cols), cols)] = value

    for slot, own_ref in ((0, w_ref), (far, near_w_ref)):
        own = own_ref[: 2 * depth, :]
        place(slot, jnp.dot(att_ref[...], own, preferred_element_type=jnp.float32))
    for k in range(far - 1):
        start = k * (depth + EXTRA)
        band = slice(start, start + depth)
        near_band = slice(start + 2 * depth + EXTRA, start + 3 * depth + EXTRA)
        for slot, weights in (
            (1 + k, (far_ref[band, :], far_other_ref[band, :])),
            (far + 1 + k, (near_w_ref[near_band, :], near_other_ref[band, :])),
        ):
            terms = [
                jnp.dot(v, w, preferred_element_type=jnp.float32) for v, w in zip(halves, weights)
            ]
            place(slot, terms[0] + terms[1])


def project(ids, mine, near, weights):
    rows, part = mine.shape
    far = (ids.shape[0] - 2) // 2
    out_cols = 2 * far * weights[0].shape[1]
    grid_spec = pltpu.PrefetchScalarGridSpec(
        num_scalar_prefetch=1,
        grid=(1,),
        in_specs=[whole(v.shape) for v in (mine, near, *weights)],
        out_specs=whole((rows, out_cols)),
        scratch_shapes=[pltpu.VMEM((rows, 2 * part), jnp.bfloat16)],
    )
    return pl.pallas_call(
        functools.partial(project_kernel, far),
        grid_spec=grid_spec,
        out_shape=jax.ShapeDtypeStruct((rows, out_cols), jnp.float32),
        compiler_params=params(BIG),
        cost_estimate=cost(4 * rows * part * out_cols, 4 * part * out_cols + 4 * rows * out_cols),
        name="project_rows",
    )(ids, mine, near, *weights)


def norm_kernel(
    ids_ref, mine_ref, theirs_ref, latent_ref, gain_ref, out_ref, normed_ref, other_ref, full_ref
):
    updated = latent_ref[...].astype(jnp.float32) + (mine_ref[...] + theirs_ref[...])
    mean_square = jnp.mean(updated * updated, axis=1, keepdims=True)
    full_ref[...] = updated * lax.rsqrt(mean_square + norm_eps) * gain_ref[...]
    half = out_ref.shape[1]
    own = full_ref[:, pl.ds(pl.multiple_of(ids_ref[0] * half, half), half)]
    out_ref[...] = own
    normed_ref[...] = own.astype(jnp.bfloat16)
    other = full_ref[:, pl.ds(pl.multiple_of((1 - ids_ref[0]) * half, half), half)]
    other_ref[...] = other.astype(jnp.bfloat16)


def normalise(place, mine, theirs, latent_array, gain):
    rows, width = mine.shape
    half = width // 2
    grid_spec = pltpu.PrefetchScalarGridSpec(
        num_scalar_prefetch=1,
        grid=(1,),
        in_specs=[whole((rows, width))] * 3 + [whole((1, width))],
        out_specs=[whole((rows, half))] * 3,
        scratch_shapes=[pltpu.VMEM((rows, width), jnp.float32)],
    )
    return pl.pallas_call(
        norm_kernel,
        grid_spec=grid_spec,
        out_shape=[
            jax.ShapeDtypeStruct((rows, half), jnp.float32),
            jax.ShapeDtypeStruct((rows, half), jnp.bfloat16),
            jax.ShapeDtypeStruct((rows, half), jnp.bfloat16),
        ],
        compiler_params=params(BIG),
        cost_estimate=cost(6 * rows * width, 13 * rows * width),
        name="norm_rows",
    )(place.reshape(1), mine, theirs, latent_array, gain)


def latents_kernel(pieces, ids_ref, *refs):
    mine, theirs = refs[:pieces], refs[pieces : 2 * pieces]
    w_refs, (out_ref, normed_ref, w_ref) = refs[2 * pieces : -3], refs[-3:]
    rows, half = mine[0].shape
    slots = ids_ref.shape[0] - 1
    depth = 2 * half // slots

    @pl.when(pl.program_id(0) == 0)
    def arrange():
        for j in range(slots):
            at = ids_ref[1 + j]
            start = pl.multiple_of((at % (slots // 2)) * depth, depth)

            def copy(pieces):
                for r, piece in enumerate(pieces):
                    normed_ref[r * rows : (r + 1) * rows, j * depth : (j + 1) * depth] = piece[
                        :, pl.ds(start, depth)
                    ]

            is_mine = at // (slots // 2) == ids_ref[0]
            pl.when(is_mine)(functools.partial(copy, mine))
            pl.when(jnp.logical_not(is_mine))(functools.partial(copy, theirs))

    start, block = 0, w_ref.shape[1]
    for band in w_refs:
        columns = pl.ds(pl.multiple_of(pl.program_id(0) * block, block), block)
        w_ref[start : start + band.shape[0], :] = band[:, columns]
        start += band.shape[0]
    out_ref[...] = jnp.dot(
        normed_ref[...], w_ref[...], preferred_element_type=jnp.float32
    ).astype(jnp.bfloat16)


def latent_keys_values(ids, mine, theirs, bands):
    pieces = len(mine)
    rows, half = mine[0].shape
    width = bands[0].shape[1]
    block = min(512, width)
    total = sum(band.shape[0] for band in bands)
    grid_spec = pltpu.PrefetchScalarGridSpec(
        num_scalar_prefetch=1,
        grid=(width // block,),
        in_specs=[pl.BlockSpec(memory_space=pltpu.VMEM)] * (2 * pieces + len(bands)),
        out_specs=pl.BlockSpec((rows * pieces, block), lambda i, ids: (0, i)),
        scratch_shapes=[
            pltpu.VMEM((rows * pieces, total), jnp.bfloat16),
            pltpu.VMEM((total, block), jnp.bfloat16),
        ],
    )
    return pl.pallas_call(
        functools.partial(latents_kernel, pieces),
        grid_spec=grid_spec,
        out_shape=jax.ShapeDtypeStruct((rows * pieces, width), jnp.bfloat16),
        compiler_params=params(24),
        cost_estimate=cost(2 * rows * pieces * total * width, 2 * total * width),
        name="latent_keys_values",
    )(ids, *mine, *theirs, *bands)


def row_chunks(lengths, size):
    chunks, open_chunk, room = [], [], size
    for i, length in enumerate(lengths):
        start = 0
        while start < length:
            take = min(room, length - start)
            open_chunk.append((i, start, start + take))
            start, room = start + take, room - take
            if room == 0:
                chunks.append(open_chunk)
                open_chunk, room = [], size
    return chunks + ([open_chunk] if open_chunk else [])


def decode_kernel(parts, q_ref, *refs):
    k_refs, v_refs, out_ref = refs[:parts], refs[parts : 2 * parts], refs[-1]

    def gathered(sources, chunk, cols):
        rows = [sources[i][start:stop, cols] for i, start, stop in chunk]
        return rows[0] if len(rows) == 1 else jnp.concatenate(rows)

    for h in range(q_ref.shape[1] // HEAD_DIM):
        cols = slice(h * HEAD_DIM, (h + 1) * HEAD_DIM)
        top = acc = None
        for chunk in row_chunks([k.shape[0] for k in k_refs], 512):
            keys, values = gathered(k_refs, chunk, cols), gathered(v_refs, chunk, cols)
            scores = lax.dot_general(q_ref[:, cols], keys, NT, preferred_element_type=jnp.float32)
            scores = scores * EXP2_SCALE
            new_top = jnp.max(scores, axis=1, keepdims=True)
            if top is not None:
                new_top = jnp.maximum(top, new_top)
            weights = jnp.exp2(scores - new_top).astype(jnp.bfloat16)
            summed = jnp.dot(
                weights,
                jnp.concatenate([values, jnp.ones((keys.shape[0], LANES), jnp.bfloat16)], axis=1),
                preferred_element_type=jnp.float32,
            )
            if top is not None:
                summed = summed + acc * jnp.exp2(top - new_top)
            top, acc = new_top, summed
        out_ref[:, cols] = (acc[:, :HEAD_DIM] / acc[:, HEAD_DIM:]).astype(out_ref.dtype)


def decode(queries, keys_values, out_type):
    tokens, width = queries.shape
    latents = sum(v.shape[0] for v in keys_values)
    pair = min(2 * HEAD_DIM, width)
    steps = width // pair
    narrow = pl.BlockSpec((tokens, pair), lambda i: (0, i))
    keys = [pl.BlockSpec((v.shape[0], pair), lambda i: (0, i)) for v in keys_values]
    values = [pl.BlockSpec((v.shape[0], pair), lambda i: (0, steps + i)) for v in keys_values]
    return pl.pallas_call(
        functools.partial(decode_kernel, len(keys_values)),
        grid=(steps,),
        in_specs=[narrow, *keys, *values],
        out_specs=narrow,
        out_shape=jax.ShapeDtypeStruct((tokens, width), out_type),
        compiler_params=params(BIG),
        cost_estimate=cost(
            16 * tokens * latents * width,
            4 * latents * width + 6 * tokens * width,
            tokens * latents * (width // HEAD_DIM),
        ),
        name="decode_rows",
    )(queries, *keys_values, *keys_values)


def swap_perm(size):
    return [(i, i ^ 1) for i in range(size)]


def shift_perm(size, k):
    far = size // 2
    return [(((z + k) % far) * 2 + y, z * 2 + y) for z in range(far) for y in range(2)]


def hop_perm(size, step, way):
    far = size // 2
    moves = [(z, z + 1) for z in range(step - 1, far - 1)]
    if way < 0:
        moves = [(far - 1 - a, far - 1 - b) for a, b in moves]
    return [(a * 2 + y, b * 2 + y) for a, b in moves for y in range(2)]


def fast_on_device(
    sizes,
    enc_keys,
    enc_values,
    input_ids,
    latent_queries,
    latent_array,
    w_out,
    norm_gain,
    w_key,
    w_value,
    query_features,
    query_ids,
    query_table,
    enc_bias,
    query_counts,
):
    groups, pos = sizes
    p = lax.axis_index("pos")
    place = lax.axis_index("head")
    rows = latent_array.shape[0]
    tokens, half_width = enc_keys.shape
    heads = half_width // HEAD_DIM
    mods = enc_bias.shape[0]
    modality = jnp.arange(mods, dtype=jnp.int32)
    far, z, y, x = pos // 2, p // 2, p % 2, lax.axis_index("groups") % 2
    near = swap_perm(pos)

    def over_groups(value):
        return lax.ppermute(value, "groups", swap_perm(groups))

    def over_near(value):
        return lax.ppermute(value, "pos", near)

    def over_far(value, k):
        return lax.ppermute(value, "pos", shift_perm(pos, k))

    def hop(step, pair):
        return [
            lax.ppermute(v, "pos", hop_perm(pos, step, way)) for v, way in zip(pair, (1, -1))
        ]

    def by_shift(hops, k):
        return jnp.where(z + k < far, hops[k][1], hops[far - k][0])

    q_onehot = (query_ids[:, None] == modality[None, :]).astype(jnp.int32)
    local_counts = jnp.sum(q_onehot, axis=0)

    def columns(arrays, which):
        part = half_width // 2
        return jnp.concatenate(
            [lax.dynamic_slice_in_dim(v, which * part, part, 1) for v in arrays], axis=1
        )

    extra = jnp.pad(input_ids[None, :], ((0, EXTRA - 1), (0, half_width - tokens)))
    extra = extra.astype(jnp.bfloat16)
    near_inputs = over_near(
        jnp.concatenate([columns((enc_keys, enc_values), 1 - y), extra], axis=0)
    )

    out_half, out_cols = w_out.shape[0] // 2, w_out.shape[1]
    counted = jnp.concatenate([local_counts // 16, local_counts % 16])
    counted = jnp.pad(counted[None, :], ((0, EXTRA - 1), (0, out_cols - 2 * mods)))
    counted = counted.astype(jnp.bfloat16)

    out_sent = jnp.concatenate(
        [lax.dynamic_slice_in_dim(w_out, x * out_half, out_half, 0), counted]
    )
    out_far = [over_far(out_sent, k) for k in range(1, far)]
    places = [((z + k) % far) * 2 + (y ^ j) for j in range(2) for k in range(far)]
    kv_for_near = columns((w_key, w_value), 1 - y)
    near_inputs, out_far, kv_for_near = lax.optimization_barrier(
        (near_inputs, out_far, kv_for_near)
    )

    kv_own = columns((w_key, w_value), y)
    kv_near = over_near(kv_for_near)

    head_bias = lax.dynamic_slice_in_dim(enc_bias, y * (heads // 2), heads // 2, 1)
    parts = encode(
        y, latent_queries, enc_keys, enc_values, extra, near_inputs, head_bias, 2 * rows
    )
    kv_near, out_far, parts = lax.optimization_barrier((kv_near, out_far, parts))
    kv_sent = jnp.where(x == 0, kv_own, kv_near)
    hops = {0: [kv_sent, kv_sent]}
    hops[1] = hop(1, hops[0])
    early = [k for k in range(1, far) if max(k, far - k) < 3]
    rest = [k for k in range(1, far) if k not in early]
    out_far = jnp.concatenate(out_far)
    out_far_other = over_groups(out_far)
    out_near = over_near(jnp.concatenate([w_out, counted, out_far]))
    out_near_other = over_groups(out_near[w_out.shape[0] + EXTRA :])
    columns_of_slice = [[2 * i + j for i in range(far)] for j in range(2)]
    parts = lax.all_to_all(parts, "pos", 0, 0, axis_index_groups=columns_of_slice, tiled=True)

    def kept_queries():
        far_counts = out_far.reshape(far - 1, out_half + EXTRA, out_cols)[:, out_half, : 2 * mods]
        near_counts = out_near.reshape(-1, EXTRA, out_cols)[:, 0, : 2 * mods]
        at = [w_out.shape[0] // EXTRA]
        at += [at[0] + k * (out_half // EXTRA + 1) for k in range(1, far)]
        near_counts = jnp.concatenate([near_counts[i : i + 1] for i in at])
        counts = jnp.concatenate([counted[:1, : 2 * mods], far_counts, near_counts])
        counts = counts.astype(jnp.int32)
        counts = counts[:, :mods] * 16 + counts[:, mods:]
        earlier = jnp.stack(places)[:, None] < p
        before = jnp.sum(jnp.where(earlier, counts, 0), axis=0)
        within = jnp.cumsum(q_onehot, axis=0) - q_onehot
        ranked = jnp.sum((within + before[None, :]) * q_onehot, axis=1)
        limits = jnp.sum(q_onehot * query_counts[None, :], axis=1)
        return ranked < limits

    lookup = jnp.dot(q_onehot.astype(jnp.bfloat16), query_table, preferred_element_type=jnp.float32)
    queries = (query_features.astype(jnp.float32) + lookup).astype(jnp.bfloat16)
    own_queries = columns((queries,), y)
    near_queries = over_near(columns((queries,), 1 - y))

    parts, out_near, out_far_other, out_near_other, near_queries = lax.optimization_barrier(
        (parts, out_near, out_far_other, out_near_other, near_queries)
    )
    attended, for_near = merge(y, parts, far)
    for_near, hops = lax.optimization_barrier((for_near, hops))
    hops[2] = hop(2, hops[1])
    from_near = over_near(for_near)
    kept = kept_queries()
    out_ids = jnp.stack([*places, y, x]).astype(jnp.int32)
    weights = [w_out, out_far, out_far_other, out_near, out_near_other]
    partial_value = project(out_ids, attended, from_near, weights)
    partial_value, hops = lax.optimization_barrier((partial_value, hops))
    kv_bands = [kv_own, kv_near]
    for k in early:
        kv_moved = by_shift(hops, k)
        kv_bands += [kv_moved, over_groups(kv_moved)]
    for step in range(3, far):
        hops[step] = hop(step, hops[step - 1])
    theirs = lax.ppermute(partial_value, "head", swap_perm(2))
    own_cols, normed, normed_other = normalise(
        place, partial_value, theirs, latent_array, norm_gain[None, :]
    )
    kv_at = [p, p ^ 1]
    for k in early + rest:
        kv_at += [((z + k) % far) * 2 + (y ^ other) for other in (x, 1 - x)]
    kv_ids = jnp.stack([place, *kv_at]).astype(jnp.int32)

    def cores(values):
        return [lax.ppermute(v, "head", swap_perm(2)) for v in values]

    def fold(mine, other):
        return latent_keys_values(kv_ids, mine, other, kv_bands)

    def arrival(hops, j):
        picked = None
        for at in range(far):
            came = [
                (step, way)
                for step in range(1, far)
                for way in (1, 0)
                if (at + step < far if way else at >= step)
            ]
            step, way = came[j - 1]
            value = hops[step][way]
            picked = value if picked is None else jnp.where(z == at, value, picked)
        return picked

    came = {0: [normed, normed]}
    came[1] = hop(1, came[0])
    normed_near = over_near(normed)
    came, hops, kv_bands, kept = lax.optimization_barrier((came, hops, kv_bands, kept))
    mine, other, keys_values = [normed, normed_near], [normed_other], []
    for step in range(1, far):
        fresh = arrival(came, step)
        fresh_near = over_near(fresh)
        if step + 1 < far:
            came[step + 1] = hop(step + 1, came[step])
            k = rest[step - 1]
            kv_moved = by_shift(hops, k)
            kv_bands += [kv_moved, over_groups(kv_moved)]
            if step > 1:
                keys_values.append(fold(mine, other))
                mine, other = [], []
            came, mine, other, kv_bands, keys_values, fresh, fresh_near = (
                lax.optimization_barrier(
                    (came, mine, other, kv_bands, keys_values, fresh, fresh_near)
                )
            )
            if step == 1:
                mine += [fresh, fresh_near]
                other += cores(mine[1:])
            else:
                mine += [fresh, fresh_near]
                other += cores([fresh, fresh_near])
    keys_values.append(fold([*mine, fresh], [*other, *cores([fresh])]))
    fresh_near, keys_values = lax.optimization_barrier((fresh_near, keys_values))
    keys_values.append(fold([fresh_near], cores([fresh_near])))
    near_state = decode(near_queries, keys_values, jnp.bfloat16)
    own_state = decode(own_queries, keys_values, jnp.float32)
    from_near = lax.ppermute(near_state, "pos", near).astype(jnp.float32)
    decoded = jnp.where(
        y == 0,
        jnp.concatenate([own_state, from_near], axis=1),
        jnp.concatenate([from_near, own_state], axis=1),
    )
    decoded = jnp.where(kept[:, None], decoded, 0.0)
    return (own_cols, decoded)


def on_device(sizes, *args):
    groups, pos, head = sizes
    enc_keys, latent_array, w_out, w_key = args[0], args[4], args[5], args[7]
    fits = (
        head == 2
        and pos % 2 == 0
        and pos > 4
        and groups % 2 == 0
        and enc_keys.shape[1] % (4 * HEAD_DIM) == 0
        and 3 * enc_keys.shape[1] <= 2 * HEAD_DIM * EXTRA
        and enc_keys.shape[0] % LANES == 0
        and enc_keys.shape[0] <= enc_keys.shape[1]
        and w_key.shape[0] % LANES == 0
        and w_out.shape[0] % (2 * LANES) == 0
        and w_out.shape[1] % LANES == 0
        and latent_array.shape[0] % LANES == 0
    )
    if fits:
        return fast_on_device((groups, pos), *args)
    return plain_on_device(*args)


def solution(mesh):
    return jax.shard_map(
        functools.partial(on_device, tuple(mesh.shape[a] for a in ("groups", "pos", "head"))),
        mesh=mesh,
        in_specs=(
            P(("groups", "pos"), "head"),
            P(("groups", "pos"), "head"),
            P(("groups", "pos")),
            P("groups", "head"),
            P(("groups", "pos"), None),
            P("head", "pos"),
            P(),
            P("pos", "head"),
            P("pos", "head"),
            P(("groups", "pos"), "head"),
            P(("groups", "pos")),
            P(None, "head"),
            P(None, "head"),
            P("groups"),
        ),
        out_specs=(P(("groups", "pos"), "head"), P(("groups", "pos"), "head")),
        check_vma=False,
    )
```

```python
import functools

import jax
import jax.numpy as jnp
from jax import lax
from jax.experimental import pallas as pl
from jax.experimental.pallas import tpu as pltpu
from jax.sharding import PartitionSpec as P

HEAD_DIM = 128


norm_eps = 1e-06


def prefix(shard, axis, combine, identity):
    peers, place = (lax.axis_size(axis), lax.axis_index(axis))
    everything = lax.all_gather(shard, axis)
    start = jnp.broadcast_to(jnp.asarray(identity, shard.dtype), shard.shape)

    def step(k, before):
        reached = k < place
        new = combine(before, everything[k])
        return jnp.where(reached, new, before)

    return lax.fori_loop(0, peers, step, start)


def plain_on_device(
    enc_keys,
    enc_values,
    input_ids,
    latent_queries,
    latent_array,
    w_out,
    norm_gain,
    w_key,
    w_value,
    query_features,
    query_ids,
    query_table,
    enc_bias,
    query_counts,
):
    tok_rows = enc_keys.shape[0]
    half_width = enc_keys.shape[1]
    local_heads = half_width // HEAD_DIM
    score_scale = HEAD_DIM ** (-0.5)
    modality = jnp.arange(enc_bias.shape[0], dtype=jnp.int32)
    in_onehot = (input_ids[:, None] == modality[None, :]).astype(jnp.float32)
    bias_rows = jnp.dot(in_onehot, enc_bias, precision=lax.Precision.HIGHEST)
    bias_heads = bias_rows.T[:, None, :]
    keys_split = enc_keys.reshape(tok_rows, local_heads, HEAD_DIM)
    values_split = enc_values.reshape(tok_rows, local_heads, HEAD_DIM)
    lat_total = latent_queries.shape[0]
    block_rows = min(512, lat_total)
    query_blocks = latent_queries.reshape(
        lat_total // block_rows, block_rows, local_heads, HEAD_DIM
    )

    def encode_block(block_queries):
        scores = (
            jnp.einsum(
                "nha,tha->hnt", block_queries, keys_split, preferred_element_type=jnp.float32
            )
            * score_scale
            + bias_heads
        )
        highest = jnp.max(scores, axis=2)
        weights = jnp.exp(scores - highest[:, :, None])
        totals = jnp.sum(weights, axis=2)
        summed = jnp.einsum(
            "hnt,tha->nha",
            weights.astype(jnp.bfloat16),
            values_split,
            preferred_element_type=jnp.float32,
        )
        return (highest.T, totals.T, summed.reshape(block_rows, half_width))

    block_max, block_tot, block_acc = lax.map(encode_block, query_blocks)
    row_highest = block_max.reshape(lat_total, local_heads)
    row_totals = block_tot.reshape(lat_total, local_heads)
    row_sums = block_acc.reshape(lat_total, half_width)
    own_rows = latent_array.shape[0]
    global_max = lax.pmax(row_highest, "pos")
    factor = jnp.exp(row_highest - global_max)
    scaled_sums = (row_sums.reshape(lat_total, local_heads, HEAD_DIM) * factor[:, :, None]).reshape(
        lat_total, half_width
    )
    totals, summed = (
        lax.psum_scatter(row_totals * factor, "pos", scatter_dimension=0, tiled=True),
        lax.psum_scatter(scaled_sums, "pos", scatter_dimension=0, tiled=True),
    )
    summed = summed.reshape(own_rows, local_heads, HEAD_DIM)
    attended = (summed / totals[:, :, None]).reshape(own_rows, half_width).astype(jnp.bfloat16)
    partial_value = jnp.dot(
        attended,
        lax.all_gather(w_out, "pos", axis=1, tiled=True),
        preferred_element_type=jnp.float32,
    )
    offset = lax.axis_index("head") * half_width
    projected = lax.psum(partial_value, "head")
    updated = latent_array.astype(jnp.float32) + projected
    mean_square = jnp.mean(updated * updated, axis=1, keepdims=True)
    normed_full = updated * lax.rsqrt(mean_square + norm_eps) * norm_gain
    normed = normed_full.astype(jnp.bfloat16)
    own_cols = lax.dynamic_slice_in_dim(normed_full, offset, half_width, 1)
    pieces = (
        lax.all_gather(w_key, "pos", axis=0, tiled=True),
        lax.all_gather(w_value, "pos", axis=0, tiled=True),
    )
    key_sum = jnp.dot(normed, pieces[0], preferred_element_type=jnp.float32)
    value_sum = jnp.dot(normed, pieces[1], preferred_element_type=jnp.float32)
    latent_keys = key_sum.astype(jnp.bfloat16)
    latent_values = value_sum.astype(jnp.bfloat16)
    q_onehot = (query_ids[:, None] == modality[None, :]).astype(jnp.int32)
    local_counts = jnp.sum(q_onehot, axis=0)
    before = prefix(
        local_counts, "pos", lambda earlier, later: earlier + later, jnp.zeros_like(local_counts)
    )
    within = jnp.cumsum(q_onehot, axis=0) - q_onehot
    ranked = jnp.sum((within + before[None, :]) * q_onehot, axis=1)
    limits = jnp.sum(q_onehot * query_counts[None, :], axis=1)
    kept_rows = ranked < limits
    lookup = jnp.dot(q_onehot.astype(jnp.bfloat16), query_table, preferred_element_type=jnp.float32)
    queries = (
        (query_features.astype(jnp.float32) + lookup)
        .astype(jnp.bfloat16)
        .reshape(tok_rows, local_heads, HEAD_DIM)
    )

    def fold_rows(running, key_rows, value_rows):
        running_max, running_tot, running_acc = running
        key_heads = key_rows.reshape(key_rows.shape[0], local_heads, HEAD_DIM)
        value_heads = value_rows.reshape(value_rows.shape[0], local_heads, HEAD_DIM)
        scores = (
            jnp.einsum("tha,rha->htr", queries, key_heads, preferred_element_type=jnp.float32)
            * score_scale
        )
        new_max = jnp.maximum(running_max, jnp.max(scores, axis=2))
        fade = jnp.exp(running_max - new_max)
        weights = jnp.exp(scores - new_max[:, :, None])
        new_tot = running_tot * fade + jnp.sum(weights, axis=2)
        new_acc = running_acc * fade[:, :, None] + jnp.einsum(
            "htr,rha->hta",
            weights.astype(jnp.bfloat16),
            value_heads,
            preferred_element_type=jnp.float32,
        )
        return (new_max, new_tot, new_acc)

    start_state = (
        jnp.full((local_heads, tok_rows), -jnp.inf, jnp.float32),
        jnp.zeros((local_heads, tok_rows), jnp.float32),
        jnp.zeros((local_heads, tok_rows, HEAD_DIM), jnp.float32),
    )
    running = start_state
    pieces = (
        lax.all_gather(latent_keys, "pos", axis=0, tiled=True),
        lax.all_gather(latent_values, "pos", axis=0, tiled=True),
    )
    row_count = pieces[0].shape[0]
    key_blocks = pieces[0].reshape(row_count // 512, 512, half_width)
    value_blocks = pieces[1].reshape(row_count // 512, 512, half_width)

    def scan_step(state, pair):
        return (fold_rows(state, pair[0], pair[1]), None)

    running, ignored = lax.scan(scan_step, running, (key_blocks, value_blocks))
    final_max, final_tot, final_acc = running
    dec_heads = final_acc / final_tot[:, :, None]
    dec_rows = jnp.transpose(dec_heads, (1, 0, 2)).reshape(tok_rows, half_width)
    decoded = jnp.where(kept_rows[:, None], dec_rows, 0.0)
    return (own_cols, decoded)


LANES = 128
EXTRA = 16
BIG = 56
LOG2E = 1.4426950408889634
EXP2_SCALE = LOG2E * HEAD_DIM**-0.5
NT = (((1,), (1,)), ((), ()))


def params(mib):
    return pltpu.CompilerParams(vmem_limit_bytes=mib << 20)


def cost(flops, nbytes, exps=0):
    return pl.CostEstimate(flops=int(flops), bytes_accessed=int(nbytes), transcendentals=int(exps))


def whole(shape):
    return pl.BlockSpec(shape, lambda *args: (0,) * len(shape))


def encode_kernel(ids_ref, q_ref, k_ref, v_ref, extra_ref, near_ref, bias_ref, out_ref):
    rows, width = q_ref.shape
    tokens = k_ref.shape[0]
    heads = width // HEAD_DIM
    ones = jnp.ones((tokens, LANES), jnp.bfloat16)
    kinds = [
        extra_ref[...].astype(jnp.float32)[:1, :tokens],
        near_ref[tokens:, :].astype(jnp.float32)[:1, :tokens],
    ]
    lane = lax.broadcasted_iota(jnp.int32, (rows, LANES), 1)
    lse_all = jnp.zeros((rows, LANES), jnp.float32)
    for h in range(heads):
        cols = slice(h * HEAD_DIM, (h + 1) * HEAD_DIM)
        late = slice(width + h * HEAD_DIM, width + (h + 1) * HEAD_DIM)
        pairs = [
            (k_ref[:, cols], v_ref[:, cols]),
            (near_ref[:tokens, cols], near_ref[:tokens, late]),
        ]
        top = acc = None
        for (keys, values), kind in zip(pairs, kinds):
            bias = jnp.zeros_like(kind)
            for m in range(bias_ref.shape[0]):
                bias = jnp.where(kind == m, bias_ref[m, h] * LOG2E, bias)
            scores = lax.dot_general(q_ref[:, cols], keys, NT, preferred_element_type=jnp.float32)
            scores = scores * EXP2_SCALE + bias
            new_top = jnp.max(scores, axis=1, keepdims=True)
            if top is not None:
                new_top = jnp.maximum(top, new_top)
            weights = jnp.exp2(scores - new_top).astype(jnp.bfloat16)
            summed = jnp.dot(
                weights, jnp.concatenate([values, ones], axis=1), preferred_element_type=jnp.float32
            )
            if top is not None:
                summed = summed + acc * jnp.exp2(top - new_top)
            top, acc = new_top, summed
        totals = acc[:, HEAD_DIM:]
        out_ref[:rows, cols] = (acc[:, :HEAD_DIM] / totals).astype(jnp.bfloat16)
        lse_all = jnp.where(lane % heads == h, top + jnp.log2(totals), lse_all)
    lse = lse_all.T[:EXTRA, :]
    high = lse.astype(jnp.bfloat16).astype(jnp.float32)
    mid = (lse - high).astype(jnp.bfloat16).astype(jnp.float32)
    low = lse - high - mid
    row = lax.broadcasted_iota(jnp.int32, lse.shape, 0)
    terms = jnp.where(row < heads, high, jnp.where(row < 2 * heads, mid, low))
    out_ref[rows:, :] = terms.astype(jnp.bfloat16)


def encode(which, queries, keys, values, extra, near, bias, rows):
    tokens = keys.shape[0]
    width = keys.shape[1] // 2
    blocks = queries.shape[0] // rows
    half = pl.BlockSpec((tokens, width), lambda i, ids: (0, ids[0]))
    grid_spec = pltpu.PrefetchScalarGridSpec(
        num_scalar_prefetch=1,
        grid=(blocks,),
        in_specs=[
            pl.BlockSpec((rows, width), lambda i, ids: (i, ids[0])),
            half,
            half,
            whole(extra.shape),
            whole(near.shape),
            pl.BlockSpec(memory_space=pltpu.SMEM),
        ],
        out_specs=pl.BlockSpec((rows + EXTRA, width), lambda i, ids: (i, 0)),
    )
    return pl.pallas_call(
        encode_kernel,
        grid_spec=grid_spec,
        out_shape=jax.ShapeDtypeStruct((blocks * (rows + EXTRA), width), jnp.bfloat16),
        compiler_params=params(BIG),
        cost_estimate=cost(
            16 * blocks * rows * tokens * width, 8 * tokens * width, blocks * rows * tokens * 8
        ),
        name="encode_rows",
    )(which.reshape(1), queries, keys, values, extra, near, bias)


def merge_kernel(count, ids_ref, parts_ref, mine_ref, near_ref, all_ref):
    rows, width = all_ref.shape
    long = rows + EXTRA
    parts = [parts_ref.at[i * long : (i + 1) * long, :] for i in range(count)]
    heads = width // HEAD_DIM
    stats = [v[rows:, :].astype(jnp.float32).T for v in parts]
    for h in range(heads):
        cols = slice(h * HEAD_DIM, (h + 1) * HEAD_DIM)
        lses = [
            s[:, h : h + 1] + s[:, heads + h : heads + h + 1] + s[:, 2 * heads + h : 2 * heads + h + 1]
            for s in stats
        ]
        top = functools.reduce(jnp.maximum, lses)
        factors = [jnp.exp2(v - top) for v in lses]
        inverse = 1.0 / functools.reduce(jnp.add, factors)
        merged = functools.reduce(
            jnp.add,
            [v[:rows, cols].astype(jnp.float32) * (f * inverse) for v, f in zip(parts, factors)],
        )
        all_ref[:, cols] = merged.astype(jnp.bfloat16)
    own = rows // 2
    mine_ref[...] = all_ref[pl.ds(pl.multiple_of(ids_ref[0] * own, own), own), :]
    near_ref[...] = all_ref[pl.ds(pl.multiple_of((1 - ids_ref[0]) * own, own), own), :]


def merge(which, parts, count):
    long, width = parts.shape[0] // count, parts.shape[1]
    rows = long - EXTRA
    grid_spec = pltpu.PrefetchScalarGridSpec(
        num_scalar_prefetch=1,
        grid=(1,),
        in_specs=[whole(parts.shape)],
        out_specs=[whole((rows // 2, width))] * 2,
        scratch_shapes=[pltpu.VMEM((rows, width), jnp.bfloat16)],
    )
    return pl.pallas_call(
        functools.partial(merge_kernel, count),
        grid_spec=grid_spec,
        out_shape=[jax.ShapeDtypeStruct((rows // 2, width), jnp.bfloat16)] * 2,
        compiler_params=params(32),
        cost_estimate=cost(8 * rows * width, 10 * rows * width),
        name="merge_rows",
    )(which.reshape(1), parts)


def project_kernel(far, ids_ref, mine_ref, near_ref, *refs):
    w_ref, far_ref, far_other_ref, near_w_ref, near_other_ref, out_ref, att_ref = refs
    part = mine_ref.shape[1]
    first = ids_ref[2 * far]
    att_ref[:, pl.ds(pl.multiple_of(first * part, part), part)] = mine_ref[...]
    att_ref[:, pl.ds(pl.multiple_of((1 - first) * part, part), part)] = near_ref[...]
    cols = w_ref.shape[1]
    depth = att_ref.shape[1] // 2
    share = ids_ref[2 * far + 1]
    halves = [
        att_ref[:, pl.ds(pl.multiple_of(v * depth, depth), depth)] for v in (share, 1 - share)
    ]

    def place(slot, value):
        out_ref[:, pl.ds(pl.multiple_of(ids_ref[slot] * cols, cols), cols)] = value

    for slot, own_ref in ((0, w_ref), (far, near_w_ref)):
        own = own_ref[: 2 * depth, :]
        place(slot, jnp.dot(att_ref[...], own, preferred_element_type=jnp.float32))
    for k in range(far - 1):
        start = k * (depth + EXTRA)
        band = slice(start, start + depth)
        near_band = slice(start + 2 * depth + EXTRA, start + 3 * depth + EXTRA)
        for slot, weights in (
            (1 + k, (far_ref[band, :], far_other_ref[band, :])),
            (far + 1 + k, (near_w_ref[near_band, :], near_other_ref[band, :])),
        ):
            terms = [
                jnp.dot(v, w, preferred_element_type=jnp.float32) for v, w in zip(halves, weights)
            ]
            place(slot, terms[0] + terms[1])


def project(ids, mine, near, weights):
    rows, part = mine.shape
    far = (ids.shape[0] - 2) // 2
    out_cols = 2 * far * weights[0].shape[1]
    grid_spec = pltpu.PrefetchScalarGridSpec(
        num_scalar_prefetch=1,
        grid=(1,),
        in_specs=[whole(v.shape) for v in (mine, near, *weights)],
        out_specs=whole((rows, out_cols)),
        scratch_shapes=[pltpu.VMEM((rows, 2 * part), jnp.bfloat16)],
    )
    return pl.pallas_call(
        functools.partial(project_kernel, far),
        grid_spec=grid_spec,
        out_shape=jax.ShapeDtypeStruct((rows, out_cols), jnp.float32),
        compiler_params=params(BIG),
        cost_estimate=cost(4 * rows * part * out_cols, 4 * part * out_cols + 4 * rows * out_cols),
        name="project_rows",
    )(ids, mine, near, *weights)


def norm_kernel(
    ids_ref, mine_ref, theirs_ref, latent_ref, gain_ref, out_ref, normed_ref, other_ref, full_ref
):
    updated = latent_ref[...].astype(jnp.float32) + (mine_ref[...] + theirs_ref[...])
    mean_square = jnp.mean(updated * updated, axis=1, keepdims=True)
    full_ref[...] = updated * lax.rsqrt(mean_square + norm_eps) * gain_ref[...]
    half = out_ref.shape[1]
    own = full_ref[:, pl.ds(pl.multiple_of(ids_ref[0] * half, half), half)]
    out_ref[...] = own
    normed_ref[...] = own.astype(jnp.bfloat16)
    other = full_ref[:, pl.ds(pl.multiple_of((1 - ids_ref[0]) * half, half), half)]
    other_ref[...] = other.astype(jnp.bfloat16)


def normalise(place, mine, theirs, latent_array, gain):
    rows, width = mine.shape
    half = width // 2
    grid_spec = pltpu.PrefetchScalarGridSpec(
        num_scalar_prefetch=1,
        grid=(1,),
        in_specs=[whole((rows, width))] * 3 + [whole((1, width))],
        out_specs=[whole((rows, half))] * 3,
        scratch_shapes=[pltpu.VMEM((rows, width), jnp.float32)],
    )
    return pl.pallas_call(
        norm_kernel,
        grid_spec=grid_spec,
        out_shape=[
            jax.ShapeDtypeStruct((rows, half), jnp.float32),
            jax.ShapeDtypeStruct((rows, half), jnp.bfloat16),
            jax.ShapeDtypeStruct((rows, half), jnp.bfloat16),
        ],
        compiler_params=params(BIG),
        cost_estimate=cost(6 * rows * width, 13 * rows * width),
        name="norm_rows",
    )(place.reshape(1), mine, theirs, latent_array, gain)


def latents_kernel(pieces, ids_ref, *refs):
    mine, theirs = refs[:pieces], refs[pieces : 2 * pieces]
    w_refs, (out_ref, normed_ref, w_ref) = refs[2 * pieces : -3], refs[-3:]
    rows, half = mine[0].shape
    slots = ids_ref.shape[0] - 1
    depth = 2 * half // slots

    @pl.when(pl.program_id(0) == 0)
    def arrange():
        for j in range(slots):
            at = ids_ref[1 + j]
            start = pl.multiple_of((at % (slots // 2)) * depth, depth)

            def copy(pieces):
                for r, piece in enumerate(pieces):
                    normed_ref[r * rows : (r + 1) * rows, j * depth : (j + 1) * depth] = piece[
                        :, pl.ds(start, depth)
                    ]

            is_mine = at // (slots // 2) == ids_ref[0]
            pl.when(is_mine)(functools.partial(copy, mine))
            pl.when(jnp.logical_not(is_mine))(functools.partial(copy, theirs))

    start, block = 0, w_ref.shape[1]
    for band in w_refs:
        columns = pl.ds(pl.multiple_of(pl.program_id(0) * block, block), block)
        w_ref[start : start + band.shape[0], :] = band[:, columns]
        start += band.shape[0]
    out_ref[...] = jnp.dot(
        normed_ref[...], w_ref[...], preferred_element_type=jnp.float32
    ).astype(jnp.bfloat16)


def latent_keys_values(ids, mine, theirs, bands):
    pieces = len(mine)
    rows, half = mine[0].shape
    width = bands[0].shape[1]
    block = min(512, width)
    total = sum(band.shape[0] for band in bands)
    grid_spec = pltpu.PrefetchScalarGridSpec(
        num_scalar_prefetch=1,
        grid=(width // block,),
        in_specs=[pl.BlockSpec(memory_space=pltpu.VMEM)] * (2 * pieces + len(bands)),
        out_specs=pl.BlockSpec((rows * pieces, block), lambda i, ids: (0, i)),
        scratch_shapes=[
            pltpu.VMEM((rows * pieces, total), jnp.bfloat16),
            pltpu.VMEM((total, block), jnp.bfloat16),
        ],
    )
    return pl.pallas_call(
        functools.partial(latents_kernel, pieces),
        grid_spec=grid_spec,
        out_shape=jax.ShapeDtypeStruct((rows * pieces, width), jnp.bfloat16),
        compiler_params=params(24),
        cost_estimate=cost(2 * rows * pieces * total * width, 2 * total * width),
        name="latent_keys_values",
    )(ids, *mine, *theirs, *bands)


def row_chunks(lengths, size):
    chunks, open_chunk, room = [], [], size
    for i, length in enumerate(lengths):
        start = 0
        while start < length:
            take = min(room, length - start)
            open_chunk.append((i, start, start + take))
            start, room = start + take, room - take
            if room == 0:
                chunks.append(open_chunk)
                open_chunk, room = [], size
    return chunks + ([open_chunk] if open_chunk else [])


def decode_kernel(parts, first, last, q_ref, *refs):
    k_refs, v_refs, rest = refs[:parts], refs[parts : 2 * parts], refs[2 * parts :]
    rows = q_ref.shape[0]
    heads = q_ref.shape[1] // HEAD_DIM
    lane = lax.broadcasted_iota(jnp.int32, (rows, LANES), 1)
    lse_all = jnp.zeros((rows, LANES), jnp.float32)

    def gathered(sources, chunk, cols):
        rows = [sources[i][start:stop, cols] for i, start, stop in chunk]
        return rows[0] if len(rows) == 1 else jnp.concatenate(rows)

    for h in range(heads):
        cols = slice(h * HEAD_DIM, (h + 1) * HEAD_DIM)
        top = acc = None
        if not first:
            top = jnp.max(
                jnp.where(lane % heads == h, rest[1][...], -jnp.inf), axis=1, keepdims=True
            )
            acc = jnp.concatenate([rest[0][:, cols], jnp.ones((rows, LANES), jnp.float32)], axis=1)
        for chunk in row_chunks([k.shape[0] for k in k_refs], 512):
            keys, values = gathered(k_refs, chunk, cols), gathered(v_refs, chunk, cols)
            scores = lax.dot_general(q_ref[:, cols], keys, NT, preferred_element_type=jnp.float32)
            scores = scores * EXP2_SCALE
            new_top = jnp.max(scores, axis=1, keepdims=True)
            if top is not None:
                new_top = jnp.maximum(top, new_top)
            weights = jnp.exp2(scores - new_top).astype(jnp.bfloat16)
            summed = jnp.dot(
                weights,
                jnp.concatenate([values, jnp.ones((keys.shape[0], LANES), jnp.bfloat16)], axis=1),
                preferred_element_type=jnp.float32,
            )
            if top is not None:
                summed = summed + acc * jnp.exp2(top - new_top)
            top, acc = new_top, summed
        totals = acc[:, HEAD_DIM:]
        out_ref = rest[-1] if last else rest[-2]
        out_ref[:, cols] = (acc[:, :HEAD_DIM] / totals).astype(out_ref.dtype)
        if not last:
            lse_all = jnp.where(lane % heads == h, top + jnp.log2(totals), lse_all)
    if not last:
        rest[-1][...] = lse_all


def decode(queries, keys_values, state, out_type):
    first, last = state is None, out_type is not None
    tokens, width = queries.shape
    latents = sum(v.shape[0] for v in keys_values)
    pair = min(2 * HEAD_DIM, width)
    steps = width // pair
    narrow = pl.BlockSpec((tokens, pair), lambda i: (0, i))
    sums = pl.BlockSpec((tokens, LANES), lambda i: (0, i))
    keys = [pl.BlockSpec((v.shape[0], pair), lambda i: (0, i)) for v in keys_values]
    values = [pl.BlockSpec((v.shape[0], pair), lambda i: (0, steps + i)) for v in keys_values]
    if last:
        out_specs, out_shape = narrow, jax.ShapeDtypeStruct((tokens, width), out_type)
    else:
        out_specs = [narrow, sums]
        out_shape = [
            jax.ShapeDtypeStruct((tokens, width), jnp.float32),
            jax.ShapeDtypeStruct((tokens, steps * LANES), jnp.float32),
        ]
    return pl.pallas_call(
        functools.partial(decode_kernel, len(keys_values), first, last),
        grid=(steps,),
        in_specs=[narrow, *keys, *values, *([] if first else [narrow, sums])],
        out_specs=out_specs,
        out_shape=out_shape,
        compiler_params=params(BIG),
        cost_estimate=cost(
            16 * tokens * latents * width,
            4 * latents * width + 6 * tokens * width,
            tokens * latents * (width // HEAD_DIM),
        ),
        name="decode_rows",
    )(queries, *keys_values, *keys_values, *([] if first else state))


def swap_perm(size):
    return [(i, i ^ 1) for i in range(size)]


def shift_perm(size, k):
    far = size // 2
    return [(((z + k) % far) * 2 + y, z * 2 + y) for z in range(far) for y in range(2)]


def hop_perm(size, step, way):
    far = size // 2
    moves = [(z, z + 1) for z in range(step - 1, far - 1)]
    if way < 0:
        moves = [(far - 1 - a, far - 1 - b) for a, b in moves]
    return [(a * 2 + y, b * 2 + y) for a, b in moves for y in range(2)]


def fast_on_device(
    sizes,
    enc_keys,
    enc_values,
    input_ids,
    latent_queries,
    latent_array,
    w_out,
    norm_gain,
    w_key,
    w_value,
    query_features,
    query_ids,
    query_table,
    enc_bias,
    query_counts,
):
    groups, pos = sizes
    p = lax.axis_index("pos")
    place = lax.axis_index("head")
    rows = latent_array.shape[0]
    tokens, half_width = enc_keys.shape
    heads = half_width // HEAD_DIM
    mods = enc_bias.shape[0]
    modality = jnp.arange(mods, dtype=jnp.int32)
    far, z, y, x = pos // 2, p // 2, p % 2, lax.axis_index("groups") % 2
    near = swap_perm(pos)

    def over_groups(value):
        return lax.ppermute(value, "groups", swap_perm(groups))

    def over_near(value):
        return lax.ppermute(value, "pos", near)

    def over_far(value, k):
        return lax.ppermute(value, "pos", shift_perm(pos, k))

    def hop(step, pair):
        return [
            lax.ppermute(v, "pos", hop_perm(pos, step, way)) for v, way in zip(pair, (1, -1))
        ]

    def by_shift(hops, k):
        return jnp.where(z + k < far, hops[k][1], hops[far - k][0])

    q_onehot = (query_ids[:, None] == modality[None, :]).astype(jnp.int32)
    local_counts = jnp.sum(q_onehot, axis=0)

    def columns(arrays, which):
        part = half_width // 2
        return jnp.concatenate(
            [lax.dynamic_slice_in_dim(v, which * part, part, 1) for v in arrays], axis=1
        )

    extra = jnp.pad(input_ids[None, :], ((0, EXTRA - 1), (0, half_width - tokens)))
    extra = extra.astype(jnp.bfloat16)
    near_inputs = over_near(
        jnp.concatenate([columns((enc_keys, enc_values), 1 - y), extra], axis=0)
    )

    out_half, out_cols = w_out.shape[0] // 2, w_out.shape[1]
    counted = jnp.concatenate([local_counts // 16, local_counts % 16])
    counted = jnp.pad(counted[None, :], ((0, EXTRA - 1), (0, out_cols - 2 * mods)))
    counted = counted.astype(jnp.bfloat16)

    out_sent = jnp.concatenate(
        [lax.dynamic_slice_in_dim(w_out, x * out_half, out_half, 0), counted]
    )
    out_far = [over_far(out_sent, k) for k in range(1, far)]
    places = [((z + k) % far) * 2 + (y ^ j) for j in range(2) for k in range(far)]
    kv_for_near = columns((w_key, w_value), 1 - y)
    near_inputs, out_far, kv_for_near = lax.optimization_barrier(
        (near_inputs, out_far, kv_for_near)
    )

    kv_own = columns((w_key, w_value), y)
    kv_near = over_near(kv_for_near)

    head_bias = lax.dynamic_slice_in_dim(enc_bias, y * (heads // 2), heads // 2, 1)
    parts = encode(
        y, latent_queries, enc_keys, enc_values, extra, near_inputs, head_bias, 2 * rows
    )
    kv_near, out_far, parts = lax.optimization_barrier((kv_near, out_far, parts))
    kv_sent = jnp.where(x == 0, kv_own, kv_near)
    hops = {0: [kv_sent, kv_sent]}
    hops[1] = hop(1, hops[0])
    early = [k for k in range(1, far) if max(k, far - k) < 3]
    rest = [k for k in range(1, far) if k not in early]
    out_far = jnp.concatenate(out_far)
    out_far_other = over_groups(out_far)
    out_near = over_near(jnp.concatenate([w_out, counted, out_far]))
    out_near_other = over_groups(out_near[w_out.shape[0] + EXTRA :])
    columns_of_slice = [[2 * i + j for i in range(far)] for j in range(2)]
    parts = lax.all_to_all(parts, "pos", 0, 0, axis_index_groups=columns_of_slice, tiled=True)

    def kept_queries():
        far_counts = out_far.reshape(far - 1, out_half + EXTRA, out_cols)[:, out_half, : 2 * mods]
        near_counts = out_near.reshape(-1, EXTRA, out_cols)[:, 0, : 2 * mods]
        at = [w_out.shape[0] // EXTRA]
        at += [at[0] + k * (out_half // EXTRA + 1) for k in range(1, far)]
        near_counts = jnp.concatenate([near_counts[i : i + 1] for i in at])
        counts = jnp.concatenate([counted[:1, : 2 * mods], far_counts, near_counts])
        counts = counts.astype(jnp.int32)
        counts = counts[:, :mods] * 16 + counts[:, mods:]
        earlier = jnp.stack(places)[:, None] < p
        before = jnp.sum(jnp.where(earlier, counts, 0), axis=0)
        within = jnp.cumsum(q_onehot, axis=0) - q_onehot
        ranked = jnp.sum((within + before[None, :]) * q_onehot, axis=1)
        limits = jnp.sum(q_onehot * query_counts[None, :], axis=1)
        return ranked < limits

    lookup = jnp.dot(q_onehot.astype(jnp.bfloat16), query_table, preferred_element_type=jnp.float32)
    queries = (query_features.astype(jnp.float32) + lookup).astype(jnp.bfloat16)
    own_queries = columns((queries,), y)
    near_queries = over_near(columns((queries,), 1 - y))

    parts, out_near, out_far_other, out_near_other, near_queries = lax.optimization_barrier(
        (parts, out_near, out_far_other, out_near_other, near_queries)
    )
    attended, for_near = merge(y, parts, far)
    _, hops = lax.optimization_barrier((for_near, hops))
    hops[2] = hop(2, hops[1])
    from_near = over_near(for_near)
    kept = kept_queries()
    out_ids = jnp.stack([*places, y, x]).astype(jnp.int32)
    weights = [w_out, out_far, out_far_other, out_near, out_near_other]
    partial_value = project(out_ids, attended, from_near, weights)
    partial_value, hops = lax.optimization_barrier((partial_value, hops))
    kv_bands = [kv_own, kv_near]
    for k in early:
        kv_moved = by_shift(hops, k)
        kv_bands += [kv_moved, over_groups(kv_moved)]
    for step in range(3, far):
        hops[step] = hop(step, hops[step - 1])
    theirs = lax.ppermute(partial_value, "head", swap_perm(2))
    own_cols, normed, normed_other = normalise(
        place, partial_value, theirs, latent_array, norm_gain[None, :]
    )
    kv_at = [p, p ^ 1]
    for k in early + rest:
        kv_at += [((z + k) % far) * 2 + (y ^ other) for other in (x, 1 - x)]
    kv_ids = jnp.stack([place, *kv_at]).astype(jnp.int32)

    def cores(values):
        return [lax.ppermute(v, "head", swap_perm(2)) for v in values]

    def fold(mine, other):
        return latent_keys_values(kv_ids, mine, other, kv_bands)

    def arrival(hops, j):
        picked = None
        for at in range(far):
            came = [
                (step, way)
                for step in range(1, far)
                for way in (1, 0)
                if (at + step < far if way else at >= step)
            ]
            step, way = came[j - 1]
            value = hops[step][way]
            picked = value if picked is None else jnp.where(z == at, value, picked)
        return picked

    came = {0: [normed, normed]}
    came[1] = hop(1, came[0])
    normed_near = over_near(normed)
    came, hops, kv_bands, kept = lax.optimization_barrier((came, hops, kv_bands, kept))
    mine, other, keys_values = [normed, normed_near], [normed_other], []
    for step in range(1, far):
        fresh = arrival(came, step)
        fresh_near = over_near(fresh)
        if step + 1 < far:
            came[step + 1] = hop(step + 1, came[step])
            k = rest[step - 1]
            kv_moved = by_shift(hops, k)
            kv_bands += [kv_moved, over_groups(kv_moved)]
            if step > 1:
                keys_values.append(fold(mine, other))
                mine, other = [], []
            came, mine, other, kv_bands, keys_values, fresh, fresh_near = (
                lax.optimization_barrier(
                    (came, mine, other, kv_bands, keys_values, fresh, fresh_near)
                )
            )
            if step == 1:
                mine += [fresh, fresh_near]
                other += cores(mine[1:])
            else:
                mine += [fresh, fresh_near]
                other += cores([fresh, fresh_near])
    keys_values.append(fold([*mine, fresh], [*other, *cores([fresh])]))
    near_state = decode(near_queries, keys_values, None, None)
    fresh_near, keys_values, near_state = lax.optimization_barrier(
        (fresh_near, keys_values, near_state)
    )
    keys_values.append(fold([fresh_near], cores([fresh_near])))
    near_state = decode(near_queries, keys_values[-1:], near_state, jnp.bfloat16)
    own_state = decode(own_queries, keys_values, None, jnp.float32)
    from_near = lax.ppermute(near_state, "pos", near).astype(jnp.float32)
    decoded = jnp.where(
        y == 0,
        jnp.concatenate([own_state, from_near], axis=1),
        jnp.concatenate([from_near, own_state], axis=1),
    )
    decoded = jnp.where(kept[:, None], decoded, 0.0)
    return (own_cols, decoded)


def on_device(sizes, *args):
    groups, pos, head = sizes
    enc_keys, latent_array, w_out, w_key = args[0], args[4], args[5], args[7]
    fits = (
        head == 2
        and pos % 2 == 0
        and pos > 4
        and groups % 2 == 0
        and enc_keys.shape[1] % (4 * HEAD_DIM) == 0
        and 3 * enc_keys.shape[1] <= 2 * HEAD_DIM * EXTRA
        and enc_keys.shape[0] % LANES == 0
        and enc_keys.shape[0] <= enc_keys.shape[1]
        and w_key.shape[0] % LANES == 0
        and w_out.shape[0] % (2 * LANES) == 0
        and w_out.shape[1] % LANES == 0
        and latent_array.shape[0] % LANES == 0
    )
    if fits:
        return fast_on_device((groups, pos), *args)
    return plain_on_device(*args)


def solution(mesh):
    return jax.shard_map(
        functools.partial(on_device, tuple(mesh.shape[a] for a in ("groups", "pos", "head"))),
        mesh=mesh,
        in_specs=(
            P(("groups", "pos"), "head"),
            P(("groups", "pos"), "head"),
            P(("groups", "pos")),
            P("groups", "head"),
            P(("groups", "pos"), None),
            P("head", "pos"),
            P(),
            P("pos", "head"),
            P("pos", "head"),
            P(("groups", "pos"), "head"),
            P(("groups", "pos")),
            P(None, "head"),
            P(None, "head"),
            P("groups"),
        ),
        out_specs=(P(("groups", "pos"), "head"), P(("groups", "pos"), "head")),
        check_vma=False,
    )
```

```python
import functools

import jax
import jax.numpy as jnp
from jax import lax
from jax.experimental import pallas as pl
from jax.experimental.pallas import tpu as pltpu
from jax.sharding import PartitionSpec as P

HEAD_DIM = 128


norm_eps = 1e-06


def prefix(shard, axis, combine, identity):
    peers, place = (lax.axis_size(axis), lax.axis_index(axis))
    everything = lax.all_gather(shard, axis)
    start = jnp.broadcast_to(jnp.asarray(identity, shard.dtype), shard.shape)

    def step(k, before):
        reached = k < place
        new = combine(before, everything[k])
        return jnp.where(reached, new, before)

    return lax.fori_loop(0, peers, step, start)


def plain_on_device(
    enc_keys,
    enc_values,
    input_ids,
    latent_queries,
    latent_array,
    w_out,
    norm_gain,
    w_key,
    w_value,
    query_features,
    query_ids,
    query_table,
    enc_bias,
    query_counts,
):
    tok_rows = enc_keys.shape[0]
    half_width = enc_keys.shape[1]
    local_heads = half_width // HEAD_DIM
    score_scale = HEAD_DIM ** (-0.5)
    modality = jnp.arange(enc_bias.shape[0], dtype=jnp.int32)
    in_onehot = (input_ids[:, None] == modality[None, :]).astype(jnp.float32)
    bias_rows = jnp.dot(in_onehot, enc_bias, precision=lax.Precision.HIGHEST)
    bias_heads = bias_rows.T[:, None, :]
    keys_split = enc_keys.reshape(tok_rows, local_heads, HEAD_DIM)
    values_split = enc_values.reshape(tok_rows, local_heads, HEAD_DIM)
    lat_total = latent_queries.shape[0]
    block_rows = min(512, lat_total)
    query_blocks = latent_queries.reshape(
        lat_total // block_rows, block_rows, local_heads, HEAD_DIM
    )

    def encode_block(block_queries):
        scores = (
            jnp.einsum(
                "nha,tha->hnt", block_queries, keys_split, preferred_element_type=jnp.float32
            )
            * score_scale
            + bias_heads
        )
        highest = jnp.max(scores, axis=2)
        weights = jnp.exp(scores - highest[:, :, None])
        totals = jnp.sum(weights, axis=2)
        summed = jnp.einsum(
            "hnt,tha->nha",
            weights.astype(jnp.bfloat16),
            values_split,
            preferred_element_type=jnp.float32,
        )
        return (highest.T, totals.T, summed.reshape(block_rows, half_width))

    block_max, block_tot, block_acc = lax.map(encode_block, query_blocks)
    row_highest = block_max.reshape(lat_total, local_heads)
    row_totals = block_tot.reshape(lat_total, local_heads)
    row_sums = block_acc.reshape(lat_total, half_width)
    own_rows = latent_array.shape[0]
    global_max = lax.pmax(row_highest, "pos")
    factor = jnp.exp(row_highest - global_max)
    scaled_sums = (row_sums.reshape(lat_total, local_heads, HEAD_DIM) * factor[:, :, None]).reshape(
        lat_total, half_width
    )
    totals, summed = (
        lax.psum_scatter(row_totals * factor, "pos", scatter_dimension=0, tiled=True),
        lax.psum_scatter(scaled_sums, "pos", scatter_dimension=0, tiled=True),
    )
    summed = summed.reshape(own_rows, local_heads, HEAD_DIM)
    attended = (summed / totals[:, :, None]).reshape(own_rows, half_width).astype(jnp.bfloat16)
    partial_value = jnp.dot(
        attended,
        lax.all_gather(w_out, "pos", axis=1, tiled=True),
        preferred_element_type=jnp.float32,
    )
    offset = lax.axis_index("head") * half_width
    projected = lax.psum(partial_value, "head")
    updated = latent_array.astype(jnp.float32) + projected
    mean_square = jnp.mean(updated * updated, axis=1, keepdims=True)
    normed_full = updated * lax.rsqrt(mean_square + norm_eps) * norm_gain
    normed = normed_full.astype(jnp.bfloat16)
    own_cols = lax.dynamic_slice_in_dim(normed_full, offset, half_width, 1)
    pieces = (
        lax.all_gather(w_key, "pos", axis=0, tiled=True),
        lax.all_gather(w_value, "pos", axis=0, tiled=True),
    )
    key_sum = jnp.dot(normed, pieces[0], preferred_element_type=jnp.float32)
    value_sum = jnp.dot(normed, pieces[1], preferred_element_type=jnp.float32)
    latent_keys = key_sum.astype(jnp.bfloat16)
    latent_values = value_sum.astype(jnp.bfloat16)
    q_onehot = (query_ids[:, None] == modality[None, :]).astype(jnp.int32)
    local_counts = jnp.sum(q_onehot, axis=0)
    before = prefix(
        local_counts, "pos", lambda earlier, later: earlier + later, jnp.zeros_like(local_counts)
    )
    within = jnp.cumsum(q_onehot, axis=0) - q_onehot
    ranked = jnp.sum((within + before[None, :]) * q_onehot, axis=1)
    limits = jnp.sum(q_onehot * query_counts[None, :], axis=1)
    kept_rows = ranked < limits
    lookup = jnp.dot(q_onehot.astype(jnp.bfloat16), query_table, preferred_element_type=jnp.float32)
    queries = (
        (query_features.astype(jnp.float32) + lookup)
        .astype(jnp.bfloat16)
        .reshape(tok_rows, local_heads, HEAD_DIM)
    )

    def fold_rows(running, key_rows, value_rows):
        running_max, running_tot, running_acc = running
        key_heads = key_rows.reshape(key_rows.shape[0], local_heads, HEAD_DIM)
        value_heads = value_rows.reshape(value_rows.shape[0], local_heads, HEAD_DIM)
        scores = (
            jnp.einsum("tha,rha->htr", queries, key_heads, preferred_element_type=jnp.float32)
            * score_scale
        )
        new_max = jnp.maximum(running_max, jnp.max(scores, axis=2))
        fade = jnp.exp(running_max - new_max)
        weights = jnp.exp(scores - new_max[:, :, None])
        new_tot = running_tot * fade + jnp.sum(weights, axis=2)
        new_acc = running_acc * fade[:, :, None] + jnp.einsum(
            "htr,rha->hta",
            weights.astype(jnp.bfloat16),
            value_heads,
            preferred_element_type=jnp.float32,
        )
        return (new_max, new_tot, new_acc)

    start_state = (
        jnp.full((local_heads, tok_rows), -jnp.inf, jnp.float32),
        jnp.zeros((local_heads, tok_rows), jnp.float32),
        jnp.zeros((local_heads, tok_rows, HEAD_DIM), jnp.float32),
    )
    running = start_state
    pieces = (
        lax.all_gather(latent_keys, "pos", axis=0, tiled=True),
        lax.all_gather(latent_values, "pos", axis=0, tiled=True),
    )
    row_count = pieces[0].shape[0]
    key_blocks = pieces[0].reshape(row_count // 512, 512, half_width)
    value_blocks = pieces[1].reshape(row_count // 512, 512, half_width)

    def scan_step(state, pair):
        return (fold_rows(state, pair[0], pair[1]), None)

    running, ignored = lax.scan(scan_step, running, (key_blocks, value_blocks))
    final_max, final_tot, final_acc = running
    dec_heads = final_acc / final_tot[:, :, None]
    dec_rows = jnp.transpose(dec_heads, (1, 0, 2)).reshape(tok_rows, half_width)
    decoded = jnp.where(kept_rows[:, None], dec_rows, 0.0)
    return (own_cols, decoded)


LANES = 128
EXTRA = 16
BIG = 56
LOG2E = 1.4426950408889634
EXP2_SCALE = LOG2E * HEAD_DIM**-0.5
NT = (((1,), (1,)), ((), ()))


def params(mib):
    return pltpu.CompilerParams(vmem_limit_bytes=mib << 20)


def cost(flops, nbytes, exps=0):
    return pl.CostEstimate(flops=int(flops), bytes_accessed=int(nbytes), transcendentals=int(exps))


def whole(shape):
    return pl.BlockSpec(shape, lambda *args: (0,) * len(shape))


def encode_kernel(ids_ref, q_ref, k_ref, v_ref, extra_ref, near_ref, bias_ref, out_ref):
    rows, width = q_ref.shape
    tokens = k_ref.shape[0]
    heads = width // HEAD_DIM
    ones = jnp.ones((tokens, LANES), jnp.bfloat16)
    kinds = [
        extra_ref[...].astype(jnp.float32)[:1, :tokens],
        near_ref[tokens:, :].astype(jnp.float32)[:1, :tokens],
    ]
    lane = lax.broadcasted_iota(jnp.int32, (rows, LANES), 1)
    lse_all = jnp.zeros((rows, LANES), jnp.float32)
    for h in range(heads):
        cols = slice(h * HEAD_DIM, (h + 1) * HEAD_DIM)
        late = slice(width + h * HEAD_DIM, width + (h + 1) * HEAD_DIM)
        pairs = [
            (k_ref[:, cols], v_ref[:, cols]),
            (near_ref[:tokens, cols], near_ref[:tokens, late]),
        ]
        top = acc = None
        for (keys, values), kind in zip(pairs, kinds):
            bias = jnp.zeros_like(kind)
            for m in range(bias_ref.shape[0]):
                bias = jnp.where(kind == m, bias_ref[m, h] * LOG2E, bias)
            scores = lax.dot_general(q_ref[:, cols], keys, NT, preferred_element_type=jnp.float32)
            scores = scores * EXP2_SCALE + bias
            new_top = jnp.max(scores, axis=1, keepdims=True)
            if top is not None:
                new_top = jnp.maximum(top, new_top)
            weights = jnp.exp2(scores - new_top).astype(jnp.bfloat16)
            summed = jnp.dot(
                weights, jnp.concatenate([values, ones], axis=1), preferred_element_type=jnp.float32
            )
            if top is not None:
                summed = summed + acc * jnp.exp2(top - new_top)
            top, acc = new_top, summed
        totals = acc[:, HEAD_DIM:]
        out_ref[:rows, cols] = (acc[:, :HEAD_DIM] / totals).astype(jnp.bfloat16)
        lse_all = jnp.where(lane % heads == h, top + jnp.log2(totals), lse_all)
    lse = lse_all.T[:EXTRA, :]
    high = lse.astype(jnp.bfloat16).astype(jnp.float32)
    mid = (lse - high).astype(jnp.bfloat16).astype(jnp.float32)
    low = lse - high - mid
    row = lax.broadcasted_iota(jnp.int32, lse.shape, 0)
    terms = jnp.where(row < heads, high, jnp.where(row < 2 * heads, mid, low))
    out_ref[rows:, :] = terms.astype(jnp.bfloat16)


def encode(which, queries, keys, values, extra, near, bias, rows):
    tokens = keys.shape[0]
    width = keys.shape[1] // 2
    blocks = queries.shape[0] // rows
    half = pl.BlockSpec((tokens, width), lambda i, ids: (0, ids[0]))
    grid_spec = pltpu.PrefetchScalarGridSpec(
        num_scalar_prefetch=1,
        grid=(blocks,),
        in_specs=[
            pl.BlockSpec((rows, width), lambda i, ids: (i, ids[0])),
            half,
            half,
            whole(extra.shape),
            whole(near.shape),
            pl.BlockSpec(memory_space=pltpu.SMEM),
        ],
        out_specs=pl.BlockSpec((rows + EXTRA, width), lambda i, ids: (i, 0)),
    )
    return pl.pallas_call(
        encode_kernel,
        grid_spec=grid_spec,
        out_shape=jax.ShapeDtypeStruct((blocks * (rows + EXTRA), width), jnp.bfloat16),
        compiler_params=params(BIG),
        cost_estimate=cost(
            16 * blocks * rows * tokens * width, 8 * tokens * width, blocks * rows * tokens * 8
        ),
        name="encode_rows",
    )(which.reshape(1), queries, keys, values, extra, near, bias)


def merge_kernel(count, ids_ref, parts_ref, mine_ref, near_ref, all_ref):
    rows, width = all_ref.shape
    long = rows + EXTRA
    parts = [parts_ref.at[i * long : (i + 1) * long, :] for i in range(count)]
    heads = width // HEAD_DIM
    stats = [v[rows:, :].astype(jnp.float32).T for v in parts]
    for h in range(heads):
        cols = slice(h * HEAD_DIM, (h + 1) * HEAD_DIM)
        lses = [
            s[:, h : h + 1] + s[:, heads + h : heads + h + 1] + s[:, 2 * heads + h : 2 * heads + h + 1]
            for s in stats
        ]
        top = functools.reduce(jnp.maximum, lses)
        factors = [jnp.exp2(v - top) for v in lses]
        inverse = 1.0 / functools.reduce(jnp.add, factors)
        merged = functools.reduce(
            jnp.add,
            [v[:rows, cols].astype(jnp.float32) * (f * inverse) for v, f in zip(parts, factors)],
        )
        all_ref[:, cols] = merged.astype(jnp.bfloat16)
    own = rows // 2
    mine_ref[...] = all_ref[pl.ds(pl.multiple_of(ids_ref[0] * own, own), own), :]
    near_ref[...] = all_ref[pl.ds(pl.multiple_of((1 - ids_ref[0]) * own, own), own), :]


def merge(which, parts, count):
    long, width = parts.shape[0] // count, parts.shape[1]
    rows = long - EXTRA
    grid_spec = pltpu.PrefetchScalarGridSpec(
        num_scalar_prefetch=1,
        grid=(1,),
        in_specs=[whole(parts.shape)],
        out_specs=[whole((rows // 2, width))] * 2,
        scratch_shapes=[pltpu.VMEM((rows, width), jnp.bfloat16)],
    )
    return pl.pallas_call(
        functools.partial(merge_kernel, count),
        grid_spec=grid_spec,
        out_shape=[jax.ShapeDtypeStruct((rows // 2, width), jnp.bfloat16)] * 2,
        compiler_params=params(32),
        cost_estimate=cost(8 * rows * width, 10 * rows * width),
        name="merge_rows",
    )(which.reshape(1), parts)


def project_kernel(far, ids_ref, mine_ref, near_ref, *refs):
    w_ref, far_ref, far_other_ref, near_w_ref, near_other_ref, out_ref, att_ref = refs
    part = mine_ref.shape[1]
    first = ids_ref[2 * far]
    att_ref[:, pl.ds(pl.multiple_of(first * part, part), part)] = mine_ref[...]
    att_ref[:, pl.ds(pl.multiple_of((1 - first) * part, part), part)] = near_ref[...]
    cols = w_ref.shape[1]
    depth = att_ref.shape[1] // 2
    share = ids_ref[2 * far + 1]
    halves = [
        att_ref[:, pl.ds(pl.multiple_of(v * depth, depth), depth)] for v in (share, 1 - share)
    ]

    def place(slot, value):
        out_ref[:, pl.ds(pl.multiple_of(ids_ref[slot] * cols, cols), cols)] = value

    for slot, own_ref in ((0, w_ref), (far, near_w_ref)):
        own = own_ref[: 2 * depth, :]
        place(slot, jnp.dot(att_ref[...], own, preferred_element_type=jnp.float32))
    for k in range(far - 1):
        start = k * (depth + EXTRA)
        band = slice(start, start + depth)
        near_band = slice(start + 2 * depth + EXTRA, start + 3 * depth + EXTRA)
        for slot, weights in (
            (1 + k, (far_ref[band, :], far_other_ref[band, :])),
            (far + 1 + k, (near_w_ref[near_band, :], near_other_ref[band, :])),
        ):
            terms = [
                jnp.dot(v, w, preferred_element_type=jnp.float32) for v, w in zip(halves, weights)
            ]
            place(slot, terms[0] + terms[1])


def project(ids, mine, near, weights):
    rows, part = mine.shape
    far = (ids.shape[0] - 2) // 2
    out_cols = 2 * far * weights[0].shape[1]
    grid_spec = pltpu.PrefetchScalarGridSpec(
        num_scalar_prefetch=1,
        grid=(1,),
        in_specs=[whole(v.shape) for v in (mine, near, *weights)],
        out_specs=whole((rows, out_cols)),
        scratch_shapes=[pltpu.VMEM((rows, 2 * part), jnp.bfloat16)],
    )
    return pl.pallas_call(
        functools.partial(project_kernel, far),
        grid_spec=grid_spec,
        out_shape=jax.ShapeDtypeStruct((rows, out_cols), jnp.float32),
        compiler_params=params(BIG),
        cost_estimate=cost(4 * rows * part * out_cols, 4 * part * out_cols + 4 * rows * out_cols),
        name="project_rows",
    )(ids, mine, near, *weights)


def norm_kernel(
    ids_ref, mine_ref, theirs_ref, latent_ref, gain_ref, out_ref, normed_ref, other_ref, full_ref
):
    updated = latent_ref[...].astype(jnp.float32) + (mine_ref[...] + theirs_ref[...])
    mean_square = jnp.mean(updated * updated, axis=1, keepdims=True)
    full_ref[...] = updated * lax.rsqrt(mean_square + norm_eps) * gain_ref[...]
    half = out_ref.shape[1]
    own = full_ref[:, pl.ds(pl.multiple_of(ids_ref[0] * half, half), half)]
    out_ref[...] = own
    normed_ref[...] = own.astype(jnp.bfloat16)
    other = full_ref[:, pl.ds(pl.multiple_of((1 - ids_ref[0]) * half, half), half)]
    other_ref[...] = other.astype(jnp.bfloat16)


def normalise(place, mine, theirs, latent_array, gain):
    rows, width = mine.shape
    half = width // 2
    grid_spec = pltpu.PrefetchScalarGridSpec(
        num_scalar_prefetch=1,
        grid=(1,),
        in_specs=[whole((rows, width))] * 3 + [whole((1, width))],
        out_specs=[whole((rows, half))] * 3,
        scratch_shapes=[pltpu.VMEM((rows, width), jnp.float32)],
    )
    return pl.pallas_call(
        norm_kernel,
        grid_spec=grid_spec,
        out_shape=[
            jax.ShapeDtypeStruct((rows, half), jnp.float32),
            jax.ShapeDtypeStruct((rows, half), jnp.bfloat16),
            jax.ShapeDtypeStruct((rows, half), jnp.bfloat16),
        ],
        compiler_params=params(BIG),
        cost_estimate=cost(6 * rows * width, 13 * rows * width),
        name="norm_rows",
    )(place.reshape(1), mine, theirs, latent_array, gain)


def latents_kernel(pieces, ids_ref, *refs):
    mine, theirs = refs[:pieces], refs[pieces : 2 * pieces]
    w_refs, (out_ref, normed_ref, w_ref) = refs[2 * pieces : -3], refs[-3:]
    rows, half = mine[0].shape
    slots = ids_ref.shape[0] - 1
    depth = 2 * half // slots

    @pl.when(pl.program_id(0) == 0)
    def arrange():
        for j in range(slots):
            at = ids_ref[1 + j]
            start = pl.multiple_of((at % (slots // 2)) * depth, depth)

            def copy(pieces):
                for r, piece in enumerate(pieces):
                    normed_ref[r * rows : (r + 1) * rows, j * depth : (j + 1) * depth] = piece[
                        :, pl.ds(start, depth)
                    ]

            is_mine = at // (slots // 2) == ids_ref[0]
            pl.when(is_mine)(functools.partial(copy, mine))
            pl.when(jnp.logical_not(is_mine))(functools.partial(copy, theirs))

    start, block = 0, w_ref.shape[1]
    for band in w_refs:
        columns = pl.ds(pl.multiple_of(pl.program_id(0) * block, block), block)
        w_ref[start : start + band.shape[0], :] = band[:, columns]
        start += band.shape[0]
    out_ref[...] = jnp.dot(
        normed_ref[...], w_ref[...], preferred_element_type=jnp.float32
    ).astype(jnp.bfloat16)


def latent_keys_values(ids, mine, theirs, bands):
    pieces = len(mine)
    rows, half = mine[0].shape
    width = bands[0].shape[1]
    block = min(512, width)
    total = sum(band.shape[0] for band in bands)
    grid_spec = pltpu.PrefetchScalarGridSpec(
        num_scalar_prefetch=1,
        grid=(width // block,),
        in_specs=[pl.BlockSpec(memory_space=pltpu.VMEM)] * (2 * pieces + len(bands)),
        out_specs=pl.BlockSpec((rows * pieces, block), lambda i, ids: (0, i)),
        scratch_shapes=[
            pltpu.VMEM((rows * pieces, total), jnp.bfloat16),
            pltpu.VMEM((total, block), jnp.bfloat16),
        ],
    )
    return pl.pallas_call(
        functools.partial(latents_kernel, pieces),
        grid_spec=grid_spec,
        out_shape=jax.ShapeDtypeStruct((rows * pieces, width), jnp.bfloat16),
        compiler_params=params(24),
        cost_estimate=cost(2 * rows * pieces * total * width, 2 * total * width),
        name="latent_keys_values",
    )(ids, *mine, *theirs, *bands)


def row_chunks(lengths, size):
    chunks, open_chunk, room = [], [], size
    for i, length in enumerate(lengths):
        start = 0
        while start < length:
            take = min(room, length - start)
            open_chunk.append((i, start, start + take))
            start, room = start + take, room - take
            if room == 0:
                chunks.append(open_chunk)
                open_chunk, room = [], size
    return chunks + ([open_chunk] if open_chunk else [])


def decode_kernel(parts, first, last, q_ref, *refs):
    k_refs, v_refs, rest = refs[:parts], refs[parts : 2 * parts], refs[2 * parts :]
    rows = q_ref.shape[0]
    heads = q_ref.shape[1] // HEAD_DIM
    lane = lax.broadcasted_iota(jnp.int32, (rows, LANES), 1)
    lse_all = jnp.zeros((rows, LANES), jnp.float32)

    def gathered(sources, chunk, cols):
        rows = [sources[i][start:stop, cols] for i, start, stop in chunk]
        return rows[0] if len(rows) == 1 else jnp.concatenate(rows)

    for h in range(heads):
        cols = slice(h * HEAD_DIM, (h + 1) * HEAD_DIM)
        top = acc = None
        if not first:
            top = jnp.max(
                jnp.where(lane % heads == h, rest[1][...], -jnp.inf), axis=1, keepdims=True
            )
            acc = jnp.concatenate([rest[0][:, cols], jnp.ones((rows, LANES), jnp.float32)], axis=1)
        for chunk in row_chunks([k.shape[0] for k in k_refs], 512):
            keys, values = gathered(k_refs, chunk, cols), gathered(v_refs, chunk, cols)
            scores = lax.dot_general(q_ref[:, cols], keys, NT, preferred_element_type=jnp.float32)
            scores = scores * EXP2_SCALE
            new_top = jnp.max(scores, axis=1, keepdims=True)
            if top is not None:
                new_top = jnp.maximum(top, new_top)
            weights = jnp.exp2(scores - new_top).astype(jnp.bfloat16)
            summed = jnp.dot(
                weights,
                jnp.concatenate([values, jnp.ones((keys.shape[0], LANES), jnp.bfloat16)], axis=1),
                preferred_element_type=jnp.float32,
            )
            if top is not None:
                summed = summed + acc * jnp.exp2(top - new_top)
            top, acc = new_top, summed
        totals = acc[:, HEAD_DIM:]
        out_ref = rest[-1] if last else rest[-2]
        out_ref[:, cols] = (acc[:, :HEAD_DIM] / totals).astype(out_ref.dtype)
        if not last:
            lse_all = jnp.where(lane % heads == h, top + jnp.log2(totals), lse_all)
    if not last:
        rest[-1][...] = lse_all


def decode(queries, keys_values, state, out_type):
    first, last = state is None, out_type is not None
    tokens, width = queries.shape
    latents = sum(v.shape[0] for v in keys_values)
    pair = min(2 * HEAD_DIM, width)
    steps = width // pair
    narrow = pl.BlockSpec((tokens, pair), lambda i: (0, i))
    sums = pl.BlockSpec((tokens, LANES), lambda i: (0, i))
    keys = [pl.BlockSpec((v.shape[0], pair), lambda i: (0, i)) for v in keys_values]
    values = [pl.BlockSpec((v.shape[0], pair), lambda i: (0, steps + i)) for v in keys_values]
    if last:
        out_specs, out_shape = narrow, jax.ShapeDtypeStruct((tokens, width), out_type)
    else:
        out_specs = [narrow, sums]
        out_shape = [
            jax.ShapeDtypeStruct((tokens, width), jnp.float32),
            jax.ShapeDtypeStruct((tokens, steps * LANES), jnp.float32),
        ]
    return pl.pallas_call(
        functools.partial(decode_kernel, len(keys_values), first, last),
        grid=(steps,),
        in_specs=[narrow, *keys, *values, *([] if first else [narrow, sums])],
        out_specs=out_specs,
        out_shape=out_shape,
        compiler_params=params(BIG),
        cost_estimate=cost(
            16 * tokens * latents * width,
            4 * latents * width + 6 * tokens * width,
            tokens * latents * (width // HEAD_DIM),
        ),
        name="decode_rows",
    )(queries, *keys_values, *keys_values, *([] if first else state))


def swap_perm(size):
    return [(i, i ^ 1) for i in range(size)]


def shift_perm(size, k):
    far = size // 2
    return [(((z + k) % far) * 2 + y, z * 2 + y) for z in range(far) for y in range(2)]


def hop_perm(size, step, way):
    far = size // 2
    moves = [(z, z + 1) for z in range(step - 1, far - 1)]
    if way < 0:
        moves = [(far - 1 - a, far - 1 - b) for a, b in moves]
    return [(a * 2 + y, b * 2 + y) for a, b in moves for y in range(2)]


def fast_on_device(
    sizes,
    enc_keys,
    enc_values,
    input_ids,
    latent_queries,
    latent_array,
    w_out,
    norm_gain,
    w_key,
    w_value,
    query_features,
    query_ids,
    query_table,
    enc_bias,
    query_counts,
):
    groups, pos = sizes
    p = lax.axis_index("pos")
    place = lax.axis_index("head")
    rows = latent_array.shape[0]
    tokens, half_width = enc_keys.shape
    heads = half_width // HEAD_DIM
    mods = enc_bias.shape[0]
    modality = jnp.arange(mods, dtype=jnp.int32)
    far, z, y, x = pos // 2, p // 2, p % 2, lax.axis_index("groups") % 2
    near = swap_perm(pos)

    def over_groups(value):
        return lax.ppermute(value, "groups", swap_perm(groups))

    def over_near(value):
        return lax.ppermute(value, "pos", near)

    def over_far(value, k):
        return lax.ppermute(value, "pos", shift_perm(pos, k))

    def hop(step, pair):
        return [
            lax.ppermute(v, "pos", hop_perm(pos, step, way)) for v, way in zip(pair, (1, -1))
        ]

    def by_shift(hops, k):
        return jnp.where(z + k < far, hops[k][1], hops[far - k][0])

    q_onehot = (query_ids[:, None] == modality[None, :]).astype(jnp.int32)
    local_counts = jnp.sum(q_onehot, axis=0)

    def columns(arrays, which):
        part = half_width // 2
        return jnp.concatenate(
            [lax.dynamic_slice_in_dim(v, which * part, part, 1) for v in arrays], axis=1
        )

    extra = jnp.pad(input_ids[None, :], ((0, EXTRA - 1), (0, half_width - tokens)))
    extra = extra.astype(jnp.bfloat16)
    near_inputs = over_near(
        jnp.concatenate([columns((enc_keys, enc_values), 1 - y), extra], axis=0)
    )

    out_half, out_cols = w_out.shape[0] // 2, w_out.shape[1]
    counted = jnp.concatenate([local_counts // 16, local_counts % 16])
    counted = jnp.pad(counted[None, :], ((0, EXTRA - 1), (0, out_cols - 2 * mods)))
    counted = counted.astype(jnp.bfloat16)

    out_sent = jnp.concatenate(
        [lax.dynamic_slice_in_dim(w_out, x * out_half, out_half, 0), counted]
    )
    out_far = [over_far(out_sent, k) for k in range(1, far)]
    places = [((z + k) % far) * 2 + (y ^ j) for j in range(2) for k in range(far)]
    kv_for_near = columns((w_key, w_value), 1 - y)
    near_inputs, out_far, kv_for_near = lax.optimization_barrier(
        (near_inputs, out_far, kv_for_near)
    )

    kv_own = columns((w_key, w_value), y)
    kv_near = over_near(kv_for_near)

    head_bias = lax.dynamic_slice_in_dim(enc_bias, y * (heads // 2), heads // 2, 1)
    parts = encode(
        y, latent_queries, enc_keys, enc_values, extra, near_inputs, head_bias, 2 * rows
    )
    kv_near, out_far, parts = lax.optimization_barrier((kv_near, out_far, parts))
    kv_sent = jnp.where(x == 0, kv_own, kv_near)
    hops = {0: [kv_sent, kv_sent]}
    hops[1] = hop(1, hops[0])
    early = [k for k in range(1, far) if max(k, far - k) < 3]
    rest = [k for k in range(1, far) if k not in early]
    out_far = jnp.concatenate(out_far)
    out_far_other = over_groups(out_far)
    out_near = over_near(jnp.concatenate([w_out, counted, out_far]))
    out_near_other = over_groups(out_near[w_out.shape[0] + EXTRA :])
    columns_of_slice = [[2 * i + j for i in range(far)] for j in range(2)]
    parts = lax.all_to_all(parts, "pos", 0, 0, axis_index_groups=columns_of_slice, tiled=True)

    def kept_queries():
        far_counts = out_far.reshape(far - 1, out_half + EXTRA, out_cols)[:, out_half, : 2 * mods]
        near_counts = out_near.reshape(-1, EXTRA, out_cols)[:, 0, : 2 * mods]
        at = [w_out.shape[0] // EXTRA]
        at += [at[0] + k * (out_half // EXTRA + 1) for k in range(1, far)]
        near_counts = jnp.concatenate([near_counts[i : i + 1] for i in at])
        counts = jnp.concatenate([counted[:1, : 2 * mods], far_counts, near_counts])
        counts = counts.astype(jnp.int32)
        counts = counts[:, :mods] * 16 + counts[:, mods:]
        earlier = jnp.stack(places)[:, None] < p
        before = jnp.sum(jnp.where(earlier, counts, 0), axis=0)
        within = jnp.cumsum(q_onehot, axis=0) - q_onehot
        ranked = jnp.sum((within + before[None, :]) * q_onehot, axis=1)
        limits = jnp.sum(q_onehot * query_counts[None, :], axis=1)
        return ranked < limits

    lookup = jnp.dot(q_onehot.astype(jnp.bfloat16), query_table, preferred_element_type=jnp.float32)
    queries = (query_features.astype(jnp.float32) + lookup).astype(jnp.bfloat16)
    own_queries = columns((queries,), y)
    near_queries = over_near(columns((queries,), 1 - y))

    parts, out_near, out_far_other, out_near_other, near_queries = lax.optimization_barrier(
        (parts, out_near, out_far_other, out_near_other, near_queries)
    )
    attended, for_near = merge(y, parts, far)
    _, hops = lax.optimization_barrier((for_near, hops))
    hops[2] = hop(2, hops[1])
    from_near = over_near(for_near)
    kept = kept_queries()
    out_ids = jnp.stack([*places, y, x]).astype(jnp.int32)
    weights = [w_out, out_far, out_far_other, out_near, out_near_other]
    partial_value = project(out_ids, attended, from_near, weights)
    partial_value, hops = lax.optimization_barrier((partial_value, hops))
    kv_bands = [kv_own, kv_near]
    for k in early:
        kv_moved = by_shift(hops, k)
        kv_bands += [kv_moved, over_groups(kv_moved)]
    for step in range(3, far):
        hops[step] = hop(step, hops[step - 1])
    theirs = lax.ppermute(partial_value, "head", swap_perm(2))
    own_cols, normed, normed_other = normalise(
        place, partial_value, theirs, latent_array, norm_gain[None, :]
    )
    kv_at = [p, p ^ 1]
    for k in early + rest:
        kv_at += [((z + k) % far) * 2 + (y ^ other) for other in (x, 1 - x)]
    kv_ids = jnp.stack([place, *kv_at]).astype(jnp.int32)

    def cores(values):
        return [lax.ppermute(v, "head", swap_perm(2)) for v in values]

    def fold(mine, other):
        return latent_keys_values(kv_ids, mine, other, kv_bands)

    def arrival(hops, j):
        picked = None
        for at in range(far):
            came = [
                (step, way)
                for step in range(1, far)
                for way in (1, 0)
                if (at + step < far if way else at >= step)
            ]
            step, way = came[j - 1]
            value = hops[step][way]
            picked = value if picked is None else jnp.where(z == at, value, picked)
        return picked

    came = {0: [normed, normed]}
    came[1] = hop(1, came[0])
    normed_near = over_near(normed)
    hops, _ = lax.optimization_barrier((hops, normed))
    for k in rest:
        kv_moved = by_shift(hops, k)
        kv_bands += [kv_moved, over_groups(kv_moved)]
    came, kept = lax.optimization_barrier((came, kept))
    mine, other, keys_values = [normed, normed_near], [normed_other], []
    for step in range(1, far):
        fresh = arrival(came, step)
        fresh_near = over_near(fresh)
        if step + 1 < far:
            came[step + 1] = hop(step + 1, came[step])
            if step > 1:
                keys_values.append(fold(mine, other))
                mine, other = [], []
            came, mine, other, kv_bands, keys_values, fresh, fresh_near = (
                lax.optimization_barrier(
                    (came, mine, other, kv_bands, keys_values, fresh, fresh_near)
                )
            )
            if step == 1:
                mine += [fresh, fresh_near]
                other += cores(mine[1:])
            else:
                mine += [fresh, fresh_near]
                other += cores([fresh, fresh_near])
    keys_values.append(fold([*mine, fresh], [*other, *cores([fresh])]))
    near_state = decode(near_queries, keys_values, None, None)
    fresh_near, keys_values, near_state = lax.optimization_barrier(
        (fresh_near, keys_values, near_state)
    )
    keys_values.append(fold([fresh_near], cores([fresh_near])))
    near_state = decode(near_queries, keys_values[-1:], near_state, jnp.bfloat16)
    own_state = decode(own_queries, keys_values, None, jnp.float32)
    from_near = lax.ppermute(near_state, "pos", near).astype(jnp.float32)
    decoded = jnp.where(
        y == 0,
        jnp.concatenate([own_state, from_near], axis=1),
        jnp.concatenate([from_near, own_state], axis=1),
    )
    decoded = jnp.where(kept[:, None], decoded, 0.0)
    return (own_cols, decoded)


def on_device(sizes, *args):
    groups, pos, head = sizes
    enc_keys, latent_array, w_out, w_key = args[0], args[4], args[5], args[7]
    fits = (
        head == 2
        and pos % 2 == 0
        and pos > 4
        and groups % 2 == 0
        and enc_keys.shape[1] % (4 * HEAD_DIM) == 0
        and 3 * enc_keys.shape[1] <= 2 * HEAD_DIM * EXTRA
        and enc_keys.shape[0] % LANES == 0
        and enc_keys.shape[0] <= enc_keys.shape[1]
        and w_key.shape[0] % LANES == 0
        and w_out.shape[0] % (2 * LANES) == 0
        and w_out.shape[1] % LANES == 0
        and latent_array.shape[0] % LANES == 0
    )
    if fits:
        return fast_on_device((groups, pos), *args)
    return plain_on_device(*args)


def solution(mesh):
    return jax.shard_map(
        functools.partial(on_device, tuple(mesh.shape[a] for a in ("groups", "pos", "head"))),
        mesh=mesh,
        in_specs=(
            P(("groups", "pos"), "head"),
            P(("groups", "pos"), "head"),
            P(("groups", "pos")),
            P("groups", "head"),
            P(("groups", "pos"), None),
            P("head", "pos"),
            P(),
            P("pos", "head"),
            P("pos", "head"),
            P(("groups", "pos"), "head"),
            P(("groups", "pos")),
            P(None, "head"),
            P(None, "head"),
            P("groups"),
        ),
        out_specs=(P(("groups", "pos"), "head"), P(("groups", "pos"), "head")),
        check_vma=False,
    )
```

```python
import functools

import jax
import jax.numpy as jnp
from jax import lax
from jax.experimental import pallas as pl
from jax.experimental.pallas import tpu as pltpu
from jax.sharding import PartitionSpec as P

HEAD_DIM = 128


norm_eps = 1e-06


def prefix(shard, axis, combine, identity):
    peers, place = (lax.axis_size(axis), lax.axis_index(axis))
    everything = lax.all_gather(shard, axis)
    start = jnp.broadcast_to(jnp.asarray(identity, shard.dtype), shard.shape)

    def step(k, before):
        reached = k < place
        new = combine(before, everything[k])
        return jnp.where(reached, new, before)

    return lax.fori_loop(0, peers, step, start)


def plain_on_device(
    enc_keys,
    enc_values,
    input_ids,
    latent_queries,
    latent_array,
    w_out,
    norm_gain,
    w_key,
    w_value,
    query_features,
    query_ids,
    query_table,
    enc_bias,
    query_counts,
):
    tok_rows = enc_keys.shape[0]
    half_width = enc_keys.shape[1]
    local_heads = half_width // HEAD_DIM
    score_scale = HEAD_DIM ** (-0.5)
    modality = jnp.arange(enc_bias.shape[0], dtype=jnp.int32)
    in_onehot = (input_ids[:, None] == modality[None, :]).astype(jnp.float32)
    bias_rows = jnp.dot(in_onehot, enc_bias, precision=lax.Precision.HIGHEST)
    bias_heads = bias_rows.T[:, None, :]
    keys_split = enc_keys.reshape(tok_rows, local_heads, HEAD_DIM)
    values_split = enc_values.reshape(tok_rows, local_heads, HEAD_DIM)
    lat_total = latent_queries.shape[0]
    block_rows = min(512, lat_total)
    query_blocks = latent_queries.reshape(
        lat_total // block_rows, block_rows, local_heads, HEAD_DIM
    )

    def encode_block(block_queries):
        scores = (
            jnp.einsum(
                "nha,tha->hnt", block_queries, keys_split, preferred_element_type=jnp.float32
            )
            * score_scale
            + bias_heads
        )
        highest = jnp.max(scores, axis=2)
        weights = jnp.exp(scores - highest[:, :, None])
        totals = jnp.sum(weights, axis=2)
        summed = jnp.einsum(
            "hnt,tha->nha",
            weights.astype(jnp.bfloat16),
            values_split,
            preferred_element_type=jnp.float32,
        )
        return (highest.T, totals.T, summed.reshape(block_rows, half_width))

    block_max, block_tot, block_acc = lax.map(encode_block, query_blocks)
    row_highest = block_max.reshape(lat_total, local_heads)
    row_totals = block_tot.reshape(lat_total, local_heads)
    row_sums = block_acc.reshape(lat_total, half_width)
    own_rows = latent_array.shape[0]
    global_max = lax.pmax(row_highest, "pos")
    factor = jnp.exp(row_highest - global_max)
    scaled_sums = (row_sums.reshape(lat_total, local_heads, HEAD_DIM) * factor[:, :, None]).reshape(
        lat_total, half_width
    )
    totals, summed = (
        lax.psum_scatter(row_totals * factor, "pos", scatter_dimension=0, tiled=True),
        lax.psum_scatter(scaled_sums, "pos", scatter_dimension=0, tiled=True),
    )
    summed = summed.reshape(own_rows, local_heads, HEAD_DIM)
    attended = (summed / totals[:, :, None]).reshape(own_rows, half_width).astype(jnp.bfloat16)
    partial_value = jnp.dot(
        attended,
        lax.all_gather(w_out, "pos", axis=1, tiled=True),
        preferred_element_type=jnp.float32,
    )
    offset = lax.axis_index("head") * half_width
    projected = lax.psum(partial_value, "head")
    updated = latent_array.astype(jnp.float32) + projected
    mean_square = jnp.mean(updated * updated, axis=1, keepdims=True)
    normed_full = updated * lax.rsqrt(mean_square + norm_eps) * norm_gain
    normed = normed_full.astype(jnp.bfloat16)
    own_cols = lax.dynamic_slice_in_dim(normed_full, offset, half_width, 1)
    pieces = (
        lax.all_gather(w_key, "pos", axis=0, tiled=True),
        lax.all_gather(w_value, "pos", axis=0, tiled=True),
    )
    key_sum = jnp.dot(normed, pieces[0], preferred_element_type=jnp.float32)
    value_sum = jnp.dot(normed, pieces[1], preferred_element_type=jnp.float32)
    latent_keys = key_sum.astype(jnp.bfloat16)
    latent_values = value_sum.astype(jnp.bfloat16)
    q_onehot = (query_ids[:, None] == modality[None, :]).astype(jnp.int32)
    local_counts = jnp.sum(q_onehot, axis=0)
    before = prefix(
        local_counts, "pos", lambda earlier, later: earlier + later, jnp.zeros_like(local_counts)
    )
    within = jnp.cumsum(q_onehot, axis=0) - q_onehot
    ranked = jnp.sum((within + before[None, :]) * q_onehot, axis=1)
    limits = jnp.sum(q_onehot * query_counts[None, :], axis=1)
    kept_rows = ranked < limits
    lookup = jnp.dot(q_onehot.astype(jnp.bfloat16), query_table, preferred_element_type=jnp.float32)
    queries = (
        (query_features.astype(jnp.float32) + lookup)
        .astype(jnp.bfloat16)
        .reshape(tok_rows, local_heads, HEAD_DIM)
    )

    def fold_rows(running, key_rows, value_rows):
        running_max, running_tot, running_acc = running
        key_heads = key_rows.reshape(key_rows.shape[0], local_heads, HEAD_DIM)
        value_heads = value_rows.reshape(value_rows.shape[0], local_heads, HEAD_DIM)
        scores = (
            jnp.einsum("tha,rha->htr", queries, key_heads, preferred_element_type=jnp.float32)
            * score_scale
        )
        new_max = jnp.maximum(running_max, jnp.max(scores, axis=2))
        fade = jnp.exp(running_max - new_max)
        weights = jnp.exp(scores - new_max[:, :, None])
        new_tot = running_tot * fade + jnp.sum(weights, axis=2)
        new_acc = running_acc * fade[:, :, None] + jnp.einsum(
            "htr,rha->hta",
            weights.astype(jnp.bfloat16),
            value_heads,
            preferred_element_type=jnp.float32,
        )
        return (new_max, new_tot, new_acc)

    start_state = (
        jnp.full((local_heads, tok_rows), -jnp.inf, jnp.float32),
        jnp.zeros((local_heads, tok_rows), jnp.float32),
        jnp.zeros((local_heads, tok_rows, HEAD_DIM), jnp.float32),
    )
    running = start_state
    pieces = (
        lax.all_gather(latent_keys, "pos", axis=0, tiled=True),
        lax.all_gather(latent_values, "pos", axis=0, tiled=True),
    )
    row_count = pieces[0].shape[0]
    key_blocks = pieces[0].reshape(row_count // 512, 512, half_width)
    value_blocks = pieces[1].reshape(row_count // 512, 512, half_width)

    def scan_step(state, pair):
        return (fold_rows(state, pair[0], pair[1]), None)

    running, ignored = lax.scan(scan_step, running, (key_blocks, value_blocks))
    final_max, final_tot, final_acc = running
    dec_heads = final_acc / final_tot[:, :, None]
    dec_rows = jnp.transpose(dec_heads, (1, 0, 2)).reshape(tok_rows, half_width)
    decoded = jnp.where(kept_rows[:, None], dec_rows, 0.0)
    return (own_cols, decoded)


LANES = 128
EXTRA = 16
BIG = 56
LOG2E = 1.4426950408889634
EXP2_SCALE = LOG2E * HEAD_DIM**-0.5
NT = (((1,), (1,)), ((), ()))


def params(mib):
    return pltpu.CompilerParams(vmem_limit_bytes=mib << 20)


def cost(flops, nbytes, exps=0):
    return pl.CostEstimate(flops=int(flops), bytes_accessed=int(nbytes), transcendentals=int(exps))


def whole(shape):
    return pl.BlockSpec(shape, lambda *args: (0,) * len(shape))


def encode_kernel(ids_ref, q_ref, k_ref, v_ref, extra_ref, near_ref, bias_ref, out_ref):
    rows, width = q_ref.shape
    tokens = k_ref.shape[0]
    heads = width // HEAD_DIM
    ones = jnp.ones((tokens, LANES), jnp.bfloat16)
    kinds = [
        extra_ref[...].astype(jnp.float32)[:1, :tokens],
        near_ref[tokens:, :].astype(jnp.float32)[:1, :tokens],
    ]
    lane = lax.broadcasted_iota(jnp.int32, (rows, LANES), 1)
    lse_all = jnp.zeros((rows, LANES), jnp.float32)
    for h in range(heads):
        cols = slice(h * HEAD_DIM, (h + 1) * HEAD_DIM)
        late = slice(width + h * HEAD_DIM, width + (h + 1) * HEAD_DIM)
        pairs = [
            (k_ref[:, cols], v_ref[:, cols]),
            (near_ref[:tokens, cols], near_ref[:tokens, late]),
        ]
        top = acc = None
        for (keys, values), kind in zip(pairs, kinds):
            bias = jnp.zeros_like(kind)
            for m in range(bias_ref.shape[0]):
                bias = jnp.where(kind == m, bias_ref[m, h] * LOG2E, bias)
            scores = lax.dot_general(q_ref[:, cols], keys, NT, preferred_element_type=jnp.float32)
            scores = scores * EXP2_SCALE + bias
            new_top = jnp.max(scores, axis=1, keepdims=True)
            if top is not None:
                new_top = jnp.maximum(top, new_top)
            weights = jnp.exp2(scores - new_top).astype(jnp.bfloat16)
            summed = jnp.dot(
                weights, jnp.concatenate([values, ones], axis=1), preferred_element_type=jnp.float32
            )
            if top is not None:
                summed = summed + acc * jnp.exp2(top - new_top)
            top, acc = new_top, summed
        totals = acc[:, HEAD_DIM:]
        out_ref[:rows, cols] = (acc[:, :HEAD_DIM] / totals).astype(jnp.bfloat16)
        lse_all = jnp.where(lane % heads == h, top + jnp.log2(totals), lse_all)
    lse = lse_all.T[:EXTRA, :]
    high = lse.astype(jnp.bfloat16).astype(jnp.float32)
    mid = (lse - high).astype(jnp.bfloat16).astype(jnp.float32)
    low = lse - high - mid
    row = lax.broadcasted_iota(jnp.int32, lse.shape, 0)
    terms = jnp.where(row < heads, high, jnp.where(row < 2 * heads, mid, low))
    out_ref[rows:, :] = terms.astype(jnp.bfloat16)


def encode(which, queries, keys, values, extra, near, bias, rows):
    tokens = keys.shape[0]
    width = keys.shape[1] // 2
    blocks = queries.shape[0] // rows
    half = pl.BlockSpec((tokens, width), lambda i, ids: (0, ids[0]))
    grid_spec = pltpu.PrefetchScalarGridSpec(
        num_scalar_prefetch=1,
        grid=(blocks,),
        in_specs=[
            pl.BlockSpec((rows, width), lambda i, ids: (i, ids[0])),
            half,
            half,
            whole(extra.shape),
            whole(near.shape),
            pl.BlockSpec(memory_space=pltpu.SMEM),
        ],
        out_specs=pl.BlockSpec((rows + EXTRA, width), lambda i, ids: (i, 0)),
    )
    return pl.pallas_call(
        encode_kernel,
        grid_spec=grid_spec,
        out_shape=jax.ShapeDtypeStruct((blocks * (rows + EXTRA), width), jnp.bfloat16),
        compiler_params=params(BIG),
        cost_estimate=cost(
            16 * blocks * rows * tokens * width, 8 * tokens * width, blocks * rows * tokens * 8
        ),
        name="encode_rows",
    )(which.reshape(1), queries, keys, values, extra, near, bias)


def merge_kernel(count, ids_ref, parts_ref, mine_ref, near_ref, all_ref):
    rows, width = all_ref.shape
    long = rows + EXTRA
    parts = [parts_ref.at[i * long : (i + 1) * long, :] for i in range(count)]
    heads = width // HEAD_DIM
    stats = [v[rows:, :].astype(jnp.float32).T for v in parts]
    for h in range(heads):
        cols = slice(h * HEAD_DIM, (h + 1) * HEAD_DIM)
        lses = [
            s[:, h : h + 1] + s[:, heads + h : heads + h + 1] + s[:, 2 * heads + h : 2 * heads + h + 1]
            for s in stats
        ]
        top = functools.reduce(jnp.maximum, lses)
        factors = [jnp.exp2(v - top) for v in lses]
        inverse = 1.0 / functools.reduce(jnp.add, factors)
        merged = functools.reduce(
            jnp.add,
            [v[:rows, cols].astype(jnp.float32) * (f * inverse) for v, f in zip(parts, factors)],
        )
        all_ref[:, cols] = merged.astype(jnp.bfloat16)
    own = rows // 2
    mine_ref[...] = all_ref[pl.ds(pl.multiple_of(ids_ref[0] * own, own), own), :]
    near_ref[...] = all_ref[pl.ds(pl.multiple_of((1 - ids_ref[0]) * own, own), own), :]


def merge(which, parts, count):
    long, width = parts.shape[0] // count, parts.shape[1]
    rows = long - EXTRA
    grid_spec = pltpu.PrefetchScalarGridSpec(
        num_scalar_prefetch=1,
        grid=(1,),
        in_specs=[whole(parts.shape)],
        out_specs=[whole((rows // 2, width))] * 2,
        scratch_shapes=[pltpu.VMEM((rows, width), jnp.bfloat16)],
    )
    return pl.pallas_call(
        functools.partial(merge_kernel, count),
        grid_spec=grid_spec,
        out_shape=[jax.ShapeDtypeStruct((rows // 2, width), jnp.bfloat16)] * 2,
        compiler_params=params(32),
        cost_estimate=cost(8 * rows * width, 10 * rows * width),
        name="merge_rows",
    )(which.reshape(1), parts)


def project_kernel(far, ids_ref, mine_ref, near_ref, *refs):
    w_ref, far_ref, far_other_ref, near_w_ref, near_other_ref, out_ref, att_ref = refs
    part = mine_ref.shape[1]
    first = ids_ref[2 * far]
    att_ref[:, pl.ds(pl.multiple_of(first * part, part), part)] = mine_ref[...]
    att_ref[:, pl.ds(pl.multiple_of((1 - first) * part, part), part)] = near_ref[...]
    cols = w_ref.shape[1]
    depth = att_ref.shape[1] // 2
    share = ids_ref[2 * far + 1]
    halves = [
        att_ref[:, pl.ds(pl.multiple_of(v * depth, depth), depth)] for v in (share, 1 - share)
    ]

    def place(slot, value):
        out_ref[:, pl.ds(pl.multiple_of(ids_ref[slot] * cols, cols), cols)] = value

    for slot, own_ref in ((0, w_ref), (far, near_w_ref)):
        own = own_ref[: 2 * depth, :]
        place(slot, jnp.dot(att_ref[...], own, preferred_element_type=jnp.float32))
    for k in range(far - 1):
        start = k * (depth + EXTRA)
        band = slice(start, start + depth)
        near_band = slice(start + 2 * depth + EXTRA, start + 3 * depth + EXTRA)
        for slot, weights in (
            (1 + k, (far_ref[band, :], far_other_ref[band, :])),
            (far + 1 + k, (near_w_ref[near_band, :], near_other_ref[band, :])),
        ):
            terms = [
                jnp.dot(v, w, preferred_element_type=jnp.float32) for v, w in zip(halves, weights)
            ]
            place(slot, terms[0] + terms[1])


def project(ids, mine, near, weights):
    rows, part = mine.shape
    far = (ids.shape[0] - 2) // 2
    out_cols = 2 * far * weights[0].shape[1]
    grid_spec = pltpu.PrefetchScalarGridSpec(
        num_scalar_prefetch=1,
        grid=(1,),
        in_specs=[whole(v.shape) for v in (mine, near, *weights)],
        out_specs=whole((rows, out_cols)),
        scratch_shapes=[pltpu.VMEM((rows, 2 * part), jnp.bfloat16)],
    )
    return pl.pallas_call(
        functools.partial(project_kernel, far),
        grid_spec=grid_spec,
        out_shape=jax.ShapeDtypeStruct((rows, out_cols), jnp.float32),
        compiler_params=params(BIG),
        cost_estimate=cost(4 * rows * part * out_cols, 4 * part * out_cols + 4 * rows * out_cols),
        name="project_rows",
    )(ids, mine, near, *weights)


def norm_kernel(
    ids_ref, mine_ref, theirs_ref, latent_ref, gain_ref, out_ref, normed_ref, other_ref, full_ref
):
    updated = latent_ref[...].astype(jnp.float32) + (mine_ref[...] + theirs_ref[...])
    mean_square = jnp.mean(updated * updated, axis=1, keepdims=True)
    full_ref[...] = updated * lax.rsqrt(mean_square + norm_eps) * gain_ref[...]
    half = out_ref.shape[1]
    own = full_ref[:, pl.ds(pl.multiple_of(ids_ref[0] * half, half), half)]
    out_ref[...] = own
    normed_ref[...] = own.astype(jnp.bfloat16)
    other = full_ref[:, pl.ds(pl.multiple_of((1 - ids_ref[0]) * half, half), half)]
    other_ref[...] = other.astype(jnp.bfloat16)


def normalise(place, mine, theirs, latent_array, gain):
    rows, width = mine.shape
    half = width // 2
    grid_spec = pltpu.PrefetchScalarGridSpec(
        num_scalar_prefetch=1,
        grid=(1,),
        in_specs=[whole((rows, width))] * 3 + [whole((1, width))],
        out_specs=[whole((rows, half))] * 3,
        scratch_shapes=[pltpu.VMEM((rows, width), jnp.float32)],
    )
    return pl.pallas_call(
        norm_kernel,
        grid_spec=grid_spec,
        out_shape=[
            jax.ShapeDtypeStruct((rows, half), jnp.float32),
            jax.ShapeDtypeStruct((rows, half), jnp.bfloat16),
            jax.ShapeDtypeStruct((rows, half), jnp.bfloat16),
        ],
        compiler_params=params(BIG),
        cost_estimate=cost(6 * rows * width, 13 * rows * width),
        name="norm_rows",
    )(place.reshape(1), mine, theirs, latent_array, gain)


def latents_kernel(pieces, ids_ref, *refs):
    mine, theirs = refs[:pieces], refs[pieces : 2 * pieces]
    w_refs, (out_ref, normed_ref, w_ref) = refs[2 * pieces : -3], refs[-3:]
    rows, half = mine[0].shape
    slots = ids_ref.shape[0] - 1
    depth = 2 * half // slots

    @pl.when(pl.program_id(0) == 0)
    def arrange():
        for j in range(slots):
            at = ids_ref[1 + j]
            start = pl.multiple_of((at % (slots // 2)) * depth, depth)

            def copy(pieces):
                for r, piece in enumerate(pieces):
                    normed_ref[r * rows : (r + 1) * rows, j * depth : (j + 1) * depth] = piece[
                        :, pl.ds(start, depth)
                    ]

            is_mine = at // (slots // 2) == ids_ref[0]
            pl.when(is_mine)(functools.partial(copy, mine))
            pl.when(jnp.logical_not(is_mine))(functools.partial(copy, theirs))

    start = 0
    for band in w_refs:
        w_ref[start : start + band.shape[0], :] = band[...]
        start += band.shape[0]
    out_ref[...] = jnp.dot(
        normed_ref[...], w_ref[...], preferred_element_type=jnp.float32
    ).astype(jnp.bfloat16)


def latent_keys_values(ids, mine, theirs, bands):
    pieces = len(mine)
    rows, half = mine[0].shape
    width = bands[0].shape[1]
    block = min(512, width)
    total = sum(band.shape[0] for band in bands)
    grid_spec = pltpu.PrefetchScalarGridSpec(
        num_scalar_prefetch=1,
        grid=(width // block,),
        in_specs=[pl.BlockSpec(memory_space=pltpu.VMEM)] * (2 * pieces)
        + [pl.BlockSpec((band.shape[0], block), lambda i, ids: (0, i)) for band in bands],
        out_specs=pl.BlockSpec((rows * pieces, block), lambda i, ids: (0, i)),
        scratch_shapes=[
            pltpu.VMEM((rows * pieces, total), jnp.bfloat16),
            pltpu.VMEM((total, block), jnp.bfloat16),
        ],
    )
    return pl.pallas_call(
        functools.partial(latents_kernel, pieces),
        grid_spec=grid_spec,
        out_shape=jax.ShapeDtypeStruct((rows * pieces, width), jnp.bfloat16),
        compiler_params=params(28),
        cost_estimate=cost(2 * rows * pieces * total * width, 2 * total * width),
        name="latent_keys_values",
    )(ids, *mine, *theirs, *bands)


def row_chunks(lengths, size):
    chunks, open_chunk, room = [], [], size
    for i, length in enumerate(lengths):
        start = 0
        while start < length:
            take = min(room, length - start)
            open_chunk.append((i, start, start + take))
            start, room = start + take, room - take
            if room == 0:
                chunks.append(open_chunk)
                open_chunk, room = [], size
    return chunks + ([open_chunk] if open_chunk else [])


def decode_kernel(parts, first, last, q_ref, *refs):
    k_refs, v_refs, rest = refs[:parts], refs[parts : 2 * parts], refs[2 * parts :]
    rows = q_ref.shape[0]
    heads = q_ref.shape[1] // HEAD_DIM
    lane = lax.broadcasted_iota(jnp.int32, (rows, LANES), 1)
    lse_all = jnp.zeros((rows, LANES), jnp.float32)

    def gathered(sources, chunk, cols):
        rows = [sources[i][start:stop, cols] for i, start, stop in chunk]
        return rows[0] if len(rows) == 1 else jnp.concatenate(rows)

    for h in range(heads):
        cols = slice(h * HEAD_DIM, (h + 1) * HEAD_DIM)
        top = acc = None
        if not first:
            top = jnp.max(
                jnp.where(lane % heads == h, rest[1][...], -jnp.inf), axis=1, keepdims=True
            )
            acc = jnp.concatenate([rest[0][:, cols], jnp.ones((rows, LANES), jnp.float32)], axis=1)
        for chunk in row_chunks([k.shape[0] for k in k_refs], 512):
            keys, values = gathered(k_refs, chunk, cols), gathered(v_refs, chunk, cols)
            scores = lax.dot_general(q_ref[:, cols], keys, NT, preferred_element_type=jnp.float32)
            scores = scores * EXP2_SCALE
            new_top = jnp.max(scores, axis=1, keepdims=True)
            if top is not None:
                new_top = jnp.maximum(top, new_top)
            weights = jnp.exp2(scores - new_top).astype(jnp.bfloat16)
            summed = jnp.dot(
                weights,
                jnp.concatenate([values, jnp.ones((keys.shape[0], LANES), jnp.bfloat16)], axis=1),
                preferred_element_type=jnp.float32,
            )
            if top is not None:
                summed = summed + acc * jnp.exp2(top - new_top)
            top, acc = new_top, summed
        totals = acc[:, HEAD_DIM:]
        out_ref = rest[-1] if last else rest[-2]
        out_ref[:, cols] = (acc[:, :HEAD_DIM] / totals).astype(out_ref.dtype)
        if not last:
            lse_all = jnp.where(lane % heads == h, top + jnp.log2(totals), lse_all)
    if not last:
        rest[-1][...] = lse_all


def decode(queries, keys_values, state, out_type):
    first, last = state is None, out_type is not None
    tokens, width = queries.shape
    latents = sum(v.shape[0] for v in keys_values)
    pair = min(2 * HEAD_DIM, width)
    steps = width // pair
    narrow = pl.BlockSpec((tokens, pair), lambda i: (0, i))
    sums = pl.BlockSpec((tokens, LANES), lambda i: (0, i))
    keys = [pl.BlockSpec((v.shape[0], pair), lambda i: (0, i)) for v in keys_values]
    values = [pl.BlockSpec((v.shape[0], pair), lambda i: (0, steps + i)) for v in keys_values]
    if last:
        out_specs, out_shape = narrow, jax.ShapeDtypeStruct((tokens, width), out_type)
    else:
        out_specs = [narrow, sums]
        out_shape = [
            jax.ShapeDtypeStruct((tokens, width), jnp.float32),
            jax.ShapeDtypeStruct((tokens, steps * LANES), jnp.float32),
        ]
    return pl.pallas_call(
        functools.partial(decode_kernel, len(keys_values), first, last),
        grid=(steps,),
        in_specs=[narrow, *keys, *values, *([] if first else [narrow, sums])],
        out_specs=out_specs,
        out_shape=out_shape,
        compiler_params=params(BIG),
        cost_estimate=cost(
            16 * tokens * latents * width,
            4 * latents * width + 6 * tokens * width,
            tokens * latents * (width // HEAD_DIM),
        ),
        name="decode_rows",
    )(queries, *keys_values, *keys_values, *([] if first else state))


def swap_perm(size):
    return [(i, i ^ 1) for i in range(size)]


def shift_perm(size, k):
    far = size // 2
    return [(((z + k) % far) * 2 + y, z * 2 + y) for z in range(far) for y in range(2)]


def hop_perm(size, step, way):
    far = size // 2
    moves = [(z, z + 1) for z in range(step - 1, far - 1)]
    if way < 0:
        moves = [(far - 1 - a, far - 1 - b) for a, b in moves]
    return [(a * 2 + y, b * 2 + y) for a, b in moves for y in range(2)]


def fast_on_device(
    sizes,
    enc_keys,
    enc_values,
    input_ids,
    latent_queries,
    latent_array,
    w_out,
    norm_gain,
    w_key,
    w_value,
    query_features,
    query_ids,
    query_table,
    enc_bias,
    query_counts,
):
    groups, pos = sizes
    p = lax.axis_index("pos")
    place = lax.axis_index("head")
    rows = latent_array.shape[0]
    tokens, half_width = enc_keys.shape
    heads = half_width // HEAD_DIM
    mods = enc_bias.shape[0]
    modality = jnp.arange(mods, dtype=jnp.int32)
    far, z, y, x = pos // 2, p // 2, p % 2, lax.axis_index("groups") % 2
    near = swap_perm(pos)

    def over_groups(value):
        return lax.ppermute(value, "groups", swap_perm(groups))

    def over_near(value):
        return lax.ppermute(value, "pos", near)

    def over_far(value, k):
        return lax.ppermute(value, "pos", shift_perm(pos, k))

    def hop(step, pair):
        return [
            lax.ppermute(v, "pos", hop_perm(pos, step, way)) for v, way in zip(pair, (1, -1))
        ]

    def by_shift(hops, k):
        return jnp.where(z + k < far, hops[k][1], hops[far - k][0])

    q_onehot = (query_ids[:, None] == modality[None, :]).astype(jnp.int32)
    local_counts = jnp.sum(q_onehot, axis=0)

    def columns(arrays, which):
        part = half_width // 2
        return jnp.concatenate(
            [lax.dynamic_slice_in_dim(v, which * part, part, 1) for v in arrays], axis=1
        )

    extra = jnp.pad(input_ids[None, :], ((0, EXTRA - 1), (0, half_width - tokens)))
    extra = extra.astype(jnp.bfloat16)
    near_inputs = over_near(
        jnp.concatenate([columns((enc_keys, enc_values), 1 - y), extra], axis=0)
    )

    out_half, out_cols = w_out.shape[0] // 2, w_out.shape[1]
    counted = jnp.concatenate([local_counts // 16, local_counts % 16])
    counted = jnp.pad(counted[None, :], ((0, EXTRA - 1), (0, out_cols - 2 * mods)))
    counted = counted.astype(jnp.bfloat16)

    out_sent = jnp.concatenate(
        [lax.dynamic_slice_in_dim(w_out, x * out_half, out_half, 0), counted]
    )
    out_far = [over_far(out_sent, k) for k in range(1, far)]
    places = [((z + k) % far) * 2 + (y ^ j) for j in range(2) for k in range(far)]
    kv_for_near = columns((w_key, w_value), 1 - y)
    near_inputs, out_far, kv_for_near = lax.optimization_barrier(
        (near_inputs, out_far, kv_for_near)
    )

    kv_own = columns((w_key, w_value), y)
    kv_near = over_near(kv_for_near)

    head_bias = lax.dynamic_slice_in_dim(enc_bias, y * (heads // 2), heads // 2, 1)
    parts = encode(
        y, latent_queries, enc_keys, enc_values, extra, near_inputs, head_bias, 2 * rows
    )
    kv_near, out_far, parts = lax.optimization_barrier((kv_near, out_far, parts))
    kv_sent = jnp.where(x == 0, kv_own, kv_near)
    hops = {0: [kv_sent, kv_sent]}
    hops[1] = hop(1, hops[0])
    early = [k for k in range(1, far) if max(k, far - k) < 3]
    rest = [k for k in range(1, far) if k not in early]
    out_far = jnp.concatenate(out_far)
    out_far_other = over_groups(out_far)
    out_near = over_near(jnp.concatenate([w_out, counted, out_far]))
    out_near_other = over_groups(out_near[w_out.shape[0] + EXTRA :])
    columns_of_slice = [[2 * i + j for i in range(far)] for j in range(2)]
    parts = lax.all_to_all(parts, "pos", 0, 0, axis_index_groups=columns_of_slice, tiled=True)

    def kept_queries():
        far_counts = out_far.reshape(far - 1, out_half + EXTRA, out_cols)[:, out_half, : 2 * mods]
        near_counts = out_near.reshape(-1, EXTRA, out_cols)[:, 0, : 2 * mods]
        at = [w_out.shape[0] // EXTRA]
        at += [at[0] + k * (out_half // EXTRA + 1) for k in range(1, far)]
        near_counts = jnp.concatenate([near_counts[i : i + 1] for i in at])
        counts = jnp.concatenate([counted[:1, : 2 * mods], far_counts, near_counts])
        counts = counts.astype(jnp.int32)
        counts = counts[:, :mods] * 16 + counts[:, mods:]
        earlier = jnp.stack(places)[:, None] < p
        before = jnp.sum(jnp.where(earlier, counts, 0), axis=0)
        within = jnp.cumsum(q_onehot, axis=0) - q_onehot
        ranked = jnp.sum((within + before[None, :]) * q_onehot, axis=1)
        limits = jnp.sum(q_onehot * query_counts[None, :], axis=1)
        return ranked < limits

    lookup = jnp.dot(q_onehot.astype(jnp.bfloat16), query_table, preferred_element_type=jnp.float32)
    queries = (query_features.astype(jnp.float32) + lookup).astype(jnp.bfloat16)
    own_queries = columns((queries,), y)
    near_queries = over_near(columns((queries,), 1 - y))

    parts, out_near, out_far_other, out_near_other, near_queries = lax.optimization_barrier(
        (parts, out_near, out_far_other, out_near_other, near_queries)
    )
    attended, for_near = merge(y, parts, far)
    _, hops = lax.optimization_barrier((for_near, hops))
    hops[2] = hop(2, hops[1])
    from_near = over_near(for_near)
    kept = kept_queries()
    out_ids = jnp.stack([*places, y, x]).astype(jnp.int32)
    weights = [w_out, out_far, out_far_other, out_near, out_near_other]
    partial_value = project(out_ids, attended, from_near, weights)
    partial_value, hops = lax.optimization_barrier((partial_value, hops))
    kv_bands = [kv_own, kv_near]
    for k in early:
        kv_moved = by_shift(hops, k)
        kv_bands += [kv_moved, over_groups(kv_moved)]
    for step in range(3, far):
        hops[step] = hop(step, hops[step - 1])
    theirs = lax.ppermute(partial_value, "head", swap_perm(2))
    own_cols, normed, normed_other = normalise(
        place, partial_value, theirs, latent_array, norm_gain[None, :]
    )
    kv_at = [p, p ^ 1]
    for k in early + rest:
        kv_at += [((z + k) % far) * 2 + (y ^ other) for other in (x, 1 - x)]
    kv_ids = jnp.stack([place, *kv_at]).astype(jnp.int32)

    def cores(values):
        return [lax.ppermute(v, "head", swap_perm(2)) for v in values]

    def fold(mine, other):
        return latent_keys_values(kv_ids, mine, other, kv_bands)

    def arrival(hops, j):
        picked = None
        for at in range(far):
            came = [
                (step, way)
                for step in range(1, far)
                for way in (1, 0)
                if (at + step < far if way else at >= step)
            ]
            step, way = came[j - 1]
            value = hops[step][way]
            picked = value if picked is None else jnp.where(z == at, value, picked)
        return picked

    came = {0: [normed, normed]}
    came[1] = hop(1, came[0])
    normed_near = over_near(normed)
    hops, _ = lax.optimization_barrier((hops, normed))
    for k in rest:
        kv_moved = by_shift(hops, k)
        kv_bands += [kv_moved, over_groups(kv_moved)]
    came, kept = lax.optimization_barrier((came, kept))
    mine, other, keys_values = [normed, normed_near], [normed_other], []
    for step in range(1, far):
        fresh = arrival(came, step)
        fresh_near = over_near(fresh)
        if step + 1 < far:
            came[step + 1] = hop(step + 1, came[step])
            if step > 1:
                keys_values.append(fold(mine, other))
                mine, other = [], []
            came, mine, other, kv_bands, keys_values, fresh, fresh_near = (
                lax.optimization_barrier(
                    (came, mine, other, kv_bands, keys_values, fresh, fresh_near)
                )
            )
            if step == 1:
                mine += [fresh, fresh_near]
                other += cores(mine[1:])
            else:
                mine += [fresh, fresh_near]
                other += cores([fresh, fresh_near])
    keys_values.append(fold([*mine, fresh], [*other, *cores([fresh])]))
    near_state = decode(near_queries, keys_values, None, None)
    fresh_near, keys_values, near_state = lax.optimization_barrier(
        (fresh_near, keys_values, near_state)
    )
    keys_values.append(fold([fresh_near], cores([fresh_near])))
    near_state = decode(near_queries, keys_values[-1:], near_state, jnp.bfloat16)
    own_state = decode(own_queries, keys_values, None, jnp.float32)
    from_near = lax.ppermute(near_state, "pos", near).astype(jnp.float32)
    decoded = jnp.where(
        y == 0,
        jnp.concatenate([own_state, from_near], axis=1),
        jnp.concatenate([from_near, own_state], axis=1),
    )
    decoded = jnp.where(kept[:, None], decoded, 0.0)
    return (own_cols, decoded)


def on_device(sizes, *args):
    groups, pos, head = sizes
    enc_keys, latent_array, w_out, w_key = args[0], args[4], args[5], args[7]
    fits = (
        head == 2
        and pos % 2 == 0
        and pos > 4
        and groups % 2 == 0
        and enc_keys.shape[1] % (4 * HEAD_DIM) == 0
        and 3 * enc_keys.shape[1] <= 2 * HEAD_DIM * EXTRA
        and enc_keys.shape[0] % LANES == 0
        and enc_keys.shape[0] <= enc_keys.shape[1]
        and w_key.shape[0] % LANES == 0
        and w_out.shape[0] % (2 * LANES) == 0
        and w_out.shape[1] % LANES == 0
        and latent_array.shape[0] % LANES == 0
    )
    if fits:
        return fast_on_device((groups, pos), *args)
    return plain_on_device(*args)


def solution(mesh):
    return jax.shard_map(
        functools.partial(on_device, tuple(mesh.shape[a] for a in ("groups", "pos", "head"))),
        mesh=mesh,
        in_specs=(
            P(("groups", "pos"), "head"),
            P(("groups", "pos"), "head"),
            P(("groups", "pos")),
            P("groups", "head"),
            P(("groups", "pos"), None),
            P("head", "pos"),
            P(),
            P("pos", "head"),
            P("pos", "head"),
            P(("groups", "pos"), "head"),
            P(("groups", "pos")),
            P(None, "head"),
            P(None, "head"),
            P("groups"),
        ),
        out_specs=(P(("groups", "pos"), "head"), P(("groups", "pos"), "head")),
        check_vma=False,
    )
```

```python
import functools

import jax
import jax.numpy as jnp
from jax import lax
from jax.experimental import pallas as pl
from jax.experimental.pallas import tpu as pltpu
from jax.sharding import PartitionSpec as P

HEAD_DIM = 128


norm_eps = 1e-06


def prefix(shard, axis, combine, identity):
    peers, place = (lax.axis_size(axis), lax.axis_index(axis))
    everything = lax.all_gather(shard, axis)
    start = jnp.broadcast_to(jnp.asarray(identity, shard.dtype), shard.shape)

    def step(k, before):
        reached = k < place
        new = combine(before, everything[k])
        return jnp.where(reached, new, before)

    return lax.fori_loop(0, peers, step, start)


def plain_on_device(
    enc_keys,
    enc_values,
    input_ids,
    latent_queries,
    latent_array,
    w_out,
    norm_gain,
    w_key,
    w_value,
    query_features,
    query_ids,
    query_table,
    enc_bias,
    query_counts,
):
    tok_rows = enc_keys.shape[0]
    half_width = enc_keys.shape[1]
    local_heads = half_width // HEAD_DIM
    score_scale = HEAD_DIM ** (-0.5)
    modality = jnp.arange(enc_bias.shape[0], dtype=jnp.int32)
    in_onehot = (input_ids[:, None] == modality[None, :]).astype(jnp.float32)
    bias_rows = jnp.dot(in_onehot, enc_bias, precision=lax.Precision.HIGHEST)
    bias_heads = bias_rows.T[:, None, :]
    keys_split = enc_keys.reshape(tok_rows, local_heads, HEAD_DIM)
    values_split = enc_values.reshape(tok_rows, local_heads, HEAD_DIM)
    lat_total = latent_queries.shape[0]
    block_rows = min(512, lat_total)
    query_blocks = latent_queries.reshape(
        lat_total // block_rows, block_rows, local_heads, HEAD_DIM
    )

    def encode_block(block_queries):
        scores = (
            jnp.einsum(
                "nha,tha->hnt", block_queries, keys_split, preferred_element_type=jnp.float32
            )
            * score_scale
            + bias_heads
        )
        highest = jnp.max(scores, axis=2)
        weights = jnp.exp(scores - highest[:, :, None])
        totals = jnp.sum(weights, axis=2)
        summed = jnp.einsum(
            "hnt,tha->nha",
            weights.astype(jnp.bfloat16),
            values_split,
            preferred_element_type=jnp.float32,
        )
        return (highest.T, totals.T, summed.reshape(block_rows, half_width))

    block_max, block_tot, block_acc = lax.map(encode_block, query_blocks)
    row_highest = block_max.reshape(lat_total, local_heads)
    row_totals = block_tot.reshape(lat_total, local_heads)
    row_sums = block_acc.reshape(lat_total, half_width)
    own_rows = latent_array.shape[0]
    global_max = lax.pmax(row_highest, "pos")
    factor = jnp.exp(row_highest - global_max)
    scaled_sums = (row_sums.reshape(lat_total, local_heads, HEAD_DIM) * factor[:, :, None]).reshape(
        lat_total, half_width
    )
    totals, summed = (
        lax.psum_scatter(row_totals * factor, "pos", scatter_dimension=0, tiled=True),
        lax.psum_scatter(scaled_sums, "pos", scatter_dimension=0, tiled=True),
    )
    summed = summed.reshape(own_rows, local_heads, HEAD_DIM)
    attended = (summed / totals[:, :, None]).reshape(own_rows, half_width).astype(jnp.bfloat16)
    partial_value = jnp.dot(
        attended,
        lax.all_gather(w_out, "pos", axis=1, tiled=True),
        preferred_element_type=jnp.float32,
    )
    offset = lax.axis_index("head") * half_width
    projected = lax.psum(partial_value, "head")
    updated = latent_array.astype(jnp.float32) + projected
    mean_square = jnp.mean(updated * updated, axis=1, keepdims=True)
    normed_full = updated * lax.rsqrt(mean_square + norm_eps) * norm_gain
    normed = normed_full.astype(jnp.bfloat16)
    own_cols = lax.dynamic_slice_in_dim(normed_full, offset, half_width, 1)
    pieces = (
        lax.all_gather(w_key, "pos", axis=0, tiled=True),
        lax.all_gather(w_value, "pos", axis=0, tiled=True),
    )
    key_sum = jnp.dot(normed, pieces[0], preferred_element_type=jnp.float32)
    value_sum = jnp.dot(normed, pieces[1], preferred_element_type=jnp.float32)
    latent_keys = key_sum.astype(jnp.bfloat16)
    latent_values = value_sum.astype(jnp.bfloat16)
    q_onehot = (query_ids[:, None] == modality[None, :]).astype(jnp.int32)
    local_counts = jnp.sum(q_onehot, axis=0)
    before = prefix(
        local_counts, "pos", lambda earlier, later: earlier + later, jnp.zeros_like(local_counts)
    )
    within = jnp.cumsum(q_onehot, axis=0) - q_onehot
    ranked = jnp.sum((within + before[None, :]) * q_onehot, axis=1)
    limits = jnp.sum(q_onehot * query_counts[None, :], axis=1)
    kept_rows = ranked < limits
    lookup = jnp.dot(q_onehot.astype(jnp.bfloat16), query_table, preferred_element_type=jnp.float32)
    queries = (
        (query_features.astype(jnp.float32) + lookup)
        .astype(jnp.bfloat16)
        .reshape(tok_rows, local_heads, HEAD_DIM)
    )

    def fold_rows(running, key_rows, value_rows):
        running_max, running_tot, running_acc = running
        key_heads = key_rows.reshape(key_rows.shape[0], local_heads, HEAD_DIM)
        value_heads = value_rows.reshape(value_rows.shape[0], local_heads, HEAD_DIM)
        scores = (
            jnp.einsum("tha,rha->htr", queries, key_heads, preferred_element_type=jnp.float32)
            * score_scale
        )
        new_max = jnp.maximum(running_max, jnp.max(scores, axis=2))
        fade = jnp.exp(running_max - new_max)
        weights = jnp.exp(scores - new_max[:, :, None])
        new_tot = running_tot * fade + jnp.sum(weights, axis=2)
        new_acc = running_acc * fade[:, :, None] + jnp.einsum(
            "htr,rha->hta",
            weights.astype(jnp.bfloat16),
            value_heads,
            preferred_element_type=jnp.float32,
        )
        return (new_max, new_tot, new_acc)

    start_state = (
        jnp.full((local_heads, tok_rows), -jnp.inf, jnp.float32),
        jnp.zeros((local_heads, tok_rows), jnp.float32),
        jnp.zeros((local_heads, tok_rows, HEAD_DIM), jnp.float32),
    )
    running = start_state
    pieces = (
        lax.all_gather(latent_keys, "pos", axis=0, tiled=True),
        lax.all_gather(latent_values, "pos", axis=0, tiled=True),
    )
    row_count = pieces[0].shape[0]
    key_blocks = pieces[0].reshape(row_count // 512, 512, half_width)
    value_blocks = pieces[1].reshape(row_count // 512, 512, half_width)

    def scan_step(state, pair):
        return (fold_rows(state, pair[0], pair[1]), None)

    running, ignored = lax.scan(scan_step, running, (key_blocks, value_blocks))
    final_max, final_tot, final_acc = running
    dec_heads = final_acc / final_tot[:, :, None]
    dec_rows = jnp.transpose(dec_heads, (1, 0, 2)).reshape(tok_rows, half_width)
    decoded = jnp.where(kept_rows[:, None], dec_rows, 0.0)
    return (own_cols, decoded)


LANES = 128
EXTRA = 16
BIG = 56
LOG2E = 1.4426950408889634
EXP2_SCALE = LOG2E * HEAD_DIM**-0.5
NT = (((1,), (1,)), ((), ()))


def params(mib):
    return pltpu.CompilerParams(vmem_limit_bytes=mib << 20)


def cost(flops, nbytes, exps=0):
    return pl.CostEstimate(flops=int(flops), bytes_accessed=int(nbytes), transcendentals=int(exps))


def whole(shape):
    return pl.BlockSpec(shape, lambda *args: (0,) * len(shape))


def encode_kernel(ids_ref, q_ref, k_ref, v_ref, extra_ref, near_ref, bias_ref, out_ref):
    rows, width = q_ref.shape
    tokens = k_ref.shape[0]
    heads = width // HEAD_DIM
    ones = jnp.ones((tokens, LANES), jnp.bfloat16)
    kinds = [
        extra_ref[...].astype(jnp.float32)[:1, :tokens],
        near_ref[tokens:, :].astype(jnp.float32)[:1, :tokens],
    ]
    lane = lax.broadcasted_iota(jnp.int32, (rows, LANES), 1)
    lse_all = jnp.zeros((rows, LANES), jnp.float32)
    for h in range(heads):
        cols = slice(h * HEAD_DIM, (h + 1) * HEAD_DIM)
        late = slice(width + h * HEAD_DIM, width + (h + 1) * HEAD_DIM)
        pairs = [
            (k_ref[:, cols], v_ref[:, cols]),
            (near_ref[:tokens, cols], near_ref[:tokens, late]),
        ]
        top = acc = None
        for (keys, values), kind in zip(pairs, kinds):
            bias = jnp.zeros_like(kind)
            for m in range(bias_ref.shape[0]):
                bias = jnp.where(kind == m, bias_ref[m, h] * LOG2E, bias)
            scores = lax.dot_general(q_ref[:, cols], keys, NT, preferred_element_type=jnp.float32)
            scores = scores * EXP2_SCALE + bias
            new_top = jnp.max(scores, axis=1, keepdims=True)
            if top is not None:
                new_top = jnp.maximum(top, new_top)
            weights = jnp.exp2(scores - new_top).astype(jnp.bfloat16)
            summed = jnp.dot(
                weights, jnp.concatenate([values, ones], axis=1), preferred_element_type=jnp.float32
            )
            if top is not None:
                summed = summed + acc * jnp.exp2(top - new_top)
            top, acc = new_top, summed
        totals = acc[:, HEAD_DIM:]
        out_ref[:rows, cols] = (acc[:, :HEAD_DIM] / totals).astype(jnp.bfloat16)
        lse_all = jnp.where(lane % heads == h, top + jnp.log2(totals), lse_all)
    lse = lse_all.T[:EXTRA, :]
    high = lse.astype(jnp.bfloat16).astype(jnp.float32)
    mid = (lse - high).astype(jnp.bfloat16).astype(jnp.float32)
    low = lse - high - mid
    row = lax.broadcasted_iota(jnp.int32, lse.shape, 0)
    terms = jnp.where(row < heads, high, jnp.where(row < 2 * heads, mid, low))
    out_ref[rows:, :] = terms.astype(jnp.bfloat16)


def encode(which, queries, keys, values, extra, near, bias, rows):
    tokens = keys.shape[0]
    width = keys.shape[1] // 2
    blocks = queries.shape[0] // rows
    half = pl.BlockSpec((tokens, width), lambda i, ids: (0, ids[0]))
    grid_spec = pltpu.PrefetchScalarGridSpec(
        num_scalar_prefetch=1,
        grid=(blocks,),
        in_specs=[
            pl.BlockSpec((rows, width), lambda i, ids: (i, ids[0])),
            half,
            half,
            whole(extra.shape),
            whole(near.shape),
            pl.BlockSpec(memory_space=pltpu.SMEM),
        ],
        out_specs=pl.BlockSpec((rows + EXTRA, width), lambda i, ids: (i, 0)),
    )
    return pl.pallas_call(
        encode_kernel,
        grid_spec=grid_spec,
        out_shape=jax.ShapeDtypeStruct((blocks * (rows + EXTRA), width), jnp.bfloat16),
        compiler_params=params(BIG),
        cost_estimate=cost(
            16 * blocks * rows * tokens * width, 8 * tokens * width, blocks * rows * tokens * 8
        ),
        name="encode_rows",
    )(which.reshape(1), queries, keys, values, extra, near, bias)


def merge_kernel(count, ids_ref, parts_ref, mine_ref, near_ref, all_ref):
    rows, width = all_ref.shape
    long = rows + EXTRA
    parts = [parts_ref.at[i * long : (i + 1) * long, :] for i in range(count)]
    heads = width // HEAD_DIM
    stats = [v[rows:, :].astype(jnp.float32).T for v in parts]
    for h in range(heads):
        cols = slice(h * HEAD_DIM, (h + 1) * HEAD_DIM)
        lses = [
            s[:, h : h + 1] + s[:, heads + h : heads + h + 1] + s[:, 2 * heads + h : 2 * heads + h + 1]
            for s in stats
        ]
        top = functools.reduce(jnp.maximum, lses)
        factors = [jnp.exp2(v - top) for v in lses]
        inverse = 1.0 / functools.reduce(jnp.add, factors)
        merged = functools.reduce(
            jnp.add,
            [v[:rows, cols].astype(jnp.float32) * (f * inverse) for v, f in zip(parts, factors)],
        )
        all_ref[:, cols] = merged.astype(jnp.bfloat16)
    own = rows // 2
    mine_ref[...] = all_ref[pl.ds(pl.multiple_of(ids_ref[0] * own, own), own), :]
    near_ref[...] = all_ref[pl.ds(pl.multiple_of((1 - ids_ref[0]) * own, own), own), :]


def merge(which, parts, count):
    long, width = parts.shape[0] // count, parts.shape[1]
    rows = long - EXTRA
    grid_spec = pltpu.PrefetchScalarGridSpec(
        num_scalar_prefetch=1,
        grid=(1,),
        in_specs=[whole(parts.shape)],
        out_specs=[whole((rows // 2, width))] * 2,
        scratch_shapes=[pltpu.VMEM((rows, width), jnp.bfloat16)],
    )
    return pl.pallas_call(
        functools.partial(merge_kernel, count),
        grid_spec=grid_spec,
        out_shape=[jax.ShapeDtypeStruct((rows // 2, width), jnp.bfloat16)] * 2,
        compiler_params=params(32),
        cost_estimate=cost(8 * rows * width, 10 * rows * width),
        name="merge_rows",
    )(which.reshape(1), parts)


def project_kernel(far, ids_ref, mine_ref, near_ref, *refs):
    w_ref, far_ref, far_other_ref, near_w_ref, near_other_ref, out_ref, att_ref = refs
    part = mine_ref.shape[1]
    first = ids_ref[2 * far]
    att_ref[:, pl.ds(pl.multiple_of(first * part, part), part)] = mine_ref[...]
    att_ref[:, pl.ds(pl.multiple_of((1 - first) * part, part), part)] = near_ref[...]
    cols = w_ref.shape[1]
    depth = att_ref.shape[1] // 2
    share = ids_ref[2 * far + 1]
    halves = [
        att_ref[:, pl.ds(pl.multiple_of(v * depth, depth), depth)] for v in (share, 1 - share)
    ]

    def place(slot, value):
        out_ref[:, pl.ds(pl.multiple_of(ids_ref[slot] * cols, cols), cols)] = value

    for slot, own_ref in ((0, w_ref), (far, near_w_ref)):
        own = own_ref[: 2 * depth, :]
        place(slot, jnp.dot(att_ref[...], own, preferred_element_type=jnp.float32))
    for k in range(far - 1):
        start = k * (depth + EXTRA)
        band = slice(start, start + depth)
        near_band = slice(start + 2 * depth + EXTRA, start + 3 * depth + EXTRA)
        for slot, weights in (
            (1 + k, (far_ref[band, :], far_other_ref[band, :])),
            (far + 1 + k, (near_w_ref[near_band, :], near_other_ref[band, :])),
        ):
            terms = [
                jnp.dot(v, w, preferred_element_type=jnp.float32) for v, w in zip(halves, weights)
            ]
            place(slot, terms[0] + terms[1])


def project(ids, mine, near, weights):
    rows, part = mine.shape
    far = (ids.shape[0] - 2) // 2
    out_cols = 2 * far * weights[0].shape[1]
    grid_spec = pltpu.PrefetchScalarGridSpec(
        num_scalar_prefetch=1,
        grid=(1,),
        in_specs=[whole(v.shape) for v in (mine, near, *weights)],
        out_specs=whole((rows, out_cols)),
        scratch_shapes=[pltpu.VMEM((rows, 2 * part), jnp.bfloat16)],
    )
    return pl.pallas_call(
        functools.partial(project_kernel, far),
        grid_spec=grid_spec,
        out_shape=jax.ShapeDtypeStruct((rows, out_cols), jnp.float32),
        compiler_params=params(BIG),
        cost_estimate=cost(4 * rows * part * out_cols, 4 * part * out_cols + 4 * rows * out_cols),
        name="project_rows",
    )(ids, mine, near, *weights)


def norm_kernel(
    ids_ref, mine_ref, theirs_ref, latent_ref, gain_ref, out_ref, normed_ref, other_ref, full_ref
):
    updated = latent_ref[...].astype(jnp.float32) + (mine_ref[...] + theirs_ref[...])
    mean_square = jnp.mean(updated * updated, axis=1, keepdims=True)
    full_ref[...] = updated * lax.rsqrt(mean_square + norm_eps) * gain_ref[...]
    half = out_ref.shape[1]
    own = full_ref[:, pl.ds(pl.multiple_of(ids_ref[0] * half, half), half)]
    out_ref[...] = own
    normed_ref[...] = own.astype(jnp.bfloat16)
    other = full_ref[:, pl.ds(pl.multiple_of((1 - ids_ref[0]) * half, half), half)]
    other_ref[...] = other.astype(jnp.bfloat16)


def normalise(place, mine, theirs, latent_array, gain):
    rows, width = mine.shape
    half = width // 2
    grid_spec = pltpu.PrefetchScalarGridSpec(
        num_scalar_prefetch=1,
        grid=(1,),
        in_specs=[whole((rows, width))] * 3 + [whole((1, width))],
        out_specs=[whole((rows, half))] * 3,
        scratch_shapes=[pltpu.VMEM((rows, width), jnp.float32)],
    )
    return pl.pallas_call(
        norm_kernel,
        grid_spec=grid_spec,
        out_shape=[
            jax.ShapeDtypeStruct((rows, half), jnp.float32),
            jax.ShapeDtypeStruct((rows, half), jnp.bfloat16),
            jax.ShapeDtypeStruct((rows, half), jnp.bfloat16),
        ],
        compiler_params=params(BIG),
        cost_estimate=cost(6 * rows * width, 13 * rows * width),
        name="norm_rows",
    )(place.reshape(1), mine, theirs, latent_array, gain)


def latents_kernel(pieces, ids_ref, *refs):
    mine, theirs = refs[:pieces], refs[pieces : 2 * pieces]
    w_refs, (out_ref, normed_ref, w_ref) = refs[2 * pieces : -3], refs[-3:]
    rows, half = mine[0].shape
    slots = ids_ref.shape[0] - 1
    depth = 2 * half // slots

    @pl.when(pl.program_id(0) == 0)
    def arrange():
        for j in range(slots):
            at = ids_ref[1 + j]
            start = pl.multiple_of((at % (slots // 2)) * depth, depth)

            def copy(pieces):
                for r, piece in enumerate(pieces):
                    normed_ref[r * rows : (r + 1) * rows, j * depth : (j + 1) * depth] = piece[
                        :, pl.ds(start, depth)
                    ]

            is_mine = at // (slots // 2) == ids_ref[0]
            pl.when(is_mine)(functools.partial(copy, mine))
            pl.when(jnp.logical_not(is_mine))(functools.partial(copy, theirs))

    start = 0
    for band in w_refs:
        w_ref[start : start + band.shape[0], :] = band[...]
        start += band.shape[0]
    out_ref[...] = jnp.dot(
        normed_ref[...], w_ref[...], preferred_element_type=jnp.float32
    ).astype(jnp.bfloat16)


def latent_keys_values(ids, mine, theirs, bands):
    pieces = len(mine)
    rows, half = mine[0].shape
    width = bands[0].shape[1]
    block = min(512, width)
    total = sum(band.shape[0] for band in bands)
    grid_spec = pltpu.PrefetchScalarGridSpec(
        num_scalar_prefetch=1,
        grid=(width // block,),
        in_specs=[pl.BlockSpec(memory_space=pltpu.VMEM)] * (2 * pieces)
        + [pl.BlockSpec((band.shape[0], block), lambda i, ids: (0, i)) for band in bands],
        out_specs=pl.BlockSpec((rows * pieces, block), lambda i, ids: (0, i)),
        scratch_shapes=[
            pltpu.VMEM((rows * pieces, total), jnp.bfloat16),
            pltpu.VMEM((total, block), jnp.bfloat16),
        ],
    )
    return pl.pallas_call(
        functools.partial(latents_kernel, pieces),
        grid_spec=grid_spec,
        out_shape=jax.ShapeDtypeStruct((rows * pieces, width), jnp.bfloat16),
        compiler_params=params(57),
        cost_estimate=cost(2 * rows * pieces * total * width, 2 * total * width),
        name="latent_keys_values",
    )(ids, *mine, *theirs, *bands)


def row_chunks(lengths, size):
    chunks, open_chunk, room = [], [], size
    for i, length in enumerate(lengths):
        start = 0
        while start < length:
            take = min(room, length - start)
            open_chunk.append((i, start, start + take))
            start, room = start + take, room - take
            if room == 0:
                chunks.append(open_chunk)
                open_chunk, room = [], size
    return chunks + ([open_chunk] if open_chunk else [])


def decode_kernel(parts, first, last, q_ref, *refs):
    k_refs, v_refs, rest = refs[:parts], refs[parts : 2 * parts], refs[2 * parts :]
    rows = q_ref.shape[0]
    heads = q_ref.shape[1] // HEAD_DIM
    lane = lax.broadcasted_iota(jnp.int32, (rows, LANES), 1)
    lse_all = jnp.zeros((rows, LANES), jnp.float32)

    def gathered(sources, chunk, cols):
        rows = [sources[i][start:stop, cols] for i, start, stop in chunk]
        return rows[0] if len(rows) == 1 else jnp.concatenate(rows)

    for h in range(heads):
        cols = slice(h * HEAD_DIM, (h + 1) * HEAD_DIM)
        top = acc = None
        if not first:
            top = jnp.max(
                jnp.where(lane % heads == h, rest[1][...], -jnp.inf), axis=1, keepdims=True
            )
            acc = jnp.concatenate([rest[0][:, cols], jnp.ones((rows, LANES), jnp.float32)], axis=1)
        for chunk in row_chunks([k.shape[0] for k in k_refs], 512):
            keys, values = gathered(k_refs, chunk, cols), gathered(v_refs, chunk, cols)
            scores = lax.dot_general(q_ref[:, cols], keys, NT, preferred_element_type=jnp.float32)
            scores = scores * EXP2_SCALE
            new_top = jnp.max(scores, axis=1, keepdims=True)
            if top is not None:
                new_top = jnp.maximum(top, new_top)
            weights = jnp.exp2(scores - new_top).astype(jnp.bfloat16)
            summed = jnp.dot(
                weights,
                jnp.concatenate([values, jnp.ones((keys.shape[0], LANES), jnp.bfloat16)], axis=1),
                preferred_element_type=jnp.float32,
            )
            if top is not None:
                summed = summed + acc * jnp.exp2(top - new_top)
            top, acc = new_top, summed
        totals = acc[:, HEAD_DIM:]
        out_ref = rest[-1] if last else rest[-2]
        out_ref[:, cols] = (acc[:, :HEAD_DIM] / totals).astype(out_ref.dtype)
        if not last:
            lse_all = jnp.where(lane % heads == h, top + jnp.log2(totals), lse_all)
    if not last:
        rest[-1][...] = lse_all


def decode(queries, keys_values, state, out_type):
    first, last = state is None, out_type is not None
    tokens, width = queries.shape
    latents = sum(v.shape[0] for v in keys_values)
    pair = min(2 * HEAD_DIM, width)
    steps = width // pair
    narrow = pl.BlockSpec((tokens, pair), lambda i: (0, i))
    sums = pl.BlockSpec((tokens, LANES), lambda i: (0, i))
    keys = [pl.BlockSpec((v.shape[0], pair), lambda i: (0, i)) for v in keys_values]
    values = [pl.BlockSpec((v.shape[0], pair), lambda i: (0, steps + i)) for v in keys_values]
    if last:
        out_specs, out_shape = narrow, jax.ShapeDtypeStruct((tokens, width), out_type)
    else:
        out_specs = [narrow, sums]
        out_shape = [
            jax.ShapeDtypeStruct((tokens, width), jnp.float32),
            jax.ShapeDtypeStruct((tokens, steps * LANES), jnp.float32),
        ]
    return pl.pallas_call(
        functools.partial(decode_kernel, len(keys_values), first, last),
        grid=(steps,),
        in_specs=[narrow, *keys, *values, *([] if first else [narrow, sums])],
        out_specs=out_specs,
        out_shape=out_shape,
        compiler_params=params(BIG),
        cost_estimate=cost(
            16 * tokens * latents * width,
            4 * latents * width + 6 * tokens * width,
            tokens * latents * (width // HEAD_DIM),
        ),
        name="decode_rows",
    )(queries, *keys_values, *keys_values, *([] if first else state))


def swap_perm(size):
    return [(i, i ^ 1) for i in range(size)]


def shift_perm(size, k):
    far = size // 2
    return [(((z + k) % far) * 2 + y, z * 2 + y) for z in range(far) for y in range(2)]


def hop_perm(size, step, way):
    far = size // 2
    moves = [(z, z + 1) for z in range(step - 1, far - 1)]
    if way < 0:
        moves = [(far - 1 - a, far - 1 - b) for a, b in moves]
    return [(a * 2 + y, b * 2 + y) for a, b in moves for y in range(2)]


def fast_on_device(
    sizes,
    enc_keys,
    enc_values,
    input_ids,
    latent_queries,
    latent_array,
    w_out,
    norm_gain,
    w_key,
    w_value,
    query_features,
    query_ids,
    query_table,
    enc_bias,
    query_counts,
):
    groups, pos = sizes
    p = lax.axis_index("pos")
    place = lax.axis_index("head")
    rows = latent_array.shape[0]
    tokens, half_width = enc_keys.shape
    heads = half_width // HEAD_DIM
    mods = enc_bias.shape[0]
    modality = jnp.arange(mods, dtype=jnp.int32)
    far, z, y, x = pos // 2, p // 2, p % 2, lax.axis_index("groups") % 2
    near = swap_perm(pos)

    def over_groups(value):
        return lax.ppermute(value, "groups", swap_perm(groups))

    def over_near(value):
        return lax.ppermute(value, "pos", near)

    def over_far(value, k):
        return lax.ppermute(value, "pos", shift_perm(pos, k))

    def hop(step, pair):
        return [
            lax.ppermute(v, "pos", hop_perm(pos, step, way)) for v, way in zip(pair, (1, -1))
        ]

    def by_shift(hops, k):
        return jnp.where(z + k < far, hops[k][1], hops[far - k][0])

    q_onehot = (query_ids[:, None] == modality[None, :]).astype(jnp.int32)
    local_counts = jnp.sum(q_onehot, axis=0)

    def columns(arrays, which):
        part = half_width // 2
        return jnp.concatenate(
            [lax.dynamic_slice_in_dim(v, which * part, part, 1) for v in arrays], axis=1
        )

    extra = jnp.pad(input_ids[None, :], ((0, EXTRA - 1), (0, half_width - tokens)))
    extra = extra.astype(jnp.bfloat16)
    near_inputs = over_near(
        jnp.concatenate([columns((enc_keys, enc_values), 1 - y), extra], axis=0)
    )

    out_half, out_cols = w_out.shape[0] // 2, w_out.shape[1]
    counted = jnp.concatenate([local_counts // 16, local_counts % 16])
    counted = jnp.pad(counted[None, :], ((0, EXTRA - 1), (0, out_cols - 2 * mods)))
    counted = counted.astype(jnp.bfloat16)

    out_sent = jnp.concatenate(
        [lax.dynamic_slice_in_dim(w_out, x * out_half, out_half, 0), counted]
    )
    out_far = [over_far(out_sent, k) for k in range(1, far)]
    places = [((z + k) % far) * 2 + (y ^ j) for j in range(2) for k in range(far)]
    kv_for_near = columns((w_key, w_value), 1 - y)
    near_inputs, out_far, kv_for_near = lax.optimization_barrier(
        (near_inputs, out_far, kv_for_near)
    )

    kv_own = columns((w_key, w_value), y)
    kv_near = over_near(kv_for_near)

    head_bias = lax.dynamic_slice_in_dim(enc_bias, y * (heads // 2), heads // 2, 1)
    parts = encode(
        y, latent_queries, enc_keys, enc_values, extra, near_inputs, head_bias, 2 * rows
    )
    kv_near, out_far, parts = lax.optimization_barrier((kv_near, out_far, parts))
    kv_sent = jnp.where(x == 0, kv_own, kv_near)
    hops = {0: [kv_sent, kv_sent]}
    hops[1] = hop(1, hops[0])
    early = [k for k in range(1, far) if max(k, far - k) < 3]
    rest = [k for k in range(1, far) if k not in early]
    out_far = jnp.concatenate(out_far)
    out_far_other = over_groups(out_far)
    out_near = over_near(jnp.concatenate([w_out, counted, out_far]))
    out_near_other = over_groups(out_near[w_out.shape[0] + EXTRA :])
    columns_of_slice = [[2 * i + j for i in range(far)] for j in range(2)]
    parts = lax.all_to_all(parts, "pos", 0, 0, axis_index_groups=columns_of_slice, tiled=True)

    def kept_queries():
        far_counts = out_far.reshape(far - 1, out_half + EXTRA, out_cols)[:, out_half, : 2 * mods]
        near_counts = out_near.reshape(-1, EXTRA, out_cols)[:, 0, : 2 * mods]
        at = [w_out.shape[0] // EXTRA]
        at += [at[0] + k * (out_half // EXTRA + 1) for k in range(1, far)]
        near_counts = jnp.concatenate([near_counts[i : i + 1] for i in at])
        counts = jnp.concatenate([counted[:1, : 2 * mods], far_counts, near_counts])
        counts = counts.astype(jnp.int32)
        counts = counts[:, :mods] * 16 + counts[:, mods:]
        earlier = jnp.stack(places)[:, None] < p
        before = jnp.sum(jnp.where(earlier, counts, 0), axis=0)
        within = jnp.cumsum(q_onehot, axis=0) - q_onehot
        ranked = jnp.sum((within + before[None, :]) * q_onehot, axis=1)
        limits = jnp.sum(q_onehot * query_counts[None, :], axis=1)
        return ranked < limits

    lookup = jnp.dot(q_onehot.astype(jnp.bfloat16), query_table, preferred_element_type=jnp.float32)
    queries = (query_features.astype(jnp.float32) + lookup).astype(jnp.bfloat16)
    own_queries = columns((queries,), y)
    near_queries = over_near(columns((queries,), 1 - y))

    parts, out_near, out_far_other, out_near_other, near_queries = lax.optimization_barrier(
        (parts, out_near, out_far_other, out_near_other, near_queries)
    )
    attended, for_near = merge(y, parts, far)
    _, hops = lax.optimization_barrier((for_near, hops))
    hops[2] = hop(2, hops[1])
    from_near = over_near(for_near)
    kept = kept_queries()
    out_ids = jnp.stack([*places, y, x]).astype(jnp.int32)
    weights = [w_out, out_far, out_far_other, out_near, out_near_other]
    partial_value = project(out_ids, attended, from_near, weights)
    partial_value, hops = lax.optimization_barrier((partial_value, hops))
    kv_bands = [kv_own, kv_near]
    for k in early:
        kv_moved = by_shift(hops, k)
        kv_bands += [kv_moved, over_groups(kv_moved)]
    for step in range(3, far):
        hops[step] = hop(step, hops[step - 1])
    theirs = lax.ppermute(partial_value, "head", swap_perm(2))
    own_cols, normed, normed_other = normalise(
        place, partial_value, theirs, latent_array, norm_gain[None, :]
    )
    kv_at = [p, p ^ 1]
    for k in early + rest:
        kv_at += [((z + k) % far) * 2 + (y ^ other) for other in (x, 1 - x)]
    kv_ids = jnp.stack([place, *kv_at]).astype(jnp.int32)

    def cores(values):
        return [lax.ppermute(v, "head", swap_perm(2)) for v in values]

    def fold(mine, other):
        return latent_keys_values(kv_ids, mine, other, kv_bands)

    def arrival(hops, j):
        picked = None
        for at in range(far):
            came = [
                (step, way)
                for step in range(1, far)
                for way in (1, 0)
                if (at + step < far if way else at >= step)
            ]
            step, way = came[j - 1]
            value = hops[step][way]
            picked = value if picked is None else jnp.where(z == at, value, picked)
        return picked

    came = {0: [normed, normed]}
    came[1] = hop(1, came[0])
    normed_near = over_near(normed)
    hops, _ = lax.optimization_barrier((hops, normed))
    for k in rest:
        kv_moved = by_shift(hops, k)
        kv_bands += [kv_moved, over_groups(kv_moved)]
    came, kept = lax.optimization_barrier((came, kept))
    mine, other, keys_values = [normed, normed_near], [normed_other], []
    for step in range(1, far):
        fresh = arrival(came, step)
        fresh_near = over_near(fresh)
        if step + 1 < far:
            came[step + 1] = hop(step + 1, came[step])
            if step > 1:
                keys_values.append(fold(mine, other))
                mine, other = [], []
            came, mine, other, kv_bands, keys_values, fresh, fresh_near = (
                lax.optimization_barrier(
                    (came, mine, other, kv_bands, keys_values, fresh, fresh_near)
                )
            )
            if step == 1:
                mine += [fresh, fresh_near]
                other += cores(mine[1:])
            else:
                mine += [fresh, fresh_near]
                other += cores([fresh, fresh_near])
    keys_values.append(fold([*mine, fresh], [*other, *cores([fresh])]))
    near_state = decode(near_queries, keys_values, None, None)
    fresh_near, keys_values, near_state = lax.optimization_barrier(
        (fresh_near, keys_values, near_state)
    )
    keys_values.append(fold([fresh_near], cores([fresh_near])))
    near_state = decode(near_queries, keys_values[-1:], near_state, jnp.bfloat16)
    own_state = decode(own_queries, keys_values, None, jnp.float32)
    from_near = lax.ppermute(near_state, "pos", near).astype(jnp.float32)
    decoded = jnp.where(
        y == 0,
        jnp.concatenate([own_state, from_near], axis=1),
        jnp.concatenate([from_near, own_state], axis=1),
    )
    decoded = jnp.where(kept[:, None], decoded, 0.0)
    return (own_cols, decoded)


def on_device(sizes, *args):
    groups, pos, head = sizes
    enc_keys, latent_array, w_out, w_key = args[0], args[4], args[5], args[7]
    fits = (
        head == 2
        and pos % 2 == 0
        and pos > 4
        and groups % 2 == 0
        and enc_keys.shape[1] % (4 * HEAD_DIM) == 0
        and 3 * enc_keys.shape[1] <= 2 * HEAD_DIM * EXTRA
        and enc_keys.shape[0] % LANES == 0
        and enc_keys.shape[0] <= enc_keys.shape[1]
        and w_key.shape[0] % LANES == 0
        and w_out.shape[0] % (2 * LANES) == 0
        and w_out.shape[1] % LANES == 0
        and latent_array.shape[0] % LANES == 0
    )
    if fits:
        return fast_on_device((groups, pos), *args)
    return plain_on_device(*args)


def solution(mesh):
    return jax.shard_map(
        functools.partial(on_device, tuple(mesh.shape[a] for a in ("groups", "pos", "head"))),
        mesh=mesh,
        in_specs=(
            P(("groups", "pos"), "head"),
            P(("groups", "pos"), "head"),
            P(("groups", "pos")),
            P("groups", "head"),
            P(("groups", "pos"), None),
            P("head", "pos"),
            P(),
            P("pos", "head"),
            P("pos", "head"),
            P(("groups", "pos"), "head"),
            P(("groups", "pos")),
            P(None, "head"),
            P(None, "head"),
            P("groups"),
        ),
        out_specs=(P(("groups", "pos"), "head"), P(("groups", "pos"), "head")),
        check_vma=False,
    )
```

```python
import functools

import jax
import jax.numpy as jnp
from jax import lax
from jax.experimental import pallas as pl
from jax.experimental.pallas import tpu as pltpu
from jax.sharding import PartitionSpec as P

HEAD_DIM = 128


norm_eps = 1e-06


def prefix(shard, axis, combine, identity):
    peers, place = (lax.axis_size(axis), lax.axis_index(axis))
    everything = lax.all_gather(shard, axis)
    start = jnp.broadcast_to(jnp.asarray(identity, shard.dtype), shard.shape)

    def step(k, before):
        reached = k < place
        new = combine(before, everything[k])
        return jnp.where(reached, new, before)

    return lax.fori_loop(0, peers, step, start)


def plain_on_device(
    enc_keys,
    enc_values,
    input_ids,
    latent_queries,
    latent_array,
    w_out,
    norm_gain,
    w_key,
    w_value,
    query_features,
    query_ids,
    query_table,
    enc_bias,
    query_counts,
):
    tok_rows = enc_keys.shape[0]
    half_width = enc_keys.shape[1]
    local_heads = half_width // HEAD_DIM
    score_scale = HEAD_DIM ** (-0.5)
    modality = jnp.arange(enc_bias.shape[0], dtype=jnp.int32)
    in_onehot = (input_ids[:, None] == modality[None, :]).astype(jnp.float32)
    bias_rows = jnp.dot(in_onehot, enc_bias, precision=lax.Precision.HIGHEST)
    bias_heads = bias_rows.T[:, None, :]
    keys_split = enc_keys.reshape(tok_rows, local_heads, HEAD_DIM)
    values_split = enc_values.reshape(tok_rows, local_heads, HEAD_DIM)
    lat_total = latent_queries.shape[0]
    block_rows = min(512, lat_total)
    query_blocks = latent_queries.reshape(
        lat_total // block_rows, block_rows, local_heads, HEAD_DIM
    )

    def encode_block(block_queries):
        scores = (
            jnp.einsum(
                "nha,tha->hnt", block_queries, keys_split, preferred_element_type=jnp.float32
            )
            * score_scale
            + bias_heads
        )
        highest = jnp.max(scores, axis=2)
        weights = jnp.exp(scores - highest[:, :, None])
        totals = jnp.sum(weights, axis=2)
        summed = jnp.einsum(
            "hnt,tha->nha",
            weights.astype(jnp.bfloat16),
            values_split,
            preferred_element_type=jnp.float32,
        )
        return (highest.T, totals.T, summed.reshape(block_rows, half_width))

    block_max, block_tot, block_acc = lax.map(encode_block, query_blocks)
    row_highest = block_max.reshape(lat_total, local_heads)
    row_totals = block_tot.reshape(lat_total, local_heads)
    row_sums = block_acc.reshape(lat_total, half_width)
    own_rows = latent_array.shape[0]
    global_max = lax.pmax(row_highest, "pos")
    factor = jnp.exp(row_highest - global_max)
    scaled_sums = (row_sums.reshape(lat_total, local_heads, HEAD_DIM) * factor[:, :, None]).reshape(
        lat_total, half_width
    )
    totals, summed = (
        lax.psum_scatter(row_totals * factor, "pos", scatter_dimension=0, tiled=True),
        lax.psum_scatter(scaled_sums, "pos", scatter_dimension=0, tiled=True),
    )
    summed = summed.reshape(own_rows, local_heads, HEAD_DIM)
    attended = (summed / totals[:, :, None]).reshape(own_rows, half_width).astype(jnp.bfloat16)
    partial_value = jnp.dot(
        attended,
        lax.all_gather(w_out, "pos", axis=1, tiled=True),
        preferred_element_type=jnp.float32,
    )
    offset = lax.axis_index("head") * half_width
    projected = lax.psum(partial_value, "head")
    updated = latent_array.astype(jnp.float32) + projected
    mean_square = jnp.mean(updated * updated, axis=1, keepdims=True)
    normed_full = updated * lax.rsqrt(mean_square + norm_eps) * norm_gain
    normed = normed_full.astype(jnp.bfloat16)
    own_cols = lax.dynamic_slice_in_dim(normed_full, offset, half_width, 1)
    pieces = (
        lax.all_gather(w_key, "pos", axis=0, tiled=True),
        lax.all_gather(w_value, "pos", axis=0, tiled=True),
    )
    key_sum = jnp.dot(normed, pieces[0], preferred_element_type=jnp.float32)
    value_sum = jnp.dot(normed, pieces[1], preferred_element_type=jnp.float32)
    latent_keys = key_sum.astype(jnp.bfloat16)
    latent_values = value_sum.astype(jnp.bfloat16)
    q_onehot = (query_ids[:, None] == modality[None, :]).astype(jnp.int32)
    local_counts = jnp.sum(q_onehot, axis=0)
    before = prefix(
        local_counts, "pos", lambda earlier, later: earlier + later, jnp.zeros_like(local_counts)
    )
    within = jnp.cumsum(q_onehot, axis=0) - q_onehot
    ranked = jnp.sum((within + before[None, :]) * q_onehot, axis=1)
    limits = jnp.sum(q_onehot * query_counts[None, :], axis=1)
    kept_rows = ranked < limits
    lookup = jnp.dot(q_onehot.astype(jnp.bfloat16), query_table, preferred_element_type=jnp.float32)
    queries = (
        (query_features.astype(jnp.float32) + lookup)
        .astype(jnp.bfloat16)
        .reshape(tok_rows, local_heads, HEAD_DIM)
    )

    def fold_rows(running, key_rows, value_rows):
        running_max, running_tot, running_acc = running
        key_heads = key_rows.reshape(key_rows.shape[0], local_heads, HEAD_DIM)
        value_heads = value_rows.reshape(value_rows.shape[0], local_heads, HEAD_DIM)
        scores = (
            jnp.einsum("tha,rha->htr", queries, key_heads, preferred_element_type=jnp.float32)
            * score_scale
        )
        new_max = jnp.maximum(running_max, jnp.max(scores, axis=2))
        fade = jnp.exp(running_max - new_max)
        weights = jnp.exp(scores - new_max[:, :, None])
        new_tot = running_tot * fade + jnp.sum(weights, axis=2)
        new_acc = running_acc * fade[:, :, None] + jnp.einsum(
            "htr,rha->hta",
            weights.astype(jnp.bfloat16),
            value_heads,
            preferred_element_type=jnp.float32,
        )
        return (new_max, new_tot, new_acc)

    start_state = (
        jnp.full((local_heads, tok_rows), -jnp.inf, jnp.float32),
        jnp.zeros((local_heads, tok_rows), jnp.float32),
        jnp.zeros((local_heads, tok_rows, HEAD_DIM), jnp.float32),
    )
    running = start_state
    pieces = (
        lax.all_gather(latent_keys, "pos", axis=0, tiled=True),
        lax.all_gather(latent_values, "pos", axis=0, tiled=True),
    )
    row_count = pieces[0].shape[0]
    key_blocks = pieces[0].reshape(row_count // 512, 512, half_width)
    value_blocks = pieces[1].reshape(row_count // 512, 512, half_width)

    def scan_step(state, pair):
        return (fold_rows(state, pair[0], pair[1]), None)

    running, ignored = lax.scan(scan_step, running, (key_blocks, value_blocks))
    final_max, final_tot, final_acc = running
    dec_heads = final_acc / final_tot[:, :, None]
    dec_rows = jnp.transpose(dec_heads, (1, 0, 2)).reshape(tok_rows, half_width)
    decoded = jnp.where(kept_rows[:, None], dec_rows, 0.0)
    return (own_cols, decoded)


LANES = 128
EXTRA = 16
BIG = 56
LOG2E = 1.4426950408889634
EXP2_SCALE = LOG2E * HEAD_DIM**-0.5
NT = (((1,), (1,)), ((), ()))


def params(mib):
    return pltpu.CompilerParams(vmem_limit_bytes=mib << 20)


def cost(flops, nbytes, exps=0):
    return pl.CostEstimate(flops=int(flops), bytes_accessed=int(nbytes), transcendentals=int(exps))


def whole(shape):
    return pl.BlockSpec(shape, lambda *args: (0,) * len(shape))


def encode_kernel(ids_ref, q_ref, k_ref, v_ref, extra_ref, near_ref, bias_ref, out_ref):
    rows, width = q_ref.shape
    tokens = k_ref.shape[0]
    heads = width // HEAD_DIM
    ones = jnp.ones((tokens, LANES), jnp.bfloat16)
    kinds = [
        extra_ref[...].astype(jnp.float32)[:1, :tokens],
        near_ref[tokens:, :].astype(jnp.float32)[:1, :tokens],
    ]
    lane = lax.broadcasted_iota(jnp.int32, (rows, LANES), 1)
    lse_all = jnp.zeros((rows, LANES), jnp.float32)
    for h in range(heads):
        cols = slice(h * HEAD_DIM, (h + 1) * HEAD_DIM)
        late = slice(width + h * HEAD_DIM, width + (h + 1) * HEAD_DIM)
        pairs = [
            (k_ref[:, cols], v_ref[:, cols]),
            (near_ref[:tokens, cols], near_ref[:tokens, late]),
        ]
        top = acc = None
        for (keys, values), kind in zip(pairs, kinds):
            bias = jnp.zeros_like(kind)
            for m in range(bias_ref.shape[0]):
                bias = jnp.where(kind == m, bias_ref[m, h] * LOG2E, bias)
            scores = lax.dot_general(q_ref[:, cols], keys, NT, preferred_element_type=jnp.float32)
            scores = scores * EXP2_SCALE + bias
            new_top = jnp.max(scores, axis=1, keepdims=True)
            if top is not None:
                new_top = jnp.maximum(top, new_top)
            weights = jnp.exp2(scores - new_top).astype(jnp.bfloat16)
            summed = jnp.dot(
                weights, jnp.concatenate([values, ones], axis=1), preferred_element_type=jnp.float32
            )
            if top is not None:
                summed = summed + acc * jnp.exp2(top - new_top)
            top, acc = new_top, summed
        totals = acc[:, HEAD_DIM:]
        out_ref[:rows, cols] = (acc[:, :HEAD_DIM] / totals).astype(jnp.bfloat16)
        lse_all = jnp.where(lane % heads == h, top + jnp.log2(totals), lse_all)
    lse = lse_all.T[:EXTRA, :]
    high = lse.astype(jnp.bfloat16).astype(jnp.float32)
    mid = (lse - high).astype(jnp.bfloat16).astype(jnp.float32)
    low = lse - high - mid
    row = lax.broadcasted_iota(jnp.int32, lse.shape, 0)
    terms = jnp.where(row < heads, high, jnp.where(row < 2 * heads, mid, low))
    out_ref[rows:, :] = terms.astype(jnp.bfloat16)


def encode(which, queries, keys, values, extra, near, bias, rows):
    tokens = keys.shape[0]
    width = keys.shape[1] // 2
    blocks = queries.shape[0] // rows
    half = pl.BlockSpec((tokens, width), lambda i, ids: (0, ids[0]))
    grid_spec = pltpu.PrefetchScalarGridSpec(
        num_scalar_prefetch=1,
        grid=(blocks,),
        in_specs=[
            pl.BlockSpec((rows, width), lambda i, ids: (i, ids[0])),
            half,
            half,
            whole(extra.shape),
            whole(near.shape),
            pl.BlockSpec(memory_space=pltpu.SMEM),
        ],
        out_specs=pl.BlockSpec((rows + EXTRA, width), lambda i, ids: (i, 0)),
    )
    return pl.pallas_call(
        encode_kernel,
        grid_spec=grid_spec,
        out_shape=jax.ShapeDtypeStruct((blocks * (rows + EXTRA), width), jnp.bfloat16),
        compiler_params=params(BIG),
        cost_estimate=cost(
            16 * blocks * rows * tokens * width, 8 * tokens * width, blocks * rows * tokens * 8
        ),
        name="encode_rows",
    )(which.reshape(1), queries, keys, values, extra, near, bias)


def merge_kernel(count, ids_ref, parts_ref, mine_ref, near_ref, all_ref):
    rows, width = all_ref.shape
    long = rows + EXTRA
    parts = [parts_ref.at[i * long : (i + 1) * long, :] for i in range(count)]
    heads = width // HEAD_DIM
    stats = [v[rows:, :].astype(jnp.float32).T for v in parts]
    for h in range(heads):
        cols = slice(h * HEAD_DIM, (h + 1) * HEAD_DIM)
        lses = [
            s[:, h : h + 1] + s[:, heads + h : heads + h + 1] + s[:, 2 * heads + h : 2 * heads + h + 1]
            for s in stats
        ]
        top = functools.reduce(jnp.maximum, lses)
        factors = [jnp.exp2(v - top) for v in lses]
        inverse = 1.0 / functools.reduce(jnp.add, factors)
        merged = functools.reduce(
            jnp.add,
            [v[:rows, cols].astype(jnp.float32) * (f * inverse) for v, f in zip(parts, factors)],
        )
        all_ref[:, cols] = merged.astype(jnp.bfloat16)
    own = rows // 2
    mine_ref[...] = all_ref[pl.ds(pl.multiple_of(ids_ref[0] * own, own), own), :]
    near_ref[...] = all_ref[pl.ds(pl.multiple_of((1 - ids_ref[0]) * own, own), own), :]


def merge(which, parts, count):
    long, width = parts.shape[0] // count, parts.shape[1]
    rows = long - EXTRA
    grid_spec = pltpu.PrefetchScalarGridSpec(
        num_scalar_prefetch=1,
        grid=(1,),
        in_specs=[whole(parts.shape)],
        out_specs=[whole((rows // 2, width))] * 2,
        scratch_shapes=[pltpu.VMEM((rows, width), jnp.bfloat16)],
    )
    return pl.pallas_call(
        functools.partial(merge_kernel, count),
        grid_spec=grid_spec,
        out_shape=[jax.ShapeDtypeStruct((rows // 2, width), jnp.bfloat16)] * 2,
        compiler_params=params(32),
        cost_estimate=cost(8 * rows * width, 10 * rows * width),
        name="merge_rows",
    )(which.reshape(1), parts)


def project_kernel(far, ids_ref, mine_ref, near_ref, *refs):
    w_ref, far_ref, far_other_ref, near_w_ref, near_other_ref, out_ref, att_ref = refs
    part = mine_ref.shape[1]
    first = ids_ref[2 * far]
    att_ref[:, pl.ds(pl.multiple_of(first * part, part), part)] = mine_ref[...]
    att_ref[:, pl.ds(pl.multiple_of((1 - first) * part, part), part)] = near_ref[...]
    cols = w_ref.shape[1]
    depth = att_ref.shape[1] // 2
    share = ids_ref[2 * far + 1]
    halves = [
        att_ref[:, pl.ds(pl.multiple_of(v * depth, depth), depth)] for v in (share, 1 - share)
    ]

    def place(slot, value):
        out_ref[:, pl.ds(pl.multiple_of(ids_ref[slot] * cols, cols), cols)] = value

    for slot, own_ref in ((0, w_ref), (far, near_w_ref)):
        own = own_ref[: 2 * depth, :]
        place(slot, jnp.dot(att_ref[...], own, preferred_element_type=jnp.float32))
    for k in range(far - 1):
        start = k * (depth + EXTRA)
        band = slice(start, start + depth)
        near_band = slice(start + 2 * depth + EXTRA, start + 3 * depth + EXTRA)
        for slot, weights in (
            (1 + k, (far_ref[band, :], far_other_ref[band, :])),
            (far + 1 + k, (near_w_ref[near_band, :], near_other_ref[band, :])),
        ):
            terms = [
                jnp.dot(v, w, preferred_element_type=jnp.float32) for v, w in zip(halves, weights)
            ]
            place(slot, terms[0] + terms[1])


def project(ids, mine, near, weights):
    rows, part = mine.shape
    far = (ids.shape[0] - 2) // 2
    out_cols = 2 * far * weights[0].shape[1]
    grid_spec = pltpu.PrefetchScalarGridSpec(
        num_scalar_prefetch=1,
        grid=(1,),
        in_specs=[whole(v.shape) for v in (mine, near, *weights)],
        out_specs=whole((rows, out_cols)),
        scratch_shapes=[pltpu.VMEM((rows, 2 * part), jnp.bfloat16)],
    )
    return pl.pallas_call(
        functools.partial(project_kernel, far),
        grid_spec=grid_spec,
        out_shape=jax.ShapeDtypeStruct((rows, out_cols), jnp.float32),
        compiler_params=params(BIG),
        cost_estimate=cost(4 * rows * part * out_cols, 4 * part * out_cols + 4 * rows * out_cols),
        name="project_rows",
    )(ids, mine, near, *weights)


def norm_kernel(
    ids_ref, mine_ref, theirs_ref, latent_ref, gain_ref, out_ref, normed_ref, other_ref, full_ref
):
    updated = latent_ref[...].astype(jnp.float32) + (mine_ref[...] + theirs_ref[...])
    mean_square = jnp.mean(updated * updated, axis=1, keepdims=True)
    full_ref[...] = updated * lax.rsqrt(mean_square + norm_eps) * gain_ref[...]
    half = out_ref.shape[1]
    own = full_ref[:, pl.ds(pl.multiple_of(ids_ref[0] * half, half), half)]
    out_ref[...] = own
    normed_ref[...] = own.astype(jnp.bfloat16)
    other = full_ref[:, pl.ds(pl.multiple_of((1 - ids_ref[0]) * half, half), half)]
    other_ref[...] = other.astype(jnp.bfloat16)


def normalise(place, mine, theirs, latent_array, gain):
    rows, width = mine.shape
    half = width // 2
    grid_spec = pltpu.PrefetchScalarGridSpec(
        num_scalar_prefetch=1,
        grid=(1,),
        in_specs=[whole((rows, width))] * 3 + [whole((1, width))],
        out_specs=[whole((rows, half))] * 3,
        scratch_shapes=[pltpu.VMEM((rows, width), jnp.float32)],
    )
    return pl.pallas_call(
        norm_kernel,
        grid_spec=grid_spec,
        out_shape=[
            jax.ShapeDtypeStruct((rows, half), jnp.float32),
            jax.ShapeDtypeStruct((rows, half), jnp.bfloat16),
            jax.ShapeDtypeStruct((rows, half), jnp.bfloat16),
        ],
        compiler_params=params(BIG),
        cost_estimate=cost(6 * rows * width, 13 * rows * width),
        name="norm_rows",
    )(place.reshape(1), mine, theirs, latent_array, gain)


def latents_kernel(pieces, ids_ref, *refs):
    mine, theirs = refs[:pieces], refs[pieces : 2 * pieces]
    w_refs, (out_ref, normed_ref, w_ref) = refs[2 * pieces : -3], refs[-3:]
    rows, half = mine[0].shape
    slots = ids_ref.shape[0] - 1
    depth = 2 * half // slots

    @pl.when(pl.program_id(0) == 0)
    def arrange():
        for j in range(slots):
            at = ids_ref[1 + j]
            start = pl.multiple_of((at % (slots // 2)) * depth, depth)

            def copy(pieces):
                for r, piece in enumerate(pieces):
                    normed_ref[r * rows : (r + 1) * rows, j * depth : (j + 1) * depth] = piece[
                        :, pl.ds(start, depth)
                    ]

            is_mine = at // (slots // 2) == ids_ref[0]
            pl.when(is_mine)(functools.partial(copy, mine))
            pl.when(jnp.logical_not(is_mine))(functools.partial(copy, theirs))

    start, block = 0, w_ref.shape[1]
    for band in w_refs:
        columns = pl.ds(pl.multiple_of(pl.program_id(0) * block, block), block)
        w_ref[start : start + band.shape[0], :] = band[:, columns]
        start += band.shape[0]
    out_ref[...] = jnp.dot(
        normed_ref[...], w_ref[...], preferred_element_type=jnp.float32
    ).astype(jnp.bfloat16)


def latent_keys_values(ids, mine, theirs, bands):
    pieces = len(mine)
    rows, half = mine[0].shape
    width = bands[0].shape[1]
    block = min(512, width)
    total = sum(band.shape[0] for band in bands)
    grid_spec = pltpu.PrefetchScalarGridSpec(
        num_scalar_prefetch=1,
        grid=(width // block,),
        in_specs=[pl.BlockSpec(memory_space=pltpu.VMEM)] * (2 * pieces + len(bands)),
        out_specs=pl.BlockSpec((rows * pieces, block), lambda i, ids: (0, i)),
        scratch_shapes=[
            pltpu.VMEM((rows * pieces, total), jnp.bfloat16),
            pltpu.VMEM((total, block), jnp.bfloat16),
        ],
    )
    return pl.pallas_call(
        functools.partial(latents_kernel, pieces),
        grid_spec=grid_spec,
        out_shape=jax.ShapeDtypeStruct((rows * pieces, width), jnp.bfloat16),
        compiler_params=params(24),
        cost_estimate=cost(2 * rows * pieces * total * width, 2 * total * width),
        name="latent_keys_values",
    )(ids, *mine, *theirs, *bands)


def row_chunks(lengths, size):
    chunks, open_chunk, room = [], [], size
    for i, length in enumerate(lengths):
        start = 0
        while start < length:
            take = min(room, length - start)
            open_chunk.append((i, start, start + take))
            start, room = start + take, room - take
            if room == 0:
                chunks.append(open_chunk)
                open_chunk, room = [], size
    return chunks + ([open_chunk] if open_chunk else [])


def decode_kernel(parts, first, last, q_ref, *refs):
    k_refs, v_refs, rest = refs[:parts], refs[parts : 2 * parts], refs[2 * parts :]
    rows = q_ref.shape[0]
    heads = q_ref.shape[1] // HEAD_DIM
    lane = lax.broadcasted_iota(jnp.int32, (rows, LANES), 1)
    lse_all = jnp.zeros((rows, LANES), jnp.float32)

    def gathered(sources, chunk, cols):
        rows = [sources[i][start:stop, cols] for i, start, stop in chunk]
        return rows[0] if len(rows) == 1 else jnp.concatenate(rows)

    for h in range(heads):
        cols = slice(h * HEAD_DIM, (h + 1) * HEAD_DIM)
        top = acc = None
        if not first:
            top = jnp.max(
                jnp.where(lane % heads == h, rest[1][...], -jnp.inf), axis=1, keepdims=True
            )
            acc = jnp.concatenate([rest[0][:, cols], jnp.ones((rows, LANES), jnp.float32)], axis=1)
        for chunk in row_chunks([k.shape[0] for k in k_refs], 512):
            keys, values = gathered(k_refs, chunk, cols), gathered(v_refs, chunk, cols)
            scores = lax.dot_general(q_ref[:, cols], keys, NT, preferred_element_type=jnp.float32)
            scores = scores * EXP2_SCALE
            new_top = jnp.max(scores, axis=1, keepdims=True)
            if top is not None:
                new_top = jnp.maximum(top, new_top)
            weights = jnp.exp2(scores - new_top).astype(jnp.bfloat16)
            summed = jnp.dot(
                weights,
                jnp.concatenate([values, jnp.ones((keys.shape[0], LANES), jnp.bfloat16)], axis=1),
                preferred_element_type=jnp.float32,
            )
            if top is not None:
                summed = summed + acc * jnp.exp2(top - new_top)
            top, acc = new_top, summed
        totals = acc[:, HEAD_DIM:]
        out_ref = rest[-1] if last else rest[-2]
        out_ref[:, cols] = (acc[:, :HEAD_DIM] / totals).astype(out_ref.dtype)
        if not last:
            lse_all = jnp.where(lane % heads == h, top + jnp.log2(totals), lse_all)
    if not last:
        rest[-1][...] = lse_all


def decode(queries, keys_values, state, out_type):
    first, last = state is None, out_type is not None
    tokens, width = queries.shape
    latents = sum(v.shape[0] for v in keys_values)
    pair = min(2 * HEAD_DIM, width)
    steps = width // pair
    narrow = pl.BlockSpec((tokens, pair), lambda i: (0, i))
    sums = pl.BlockSpec((tokens, LANES), lambda i: (0, i))
    keys = [pl.BlockSpec((v.shape[0], pair), lambda i: (0, i)) for v in keys_values]
    values = [pl.BlockSpec((v.shape[0], pair), lambda i: (0, steps + i)) for v in keys_values]
    if last:
        out_specs, out_shape = narrow, jax.ShapeDtypeStruct((tokens, width), out_type)
    else:
        out_specs = [narrow, sums]
        out_shape = [
            jax.ShapeDtypeStruct((tokens, width), jnp.float32),
            jax.ShapeDtypeStruct((tokens, steps * LANES), jnp.float32),
        ]
    return pl.pallas_call(
        functools.partial(decode_kernel, len(keys_values), first, last),
        grid=(steps,),
        in_specs=[narrow, *keys, *values, *([] if first else [narrow, sums])],
        out_specs=out_specs,
        out_shape=out_shape,
        compiler_params=params(BIG),
        cost_estimate=cost(
            16 * tokens * latents * width,
            4 * latents * width + 6 * tokens * width,
            tokens * latents * (width // HEAD_DIM),
        ),
        name="decode_rows",
    )(queries, *keys_values, *keys_values, *([] if first else state))


def swap_perm(size):
    return [(i, i ^ 1) for i in range(size)]


def shift_perm(size, k):
    far = size // 2
    return [(((z + k) % far) * 2 + y, z * 2 + y) for z in range(far) for y in range(2)]


def hop_perm(size, step, way):
    far = size // 2
    moves = [(z, z + 1) for z in range(step - 1, far - 1)]
    if way < 0:
        moves = [(far - 1 - a, far - 1 - b) for a, b in moves]
    return [(a * 2 + y, b * 2 + y) for a, b in moves for y in range(2)]


def fast_on_device(
    sizes,
    enc_keys,
    enc_values,
    input_ids,
    latent_queries,
    latent_array,
    w_out,
    norm_gain,
    w_key,
    w_value,
    query_features,
    query_ids,
    query_table,
    enc_bias,
    query_counts,
):
    groups, pos = sizes
    p = lax.axis_index("pos")
    place = lax.axis_index("head")
    rows = latent_array.shape[0]
    tokens, half_width = enc_keys.shape
    heads = half_width // HEAD_DIM
    mods = enc_bias.shape[0]
    modality = jnp.arange(mods, dtype=jnp.int32)
    far, z, y, x = pos // 2, p // 2, p % 2, lax.axis_index("groups") % 2
    near = swap_perm(pos)

    def over_groups(value):
        return lax.ppermute(value, "groups", swap_perm(groups))

    def over_near(value):
        return lax.ppermute(value, "pos", near)

    def over_far(value, k):
        return lax.ppermute(value, "pos", shift_perm(pos, k))

    def hop(step, pair):
        return [
            lax.ppermute(v, "pos", hop_perm(pos, step, way)) for v, way in zip(pair, (1, -1))
        ]

    def by_shift(hops, k):
        return jnp.where(z + k < far, hops[k][1], hops[far - k][0])

    q_onehot = (query_ids[:, None] == modality[None, :]).astype(jnp.int32)
    local_counts = jnp.sum(q_onehot, axis=0)

    def columns(arrays, which):
        part = half_width // 2
        return jnp.concatenate(
            [lax.dynamic_slice_in_dim(v, which * part, part, 1) for v in arrays], axis=1
        )

    extra = jnp.pad(input_ids[None, :], ((0, EXTRA - 1), (0, half_width - tokens)))
    extra = extra.astype(jnp.bfloat16)
    near_inputs = over_near(
        jnp.concatenate([columns((enc_keys, enc_values), 1 - y), extra], axis=0)
    )

    out_half, out_cols = w_out.shape[0] // 2, w_out.shape[1]
    counted = jnp.concatenate([local_counts // 16, local_counts % 16])
    counted = jnp.pad(counted[None, :], ((0, EXTRA - 1), (0, out_cols - 2 * mods)))
    counted = counted.astype(jnp.bfloat16)

    out_sent = jnp.concatenate(
        [lax.dynamic_slice_in_dim(w_out, x * out_half, out_half, 0), counted]
    )
    out_far = [over_far(out_sent, k) for k in range(1, far)]
    places = [((z + k) % far) * 2 + (y ^ j) for j in range(2) for k in range(far)]
    kv_for_near = columns((w_key, w_value), 1 - y)
    near_inputs, out_far, kv_for_near = lax.optimization_barrier(
        (near_inputs, out_far, kv_for_near)
    )

    kv_own = columns((w_key, w_value), y)
    kv_near = over_near(kv_for_near)

    head_bias = lax.dynamic_slice_in_dim(enc_bias, y * (heads // 2), heads // 2, 1)
    parts = encode(
        y, latent_queries, enc_keys, enc_values, extra, near_inputs, head_bias, 2 * rows
    )
    kv_near, out_far, parts = lax.optimization_barrier((kv_near, out_far, parts))
    kv_sent = jnp.where(x == 0, kv_own, kv_near)
    hops = {0: [kv_sent, kv_sent]}
    hops[1] = hop(1, hops[0])
    early = [k for k in range(1, far) if max(k, far - k) < 3]
    rest = [k for k in range(1, far) if k not in early]
    out_far = jnp.concatenate(out_far)
    out_far_other = over_groups(out_far)
    out_near = over_near(jnp.concatenate([w_out, counted, out_far]))
    out_near_other = over_groups(out_near[w_out.shape[0] + EXTRA :])
    columns_of_slice = [[2 * i + j for i in range(far)] for j in range(2)]
    parts = lax.all_to_all(parts, "pos", 0, 0, axis_index_groups=columns_of_slice, tiled=True)

    def kept_queries():
        far_counts = out_far.reshape(far - 1, out_half + EXTRA, out_cols)[:, out_half, : 2 * mods]
        near_counts = out_near.reshape(-1, EXTRA, out_cols)[:, 0, : 2 * mods]
        at = [w_out.shape[0] // EXTRA]
        at += [at[0] + k * (out_half // EXTRA + 1) for k in range(1, far)]
        near_counts = jnp.concatenate([near_counts[i : i + 1] for i in at])
        counts = jnp.concatenate([counted[:1, : 2 * mods], far_counts, near_counts])
        counts = counts.astype(jnp.int32)
        counts = counts[:, :mods] * 16 + counts[:, mods:]
        earlier = jnp.stack(places)[:, None] < p
        before = jnp.sum(jnp.where(earlier, counts, 0), axis=0)
        within = jnp.cumsum(q_onehot, axis=0) - q_onehot
        ranked = jnp.sum((within + before[None, :]) * q_onehot, axis=1)
        limits = jnp.sum(q_onehot * query_counts[None, :], axis=1)
        return ranked < limits

    lookup = jnp.dot(q_onehot.astype(jnp.bfloat16), query_table, preferred_element_type=jnp.float32)
    queries = (query_features.astype(jnp.float32) + lookup).astype(jnp.bfloat16)
    own_queries = columns((queries,), y)
    near_queries = over_near(columns((queries,), 1 - y))

    parts, out_near, out_far_other, out_near_other = lax.optimization_barrier(
        (parts, out_near, out_far_other, out_near_other)
    )
    attended, for_near = merge(y, parts, far)
    _, hops = lax.optimization_barrier((for_near, hops))
    hops[2] = hop(2, hops[1])
    from_near = over_near(for_near)
    kept = kept_queries()
    out_ids = jnp.stack([*places, y, x]).astype(jnp.int32)
    weights = [w_out, out_far, out_far_other, out_near, out_near_other]
    partial_value = project(out_ids, attended, from_near, weights)
    partial_value, hops, near_queries = lax.optimization_barrier(
        (partial_value, hops, near_queries)
    )
    kv_bands = [kv_own, kv_near]
    for k in early:
        kv_moved = by_shift(hops, k)
        kv_bands += [kv_moved, over_groups(kv_moved)]
    for step in range(3, far):
        hops[step] = hop(step, hops[step - 1])
    theirs = lax.ppermute(partial_value, "head", swap_perm(2))
    own_cols, normed, normed_other = normalise(
        place, partial_value, theirs, latent_array, norm_gain[None, :]
    )
    kv_at = [p, p ^ 1]
    for k in early + rest:
        kv_at += [((z + k) % far) * 2 + (y ^ other) for other in (x, 1 - x)]
    kv_ids = jnp.stack([place, *kv_at]).astype(jnp.int32)

    def cores(values):
        return [lax.ppermute(v, "head", swap_perm(2)) for v in values]

    def fold(mine, other):
        return latent_keys_values(kv_ids, mine, other, kv_bands)

    def arrival(hops, j):
        picked = None
        for at in range(far):
            came = [
                (step, way)
                for step in range(1, far)
                for way in (1, 0)
                if (at + step < far if way else at >= step)
            ]
            step, way = came[j - 1]
            value = hops[step][way]
            picked = value if picked is None else jnp.where(z == at, value, picked)
        return picked

    came = {0: [normed, normed]}
    came[1] = hop(1, came[0])
    normed_near = over_near(normed)
    hops, _ = lax.optimization_barrier((hops, normed))
    for k in rest:
        kv_moved = by_shift(hops, k)
        kv_bands += [kv_moved, over_groups(kv_moved)]
    came, kept = lax.optimization_barrier((came, kept))
    mine, other, keys_values = [normed, normed_near], [normed_other], []
    for step in range(1, far):
        fresh = arrival(came, step)
        fresh_near = over_near(fresh)
        if step + 1 < far:
            came[step + 1] = hop(step + 1, came[step])
            if step > 1:
                keys_values.append(fold(mine, other))
                mine, other = [], []
            came, mine, other, kv_bands, keys_values, fresh, fresh_near = (
                lax.optimization_barrier(
                    (came, mine, other, kv_bands, keys_values, fresh, fresh_near)
                )
            )
            if step == 1:
                mine += [fresh, fresh_near]
                other += cores(mine[1:])
            else:
                mine += [fresh, fresh_near]
                other += cores([fresh, fresh_near])
    keys_values.append(fold([*mine, fresh], [*other, *cores([fresh])]))
    near_state = decode(near_queries, keys_values, None, None)
    fresh_near, keys_values, near_state = lax.optimization_barrier(
        (fresh_near, keys_values, near_state)
    )
    keys_values.append(fold([fresh_near], cores([fresh_near])))
    near_state = decode(near_queries, keys_values[-1:], near_state, jnp.bfloat16)
    own_state = decode(own_queries, keys_values, None, jnp.float32)
    from_near = lax.ppermute(near_state, "pos", near).astype(jnp.float32)
    decoded = jnp.where(
        y == 0,
        jnp.concatenate([own_state, from_near], axis=1),
        jnp.concatenate([from_near, own_state], axis=1),
    )
    decoded = jnp.where(kept[:, None], decoded, 0.0)
    return (own_cols, decoded)


def on_device(sizes, *args):
    groups, pos, head = sizes
    enc_keys, latent_array, w_out, w_key = args[0], args[4], args[5], args[7]
    fits = (
        head == 2
        and pos % 2 == 0
        and pos > 4
        and groups % 2 == 0
        and enc_keys.shape[1] % (4 * HEAD_DIM) == 0
        and 3 * enc_keys.shape[1] <= 2 * HEAD_DIM * EXTRA
        and enc_keys.shape[0] % LANES == 0
        and enc_keys.shape[0] <= enc_keys.shape[1]
        and w_key.shape[0] % LANES == 0
        and w_out.shape[0] % (2 * LANES) == 0
        and w_out.shape[1] % LANES == 0
        and latent_array.shape[0] % LANES == 0
    )
    if fits:
        return fast_on_device((groups, pos), *args)
    return plain_on_device(*args)


def solution(mesh):
    return jax.shard_map(
        functools.partial(on_device, tuple(mesh.shape[a] for a in ("groups", "pos", "head"))),
        mesh=mesh,
        in_specs=(
            P(("groups", "pos"), "head"),
            P(("groups", "pos"), "head"),
            P(("groups", "pos")),
            P("groups", "head"),
            P(("groups", "pos"), None),
            P("head", "pos"),
            P(),
            P("pos", "head"),
            P("pos", "head"),
            P(("groups", "pos"), "head"),
            P(("groups", "pos")),
            P(None, "head"),
            P(None, "head"),
            P("groups"),
        ),
        out_specs=(P(("groups", "pos"), "head"), P(("groups", "pos"), "head")),
        check_vma=False,
    )
```
